32 devices in a mesh: groups: 2 (over y), latent: 8 (over z, x), hidden: 2 (over core).
Axes of the slice: x: 2, y: 2, z: 4, core: 2. Of those that a mesh axis runs over, the one named last changes fastest.
Arguments:
- input_codes: int32 [288, 2304], P('groups', ('latent', 'hidden')), parts along dimension 0, may hold values from -128 to 127
- cotangent_codes: int32 [288, 2304], P('groups', ('latent', 'hidden')), parts along dimension 0, may hold values from -128 to 127
- dictionary: bfloat16 [8192, 2304], P(('latent', 'hidden')), as said below
- encoder_bias: float32 [8192], P(('latent', 'hidden')), may hold values from -12 to 0, as said below
- decoder_bias: float32 [2304], replicated, may hold values from -1.2 to 1.2
- norm_gain: float32 [2304], replicated, may hold values from 0.1 to 1.9
- gate_weight: bfloat16 [8192, 2304], P(('latent', 'hidden')), may hold values from -0.1875 to 0.1875
- up_weight: bfloat16 [8192, 2304], P(('latent', 'hidden')), may hold values from -0.1875 to 0.1875
- down_weight: bfloat16 [8192, 2304], P(('latent', 'hidden')), may hold values from -0.09375 to 0.09375
Outputs:
- block_output: bfloat16 [288, 2304], P('groups', ('latent', 'hidden')), parts along dimension 0
- dictionary_grad: bfloat16 [8192, 4608], P(('latent', 'hidden'), 'groups'), parts along dimension 1
The draws below stay inside these ranges and needn't reach their ends.
There are 2 independent parts, one for each index of `groups`. The reference program is written for one: setup_inputs(seed, part) draws one part's arguments, and reference() takes and returns one part's arrays. A program takes and returns all parts, laid end to end along the dimension named above; an argument that names none is the same for every part. Nothing has to cross between parts.
Inputs may be any that keep to these rules, and one draw needn't show every extreme that they name: `dictionary`: every entry is a whole multiple of 2^-10, at most 119 such units in magnitude. `encoder_bias`: every entry is a whole multiple of 2^-16.
All inputs are finite; a program needn't handle non-finite values.
Results may differ from the reference program's by a relative error of at most 0.0072.
Values may be sent and summed in bfloat16 or wider, within the bound.
No kernel may reach another device: no remote copies, remote signals or barrier semaphores. Data moves between devices by JAX's collectives and lax.ppermute only.
A program may use at most 64 MiB of HBM per device.

```python
import math
import jax
import jax.numpy as jnp
from jax import lax

D = 2304
FF = 8192
LAT = 8192
B = 144


INPUT_SPREAD = 1.1547


def upper_tail(point):
    factor = 1.0 / (1.0 + 0.3275911 * point / math.sqrt(2.0))
    series = factor * (0.254829592 + factor * (-0.284496736 + factor * (1.421413741 + factor * (-1.453152027 + factor * 1.061405429))))
    return 0.5 * series * math.exp(-0.5 * point * point)


def normal_quantile(upper_share):
    lower_end = 0.0
    upper_end = 10.0
    for counter in range(80):
        middle = 0.5 * (lower_end + upper_end)
        if upper_tail(middle) > upper_share:
            lower_end = middle
        else:
            upper_end = middle
    return 0.5 * (lower_end + upper_end)


def row_limits():
    position = jnp.arange(LAT, dtype=jnp.int32)
    return 16 + position * 48 // LAT


def draw_dictionary(key, part):
    limits = row_limits()[:, None]
    integer_codes = jax.random.randint(key, (LAT, D), -limits, limits + 1)
    return (integer_codes.astype(jnp.float32) * 2.0 ** (-10)).astype(jnp.bfloat16)


def draw_encoder_bias(key, part):
    active_share = min(0.25, 400.0 / LAT)
    limits = row_limits().astype(jnp.float32)
    spread = INPUT_SPREAD * jnp.sqrt(limits * (limits + 1.0) / 3.0) * 2.0 ** (-10)
    depth = normal_quantile(active_share) * math.sqrt(D) * spread
    center_units = jnp.floor(depth * 65536.0)
    jitter_codes = jax.random.randint(key, (LAT,), -512, 513)
    jitter_units = jnp.floor(jitter_codes.astype(jnp.float32) * (center_units * 0.15 / 512.0))
    return (jitter_units - center_units) * 2.0 ** (-16)


def plant(drawn, rng, low, largest):
    longest = drawn.shape.index(max(drawn.shape))
    spots = []
    for shift in (0, 1):
        where = [jax.random.randint(jax.random.fold_in(rng, axis), (), 0, length) for axis, length in enumerate(drawn.shape)]
        where[longest] = (where[longest] + shift) % drawn.shape[longest]
        spots.append(tuple(where))
    return drawn.at[spots[0]].set(low).at[spots[1]].set(largest)


def spiked(values, key, source, target, shards_of, factor):
    owner, partner = [(jnp.arange(values.shape[dim]) // (values.shape[dim] // shards_of)).reshape([-1 if axis == dim else 1 for axis in range(values.ndim)]) for dim in (source, target)]
    chosen = jax.random.permutation(key, shards_of)[partner]
    strong = (owner == chosen) | (owner == (partner + shards_of // 2) % shards_of)
    return jnp.where(strong, factor * values, values)


def shard_levels(stream_key, extent, cuts, least, top_value):
    def one(axis_at, shards_of):
        steps = jax.random.uniform(jax.random.fold_in(jax.random.fold_in(stream_key, 6), axis_at), (shards_of,), jnp.float32, least / len(cuts), top_value / len(cuts))
        return jnp.repeat(jnp.exp(steps), extent[axis_at] // shards_of).reshape((-1,) + (1,) * (len(extent) - axis_at - 1))

    factor_of = one(*cuts[0])
    for cut in cuts[1:]:
        factor_of = factor_of * one(*cut)
    return factor_of


def bell_draw(stream_key, dims, width, most, shards=(), held_as=jnp.bfloat16):
    entries = jax.random.normal(stream_key, dims, jnp.float32) * width
    if len(shards) > 0:
        entries = shard_levels(stream_key, dims, shards, -0.22, 0.18) * entries
    return jnp.clip(entries, min=-most, max=most).astype(held_as)


def noise_with(stream_key, extent, width, reach, shards, heavy, held_as=jnp.bfloat16):
    entries = width * jax.random.normal(stream_key, extent, jnp.float32)
    if shards:
        entries = entries * shard_levels(stream_key, extent, shards, -0.22, 0.18)
    return jnp.clip(spiked(entries, jax.random.fold_in(stream_key, 3), *heavy), -reach, reach).astype(held_as)


def setup_inputs(seed: int = 0, part: int = 0) -> dict:
    splits = jax.random.split(jax.random.key(seed), 10)
    part_keys = jax.random.split(jax.random.fold_in(splits[9], part), 10)
    return {
        "input_codes": plant(jax.random.randint(part_keys[0], (B, D), -128, 128), jax.random.fold_in(part_keys[0], 1), -128, 127).astype(jnp.int32),
        "cotangent_codes": plant(jax.random.randint(part_keys[1], (B, D), -128, 128), jax.random.fold_in(part_keys[1], 1), -128, 127).astype(jnp.int32),
        "dictionary": draw_dictionary(jax.random.fold_in(splits[9], 71), part),
        "encoder_bias": draw_encoder_bias(jax.random.fold_in(splits[9], 71), part),
        "decoder_bias": bell_draw(splits[4], (D,), 0.2, 1.2, (), jnp.float32),
        "norm_gain": jnp.clip(1.0 + 0.18 * jax.random.normal(splits[5], (D,), jnp.float32), 0.1, 1.9),
        "gate_weight": noise_with(splits[6], (FF, D), D ** -0.5, 0.1875, ((0, 16),), (0, 1, 16, 2.0)),
        "up_weight": noise_with(splits[7], (FF, D), D ** -0.5, 0.1875, ((0, 16),), (0, 1, 16, 2.0)),
        "down_weight": noise_with(splits[8], (FF, D), FF ** -0.5, 0.09375, ((0, 16),), (0, 1, 16, 2.0)),
    }


CODE_STEP = 2.0 ** (-6)
NORM_EPSILON = 1e-06
GELU_ROOT = 0.7978845608028654
GELU_CUBIC = 0.044715
ACROSS = (((1,), (1,)), ((), ()))
DOWNWARD = (((0,), (0,)), ((), ()))

def gelu_parts(values):
    argument = GELU_ROOT * (values + GELU_CUBIC * values * values * values)
    tanh_value = jnp.tanh(argument)
    result = 0.5 * values * (1.0 + tanh_value)
    derivative = 0.5 * (1.0 + tanh_value) + 0.5 * values * (1.0 - tanh_value * tanh_value) * GELU_ROOT * (1.0 + 3.0 * GELU_CUBIC * values * values)
    return (result, derivative)

def reference(input_codes, cotangent_codes, dictionary, encoder_bias, decoder_bias, norm_gain, gate_weight, up_weight, down_weight):
    inputs = (input_codes.astype(jnp.float32) * CODE_STEP).astype(jnp.bfloat16)
    preact = lax.dot_general(inputs, dictionary, ACROSS, preferred_element_type=jnp.float32) + encoder_bias
    latents = jnp.maximum(preact, 0.0).astype(jnp.bfloat16)
    rebuilt = jnp.dot(latents, dictionary, preferred_element_type=jnp.float32) + decoder_bias
    inverse = lax.rsqrt(lax.optimization_barrier(jnp.sum(rebuilt * rebuilt, axis=1, keepdims=True)) / D + NORM_EPSILON)
    normed = (rebuilt * inverse * norm_gain).astype(jnp.bfloat16)
    gate_proj = lax.dot_general(normed, gate_weight, ACROSS, preferred_element_type=jnp.float32)
    up_proj = lax.dot_general(normed, up_weight, ACROSS, preferred_element_type=jnp.float32)
    gelu_value, gelu_slope = gelu_parts(gate_proj)
    hidden = (gelu_value * up_proj).astype(jnp.bfloat16)
    block_output = jnp.dot(hidden, down_weight, preferred_element_type=jnp.float32).astype(jnp.bfloat16)
    upstream = (cotangent_codes.astype(jnp.float32) * CODE_STEP).astype(jnp.bfloat16)
    hidden_grad = lax.dot_general(upstream, down_weight, ACROSS, preferred_element_type=jnp.float32)
    gate_grad = (hidden_grad * up_proj * gelu_slope).astype(jnp.bfloat16)
    up_grad = (hidden_grad * gelu_value).astype(jnp.bfloat16)
    normed_grad = jnp.dot(gate_grad, gate_weight, preferred_element_type=jnp.float32) + jnp.dot(up_grad, up_weight, preferred_element_type=jnp.float32)
    scaled = normed_grad * norm_gain
    inner_row = lax.optimization_barrier(jnp.sum(scaled * rebuilt, axis=1, keepdims=True))
    inverse_cube = inverse * inverse * inverse
    rebuilt_grad = (inverse * scaled - inverse_cube * rebuilt * (inner_row / D) + (rebuilt - inputs.astype(jnp.float32))).astype(jnp.bfloat16)
    latent_grad = lax.dot_general(rebuilt_grad, dictionary, ACROSS, preferred_element_type=jnp.float32)
    preact_grad = jnp.where(preact > 0.0, latent_grad, 0.0).astype(jnp.bfloat16)
    dictionary_grad = lax.dot_general(latents, rebuilt_grad, DOWNWARD, preferred_element_type=jnp.float32) + lax.dot_general(preact_grad, inputs, DOWNWARD, preferred_element_type=jnp.float32)
    return (block_output, dictionary_grad.astype(jnp.bfloat16))
```

```python
import jax
import jax.numpy as jnp
from jax import lax
from jax.sharding import PartitionSpec as P

CODE_STEP = 2.0 ** (-6)
NORM_EPSILON = 1e-06
GELU_ROOT = 0.7978845608028654
GELU_CUBIC = 0.044715
ACROSS = (((1,), (1,)), ((), ()))
DOWNWARD = (((0,), (0,)), ((), ()))
SUBLANES = 8
LANES = 128
DIRECT_LIMIT = 16


def gelu_parts(values):
    argument = GELU_ROOT * (values + GELU_CUBIC * values * values * values)
    tanh_value = jnp.tanh(argument)
    result = 0.5 * values * (1.0 + tanh_value)
    derivative = 0.5 * (1.0 + tanh_value) + 0.5 * values * (
        1.0 - tanh_value * tanh_value
    ) * GELU_ROOT * (1.0 + 3.0 * GELU_CUBIC * values * values)
    return (result, derivative)


def shift_by(value, axis, step):
    size = lax.axis_size(axis)
    return lax.ppermute(value, axis, [(i, (i + step) % size) for i in range(size)])


def pick(stack, index):
    return lax.dynamic_index_in_dim(stack, index, 0, keepdims=False)


def exchange_sum(stack, axis, direct):
    size = lax.axis_size(axis)
    if not direct or size > DIRECT_LIMIT:
        got = lax.all_to_all(stack, axis, 0, 0, tiled=False)
        return jnp.sum(got.astype(jnp.float32), axis=0)
    me = lax.axis_index(axis)
    got = [
        shift_by(pick(stack, lax.rem(me + step, size)), axis, step) for step in range(1, size)
    ]
    total = pick(stack, me).astype(jnp.float32)
    for term in got:
        total = total + term.astype(jnp.float32)
    return total


def collect(block, axis, direct):
    size = lax.axis_size(axis)
    if not direct or size > DIRECT_LIMIT:
        return lax.all_gather(block, axis, axis=0, tiled=False)
    me = lax.axis_index(axis)
    got = [block] + [shift_by(block, axis, step) for step in range(1, size)]
    stack = jnp.zeros((size,) + block.shape, block.dtype)
    for step, one in enumerate(got):
        stack = lax.dynamic_update_index_in_dim(stack, one, lax.rem(me + size - step, size), 0)
    return stack


def to_tiles(value, first, second):
    rows, columns = value.shape
    tiles = value.reshape(rows // SUBLANES, SUBLANES, columns // LANES, LANES)
    tiles = tiles.transpose(0, 2, 1, 3).reshape(-1, SUBLANES, LANES)
    count = tiles.shape[0]
    each = -(-count // (first * second))
    tiles = jnp.pad(tiles, ((0, each * first * second - count), (0, 0), (0, 0)))
    return tiles.reshape(first, second, each * SUBLANES, LANES)


def from_tiles(stack, rows, columns):
    count = (rows // SUBLANES) * (columns // LANES)
    tiles = stack.reshape(-1, SUBLANES, LANES)[:count]
    tiles = tiles.reshape(rows // SUBLANES, columns // LANES, SUBLANES, LANES)
    return tiles.transpose(0, 2, 1, 3).reshape(rows, columns)


def sum_over_all(partial_value, direct):
    rows, columns = partial_value.shape
    halves = to_tiles(partial_value, lax.axis_size("hidden"), lax.axis_size("latent"))
    half = exchange_sum(halves, "hidden", True)
    own = exchange_sum(half.astype(jnp.bfloat16), "latent", direct).astype(jnp.bfloat16)
    half_full = collect(own, "latent", direct)
    return from_tiles(collect(half_full, "hidden", True), rows, columns)


def gather_features(block, direct):
    rows, own = block.shape
    stack = collect(collect(block, "latent", direct), "hidden", True)
    return stack.transpose(2, 1, 0, 3).reshape(rows, -1)


def per_device(
    input_codes,
    cotangent_codes,
    dictionary,
    encoder_bias,
    decoder_bias,
    norm_gain,
    gate_weight,
    up_weight,
    down_weight,
):
    own_width = input_codes.shape[1]
    chips = lax.axis_size("latent")
    cores = lax.axis_size("hidden")
    model_width = own_width * chips * cores
    rows = input_codes.shape[0]
    inputs_local = (input_codes.astype(jnp.float32) * CODE_STEP).astype(jnp.bfloat16)
    cotangent_local = (cotangent_codes.astype(jnp.float32) * CODE_STEP).astype(jnp.bfloat16)
    inputs = gather_features(inputs_local, True)
    preact = (
        lax.dot_general(inputs, dictionary, ACROSS, preferred_element_type=jnp.float32)
        + encoder_bias
    )
    latents = jnp.maximum(preact, 0.0).astype(jnp.bfloat16)
    partial_value = jnp.dot(latents, dictionary, preferred_element_type=jnp.float32)
    rebuilt = sum_over_all(partial_value, False).astype(jnp.float32) + decoder_bias
    inverse = lax.rsqrt(
        jnp.sum(rebuilt * rebuilt, axis=1, keepdims=True) / model_width + NORM_EPSILON
    )
    normed = (rebuilt * inverse * norm_gain).astype(jnp.bfloat16)
    target = inputs.astype(jnp.float32)
    gate_proj = lax.dot_general(normed, gate_weight, ACROSS, preferred_element_type=jnp.float32)
    up_proj = lax.dot_general(normed, up_weight, ACROSS, preferred_element_type=jnp.float32)
    gelu_value, gelu_slope = gelu_parts(gate_proj)
    hidden = (gelu_value * up_proj).astype(jnp.bfloat16)
    hidden_grad = lax.dot_general(
        gather_features(cotangent_local, False),
        down_weight,
        ACROSS,
        preferred_element_type=jnp.float32,
    )
    gate_grad = (hidden_grad * up_proj * gelu_slope).astype(jnp.bfloat16)
    up_grad = (hidden_grad * gelu_value).astype(jnp.bfloat16)
    partial_grad = jnp.dot(gate_grad, gate_weight, preferred_element_type=jnp.float32) + jnp.dot(
        up_grad, up_weight, preferred_element_type=jnp.float32
    )
    scaled = sum_over_all(partial_grad, True).astype(jnp.float32) * norm_gain
    output_terms = jnp.dot(hidden, down_weight, preferred_element_type=jnp.float32)
    output_stack = output_terms.reshape(rows, chips, cores, own_width).transpose(2, 1, 0, 3)
    output_half = exchange_sum(output_stack, "hidden", True).astype(jnp.bfloat16)
    block_output = exchange_sum(output_half, "latent", True).astype(jnp.bfloat16)
    inner_row = jnp.sum(scaled * rebuilt, axis=1, keepdims=True)
    inverse_cube = inverse * inverse * inverse
    rebuilt_grad = (
        inverse * scaled - inverse_cube * rebuilt * (inner_row / model_width) + (rebuilt - target)
    ).astype(jnp.bfloat16)
    latent_grad = lax.dot_general(
        rebuilt_grad, dictionary, ACROSS, preferred_element_type=jnp.float32
    )
    preact_grad = jnp.where(preact > 0.0, latent_grad, 0.0).astype(jnp.bfloat16)
    dictionary_grad = lax.dot_general(
        latents, rebuilt_grad, DOWNWARD, preferred_element_type=jnp.float32
    ) + lax.dot_general(preact_grad, inputs, DOWNWARD, preferred_element_type=jnp.float32)
    return (block_output, dictionary_grad.astype(jnp.bfloat16))


def solution(mesh):
    in_specs = (
        P("groups", ("latent", "hidden")),
        P("groups", ("latent", "hidden")),
        P(("latent", "hidden"), None),
        P(("latent", "hidden")),
        P(),
        P(),
        P(("latent", "hidden"), None),
        P(("latent", "hidden"), None),
        P(("latent", "hidden"), None),
    )
    out_specs = (P("groups", ("latent", "hidden")), P(("latent", "hidden"), "groups"))
    return jax.shard_map(
        per_device, mesh=mesh, in_specs=in_specs, out_specs=out_specs, check_vma=False
    )
```

```python
import functools

import jax
import jax.numpy as jnp
from jax import lax
from jax.experimental import pallas as pl
from jax.experimental.pallas import tpu as pltpu
from jax.sharding import PartitionSpec as P

CODE_STEP = 2.0 ** (-6)
NORM_EPSILON = 1e-06
GELU_ROOT = 0.7978845608028654
GELU_CUBIC = 0.044715
ACROSS = (((1,), (1,)), ((), ()))
DOWNWARD = (((0,), (0,)), ((), ()))
LANES = 128
ROW_TILE = 16
VMEM_BYTES = 40 * 1024 * 1024
F32 = jnp.float32
BF16 = jnp.bfloat16


def gelu_parts(values):
    argument = GELU_ROOT * (values + GELU_CUBIC * values * values * values)
    tanh_value = jnp.tanh(argument)
    result = 0.5 * values * (1.0 + tanh_value)
    derivative = 0.5 * (1.0 + tanh_value) + 0.5 * values * (
        1.0 - tanh_value * tanh_value
    ) * GELU_ROOT * (1.0 + 3.0 * GELU_CUBIC * values * values)
    return (result, derivative)


def up_to(value, unit):
    return -(-value // unit) * unit


class Plan:
    def __init__(self, chips, cores, rows, own):
        self.chips, self.cores, self.rows, self.own = chips, cores, rows, own
        self.width = own * chips * cores
        self.half = self.width // cores
        self.tiles = self.half // LANES
        self.chunk = up_to(-(-self.tiles * rows // chips), ROW_TILE)
        self.flat = self.chunk * chips
        self.tail = own - LANES
        if self.tail > 0:
            self.folds = max(
                g
                for g in range(1, rows + 1)
                if rows % g == 0 and g * self.tail <= LANES and (rows // g) % ROW_TILE == 0
            )
            self.fold_rows = rows // self.folds
            self.packed = rows + self.fold_rows

    def fits(self):
        return (
            self.cores == 2
            and self.rows % ROW_TILE == 0
            and self.half % LANES == 0
            and 0 < self.tail < LANES
        )


def call(body, out_shapes, operands, scratch=(), flops=0, moved=0):
    spec = pl.BlockSpec(memory_space=pltpu.VMEM)
    return pl.pallas_call(
        body,
        out_shape=out_shapes,
        in_specs=[spec] * len(operands),
        out_specs=jax.tree.map(lambda _: spec, out_shapes),
        scratch_shapes=list(scratch),
        compiler_params=pltpu.CompilerParams(vmem_limit_bytes=VMEM_BYTES),
        cost_estimate=pl.CostEstimate(flops=flops, bytes_accessed=moved, transcendentals=0),
    )(*operands)


def pack_block(plan, block):
    tail = block[:, LANES:]
    folded = [
        tail[g * plan.fold_rows : (g + 1) * plan.fold_rows, :] for g in range(plan.folds)
    ]
    fill = LANES - plan.folds * plan.tail
    if fill:
        folded.append(jnp.zeros((plan.fold_rows, fill), block.dtype))
    return block[:, :LANES], jnp.concatenate(folded, axis=1)


def unpack_block(plan, packed):
    tail = jnp.concatenate(
        [
            packed[plan.rows :, g * plan.tail : (g + 1) * plan.tail]
            for g in range(plan.folds)
        ],
        axis=0,
    )
    return jnp.concatenate([packed[: plan.rows, :], tail], axis=1)


def pack_codes_body(plan, codes_ref, out_ref):
    block = codes_ref[...].astype(F32) * CODE_STEP
    main, tail = pack_block(plan, block)
    for chip in range(plan.chips):
        out_ref[chip, : plan.rows, :] = main.astype(BF16)
        out_ref[chip, plan.rows :, :] = tail.astype(BF16)


def pack_codes(plan, codes):
    return call(
        functools.partial(pack_codes_body, plan),
        jax.ShapeDtypeStruct((plan.chips, plan.packed, LANES), BF16),
        (codes,),
        moved=plan.rows * plan.own * 4,
    )


def assemble(plan, own_ref, other_ref, both, full_ref):
    core = lax.axis_index("hidden")
    both[core] = own_ref[...]
    both[1 - core] = other_ref[...]
    for chip in range(plan.chips):
        for side in range(plan.cores):
            start = (chip * plan.cores + side) * plan.own
            block = unpack_block(plan, both[side, chip].astype(F32))
            full_ref[:, start : start + plan.own] = block.astype(BF16)


def encode_body(plan, own_ref, other_ref, dict_ref, bias_ref, inputs_ref, latents_ref, mine_ref, theirs_ref, both):
    assemble(plan, own_ref, other_ref, both, inputs_ref)
    preact = (
        lax.dot_general(inputs_ref[...], dict_ref[...], ACROSS, preferred_element_type=F32)
        + bias_ref[...]
    )
    latents = jnp.maximum(preact, 0.0).astype(BF16)
    latents_ref[...] = latents
    halves_of_product(plan, [(latents, dict_ref)], mine_ref, theirs_ref)


def halves_of_product(plan, pairs, mine_ref, theirs_ref):
    core = lax.axis_index("hidden")
    for target, side in ((theirs_ref, 1 - core), (mine_ref, core)):
        start = pl.multiple_of(side * plan.half, LANES)
        total = None
        for left, right_ref in pairs:
            term = jnp.dot(
                left, right_ref[:, pl.ds(start, plan.half)], preferred_element_type=F32
            )
            total = term if total is None else total + term
        for tile in range(plan.tiles):
            target[tile * plan.rows : (tile + 1) * plan.rows, :] = total[
                :, tile * LANES : (tile + 1) * LANES
            ].astype(target.dtype)
        used = plan.tiles * plan.rows
        if used < plan.flat:
            target[used:, :] = jnp.zeros((plan.flat - used, LANES), target.dtype)


def encode(plan, own, other, dictionary, encoder_bias):
    latents = dictionary.shape[0]
    flat = jax.ShapeDtypeStruct((plan.flat, LANES), F32)
    return call(
        functools.partial(encode_body, plan),
        [
            jax.ShapeDtypeStruct((plan.rows, plan.width), BF16),
            jax.ShapeDtypeStruct((plan.rows, latents), BF16),
            flat,
            flat,
        ],
        (own, other, dictionary, encoder_bias.reshape(1, -1)),
        [pltpu.VMEM((plan.cores, plan.chips, plan.packed, LANES), BF16)],
        flops=4 * plan.rows * plan.width * latents,
        moved=dictionary.size * 2,
    )


def back_project_body(plan, own_ref, other_ref, down_ref, grad_ref, both, full):
    assemble(plan, own_ref, other_ref, both, full)
    grad_ref[...] = lax.dot_general(
        full[...], down_ref[...], ACROSS, preferred_element_type=F32
    )


def back_project(plan, own, other, down_weight):
    units = down_weight.shape[0]
    return call(
        functools.partial(back_project_body, plan),
        jax.ShapeDtypeStruct((plan.rows, units), F32),
        (own, other, down_weight),
        [
            pltpu.VMEM((plan.cores, plan.chips, plan.packed, LANES), BF16),
            pltpu.VMEM((plan.rows, plan.width), BF16),
        ],
        flops=2 * plan.rows * plan.width * units,
        moved=down_weight.size * 2,
    )


def join_halves(plan, own_ref, other_ref, full_ref):
    core = lax.axis_index("hidden")
    for source, side in ((own_ref, core), (other_ref, 1 - core)):
        for tile in range(plan.tiles):
            start = pl.multiple_of(side * plan.half + tile * LANES, LANES)
            full_ref[:, pl.ds(start, LANES)] = source[
                tile * plan.rows : (tile + 1) * plan.rows, :
            ]


def mlp_body(plan, own_ref, other_ref, gain_ref, grad_ref, gate_ref, up_ref, scaled_ref, inverse_ref, hidden_ref, mine_ref, theirs_ref):
    join_halves(plan, own_ref, other_ref, scaled_ref)
    scaled = scaled_ref[...]
    rebuilt = scaled.astype(F32) / gain_ref[...]
    inverse = lax.rsqrt(
        jnp.sum(rebuilt * rebuilt, axis=1, keepdims=True) / plan.width + NORM_EPSILON
    )
    inverse_ref[...] = inverse
    gate_proj = inverse * lax.dot_general(
        scaled, gate_ref[...], ACROSS, preferred_element_type=F32
    )
    up_proj = inverse * lax.dot_general(
        scaled, up_ref[...], ACROSS, preferred_element_type=F32
    )
    gelu_value, gelu_slope = gelu_parts(gate_proj)
    hidden_ref[...] = (gelu_value * up_proj).astype(BF16)
    hidden_grad = grad_ref[...]
    gate_grad = (hidden_grad * up_proj * gelu_slope).astype(BF16)
    up_grad = (hidden_grad * gelu_value).astype(BF16)
    halves_of_product(plan, [(gate_grad, gate_ref), (up_grad, up_ref)], mine_ref, theirs_ref)


def mlp(plan, own, other, gain, hidden_grad, gate_weight, up_weight):
    units = gate_weight.shape[0]
    flat = jax.ShapeDtypeStruct((plan.flat, LANES), F32)
    return call(
        functools.partial(mlp_body, plan),
        [
            jax.ShapeDtypeStruct((plan.rows, plan.width), BF16),
            jax.ShapeDtypeStruct((plan.rows, 1), F32),
            jax.ShapeDtypeStruct((plan.rows, units), BF16),
            flat,
            flat,
        ],
        (own, other, gain.reshape(1, -1), hidden_grad, gate_weight, up_weight),
        flops=8 * plan.rows * plan.width * units,
        moved=gate_weight.size * 4,
    )


def project_body(plan, hidden_ref, down_ref, mine_ref, theirs_ref, both):
    core = lax.axis_index("hidden")
    terms = jnp.dot(hidden_ref[...], down_ref[...], preferred_element_type=F32)
    for chip in range(plan.chips):
        for side in range(plan.cores):
            start = (chip * plan.cores + side) * plan.own
            main, tail = pack_block(plan, terms[:, start : start + plan.own])
            both[side, chip, : plan.rows, :] = main
            both[side, chip, plan.rows :, :] = tail
    mine_ref[...] = both[core]
    theirs_ref[...] = both[1 - core]


def project(plan, hidden, down_weight):
    units = down_weight.shape[0]
    shape = (plan.chips, plan.packed, LANES)
    return call(
        functools.partial(project_body, plan),
        [jax.ShapeDtypeStruct(shape, F32)] * 2,
        (hidden, down_weight),
        [pltpu.VMEM((plan.cores,) + shape, F32)],
        flops=2 * plan.rows * plan.width * units,
        moved=down_weight.size * 2,
    )


def finish_output_body(plan, terms_ref, out_ref):
    total = terms_ref[0].astype(F32)
    for chip in range(1, plan.chips):
        total = total + terms_ref[chip].astype(F32)
    out_ref[...] = unpack_block(plan, total).astype(BF16)


def finish_output(plan, terms):
    return call(
        functools.partial(finish_output_body, plan),
        jax.ShapeDtypeStruct((plan.rows, plan.own), BF16),
        (terms,),
        moved=terms.size * 2,
    )


def dictionary_body(plan, own_ref, other_ref, gain_ref, scaled_ref, inverse_ref, inputs_ref, latents_ref, dict_ref, out_ref, full):
    join_halves(plan, own_ref, other_ref, full)
    grad = full[...].astype(F32)
    gain = gain_ref[...]
    scaled_rebuilt = scaled_ref[...].astype(F32)
    rebuilt = scaled_rebuilt / gain
    inverse = inverse_ref[...]
    inner_row = jnp.sum(grad * scaled_rebuilt, axis=1, keepdims=True)
    inverse_cube = inverse * inverse * inverse
    inputs = inputs_ref[...]
    rebuilt_grad = (
        inverse * (grad * gain)
        - (inverse_cube * (inner_row / plan.width)) * rebuilt
        + (rebuilt - inputs.astype(F32))
    ).astype(BF16)
    dictionary = dict_ref[...]
    latents = latents_ref[...]
    latent_grad = lax.dot_general(rebuilt_grad, dictionary, ACROSS, preferred_element_type=F32)
    preact_grad = jnp.where(latents.astype(F32) > 0.0, latent_grad, 0.0).astype(BF16)
    out_ref[...] = (
        lax.dot_general(latents, rebuilt_grad, DOWNWARD, preferred_element_type=F32)
        + lax.dot_general(preact_grad, inputs, DOWNWARD, preferred_element_type=F32)
    ).astype(BF16)


def dictionary_step(plan, own, other, gain, scaled, inverse, inputs, latents, dictionary):
    return call(
        functools.partial(dictionary_body, plan),
        jax.ShapeDtypeStruct(dictionary.shape, BF16),
        (own, other, gain.reshape(1, -1), scaled, inverse, inputs, latents, dictionary),
        [pltpu.VMEM((plan.rows, plan.width), BF16)],
        flops=6 * plan.rows * plan.width * dictionary.shape[0],
        moved=dictionary.size * 4,
    )


def swap(value):
    size = lax.axis_size("hidden")
    return lax.ppermute(value, "hidden", [(i, (i + 1) % size) for i in range(size)])


def trade(stack):
    return lax.all_to_all(stack, "latent", 0, 0, tiled=False)


def own_chunk(plan, vector):
    flat = vector.reshape(plan.cores, plan.tiles, 1, LANES)
    flat = jnp.broadcast_to(flat, (plan.cores, plan.tiles, plan.rows, LANES))
    flat = flat.reshape(plan.cores, -1, LANES)
    flat = jnp.pad(flat, ((0, 0), (0, plan.flat - flat.shape[1]), (0, 0)))
    flat = lax.dynamic_index_in_dim(flat, lax.axis_index("hidden"), 0, keepdims=False)
    return lax.dynamic_slice_in_dim(
        flat, lax.axis_index("latent") * plan.chunk, plan.chunk, 0
    )


def sum_of_chunks(plan, mine, theirs):
    half = (mine + swap(theirs)).astype(BF16)
    terms = trade(half.reshape(plan.chips, plan.chunk, LANES))
    return jnp.sum(terms.astype(F32), axis=0)


def spread(plan, chunk):
    stack = jnp.broadcast_to(chunk.astype(BF16)[None], (plan.chips, plan.chunk, LANES))
    own = trade(stack).reshape(plan.flat, LANES)
    return own, swap(own)


def per_device(
    input_codes,
    cotangent_codes,
    dictionary,
    encoder_bias,
    decoder_bias,
    norm_gain,
    gate_weight,
    up_weight,
    down_weight,
):
    plan = Plan(
        lax.axis_size("latent"), lax.axis_size("hidden"), input_codes.shape[0], input_codes.shape[1]
    )
    if not plan.fits():
        return per_device_plain(
            input_codes,
            cotangent_codes,
            dictionary,
            encoder_bias,
            decoder_bias,
            norm_gain,
            gate_weight,
            up_weight,
            down_weight,
        )
    bias_chunk = own_chunk(plan, decoder_bias)
    gain_chunk = own_chunk(plan, norm_gain)
    inputs_own = trade(pack_codes(plan, input_codes))
    cotangent_own = trade(pack_codes(plan, cotangent_codes))
    inputs, latents, mine, theirs = encode(
        plan, inputs_own, swap(inputs_own), dictionary, encoder_bias
    )
    rebuilt_chunk = sum_of_chunks(plan, mine, theirs) + bias_chunk
    scaled_own, scaled_other = spread(plan, rebuilt_chunk * gain_chunk)
    hidden_grad = back_project(plan, cotangent_own, swap(cotangent_own), down_weight)
    scaled, inverse, hidden, mine, theirs = mlp(
        plan, scaled_own, scaled_other, norm_gain, hidden_grad, gate_weight, up_weight
    )
    grad_own, grad_other = spread(plan, sum_of_chunks(plan, mine, theirs))
    out_mine, out_theirs = project(plan, hidden, down_weight)
    out_half = (out_mine + swap(out_theirs)).astype(BF16)
    block_output = finish_output(plan, trade(out_half))
    dictionary_grad = dictionary_step(
        plan, grad_own, grad_other, norm_gain, scaled, inverse, inputs, latents, dictionary
    )
    return (block_output, dictionary_grad)


def per_device_plain(
    input_codes,
    cotangent_codes,
    dictionary,
    encoder_bias,
    decoder_bias,
    norm_gain,
    gate_weight,
    up_weight,
    down_weight,
):
    own_width = input_codes.shape[1]
    model_width = own_width * lax.axis_size(("latent", "hidden"))
    cotangent_local = (cotangent_codes.astype(jnp.float32) * CODE_STEP).astype(jnp.bfloat16)
    inputs_local = (input_codes.astype(jnp.float32) * CODE_STEP).astype(jnp.bfloat16)
    inputs = lax.all_gather(inputs_local, ("latent", "hidden"), axis=1, tiled=True)
    preact = (
        lax.dot_general(inputs, dictionary, ACROSS, preferred_element_type=jnp.float32)
        + encoder_bias
    )
    latents = jnp.maximum(preact, 0.0).astype(jnp.bfloat16)
    partial_value = jnp.dot(latents, dictionary, preferred_element_type=jnp.float32)
    rebuilt = lax.psum(partial_value, ("latent", "hidden")) + decoder_bias
    inverse = lax.rsqrt(
        jnp.sum(rebuilt * rebuilt, axis=1, keepdims=True) / model_width + NORM_EPSILON
    )
    normed = (rebuilt * inverse * norm_gain).astype(jnp.bfloat16)
    target = inputs.astype(jnp.float32)
    gate_proj = lax.dot_general(normed, gate_weight, ACROSS, preferred_element_type=jnp.float32)
    up_proj = lax.dot_general(normed, up_weight, ACROSS, preferred_element_type=jnp.float32)
    gelu_value, gelu_slope = gelu_parts(gate_proj)
    hidden = (gelu_value * up_proj).astype(jnp.bfloat16)
    output_terms = jnp.dot(hidden, down_weight, preferred_element_type=jnp.float32)
    block_output = lax.psum_scatter(
        output_terms, ("latent", "hidden"), scatter_dimension=1, tiled=True
    ).astype(jnp.bfloat16)
    hidden_grad = lax.dot_general(
        lax.all_gather(cotangent_local, ("latent", "hidden"), axis=1, tiled=True),
        down_weight,
        ACROSS,
        preferred_element_type=jnp.float32,
    )
    gate_grad = (hidden_grad * up_proj * gelu_slope).astype(jnp.bfloat16)
    up_grad = (hidden_grad * gelu_value).astype(jnp.bfloat16)
    partial_grad = jnp.dot(gate_grad, gate_weight, preferred_element_type=jnp.float32) + jnp.dot(
        up_grad, up_weight, preferred_element_type=jnp.float32
    )
    scaled = lax.psum(partial_grad, ("latent", "hidden")) * norm_gain
    inner_row = jnp.sum(scaled * rebuilt, axis=1, keepdims=True)
    inverse_cube = inverse * inverse * inverse
    rebuilt_grad = (
        inverse * scaled - inverse_cube * rebuilt * (inner_row / model_width) + (rebuilt - target)
    ).astype(jnp.bfloat16)
    latent_grad = lax.dot_general(
        rebuilt_grad, dictionary, ACROSS, preferred_element_type=jnp.float32
    )
    preact_grad = jnp.where(preact > 0.0, latent_grad, 0.0).astype(jnp.bfloat16)
    dictionary_grad = lax.dot_general(
        latents, rebuilt_grad, DOWNWARD, preferred_element_type=jnp.float32
    ) + lax.dot_general(preact_grad, inputs, DOWNWARD, preferred_element_type=jnp.float32)
    return (block_output, dictionary_grad.astype(jnp.bfloat16))


def solution(mesh):
    in_specs = (
        P("groups", ("latent", "hidden")),
        P("groups", ("latent", "hidden")),
        P(("latent", "hidden"), None),
        P(("latent", "hidden")),
        P(),
        P(),
        P(("latent", "hidden"), None),
        P(("latent", "hidden"), None),
        P(("latent", "hidden"), None),
    )
    out_specs = (P("groups", ("latent", "hidden")), P(("latent", "hidden"), "groups"))
    return jax.shard_map(
        per_device, mesh=mesh, in_specs=in_specs, out_specs=out_specs, check_vma=False
    )
```

```python
import functools

import jax
import jax.numpy as jnp
from jax import lax
from jax.experimental import pallas as pl
from jax.experimental.pallas import tpu as pltpu
from jax.sharding import PartitionSpec as P

CODE_STEP = 2.0 ** (-6)
NORM_EPSILON = 1e-06
GELU_ROOT = 0.7978845608028654
GELU_CUBIC = 0.044715
ACROSS = (((1,), (1,)), ((), ()))
DOWNWARD = (((0,), (0,)), ((), ()))
LANES = 128
ROW_TILE = 16
VMEM_BYTES = 40 * 1024 * 1024
F32 = jnp.float32
BF16 = jnp.bfloat16


def gelu_parts(values):
    argument = GELU_ROOT * (values + GELU_CUBIC * values * values * values)
    tanh_value = jnp.tanh(argument)
    result = 0.5 * values * (1.0 + tanh_value)
    derivative = 0.5 * (1.0 + tanh_value) + 0.5 * values * (
        1.0 - tanh_value * tanh_value
    ) * GELU_ROOT * (1.0 + 3.0 * GELU_CUBIC * values * values)
    return (result, derivative)


def up_to(value, unit):
    return -(-value // unit) * unit


class Plan:
    def __init__(self, chips, cores, rows, own):
        self.chips, self.cores, self.rows, self.own = chips, cores, rows, own
        self.width = own * chips * cores
        self.half = self.width // cores
        self.tiles = self.half // LANES
        self.chunk = up_to(-(-self.tiles * rows // chips), ROW_TILE)
        self.flat = self.chunk * chips
        self.tail = own - LANES
        if self.tail > 0:
            self.folds = max(
                g
                for g in range(1, rows + 1)
                if rows % g == 0 and g * self.tail <= LANES and (rows // g) % ROW_TILE == 0
            )
            self.fold_rows = rows // self.folds
            self.packed = rows + self.fold_rows

    def fits(self):
        return (
            self.cores == 2
            and self.rows % ROW_TILE == 0
            and self.half % LANES == 0
            and 0 < self.tail < LANES
        )


HBM = pl.BlockSpec(memory_space=pl.ANY)
ONCHIP = pl.BlockSpec(memory_space=pltpu.VMEM)


def shaped(*dims, dtype=F32):
    return jax.ShapeDtypeStruct(dims, dtype)


def call(body, out_shapes, operands, fetched=(), scratch=(), out_specs=None, flops=0, moved=0):
    return pl.pallas_call(
        body,
        out_shape=out_shapes,
        in_specs=[ONCHIP] * len(operands) + [HBM] * len(fetched),
        out_specs=jax.tree.map(lambda _: ONCHIP, out_shapes) if out_specs is None else out_specs,
        scratch_shapes=[pltpu.VMEM(one.shape, one.dtype) for one in fetched] + list(scratch),
        compiler_params=pltpu.CompilerParams(vmem_limit_bytes=VMEM_BYTES),
        cost_estimate=pl.CostEstimate(flops=flops, bytes_accessed=moved, transcendentals=0),
    )(*operands, *fetched)


def copies(sources, targets, sems):
    started = []
    for index, (source, target) in enumerate(zip(sources, targets)):
        one = pltpu.make_async_copy(source, target, sems.at[index])
        one.start()
        started.append(one)
    return started


def pack_block(plan, block):
    tail = block[:, LANES:]
    folded = [
        tail[g * plan.fold_rows : (g + 1) * plan.fold_rows, :] for g in range(plan.folds)
    ]
    fill = LANES - plan.folds * plan.tail
    if fill:
        folded.append(jnp.zeros((plan.fold_rows, fill), block.dtype))
    return block[:, :LANES], jnp.concatenate(folded, axis=1)


def unpack_block(plan, packed):
    tail = jnp.concatenate(
        [
            packed[plan.rows :, g * plan.tail : (g + 1) * plan.tail]
            for g in range(plan.folds)
        ],
        axis=0,
    )
    return jnp.concatenate([packed[: plan.rows, :], tail], axis=1)


def pack_codes_body(plan, input_ref, cotangent_ref, out_ref):
    for index, codes_ref in enumerate((input_ref, cotangent_ref)):
        block = codes_ref[...].astype(F32) * CODE_STEP
        main, tail = pack_block(plan, block)
        start = index * plan.packed
        for chip in range(plan.chips):
            out_ref[chip, start : start + plan.rows, :] = main.astype(BF16)
            out_ref[chip, start + plan.rows : start + plan.packed, :] = tail.astype(BF16)


def pack_codes(plan, input_codes, cotangent_codes):
    return call(
        functools.partial(pack_codes_body, plan),
        shaped(plan.chips, 2 * plan.packed, LANES, dtype=BF16),
        (input_codes, cotangent_codes),
        moved=plan.rows * plan.own * 8,
    )


def assemble(plan, start, own_ref, other_ref, both, full_ref):
    core = lax.axis_index("hidden")
    both[core] = own_ref[:, start : start + plan.packed, :]
    both[1 - core] = other_ref[:, start : start + plan.packed, :]
    for chip in range(plan.chips):
        for side in range(plan.cores):
            column = (chip * plan.cores + side) * plan.own
            block = unpack_block(plan, both[side, chip].astype(F32))
            full_ref[:, column : column + plan.own] = block.astype(BF16)


def both_scratch(plan, dtype=BF16):
    return pltpu.VMEM((plan.cores, plan.chips, plan.packed, LANES), dtype)


def halves_of_product(plan, pairs, mine_ref, theirs_ref):
    core = lax.axis_index("hidden")
    for target, side in ((theirs_ref, 1 - core), (mine_ref, core)):
        start = pl.multiple_of(side * plan.half, LANES)
        total = None
        for left, right_ref in pairs:
            term = jnp.dot(
                left, right_ref[:, pl.ds(start, plan.half)], preferred_element_type=F32
            )
            total = term if total is None else total + term
        for tile in range(plan.tiles):
            target[tile * plan.rows : (tile + 1) * plan.rows, :] = total[
                :, tile * LANES : (tile + 1) * LANES
            ].astype(target.dtype)
        used = plan.tiles * plan.rows
        if used < plan.flat:
            target[used:, :] = jnp.zeros((plan.flat - used, LANES), target.dtype)


def encode_body(plan, own_ref, other_ref, bias_ref, dict_hbm, inputs_ref, latents_ref, mine_ref, theirs_ref, dict_ref, both, sems):
    (copy,) = copies([dict_hbm], [dict_ref], sems)
    assemble(plan, 0, own_ref, other_ref, both, inputs_ref)
    copy.wait()
    preact = (
        lax.dot_general(inputs_ref[...], dict_ref[...], ACROSS, preferred_element_type=F32)
        + bias_ref[...]
    )
    latents = jnp.maximum(preact, 0.0).astype(BF16)
    latents_ref[...] = latents
    halves_of_product(plan, [(latents, dict_ref)], mine_ref, theirs_ref)


def encode(plan, own, other, dictionary, encoder_bias):
    latents = dictionary.shape[0]
    return call(
        functools.partial(encode_body, plan),
        [
            shaped(plan.rows, plan.width, dtype=BF16),
            shaped(plan.rows, latents, dtype=BF16),
            shaped(plan.flat, LANES),
            shaped(plan.flat, LANES),
        ],
        (own, other, encoder_bias.reshape(1, -1)),
        (dictionary,),
        [both_scratch(plan), pltpu.SemaphoreType.DMA((1,))],
        flops=4 * plan.rows * plan.width * latents,
        moved=dictionary.size * 2,
    )


def back_project_body(plan, own_ref, other_ref, down_hbm, grad_ref, down_ref, both, full, sems):
    (copy,) = copies([down_hbm], [down_ref], sems)
    assemble(plan, plan.packed, own_ref, other_ref, both, full)
    copy.wait()
    grad_ref[...] = lax.dot_general(
        full[...], down_ref[...], ACROSS, preferred_element_type=F32
    )


def back_project(plan, own, other, down_weight):
    units = down_weight.shape[0]
    return call(
        functools.partial(back_project_body, plan),
        shaped(plan.rows, units),
        (own, other),
        (down_weight,),
        [both_scratch(plan), pltpu.VMEM((plan.rows, plan.width), BF16), pltpu.SemaphoreType.DMA((1,))],
        flops=2 * plan.rows * plan.width * units,
        moved=down_weight.size * 2,
    )


def join_halves(plan, own_ref, other_ref, full_ref):
    core = lax.axis_index("hidden")
    for source, side in ((own_ref, core), (other_ref, 1 - core)):
        for tile in range(plan.tiles):
            column = pl.multiple_of(side * plan.half + tile * LANES, LANES)
            row = 0
            while row < plan.rows:
                chip, place = divmod(tile * plan.rows + row, plan.chunk)
                count = min(plan.rows - row, plan.chunk - place)
                full_ref[row : row + count, pl.ds(column, LANES)] = source[
                    chip, place : place + count, :
                ]
                row += count


def mlp_body(plan, own_ref, other_ref, gain_ref, grad_ref, gate_hbm, up_hbm, scaled_ref, inverse_ref, hidden_ref, mine_ref, theirs_ref, gate_ref, up_ref, sems):
    gate_copy, up_copy = copies([gate_hbm, up_hbm], [gate_ref, up_ref], sems)
    join_halves(plan, own_ref, other_ref, scaled_ref)
    scaled = scaled_ref[...]
    rebuilt = scaled.astype(F32) / gain_ref[...]
    inverse = lax.rsqrt(
        jnp.sum(rebuilt * rebuilt, axis=1, keepdims=True) / plan.width + NORM_EPSILON
    )
    inverse_ref[...] = inverse
    gate_copy.wait()
    gate_proj = inverse * lax.dot_general(
        scaled, gate_ref[...], ACROSS, preferred_element_type=F32
    )
    up_copy.wait()
    up_proj = inverse * lax.dot_general(
        scaled, up_ref[...], ACROSS, preferred_element_type=F32
    )
    gelu_value, gelu_slope = gelu_parts(gate_proj)
    hidden_ref[...] = (gelu_value * up_proj).astype(BF16)
    hidden_grad = grad_ref[...]
    gate_grad = (hidden_grad * up_proj * gelu_slope).astype(BF16)
    up_grad = (hidden_grad * gelu_value).astype(BF16)
    halves_of_product(plan, [(gate_grad, gate_ref), (up_grad, up_ref)], mine_ref, theirs_ref)


def mlp(plan, own, other, gain, hidden_grad, gate_weight, up_weight):
    units = gate_weight.shape[0]
    return call(
        functools.partial(mlp_body, plan),
        [
            shaped(plan.rows, plan.width, dtype=BF16),
            shaped(plan.rows, 1),
            shaped(plan.rows, units, dtype=BF16),
            shaped(plan.flat, LANES),
            shaped(plan.flat, LANES),
        ],
        (own, other, gain.reshape(1, -1), hidden_grad),
        (gate_weight, up_weight),
        [pltpu.SemaphoreType.DMA((2,))],
        flops=8 * plan.rows * plan.width * units,
        moved=gate_weight.size * 4,
    )


def project_body(plan, hidden_ref, down_hbm, mine_ref, theirs_ref, down_ref, both, sems):
    (copy,) = copies([down_hbm], [down_ref], sems)
    core = lax.axis_index("hidden")
    copy.wait()
    terms = jnp.dot(hidden_ref[...], down_ref[...], preferred_element_type=F32)
    for chip in range(plan.chips):
        for side in range(plan.cores):
            start = (chip * plan.cores + side) * plan.own
            main, tail = pack_block(plan, terms[:, start : start + plan.own])
            both[side, chip, : plan.rows, :] = main
            both[side, chip, plan.rows :, :] = tail
    mine_ref[...] = both[core]
    theirs_ref[...] = both[1 - core]


def project(plan, hidden, down_weight):
    units = down_weight.shape[0]
    return call(
        functools.partial(project_body, plan),
        [shaped(plan.chips, plan.packed, LANES)] * 2,
        (hidden,),
        (down_weight,),
        [both_scratch(plan, F32), pltpu.SemaphoreType.DMA((1,))],
        flops=2 * plan.rows * plan.width * units,
        moved=down_weight.size * 2,
    )


def total_of(plan, terms_ref, start, count):
    total = terms_ref[0, start : start + count, :].astype(F32)
    for chip in range(1, plan.chips):
        total = total + terms_ref[chip, start : start + count, :].astype(F32)
    return total


def sum_rebuilt_body(plan, terms_ref, bias_ref, gain_ref, out_ref):
    total = (total_of(plan, terms_ref, 0, plan.chunk) + bias_ref[...]) * gain_ref[...]
    for chip in range(plan.chips):
        out_ref[chip] = total.astype(BF16)


def sum_rebuilt(plan, terms, bias_chunk, gain_chunk):
    return call(
        functools.partial(sum_rebuilt_body, plan),
        shaped(plan.chips, plan.chunk, LANES, dtype=BF16),
        (terms, bias_chunk, gain_chunk),
        moved=terms.size * 4,
    )


def sum_grad_body(plan, terms_ref, mine_ref, theirs_ref, out_ref):
    total = total_of(plan, terms_ref, 0, plan.chunk).astype(BF16)
    for chip in range(plan.chips):
        out_ref[chip, : plan.chunk, :] = total
        out_ref[chip, plan.chunk :, :] = (mine_ref[chip] + theirs_ref[chip]).astype(BF16)


def sum_grad(plan, terms, out_mine, out_theirs):
    return call(
        functools.partial(sum_grad_body, plan),
        shaped(plan.chips, plan.chunk + plan.packed, LANES, dtype=BF16),
        (terms, out_mine, out_theirs),
        moved=terms.size * 4,
    )


def finish_output_body(plan, terms_ref, out_ref):
    total = total_of(plan, terms_ref, plan.chunk, plan.packed)
    out_ref[...] = unpack_block(plan, total).astype(BF16)


def finish_output(plan, terms):
    return call(
        functools.partial(finish_output_body, plan),
        shaped(plan.rows, plan.own, dtype=BF16),
        (terms,),
        moved=terms.size * 2,
    )


def dictionary_body(plan, pieces, own_ref, other_ref, gain_ref, inverse_ref, scaled_hbm, inputs_hbm, latents_hbm, dict_hbm, out_hbm, scaled_ref, inputs_ref, latents_ref, dict_ref, full, out_ref, sems, out_sems):
    started = copies(
        [scaled_hbm, inputs_hbm, latents_hbm, dict_hbm],
        [scaled_ref, inputs_ref, latents_ref, dict_ref],
        sems,
    )
    join_halves(plan, own_ref, other_ref, full)
    grad = full[...].astype(F32)
    gain = gain_ref[...]
    started[0].wait()
    scaled_rebuilt = scaled_ref[...].astype(F32)
    rebuilt = scaled_rebuilt / gain
    inverse = inverse_ref[...]
    inner_row = jnp.sum(grad * scaled_rebuilt, axis=1, keepdims=True)
    inverse_cube = inverse * inverse * inverse
    started[1].wait()
    inputs = inputs_ref[...]
    rebuilt_grad = (
        inverse * (grad * gain)
        - (inverse_cube * (inner_row / plan.width)) * rebuilt
        + (rebuilt - inputs.astype(F32))
    ).astype(BF16)
    started[2].wait()
    started[3].wait()
    size = dict_ref.shape[0] // pieces
    writes = []
    for piece in range(pieces):
        span = slice(piece * size, (piece + 1) * size)
        latents = latents_ref[:, span]
        latent_grad = lax.dot_general(
            rebuilt_grad, dict_ref[span, :], ACROSS, preferred_element_type=F32
        )
        preact_grad = jnp.where(latents.astype(F32) > 0.0, latent_grad, 0.0).astype(BF16)
        out_ref[span, :] = (
            lax.dot_general(latents, rebuilt_grad, DOWNWARD, preferred_element_type=F32)
            + lax.dot_general(preact_grad, inputs, DOWNWARD, preferred_element_type=F32)
        ).astype(BF16)
        one = pltpu.make_async_copy(
            out_ref.at[span, :], out_hbm.at[span, :], out_sems.at[piece]
        )
        one.start()
        writes.append(one)
    for one in writes:
        one.wait()


def dictionary_step(plan, own, other, gain, scaled, inverse, inputs, latents, dictionary):
    units = dictionary.shape[0]
    pieces = units // (2 * LANES) if units % (2 * LANES) == 0 else 1
    return call(
        functools.partial(dictionary_body, plan, pieces),
        shaped(*dictionary.shape, dtype=BF16),
        (own, other, gain.reshape(1, -1), inverse),
        (scaled, inputs, latents, dictionary),
        [
            pltpu.VMEM((plan.rows, plan.width), BF16),
            pltpu.VMEM(dictionary.shape, BF16),
            pltpu.SemaphoreType.DMA((4,)),
            pltpu.SemaphoreType.DMA((pieces,)),
        ],
        out_specs=HBM,
        flops=6 * plan.rows * plan.width * units,
        moved=dictionary.size * 4,
    )


def swap(value):
    size = lax.axis_size("hidden")
    return lax.ppermute(value, "hidden", [(i, (i + 1) % size) for i in range(size)])


def trade(stack):
    return lax.all_to_all(stack, "latent", 0, 0, tiled=False)


def own_chunk(plan, vector):
    flat = vector.reshape(plan.cores, plan.tiles, 1, LANES)
    flat = jnp.broadcast_to(flat, (plan.cores, plan.tiles, plan.rows, LANES))
    flat = flat.reshape(plan.cores, -1, LANES)
    flat = jnp.pad(flat, ((0, 0), (0, plan.flat - flat.shape[1]), (0, 0)))
    flat = lax.dynamic_index_in_dim(flat, lax.axis_index("hidden"), 0, keepdims=False)
    return lax.dynamic_slice_in_dim(
        flat, lax.axis_index("latent") * plan.chunk, plan.chunk, 0
    )


def traded_terms(plan, mine, theirs):
    half = (mine + swap(theirs)).astype(BF16)
    return trade(half.reshape(plan.chips, plan.chunk, LANES))


def per_device(
    input_codes,
    cotangent_codes,
    dictionary,
    encoder_bias,
    decoder_bias,
    norm_gain,
    gate_weight,
    up_weight,
    down_weight,
):
    plan = Plan(
        lax.axis_size("latent"), lax.axis_size("hidden"), input_codes.shape[0], input_codes.shape[1]
    )
    if not plan.fits():
        return per_device_plain(
            input_codes,
            cotangent_codes,
            dictionary,
            encoder_bias,
            decoder_bias,
            norm_gain,
            gate_weight,
            up_weight,
            down_weight,
        )
    bias_chunk = own_chunk(plan, decoder_bias)
    gain_chunk = own_chunk(plan, norm_gain)
    codes_own = trade(pack_codes(plan, input_codes, cotangent_codes))
    codes_other = swap(codes_own)
    inputs, latents, mine, theirs = encode(plan, codes_own, codes_other, dictionary, encoder_bias)
    terms = traded_terms(plan, mine, theirs)
    hidden_grad = back_project(plan, codes_own, codes_other, down_weight)
    scaled_own = trade(sum_rebuilt(plan, terms, bias_chunk, gain_chunk))
    scaled, inverse, hidden, mine, theirs = mlp(
        plan, scaled_own, swap(scaled_own), norm_gain, hidden_grad, gate_weight, up_weight
    )
    terms = traded_terms(plan, mine, theirs)
    out_mine, out_theirs = project(plan, hidden, down_weight)
    last_own = trade(sum_grad(plan, terms, out_mine, swap(out_theirs)))
    block_output = finish_output(plan, last_own)
    dictionary_grad = dictionary_step(
        plan, last_own, swap(last_own), norm_gain, scaled, inverse, inputs, latents, dictionary
    )
    return (block_output, dictionary_grad)


def per_device_plain(
    input_codes,
    cotangent_codes,
    dictionary,
    encoder_bias,
    decoder_bias,
    norm_gain,
    gate_weight,
    up_weight,
    down_weight,
):
    own_width = input_codes.shape[1]
    model_width = own_width * lax.axis_size(("latent", "hidden"))
    cotangent_local = (cotangent_codes.astype(jnp.float32) * CODE_STEP).astype(jnp.bfloat16)
    inputs_local = (input_codes.astype(jnp.float32) * CODE_STEP).astype(jnp.bfloat16)
    inputs = lax.all_gather(inputs_local, ("latent", "hidden"), axis=1, tiled=True)
    preact = (
        lax.dot_general(inputs, dictionary, ACROSS, preferred_element_type=jnp.float32)
        + encoder_bias
    )
    latents = jnp.maximum(preact, 0.0).astype(jnp.bfloat16)
    partial_value = jnp.dot(latents, dictionary, preferred_element_type=jnp.float32)
    rebuilt = lax.psum(partial_value, ("latent", "hidden")) + decoder_bias
    inverse = lax.rsqrt(
        jnp.sum(rebuilt * rebuilt, axis=1, keepdims=True) / model_width + NORM_EPSILON
    )
    normed = (rebuilt * inverse * norm_gain).astype(jnp.bfloat16)
    target = inputs.astype(jnp.float32)
    gate_proj = lax.dot_general(normed, gate_weight, ACROSS, preferred_element_type=jnp.float32)
    up_proj = lax.dot_general(normed, up_weight, ACROSS, preferred_element_type=jnp.float32)
    gelu_value, gelu_slope = gelu_parts(gate_proj)
    hidden = (gelu_value * up_proj).astype(jnp.bfloat16)
    output_terms = jnp.dot(hidden, down_weight, preferred_element_type=jnp.float32)
    block_output = lax.psum_scatter(
        output_terms, ("latent", "hidden"), scatter_dimension=1, tiled=True
    ).astype(jnp.bfloat16)
    hidden_grad = lax.dot_general(
        lax.all_gather(cotangent_local, ("latent", "hidden"), axis=1, tiled=True),
        down_weight,
        ACROSS,
        preferred_element_type=jnp.float32,
    )
    gate_grad = (hidden_grad * up_proj * gelu_slope).astype(jnp.bfloat16)
    up_grad = (hidden_grad * gelu_value).astype(jnp.bfloat16)
    partial_grad = jnp.dot(gate_grad, gate_weight, preferred_element_type=jnp.float32) + jnp.dot(
        up_grad, up_weight, preferred_element_type=jnp.float32
    )
    scaled = lax.psum(partial_grad, ("latent", "hidden")) * norm_gain
    inner_row = jnp.sum(scaled * rebuilt, axis=1, keepdims=True)
    inverse_cube = inverse * inverse * inverse
    rebuilt_grad = (
        inverse * scaled - inverse_cube * rebuilt * (inner_row / model_width) + (rebuilt - target)
    ).astype(jnp.bfloat16)
    latent_grad = lax.dot_general(
        rebuilt_grad, dictionary, ACROSS, preferred_element_type=jnp.float32
    )
    preact_grad = jnp.where(preact > 0.0, latent_grad, 0.0).astype(jnp.bfloat16)
    dictionary_grad = lax.dot_general(
        latents, rebuilt_grad, DOWNWARD, preferred_element_type=jnp.float32
    ) + lax.dot_general(preact_grad, inputs, DOWNWARD, preferred_element_type=jnp.float32)
    return (block_output, dictionary_grad.astype(jnp.bfloat16))


def solution(mesh):
    in_specs = (
        P("groups", ("latent", "hidden")),
        P("groups", ("latent", "hidden")),
        P(("latent", "hidden"), None),
        P(("latent", "hidden")),
        P(),
        P(),
        P(("latent", "hidden"), None),
        P(("latent", "hidden"), None),
        P(("latent", "hidden"), None),
    )
    out_specs = (P("groups", ("latent", "hidden")), P(("latent", "hidden"), "groups"))
    return jax.shard_map(
        per_device, mesh=mesh, in_specs=in_specs, out_specs=out_specs, check_vma=False
    )
```

```python
import functools

import jax
import jax.numpy as jnp
from jax import lax
from jax.experimental import pallas as pl
from jax.experimental.pallas import tpu as pltpu
from jax.sharding import PartitionSpec as P

CODE_STEP = 2.0 ** (-6)
NORM_EPSILON = 1e-06
GELU_ROOT = 0.7978845608028654
GELU_CUBIC = 0.044715
ACROSS = (((1,), (1,)), ((), ()))
DOWNWARD = (((0,), (0,)), ((), ()))
LANES = 128
ROW_TILE = 16
VMEM_BYTES = 40 * 1024 * 1024
F32 = jnp.float32
BF16 = jnp.bfloat16


def gelu_parts(values):
    argument = GELU_ROOT * (values + GELU_CUBIC * values * values * values)
    tanh_value = jnp.tanh(argument)
    result = 0.5 * values * (1.0 + tanh_value)
    derivative = 0.5 * (1.0 + tanh_value) + 0.5 * values * (
        1.0 - tanh_value * tanh_value
    ) * GELU_ROOT * (1.0 + 3.0 * GELU_CUBIC * values * values)
    return (result, derivative)


def up_to(value, unit):
    return -(-value // unit) * unit


class Plan:
    def __init__(self, chips, cores, rows, own):
        self.chips, self.cores, self.rows, self.own = chips, cores, rows, own
        self.width = own * chips * cores
        self.half = self.width // cores
        self.tiles = self.half // LANES
        self.chunk = up_to(-(-self.tiles * rows // chips), ROW_TILE)
        self.flat = self.chunk * chips
        self.tail = own - LANES
        if self.tail > 0:
            self.folds = max(
                g
                for g in range(1, rows + 1)
                if rows % g == 0 and g * self.tail <= LANES and (rows // g) % ROW_TILE == 0
            )
            self.fold_rows = rows // self.folds
            self.packed = rows + self.fold_rows
        self.bits = [1 << k for k in reversed(range((chips - 1).bit_length()))]
        self.order = [0]
        for bit in self.bits:
            self.order = self.order + [place ^ bit for place in self.order]

    def fits(self):
        return (
            self.cores == 2
            and len(self.order) == self.chips
            and self.rows % ROW_TILE == 0
            and self.half % LANES == 0
            and 0 < self.tail < LANES
        )


HBM = pl.BlockSpec(memory_space=pl.ANY)
ONCHIP = pl.BlockSpec(memory_space=pltpu.VMEM)


def shaped(*dims, dtype=F32):
    return jax.ShapeDtypeStruct(dims, dtype)


def call(body, out_shapes, operands, fetched=(), scratch=(), out_specs=None, flops=0, moved=0):
    return pl.pallas_call(
        body,
        out_shape=out_shapes,
        in_specs=[ONCHIP] * len(operands) + [HBM] * len(fetched),
        out_specs=jax.tree.map(lambda _: ONCHIP, out_shapes) if out_specs is None else out_specs,
        scratch_shapes=[pltpu.VMEM(one.shape, one.dtype) for one in fetched] + list(scratch),
        compiler_params=pltpu.CompilerParams(vmem_limit_bytes=VMEM_BYTES),
        cost_estimate=pl.CostEstimate(flops=flops, bytes_accessed=moved, transcendentals=0),
    )(*operands, *fetched)


def copies(sources, targets, sems):
    started = []
    for index, (source, target) in enumerate(zip(sources, targets)):
        one = pltpu.make_async_copy(source, target, sems.at[index])
        one.start()
        started.append(one)
    return started


def pack_block(plan, block):
    tail = block[:, LANES:]
    folded = [
        tail[g * plan.fold_rows : (g + 1) * plan.fold_rows, :] for g in range(plan.folds)
    ]
    fill = LANES - plan.folds * plan.tail
    if fill:
        folded.append(jnp.zeros((plan.fold_rows, fill), block.dtype))
    return block[:, :LANES], jnp.concatenate(folded, axis=1)


def unpack_block(plan, packed):
    tail = jnp.concatenate(
        [
            packed[plan.rows :, g * plan.tail : (g + 1) * plan.tail]
            for g in range(plan.folds)
        ],
        axis=0,
    )
    return jnp.concatenate([packed[: plan.rows, :], tail], axis=1)


def pack_codes_body(plan, input_ref, cotangent_ref, inputs_ref, cotangent_out_ref):
    main, tail = pack_block(plan, input_ref[...].astype(F32) * CODE_STEP)
    for chip in range(plan.chips):
        inputs_ref[chip, : plan.rows, :] = main.astype(BF16)
        inputs_ref[chip, plan.rows :, :] = tail.astype(BF16)
    main, tail = pack_block(plan, cotangent_ref[...].astype(F32) * CODE_STEP)
    cotangent_out_ref[0, : plan.rows, :] = main.astype(BF16)
    cotangent_out_ref[0, plan.rows :, :] = tail.astype(BF16)


def pack_codes(plan, input_codes, cotangent_codes):
    return call(
        functools.partial(pack_codes_body, plan),
        [
            shaped(plan.chips, plan.packed, LANES, dtype=BF16),
            shaped(1, plan.packed, LANES, dtype=BF16),
        ],
        (input_codes, cotangent_codes),
        moved=plan.rows * plan.own * 8,
    )


def assemble(plan, relative, own_ref, other_ref, both, full_ref):
    core = lax.axis_index("hidden")
    if relative:
        me = lax.axis_index("latent")
        for place, partner in enumerate(plan.order):
            chip = me ^ partner
            both[core, chip] = own_ref[place]
            both[1 - core, chip] = other_ref[place]
    else:
        both[core] = own_ref[...]
        both[1 - core] = other_ref[...]
    for chip in range(plan.chips):
        for side in range(plan.cores):
            column = (chip * plan.cores + side) * plan.own
            block = unpack_block(plan, both[side, chip].astype(F32))
            full_ref[:, column : column + plan.own] = block.astype(BF16)


def both_scratch(plan, dtype=BF16):
    return pltpu.VMEM((plan.cores, plan.chips, plan.packed, LANES), dtype)


def halves_of_product(plan, pairs, mine_ref, theirs_ref):
    core = lax.axis_index("hidden")
    for target, side in ((theirs_ref, 1 - core), (mine_ref, core)):
        start = pl.multiple_of(side * plan.half, LANES)
        total = None
        for left, right_ref in pairs:
            term = jnp.dot(
                left, right_ref[:, pl.ds(start, plan.half)], preferred_element_type=F32
            )
            total = term if total is None else total + term
        for tile in range(plan.tiles):
            target[tile * plan.rows : (tile + 1) * plan.rows, :] = total[
                :, tile * LANES : (tile + 1) * LANES
            ].astype(target.dtype)
        used = plan.tiles * plan.rows
        if used < plan.flat:
            target[used:, :] = jnp.zeros((plan.flat - used, LANES), target.dtype)


def encode_body(plan, own_ref, other_ref, bias_ref, dict_hbm, inputs_ref, latents_ref, mine_ref, theirs_ref, dict_ref, both, sems):
    (copy,) = copies([dict_hbm], [dict_ref], sems)
    assemble(plan, False, own_ref, other_ref, both, inputs_ref)
    copy.wait()
    preact = (
        lax.dot_general(inputs_ref[...], dict_ref[...], ACROSS, preferred_element_type=F32)
        + bias_ref[...]
    )
    latents = jnp.maximum(preact, 0.0).astype(BF16)
    latents_ref[...] = latents
    halves_of_product(plan, [(latents, dict_ref)], mine_ref, theirs_ref)


def encode(plan, own, other, dictionary, encoder_bias):
    latents = dictionary.shape[0]
    return call(
        functools.partial(encode_body, plan),
        [
            shaped(plan.rows, plan.width, dtype=BF16),
            shaped(plan.rows, latents, dtype=BF16),
            shaped(plan.flat, LANES),
            shaped(plan.flat, LANES),
        ],
        (own, other, encoder_bias.reshape(1, -1)),
        (dictionary,),
        [both_scratch(plan), pltpu.SemaphoreType.DMA((1,))],
        flops=4 * plan.rows * plan.width * latents,
        moved=dictionary.size * 2,
    )


def back_project_body(plan, own_ref, other_ref, down_hbm, grad_ref, down_ref, both, full, sems):
    (copy,) = copies([down_hbm], [down_ref], sems)
    assemble(plan, True, own_ref, other_ref, both, full)
    copy.wait()
    grad_ref[...] = lax.dot_general(
        full[...], down_ref[...], ACROSS, preferred_element_type=F32
    )


def back_project(plan, own, other, down_weight):
    units = down_weight.shape[0]
    return call(
        functools.partial(back_project_body, plan),
        shaped(plan.rows, units),
        (own, other),
        (down_weight,),
        [both_scratch(plan), pltpu.VMEM((plan.rows, plan.width), BF16), pltpu.SemaphoreType.DMA((1,))],
        flops=2 * plan.rows * plan.width * units,
        moved=down_weight.size * 2,
    )


def join_halves(plan, own_ref, other_ref, full_ref):
    core = lax.axis_index("hidden")
    for source, side in ((own_ref, core), (other_ref, 1 - core)):
        for tile in range(plan.tiles):
            column = pl.multiple_of(side * plan.half + tile * LANES, LANES)
            row = 0
            while row < plan.rows:
                chip, place = divmod(tile * plan.rows + row, plan.chunk)
                count = min(plan.rows - row, plan.chunk - place)
                full_ref[row : row + count, pl.ds(column, LANES)] = source[
                    chip, place : place + count, :
                ]
                row += count


def mlp_body(plan, own_ref, other_ref, gain_ref, grad_ref, gate_hbm, up_hbm, scaled_ref, inverse_ref, hidden_ref, mine_ref, theirs_ref, gate_ref, up_ref, sems):
    gate_copy, up_copy = copies([gate_hbm, up_hbm], [gate_ref, up_ref], sems)
    join_halves(plan, own_ref, other_ref, scaled_ref)
    scaled = scaled_ref[...]
    rebuilt = scaled.astype(F32) / gain_ref[...]
    inverse = lax.rsqrt(
        jnp.sum(rebuilt * rebuilt, axis=1, keepdims=True) / plan.width + NORM_EPSILON
    )
    inverse_ref[...] = inverse
    gate_copy.wait()
    gate_proj = inverse * lax.dot_general(
        scaled, gate_ref[...], ACROSS, preferred_element_type=F32
    )
    up_copy.wait()
    up_proj = inverse * lax.dot_general(
        scaled, up_ref[...], ACROSS, preferred_element_type=F32
    )
    gelu_value, gelu_slope = gelu_parts(gate_proj)
    hidden_ref[...] = (gelu_value * up_proj).astype(BF16)
    hidden_grad = grad_ref[...]
    gate_grad = (hidden_grad * up_proj * gelu_slope).astype(BF16)
    up_grad = (hidden_grad * gelu_value).astype(BF16)
    halves_of_product(plan, [(gate_grad, gate_ref), (up_grad, up_ref)], mine_ref, theirs_ref)


def mlp(plan, own, other, gain, hidden_grad, gate_weight, up_weight):
    units = gate_weight.shape[0]
    return call(
        functools.partial(mlp_body, plan),
        [
            shaped(plan.rows, plan.width, dtype=BF16),
            shaped(plan.rows, 1),
            shaped(plan.rows, units, dtype=BF16),
            shaped(plan.flat, LANES),
            shaped(plan.flat, LANES),
        ],
        (own, other, gain.reshape(1, -1), hidden_grad),
        (gate_weight, up_weight),
        [pltpu.SemaphoreType.DMA((2,))],
        flops=8 * plan.rows * plan.width * units,
        moved=gate_weight.size * 4,
    )


def project_body(plan, hidden_ref, down_hbm, mine_ref, theirs_ref, down_ref, both, sems):
    (copy,) = copies([down_hbm], [down_ref], sems)
    core = lax.axis_index("hidden")
    copy.wait()
    terms = jnp.dot(hidden_ref[...], down_ref[...], preferred_element_type=F32)
    for chip in range(plan.chips):
        for side in range(plan.cores):
            start = (chip * plan.cores + side) * plan.own
            main, tail = pack_block(plan, terms[:, start : start + plan.own])
            both[side, chip, : plan.rows, :] = main
            both[side, chip, plan.rows :, :] = tail
    me = lax.axis_index("latent")
    for place, partner in enumerate(plan.order):
        chip = me ^ partner
        mine_ref[place] = both[core, chip]
        theirs_ref[place] = both[1 - core, chip]


def project(plan, hidden, down_weight):
    units = down_weight.shape[0]
    return call(
        functools.partial(project_body, plan),
        [shaped(plan.chips, plan.packed, LANES)] * 2,
        (hidden,),
        (down_weight,),
        [both_scratch(plan, F32), pltpu.SemaphoreType.DMA((1,))],
        flops=2 * plan.rows * plan.width * units,
        moved=down_weight.size * 2,
    )


def total_of(plan, terms_ref, start, count):
    total = terms_ref[0, start : start + count, :].astype(F32)
    for chip in range(1, plan.chips):
        total = total + terms_ref[chip, start : start + count, :].astype(F32)
    return total


def sum_rebuilt_body(plan, terms_ref, bias_ref, gain_ref, out_ref):
    total = (total_of(plan, terms_ref, 0, plan.chunk) + bias_ref[...]) * gain_ref[...]
    for chip in range(plan.chips):
        out_ref[chip] = total.astype(BF16)


def sum_rebuilt(plan, terms, bias_chunk, gain_chunk):
    return call(
        functools.partial(sum_rebuilt_body, plan),
        shaped(plan.chips, plan.chunk, LANES, dtype=BF16),
        (terms, bias_chunk, gain_chunk),
        moved=terms.size * 4,
    )


def sum_grad_body(plan, terms_ref, out_ref):
    total = total_of(plan, terms_ref, 0, plan.chunk).astype(BF16)
    for chip in range(plan.chips):
        out_ref[chip] = total


def sum_grad(plan, terms):
    return call(
        functools.partial(sum_grad_body, plan),
        shaped(plan.chips, plan.chunk, LANES, dtype=BF16),
        (terms,),
        moved=terms.size * 4,
    )


def finish_output_body(plan, kept_ref, got_ref, out_ref):
    total = kept_ref[0] + got_ref[0].astype(F32)
    out_ref[...] = unpack_block(plan, total).astype(BF16)


def finish_output(plan, kept, got):
    return call(
        functools.partial(finish_output_body, plan),
        shaped(plan.rows, plan.own, dtype=BF16),
        (kept, got),
        moved=kept.size * 4,
    )


def dictionary_body(plan, pieces, own_ref, other_ref, gain_ref, inverse_ref, scaled_hbm, inputs_hbm, latents_hbm, dict_hbm, out_hbm, scaled_ref, inputs_ref, latents_ref, dict_ref, full, out_ref, sems, out_sems):
    started = copies(
        [scaled_hbm, inputs_hbm, latents_hbm, dict_hbm],
        [scaled_ref, inputs_ref, latents_ref, dict_ref],
        sems,
    )
    join_halves(plan, own_ref, other_ref, full)
    grad = full[...].astype(F32)
    gain = gain_ref[...]
    started[0].wait()
    scaled_rebuilt = scaled_ref[...].astype(F32)
    rebuilt = scaled_rebuilt / gain
    inverse = inverse_ref[...]
    inner_row = jnp.sum(grad * scaled_rebuilt, axis=1, keepdims=True)
    inverse_cube = inverse * inverse * inverse
    started[1].wait()
    inputs = inputs_ref[...]
    rebuilt_grad = (
        inverse * (grad * gain)
        - (inverse_cube * (inner_row / plan.width)) * rebuilt
        + (rebuilt - inputs.astype(F32))
    ).astype(BF16)
    started[2].wait()
    started[3].wait()
    size = dict_ref.shape[0] // pieces
    writes = []
    for piece in range(pieces):
        span = slice(piece * size, (piece + 1) * size)
        latents = latents_ref[:, span]
        latent_grad = lax.dot_general(
            rebuilt_grad, dict_ref[span, :], ACROSS, preferred_element_type=F32
        )
        preact_grad = jnp.where(latents.astype(F32) > 0.0, latent_grad, 0.0).astype(BF16)
        out_ref[span, :] = (
            lax.dot_general(latents, rebuilt_grad, DOWNWARD, preferred_element_type=F32)
            + lax.dot_general(preact_grad, inputs, DOWNWARD, preferred_element_type=F32)
        ).astype(BF16)
        one = pltpu.make_async_copy(
            out_ref.at[span, :], out_hbm.at[span, :], out_sems.at[piece]
        )
        one.start()
        writes.append(one)
    for one in writes:
        one.wait()


def dictionary_step(plan, own, other, gain, scaled, inverse, inputs, latents, dictionary):
    units = dictionary.shape[0]
    pieces = units // (2 * LANES) if units % (2 * LANES) == 0 else 1
    return call(
        functools.partial(dictionary_body, plan, pieces),
        shaped(*dictionary.shape, dtype=BF16),
        (own, other, gain.reshape(1, -1), inverse),
        (scaled, inputs, latents, dictionary),
        [
            pltpu.VMEM((plan.rows, plan.width), BF16),
            pltpu.VMEM(dictionary.shape, BF16),
            pltpu.SemaphoreType.DMA((4,)),
            pltpu.SemaphoreType.DMA((pieces,)),
        ],
        out_specs=HBM,
        flops=6 * plan.rows * plan.width * units,
        moved=dictionary.size * 4,
    )


def swap(value):
    size = lax.axis_size("hidden")
    return lax.ppermute(value, "hidden", [(i, (i + 1) % size) for i in range(size)])


def partner_swap(value, bit):
    size = lax.axis_size("latent")
    return lax.ppermute(value, "latent", [(i, i ^ bit) for i in range(size)])


def grow(stack, bit):
    return jnp.concatenate([stack, partner_swap(stack, bit)], axis=0)


def shrink(kept, sent, bit):
    return kept + partner_swap(sent, bit).astype(F32)


def halved(stack):
    middle = stack.shape[0] // 2
    return stack[:middle], stack[middle:].astype(BF16)


def trade(stack):
    return lax.all_to_all(stack, "latent", 0, 0, tiled=False)


def own_chunk(plan, vector):
    flat = vector.reshape(plan.cores, plan.tiles, 1, LANES)
    flat = jnp.broadcast_to(flat, (plan.cores, plan.tiles, plan.rows, LANES))
    flat = flat.reshape(plan.cores, -1, LANES)
    flat = jnp.pad(flat, ((0, 0), (0, plan.flat - flat.shape[1]), (0, 0)))
    flat = lax.dynamic_index_in_dim(flat, lax.axis_index("hidden"), 0, keepdims=False)
    return lax.dynamic_slice_in_dim(
        flat, lax.axis_index("latent") * plan.chunk, plan.chunk, 0
    )


def traded_terms(plan, mine, theirs):
    half = (mine + swap(theirs)).astype(BF16)
    return trade(half.reshape(plan.chips, plan.chunk, LANES))


def per_device(
    input_codes,
    cotangent_codes,
    dictionary,
    encoder_bias,
    decoder_bias,
    norm_gain,
    gate_weight,
    up_weight,
    down_weight,
):
    plan = Plan(
        lax.axis_size("latent"), lax.axis_size("hidden"), input_codes.shape[0], input_codes.shape[1]
    )
    if not plan.fits():
        return per_device_plain(
            input_codes,
            cotangent_codes,
            dictionary,
            encoder_bias,
            decoder_bias,
            norm_gain,
            gate_weight,
            up_weight,
            down_weight,
        )
    bias_chunk = own_chunk(plan, decoder_bias)
    gain_chunk = own_chunk(plan, norm_gain)
    inputs_stack, cotangent = pack_codes(plan, input_codes, cotangent_codes)
    inputs_own = trade(inputs_stack)
    inputs_own, cotangent = lax.optimization_barrier((inputs_own, cotangent))
    for bit in plan.bits[:-1]:
        cotangent = grow(cotangent, bit)
    inputs, latents, mine, theirs = encode(
        plan, inputs_own, swap(inputs_own), dictionary, encoder_bias
    )
    half = (mine + swap(theirs)).astype(BF16)
    half, cotangent = lax.optimization_barrier((half, cotangent))
    terms = trade(half.reshape(plan.chips, plan.chunk, LANES))
    cotangent = grow(cotangent, plan.bits[-1])
    hidden_grad = back_project(plan, cotangent, swap(cotangent), down_weight)
    scaled_own = trade(sum_rebuilt(plan, terms, bias_chunk, gain_chunk))
    scaled, inverse, hidden, mine, theirs = mlp(
        plan, scaled_own, swap(scaled_own), norm_gain, hidden_grad, gate_weight, up_weight
    )
    terms = traded_terms(plan, mine, theirs)
    out_mine, out_theirs = project(plan, hidden, down_weight)
    kept, sent = halved(out_mine + swap(out_theirs))
    kept = shrink(kept, sent, plan.bits[-1])
    grad_own = trade(sum_grad(plan, terms))
    grad_own, kept = lax.optimization_barrier((grad_own, kept))
    kept, sent = halved(kept)
    grad_other = swap(grad_own)
    for bit in reversed(plan.bits[1:-1]):
        kept, sent = halved(shrink(kept, sent, bit))
    grad_other, kept, sent = lax.optimization_barrier((grad_other, kept, sent))
    block_output = finish_output(plan, kept, partner_swap(sent, plan.bits[0]))
    dictionary_grad = dictionary_step(
        plan, grad_own, grad_other, norm_gain, scaled, inverse, inputs, latents, dictionary
    )
    return (block_output, dictionary_grad)


def per_device_plain(
    input_codes,
    cotangent_codes,
    dictionary,
    encoder_bias,
    decoder_bias,
    norm_gain,
    gate_weight,
    up_weight,
    down_weight,
):
    own_width = input_codes.shape[1]
    model_width = own_width * lax.axis_size(("latent", "hidden"))
    cotangent_local = (cotangent_codes.astype(jnp.float32) * CODE_STEP).astype(jnp.bfloat16)
    inputs_local = (input_codes.astype(jnp.float32) * CODE_STEP).astype(jnp.bfloat16)
    inputs = lax.all_gather(inputs_local, ("latent", "hidden"), axis=1, tiled=True)
    preact = (
        lax.dot_general(inputs, dictionary, ACROSS, preferred_element_type=jnp.float32)
        + encoder_bias
    )
    latents = jnp.maximum(preact, 0.0).astype(jnp.bfloat16)
    partial_value = jnp.dot(latents, dictionary, preferred_element_type=jnp.float32)
    rebuilt = lax.psum(partial_value, ("latent", "hidden")) + decoder_bias
    inverse = lax.rsqrt(
        jnp.sum(rebuilt * rebuilt, axis=1, keepdims=True) / model_width + NORM_EPSILON
    )
    normed = (rebuilt * inverse * norm_gain).astype(jnp.bfloat16)
    target = inputs.astype(jnp.float32)
    gate_proj = lax.dot_general(normed, gate_weight, ACROSS, preferred_element_type=jnp.float32)
    up_proj = lax.dot_general(normed, up_weight, ACROSS, preferred_element_type=jnp.float32)
    gelu_value, gelu_slope = gelu_parts(gate_proj)
    hidden = (gelu_value * up_proj).astype(jnp.bfloat16)
    output_terms = jnp.dot(hidden, down_weight, preferred_element_type=jnp.float32)
    block_output = lax.psum_scatter(
        output_terms, ("latent", "hidden"), scatter_dimension=1, tiled=True
    ).astype(jnp.bfloat16)
    hidden_grad = lax.dot_general(
        lax.all_gather(cotangent_local, ("latent", "hidden"), axis=1, tiled=True),
        down_weight,
        ACROSS,
        preferred_element_type=jnp.float32,
    )
    gate_grad = (hidden_grad * up_proj * gelu_slope).astype(jnp.bfloat16)
    up_grad = (hidden_grad * gelu_value).astype(jnp.bfloat16)
    partial_grad = jnp.dot(gate_grad, gate_weight, preferred_element_type=jnp.float32) + jnp.dot(
        up_grad, up_weight, preferred_element_type=jnp.float32
    )
    scaled = lax.psum(partial_grad, ("latent", "hidden")) * norm_gain
    inner_row = jnp.sum(scaled * rebuilt, axis=1, keepdims=True)
    inverse_cube = inverse * inverse * inverse
    rebuilt_grad = (
        inverse * scaled - inverse_cube * rebuilt * (inner_row / model_width) + (rebuilt - target)
    ).astype(jnp.bfloat16)
    latent_grad = lax.dot_general(
        rebuilt_grad, dictionary, ACROSS, preferred_element_type=jnp.float32
    )
    preact_grad = jnp.where(preact > 0.0, latent_grad, 0.0).astype(jnp.bfloat16)
    dictionary_grad = lax.dot_general(
        latents, rebuilt_grad, DOWNWARD, preferred_element_type=jnp.float32
    ) + lax.dot_general(preact_grad, inputs, DOWNWARD, preferred_element_type=jnp.float32)
    return (block_output, dictionary_grad.astype(jnp.bfloat16))


def solution(mesh):
    in_specs = (
        P("groups", ("latent", "hidden")),
        P("groups", ("latent", "hidden")),
        P(("latent", "hidden"), None),
        P(("latent", "hidden")),
        P(),
        P(),
        P(("latent", "hidden"), None),
        P(("latent", "hidden"), None),
        P(("latent", "hidden"), None),
    )
    out_specs = (P("groups", ("latent", "hidden")), P(("latent", "hidden"), "groups"))
    return jax.shard_map(
        per_device, mesh=mesh, in_specs=in_specs, out_specs=out_specs, check_vma=False
    )
```

```python
import functools
import math

import jax
import jax.numpy as jnp
from jax import lax
from jax.experimental import pallas as pl
from jax.experimental.pallas import tpu as pltpu
from jax.sharding import PartitionSpec as P

CODE_STEP = 2.0 ** (-6)
NORM_EPSILON = 1e-06
GELU_ROOT = 0.7978845608028654
GELU_CUBIC = 0.044715
ACROSS = (((1,), (1,)), ((), ()))
DOWNWARD = (((0,), (0,)), ((), ()))
LANES = 128
ROW_TILE = 16
VMEM_BYTES = 53 * 1024 * 1024
VMEM_MOST = 60 * 1024 * 1024
F32 = jnp.float32
BF16 = jnp.bfloat16


def gelu_parts(values):
    argument = GELU_ROOT * (values + GELU_CUBIC * values * values * values)
    tanh_value = jnp.tanh(argument)
    result = 0.5 * values * (1.0 + tanh_value)
    derivative = 0.5 * (1.0 + tanh_value) + 0.5 * values * (
        1.0 - tanh_value * tanh_value
    ) * GELU_ROOT * (1.0 + 3.0 * GELU_CUBIC * values * values)
    return (result, derivative)


def up_to(value, unit):
    return -(-value // unit) * unit


class Plan:
    def __init__(self, chips, cores, rows, own):
        self.chips, self.cores, self.rows, self.own = chips, cores, rows, own
        self.width = own * chips * cores
        self.half = self.width // cores
        self.tiles = self.half // LANES
        self.chunk = up_to(-(-self.tiles * rows // chips), ROW_TILE)
        self.flat = self.chunk * chips
        self.tail = own - LANES
        if self.tail > 0:
            self.fold_rows = min(
                size
                for size in range(ROW_TILE, rows + ROW_TILE, ROW_TILE)
                if -(-rows // size) * self.tail <= LANES
            )
            self.packed = rows + self.fold_rows
        self.bits = [1 << k for k in reversed(range((chips - 1).bit_length()))]
        self.order = [0]
        for bit in self.bits:
            self.order = self.order + [place ^ bit for place in self.order]

    def fits(self):
        return (
            self.cores == 2
            and len(self.order) == self.chips
            and self.rows % ROW_TILE == 0
            and self.half % LANES == 0
            and 0 < self.tail < LANES
        )


HBM = pl.BlockSpec(memory_space=pltpu.HBM)
ONCHIP = pl.BlockSpec(memory_space=pltpu.VMEM)


def shaped(*dims, dtype=F32):
    return jax.ShapeDtypeStruct(dims, dtype)


def padded_bytes(array):
    *lead, rows, columns = array.shape
    item = jnp.dtype(array.dtype).itemsize
    return math.prod(lead) * up_to(rows, ROW_TILE) * up_to(columns, LANES) * item


def call(body, out_shapes, operands, fetched=(), scratch=(), out_specs=None, flops=0, moved=0, grant=VMEM_BYTES):
    outputs = jax.tree.leaves(out_shapes) if out_specs is None else []
    taken = sum(padded_bytes(one) for one in list(operands) + outputs)
    return pl.pallas_call(
        body,
        out_shape=out_shapes,
        in_specs=[ONCHIP] * len(operands) + [HBM] * len(fetched),
        out_specs=jax.tree.map(lambda _: ONCHIP, out_shapes) if out_specs is None else out_specs,
        scratch_shapes=[pltpu.VMEM(one.shape, one.dtype) for one in fetched] + list(scratch),
        compiler_params=pltpu.CompilerParams(vmem_limit_bytes=grant - taken),
        cost_estimate=pl.CostEstimate(flops=flops, bytes_accessed=moved, transcendentals=0),
    )(*operands, *fetched)


def copies(sources, targets, sems, first=0):
    started = []
    for index, (source, target) in enumerate(zip(sources, targets)):
        one = pltpu.make_async_copy(source, target, sems.at[first + index])
        one.start()
        started.append(one)
    return started


def pack_block(plan, block):
    tail = block[:, LANES:]
    folded = []
    for start in range(0, plan.rows, plan.fold_rows):
        piece = tail[start : min(start + plan.fold_rows, plan.rows), :]
        short = plan.fold_rows - piece.shape[0]
        if short:
            piece = jnp.concatenate([piece, jnp.zeros((short, plan.tail), block.dtype)], axis=0)
        folded.append(piece)
    fill = LANES - len(folded) * plan.tail
    if fill:
        folded.append(jnp.zeros((plan.fold_rows, fill), block.dtype))
    return block[:, :LANES], jnp.concatenate(folded, axis=1)


def unpack_block(plan, packed):
    pieces = []
    for fold, start in enumerate(range(0, plan.rows, plan.fold_rows)):
        count = min(plan.fold_rows, plan.rows - start)
        pieces.append(
            packed[plan.rows : plan.rows + count, fold * plan.tail : (fold + 1) * plan.tail]
        )
    return jnp.concatenate([packed[: plan.rows, :], jnp.concatenate(pieces, axis=0)], axis=1)


def pack_codes_body(plan, input_hbm, cotangent_hbm, inputs_ref, cotangent_out_ref, input_ref, cotangent_ref, sems):
    for copy in copies([input_hbm, cotangent_hbm], [input_ref, cotangent_ref], sems):
        copy.wait()
    main, tail = pack_block(plan, input_ref[...].astype(F32) * CODE_STEP)
    for chip in range(plan.chips):
        inputs_ref[chip, : plan.rows, :] = main.astype(BF16)
        inputs_ref[chip, plan.rows :, :] = tail.astype(BF16)
    main, tail = pack_block(plan, cotangent_ref[...].astype(F32) * CODE_STEP)
    cotangent_out_ref[0, : plan.rows, :] = main.astype(BF16)
    cotangent_out_ref[0, plan.rows :, :] = tail.astype(BF16)


def pack_codes(plan, input_codes, cotangent_codes):
    return call(
        functools.partial(pack_codes_body, plan),
        [
            shaped(plan.chips, plan.packed, LANES, dtype=BF16),
            shaped(1, plan.packed, LANES, dtype=BF16),
        ],
        (),
        (input_codes, cotangent_codes),
        [pltpu.SemaphoreType.DMA((2,))],
        moved=plan.rows * plan.own * 8,
        grant=VMEM_MOST,
    )


def assemble(plan, relative, own_ref, other_ref, both, full_ref):
    core = lax.axis_index("hidden")
    if relative:
        me = lax.axis_index("latent")
        for place, partner in enumerate(plan.order):
            chip = me ^ partner
            both[core, chip] = own_ref[place]
            both[1 - core, chip] = other_ref[place]
    else:
        both[core] = own_ref[...]
        both[1 - core] = other_ref[...]
    for chip in range(plan.chips):
        for side in range(plan.cores):
            column = (chip * plan.cores + side) * plan.own
            block = unpack_block(plan, both[side, chip].astype(F32))
            full_ref[:, column : column + plan.own] = block.astype(BF16)


def both_scratch(plan, dtype=BF16):
    return pltpu.VMEM((plan.cores, plan.chips, plan.packed, LANES), dtype)


def halves_of_product(plan, pairs, mine_ref, theirs_ref, gain_ref=None, bias_ref=None):
    core = lax.axis_index("hidden")
    for target, side in ((theirs_ref, 1 - core), (mine_ref, core)):
        start = pl.multiple_of(side * plan.half, LANES)
        total = None
        for left, right_ref in pairs:
            term = jnp.dot(
                left, right_ref[:, pl.ds(start, plan.half)], preferred_element_type=F32
            )
            total = term if total is None else total + term
        if gain_ref is not None:
            once = jnp.where((lax.axis_index("latent") == 0) & (side == core), 1.0, 0.0)
            bias = bias_ref[:, pl.ds(start, plan.half)] * once
            total = (total + bias) * gain_ref[:, pl.ds(start, plan.half)]
        for tile in range(plan.tiles):
            target[tile * plan.rows : (tile + 1) * plan.rows, :] = total[
                :, tile * LANES : (tile + 1) * LANES
            ].astype(target.dtype)
        used = plan.tiles * plan.rows
        if used < plan.flat:
            target[used:, :] = jnp.zeros((plan.flat - used, LANES), target.dtype)


def encode_body(plan, own_ref, other_ref, dict_hbm, bias_hbm, decoder_hbm, gain_hbm, inputs_ref, latents_ref, mine_ref, theirs_ref, dict_ref, bias_ref, decoder_ref, gain_ref, both, sems):
    started = copies(
        [dict_hbm, bias_hbm, decoder_hbm, gain_hbm], [dict_ref, bias_ref, decoder_ref, gain_ref], sems
    )
    assemble(plan, False, own_ref, other_ref, both, inputs_ref)
    for copy in started:
        copy.wait()
    preact = (
        lax.dot_general(inputs_ref[...], dict_ref[...], ACROSS, preferred_element_type=F32)
        + bias_ref[...]
    )
    latents = jnp.maximum(preact, 0.0).astype(BF16)
    latents_ref[...] = latents
    halves_of_product(plan, [(latents, dict_ref)], mine_ref, theirs_ref, gain_ref, decoder_ref)


def encode(plan, own, other, dictionary, encoder_bias, decoder_bias, gain):
    latents = dictionary.shape[0]
    return call(
        functools.partial(encode_body, plan),
        [
            shaped(plan.rows, plan.width, dtype=BF16),
            shaped(plan.rows, latents, dtype=BF16),
            shaped(plan.flat, LANES),
            shaped(plan.flat, LANES),
        ],
        (own, other),
        (dictionary, encoder_bias.reshape(1, -1), decoder_bias.reshape(1, -1), gain.reshape(1, -1)),
        [both_scratch(plan), pltpu.SemaphoreType.DMA((4,))],
        flops=4 * plan.rows * plan.width * latents,
        moved=dictionary.size * 2,
    )


def back_project_body(plan, own_ref, other_ref, down_hbm, grad_ref, down_ref, both, full, sems):
    (copy,) = copies([down_hbm], [down_ref], sems)
    assemble(plan, True, own_ref, other_ref, both, full)
    copy.wait()
    grad_ref[...] = lax.dot_general(
        full[...], down_ref[...], ACROSS, preferred_element_type=F32
    )


def back_project(plan, own, other, down_weight):
    units = down_weight.shape[0]
    return call(
        functools.partial(back_project_body, plan),
        shaped(plan.rows, units),
        (own, other),
        (down_weight,),
        [both_scratch(plan), pltpu.VMEM((plan.rows, plan.width), BF16), pltpu.SemaphoreType.DMA((1,))],
        flops=2 * plan.rows * plan.width * units,
        moved=down_weight.size * 2,
    )


def join_halves(plan, own_ref, other_ref, full_ref):
    core = lax.axis_index("hidden")
    for source, side in ((own_ref, core), (other_ref, 1 - core)):
        for tile in range(plan.tiles):
            column = pl.multiple_of(side * plan.half + tile * LANES, LANES)
            row = 0
            while row < plan.rows:
                chip, place = divmod(tile * plan.rows + row, plan.chunk)
                count = min(plan.rows - row, plan.chunk - place)
                full_ref[row : row + count, pl.ds(column, LANES)] = source[
                    chip, place : place + count, :
                ]
                row += count


def mlp_body(plan, own_ref, other_ref, gate_hbm, up_hbm, gain_hbm, grad_hbm, scaled_ref, inverse_ref, hidden_ref, mine_ref, theirs_ref, gate_ref, up_ref, gain_ref, grad_ref, sems):
    gain_copy, gate_copy, up_copy, grad_copy = copies(
        [gain_hbm, gate_hbm, up_hbm, grad_hbm], [gain_ref, gate_ref, up_ref, grad_ref], sems
    )
    join_halves(plan, own_ref, other_ref, scaled_ref)
    scaled = scaled_ref[...]
    gain_copy.wait()
    rebuilt = scaled.astype(F32) / gain_ref[...]
    inverse = lax.rsqrt(
        jnp.sum(rebuilt * rebuilt, axis=1, keepdims=True) / plan.width + NORM_EPSILON
    )
    inverse_ref[...] = inverse
    gate_copy.wait()
    gate_proj = inverse * lax.dot_general(
        scaled, gate_ref[...], ACROSS, preferred_element_type=F32
    )
    up_copy.wait()
    up_proj = inverse * lax.dot_general(
        scaled, up_ref[...], ACROSS, preferred_element_type=F32
    )
    gelu_value, gelu_slope = gelu_parts(gate_proj)
    hidden_ref[...] = (gelu_value * up_proj).astype(BF16)
    grad_copy.wait()
    hidden_grad = grad_ref[...]
    gate_grad = (hidden_grad * up_proj * gelu_slope).astype(BF16)
    up_grad = (hidden_grad * gelu_value).astype(BF16)
    halves_of_product(plan, [(gate_grad, gate_ref), (up_grad, up_ref)], mine_ref, theirs_ref)


def mlp(plan, own, other, gain, hidden_grad, gate_weight, up_weight):
    units = gate_weight.shape[0]
    return call(
        functools.partial(mlp_body, plan),
        [
            shaped(plan.rows, plan.width, dtype=BF16),
            shaped(plan.rows, 1),
            shaped(plan.rows, units, dtype=BF16),
            shaped(plan.flat, LANES),
            shaped(plan.flat, LANES),
        ],
        (own, other),
        (gate_weight, up_weight, gain.reshape(1, -1), hidden_grad),
        [pltpu.SemaphoreType.DMA((4,))],
        flops=8 * plan.rows * plan.width * units,
        moved=gate_weight.size * 4,
    )


def project_body(plan, hidden_ref, down_hbm, mine_ref, theirs_ref, down_ref, both, sems):
    (copy,) = copies([down_hbm], [down_ref], sems)
    core = lax.axis_index("hidden")
    copy.wait()
    terms = jnp.dot(hidden_ref[...], down_ref[...], preferred_element_type=F32)
    for chip in range(plan.chips):
        for side in range(plan.cores):
            start = (chip * plan.cores + side) * plan.own
            main, tail = pack_block(plan, terms[:, start : start + plan.own])
            both[side, chip, : plan.rows, :] = main
            both[side, chip, plan.rows :, :] = tail
    me = lax.axis_index("latent")
    for place, partner in enumerate(plan.order):
        chip = me ^ partner
        mine_ref[place] = both[core, chip]
        theirs_ref[place] = both[1 - core, chip]


def project(plan, hidden, down_weight):
    units = down_weight.shape[0]
    return call(
        functools.partial(project_body, plan),
        [shaped(plan.chips, plan.packed, LANES)] * 2,
        (hidden,),
        (down_weight,),
        [both_scratch(plan, F32), pltpu.SemaphoreType.DMA((1,))],
        flops=2 * plan.rows * plan.width * units,
        moved=down_weight.size * 2,
    )


def total_of(plan, terms_ref, start, count):
    total = terms_ref[0, start : start + count, :].astype(F32)
    for chip in range(1, plan.chips):
        total = total + terms_ref[chip, start : start + count, :].astype(F32)
    return total


def sum_body(plan, terms_ref, out_ref):
    total = total_of(plan, terms_ref, 0, plan.chunk).astype(BF16)
    for chip in range(plan.chips):
        out_ref[chip] = total


def sum_terms(plan, terms):
    return call(
        functools.partial(sum_body, plan),
        shaped(plan.chips, plan.chunk, LANES, dtype=BF16),
        (terms,),
        moved=terms.size * 4,
    )


def finish_output_body(plan, kept_ref, out_ref):
    out_ref[...] = unpack_block(plan, kept_ref[0]).astype(BF16)


def finish_output(plan, kept):
    return call(
        functools.partial(finish_output_body, plan),
        shaped(plan.rows, plan.own, dtype=BF16),
        (kept,),
        moved=kept.size * 4,
    )


def dictionary_body(plan, pieces, own_ref, other_ref, gain_hbm, inverse_hbm, scaled_hbm, inputs_hbm, latents_hbm, dict_hbm, out_hbm, gain_ref, inverse_ref, scaled_ref, inputs_ref, latents_ref, dict_ref, full, out_ref, sems, out_sems):
    started = copies(
        [gain_hbm, inverse_hbm, scaled_hbm, inputs_hbm, latents_hbm, dict_hbm],
        [gain_ref, inverse_ref, scaled_ref, inputs_ref, latents_ref, dict_ref],
        sems,
    )
    join_halves(plan, own_ref, other_ref, full)
    grad = full[...].astype(F32)
    for copy in started[:3]:
        copy.wait()
    gain = gain_ref[...]
    scaled_rebuilt = scaled_ref[...].astype(F32)
    rebuilt = scaled_rebuilt / gain
    inverse = inverse_ref[...]
    inner_row = jnp.sum(grad * scaled_rebuilt, axis=1, keepdims=True)
    inverse_cube = inverse * inverse * inverse
    started[3].wait()
    inputs = inputs_ref[...]
    rebuilt_grad = (
        inverse * (grad * gain)
        - (inverse_cube * (inner_row / plan.width)) * rebuilt
        + (rebuilt - inputs.astype(F32))
    ).astype(BF16)
    started[4].wait()
    started[5].wait()
    size = dict_ref.shape[0] // pieces
    writes = []
    for piece in range(pieces):
        span = slice(piece * size, (piece + 1) * size)
        latents = latents_ref[:, span]
        latent_grad = lax.dot_general(
            rebuilt_grad, dict_ref[span, :], ACROSS, preferred_element_type=F32
        )
        preact_grad = jnp.where(latents.astype(F32) > 0.0, latent_grad, 0.0).astype(BF16)
        out_ref[span, :] = (
            lax.dot_general(latents, rebuilt_grad, DOWNWARD, preferred_element_type=F32)
            + lax.dot_general(preact_grad, inputs, DOWNWARD, preferred_element_type=F32)
        ).astype(BF16)
        one = pltpu.make_async_copy(
            out_ref.at[span, :], out_hbm.at[span, :], out_sems.at[piece]
        )
        one.start()
        writes.append(one)
    for one in writes:
        one.wait()


def dictionary_step(plan, own, other, gain, scaled, inverse, inputs, latents, dictionary):
    units = dictionary.shape[0]
    pieces = units // (2 * LANES) if units % (2 * LANES) == 0 else 1
    return call(
        functools.partial(dictionary_body, plan, pieces),
        shaped(*dictionary.shape, dtype=BF16),
        (own, other),
        (gain.reshape(1, -1), inverse, scaled, inputs, latents, dictionary),
        [
            pltpu.VMEM((plan.rows, plan.width), BF16),
            pltpu.VMEM(dictionary.shape, BF16),
            pltpu.SemaphoreType.DMA((6,)),
            pltpu.SemaphoreType.DMA((pieces,)),
        ],
        out_specs=HBM,
        flops=6 * plan.rows * plan.width * units,
        moved=dictionary.size * 4,
    )


def swap(value):
    size = lax.axis_size("hidden")
    return lax.ppermute(value, "hidden", [(i, (i + 1) % size) for i in range(size)])


def partner_swap(value, bit):
    size = lax.axis_size("latent")
    return lax.ppermute(value, "latent", [(i, i ^ bit) for i in range(size)])


def grow(stack, bit):
    return jnp.concatenate([stack, partner_swap(stack, bit)], axis=0)


def shrink(kept, sent, bit):
    return kept + partner_swap(sent, bit).astype(F32)


def halved(stack):
    middle = stack.shape[0] // 2
    return stack[:middle], stack[middle:].astype(BF16)


def trade(stack):
    return lax.all_to_all(stack, "latent", 0, 0, tiled=False)


def per_device(
    input_codes,
    cotangent_codes,
    dictionary,
    encoder_bias,
    decoder_bias,
    norm_gain,
    gate_weight,
    up_weight,
    down_weight,
):
    plan = Plan(
        lax.axis_size("latent"), lax.axis_size("hidden"), input_codes.shape[0], input_codes.shape[1]
    )
    if not plan.fits():
        return per_device_plain(
            input_codes,
            cotangent_codes,
            dictionary,
            encoder_bias,
            decoder_bias,
            norm_gain,
            gate_weight,
            up_weight,
            down_weight,
        )
    inputs_stack, cotangent = pack_codes(plan, input_codes, cotangent_codes)
    inputs_own = trade(inputs_stack)
    cotangent = grow(cotangent, plan.bits[0])
    inputs_own, cotangent = lax.optimization_barrier((inputs_own, cotangent))
    inputs, latents, mine, theirs = encode(
        plan, inputs_own, swap(inputs_own), dictionary, encoder_bias, decoder_bias, norm_gain
    )
    half = (mine + swap(theirs)).astype(BF16)
    half, cotangent = lax.optimization_barrier((half, cotangent))
    terms = trade(half.reshape(plan.chips, plan.chunk, LANES))
    for bit in plan.bits[1:]:
        cotangent = grow(cotangent, bit)
    scaled_stack = sum_terms(plan, terms)
    scaled_stack, cotangent = lax.optimization_barrier((scaled_stack, cotangent))
    scaled_own = trade(scaled_stack)
    hidden_grad = back_project(plan, cotangent, swap(cotangent), down_weight)
    scaled_own, hidden_grad = lax.optimization_barrier((scaled_own, hidden_grad))
    scaled, inverse, hidden, mine, theirs = mlp(
        plan, scaled_own, swap(scaled_own), norm_gain, hidden_grad, gate_weight, up_weight
    )
    half = (mine + swap(theirs)).astype(BF16)
    out_mine, out_theirs = project(plan, hidden, down_weight)
    half, out_mine, out_theirs = lax.optimization_barrier((half, out_mine, out_theirs))
    terms = trade(half.reshape(plan.chips, plan.chunk, LANES))
    kept, sent = halved(out_mine + swap(out_theirs))
    kept = shrink(kept, sent, plan.bits[-1])
    grad_stack = sum_terms(plan, terms)
    grad_stack, kept = lax.optimization_barrier((grad_stack, kept))
    grad_own = trade(grad_stack)
    for bit in reversed(plan.bits[:-1]):
        kept, sent = halved(kept)
        kept = shrink(kept, sent, bit)
    grad_own, kept = lax.optimization_barrier((grad_own, kept))
    block_output = finish_output(plan, kept)
    dictionary_grad = dictionary_step(
        plan, grad_own, swap(grad_own), norm_gain, scaled, inverse, inputs, latents, dictionary
    )
    return (block_output, dictionary_grad)


def per_device_plain(
    input_codes,
    cotangent_codes,
    dictionary,
    encoder_bias,
    decoder_bias,
    norm_gain,
    gate_weight,
    up_weight,
    down_weight,
):
    own_width = input_codes.shape[1]
    model_width = own_width * lax.axis_size(("latent", "hidden"))
    cotangent_local = (cotangent_codes.astype(jnp.float32) * CODE_STEP).astype(jnp.bfloat16)
    inputs_local = (input_codes.astype(jnp.float32) * CODE_STEP).astype(jnp.bfloat16)
    inputs = lax.all_gather(inputs_local, ("latent", "hidden"), axis=1, tiled=True)
    preact = (
        lax.dot_general(inputs, dictionary, ACROSS, preferred_element_type=jnp.float32)
        + encoder_bias
    )
    latents = jnp.maximum(preact, 0.0).astype(jnp.bfloat16)
    partial_value = jnp.dot(latents, dictionary, preferred_element_type=jnp.float32)
    rebuilt = lax.psum(partial_value, ("latent", "hidden")) + decoder_bias
    inverse = lax.rsqrt(
        jnp.sum(rebuilt * rebuilt, axis=1, keepdims=True) / model_width + NORM_EPSILON
    )
    normed = (rebuilt * inverse * norm_gain).astype(jnp.bfloat16)
    target = inputs.astype(jnp.float32)
    gate_proj = lax.dot_general(normed, gate_weight, ACROSS, preferred_element_type=jnp.float32)
    up_proj = lax.dot_general(normed, up_weight, ACROSS, preferred_element_type=jnp.float32)
    gelu_value, gelu_slope = gelu_parts(gate_proj)
    hidden = (gelu_value * up_proj).astype(jnp.bfloat16)
    output_terms = jnp.dot(hidden, down_weight, preferred_element_type=jnp.float32)
    block_output = lax.psum_scatter(
        output_terms, ("latent", "hidden"), scatter_dimension=1, tiled=True
    ).astype(jnp.bfloat16)
    hidden_grad = lax.dot_general(
        lax.all_gather(cotangent_local, ("latent", "hidden"), axis=1, tiled=True),
        down_weight,
        ACROSS,
        preferred_element_type=jnp.float32,
    )
    gate_grad = (hidden_grad * up_proj * gelu_slope).astype(jnp.bfloat16)
    up_grad = (hidden_grad * gelu_value).astype(jnp.bfloat16)
    partial_grad = jnp.dot(gate_grad, gate_weight, preferred_element_type=jnp.float32) + jnp.dot(
        up_grad, up_weight, preferred_element_type=jnp.float32
    )
    scaled = lax.psum(partial_grad, ("latent", "hidden")) * norm_gain
    inner_row = jnp.sum(scaled * rebuilt, axis=1, keepdims=True)
    inverse_cube = inverse * inverse * inverse
    rebuilt_grad = (
        inverse * scaled - inverse_cube * rebuilt * (inner_row / model_width) + (rebuilt - target)
    ).astype(jnp.bfloat16)
    latent_grad = lax.dot_general(
        rebuilt_grad, dictionary, ACROSS, preferred_element_type=jnp.float32
    )
    preact_grad = jnp.where(preact > 0.0, latent_grad, 0.0).astype(jnp.bfloat16)
    dictionary_grad = lax.dot_general(
        latents, rebuilt_grad, DOWNWARD, preferred_element_type=jnp.float32
    ) + lax.dot_general(preact_grad, inputs, DOWNWARD, preferred_element_type=jnp.float32)
    return (block_output, dictionary_grad.astype(jnp.bfloat16))


def solution(mesh):
    in_specs = (
        P("groups", ("latent", "hidden")),
        P("groups", ("latent", "hidden")),
        P(("latent", "hidden"), None),
        P(("latent", "hidden")),
        P(),
        P(),
        P(("latent", "hidden"), None),
        P(("latent", "hidden"), None),
        P(("latent", "hidden"), None),
    )
    out_specs = (P("groups", ("latent", "hidden")), P(("latent", "hidden"), "groups"))
    return jax.shard_map(
        per_device, mesh=mesh, in_specs=in_specs, out_specs=out_specs, check_vma=False
    )
```

```python
import functools
import math

import jax
import jax.numpy as jnp
from jax import lax
from jax.experimental import pallas as pl
from jax.experimental.pallas import tpu as pltpu
from jax.sharding import PartitionSpec as P

CODE_STEP = 2.0 ** (-6)
NORM_EPSILON = 1e-06
GELU_ROOT = 0.7978845608028654
GELU_CUBIC = 0.044715
ACROSS = (((1,), (1,)), ((), ()))
DOWNWARD = (((0,), (0,)), ((), ()))
LANES = 128
ROW_TILE = 16
VMEM_BYTES = 53 * 1024 * 1024
VMEM_MOST = 60 * 1024 * 1024
F32 = jnp.float32
BF16 = jnp.bfloat16


def gelu_parts(values):
    argument = GELU_ROOT * (values + GELU_CUBIC * values * values * values)
    tanh_value = jnp.tanh(argument)
    result = 0.5 * values * (1.0 + tanh_value)
    derivative = 0.5 * (1.0 + tanh_value) + 0.5 * values * (
        1.0 - tanh_value * tanh_value
    ) * GELU_ROOT * (1.0 + 3.0 * GELU_CUBIC * values * values)
    return (result, derivative)


def up_to(value, unit):
    return -(-value // unit) * unit


class Plan:
    def __init__(self, chips, cores, rows, own):
        self.chips, self.cores, self.rows, self.own = chips, cores, rows, own
        self.width = own * chips * cores
        self.half = self.width // cores
        self.tiles = self.half // LANES
        self.chunk = up_to(-(-self.tiles * rows // chips), ROW_TILE)
        self.flat = self.chunk * chips
        self.tail = own - LANES
        if self.tail > 0:
            self.fold_rows = min(
                size
                for size in range(ROW_TILE, rows + ROW_TILE, ROW_TILE)
                if -(-rows // size) * self.tail <= LANES
            )
            self.packed = rows + self.fold_rows
        self.bits = [1 << k for k in reversed(range((chips - 1).bit_length()))]
        self.order = [0]
        for bit in self.bits:
            self.order = self.order + [place ^ bit for place in self.order]

    def fits(self):
        return (
            self.cores == 2
            and len(self.order) == self.chips
            and self.rows % ROW_TILE == 0
            and self.half % LANES == 0
            and 0 < self.tail < LANES
        )


HBM = pl.BlockSpec(memory_space=pltpu.HBM)
ONCHIP = pl.BlockSpec(memory_space=pltpu.VMEM)


def shaped(*dims, dtype=F32):
    return jax.ShapeDtypeStruct(dims, dtype)


def padded_bytes(array):
    *lead, rows, columns = array.shape
    item = jnp.dtype(array.dtype).itemsize
    return math.prod(lead) * up_to(rows, ROW_TILE) * up_to(columns, LANES) * item


def call(body, out_shapes, operands, fetched=(), scratch=(), out_specs=None, flops=0, moved=0, grant=VMEM_BYTES):
    outputs = jax.tree.leaves(out_shapes) if out_specs is None else []
    taken = sum(padded_bytes(one) for one in list(operands) + outputs)
    return pl.pallas_call(
        body,
        out_shape=out_shapes,
        in_specs=[ONCHIP] * len(operands) + [HBM] * len(fetched),
        out_specs=jax.tree.map(lambda _: ONCHIP, out_shapes) if out_specs is None else out_specs,
        scratch_shapes=[pltpu.VMEM(one.shape, one.dtype) for one in fetched] + list(scratch),
        compiler_params=pltpu.CompilerParams(vmem_limit_bytes=grant - taken),
        cost_estimate=pl.CostEstimate(flops=flops, bytes_accessed=moved, transcendentals=0),
    )(*operands, *fetched)


def copies(sources, targets, sems, first=0):
    started = []
    for index, (source, target) in enumerate(zip(sources, targets)):
        one = pltpu.make_async_copy(source, target, sems.at[first + index])
        one.start()
        started.append(one)
    return started


def bring_body(count, *refs):
    sources, targets, sems = refs[:count], refs[count : 2 * count], refs[2 * count]
    for copy in copies(sources, targets, sems):
        copy.wait()


def bring(*arrays):
    return pl.pallas_call(
        functools.partial(bring_body, len(arrays)),
        out_shape=[jax.ShapeDtypeStruct(one.shape, one.dtype) for one in arrays],
        in_specs=[HBM] * len(arrays),
        out_specs=[ONCHIP] * len(arrays),
        scratch_shapes=[pltpu.SemaphoreType.DMA((len(arrays),))],
        compiler_params=pltpu.CompilerParams(
            vmem_limit_bytes=VMEM_BYTES - sum(map(padded_bytes, arrays))
        ),
        cost_estimate=pl.CostEstimate(
            flops=0, bytes_accessed=2 * sum(map(padded_bytes, arrays)), transcendentals=0
        ),
    )(*arrays)


def pack_block(plan, block):
    tail = block[:, LANES:]
    folded = []
    for start in range(0, plan.rows, plan.fold_rows):
        piece = tail[start : min(start + plan.fold_rows, plan.rows), :]
        short = plan.fold_rows - piece.shape[0]
        if short:
            piece = jnp.concatenate([piece, jnp.zeros((short, plan.tail), block.dtype)], axis=0)
        folded.append(piece)
    fill = LANES - len(folded) * plan.tail
    if fill:
        folded.append(jnp.zeros((plan.fold_rows, fill), block.dtype))
    return block[:, :LANES], jnp.concatenate(folded, axis=1)


def unpack_block(plan, packed):
    pieces = []
    for fold, start in enumerate(range(0, plan.rows, plan.fold_rows)):
        count = min(plan.fold_rows, plan.rows - start)
        pieces.append(
            packed[plan.rows : plan.rows + count, fold * plan.tail : (fold + 1) * plan.tail]
        )
    return jnp.concatenate([packed[: plan.rows, :], jnp.concatenate(pieces, axis=0)], axis=1)


def pack_codes_body(plan, input_hbm, cotangent_hbm, inputs_ref, cotangent_out_ref, input_ref, cotangent_ref, sems):
    for copy in copies([input_hbm, cotangent_hbm], [input_ref, cotangent_ref], sems):
        copy.wait()
    main, tail = pack_block(plan, input_ref[...].astype(F32) * CODE_STEP)
    for chip in range(plan.chips):
        inputs_ref[chip, : plan.rows, :] = main.astype(BF16)
        inputs_ref[chip, plan.rows :, :] = tail.astype(BF16)
    main, tail = pack_block(plan, cotangent_ref[...].astype(F32) * CODE_STEP)
    cotangent_out_ref[0, : plan.rows, :] = main.astype(BF16)
    cotangent_out_ref[0, plan.rows :, :] = tail.astype(BF16)


def pack_codes(plan, input_codes, cotangent_codes):
    return call(
        functools.partial(pack_codes_body, plan),
        [
            shaped(plan.chips, plan.packed, LANES, dtype=BF16),
            shaped(1, plan.packed, LANES, dtype=BF16),
        ],
        (),
        (input_codes, cotangent_codes),
        [pltpu.SemaphoreType.DMA((2,))],
        moved=plan.rows * plan.own * 8,
        grant=VMEM_MOST,
    )


def assemble(plan, relative, own_ref, other_ref, both, full_ref):
    core = lax.axis_index("hidden")
    if relative:
        me = lax.axis_index("latent")
        for place, partner in enumerate(plan.order):
            chip = me ^ partner
            both[core, chip] = own_ref[place]
            both[1 - core, chip] = other_ref[place]
    else:
        both[core] = own_ref[...]
        both[1 - core] = other_ref[...]
    for chip in range(plan.chips):
        for side in range(plan.cores):
            column = (chip * plan.cores + side) * plan.own
            block = unpack_block(plan, both[side, chip].astype(F32))
            full_ref[:, column : column + plan.own] = block.astype(BF16)


def both_scratch(plan, dtype=BF16):
    return pltpu.VMEM((plan.cores, plan.chips, plan.packed, LANES), dtype)


def halves_of_product(plan, pairs, mine_ref, theirs_ref, gain_ref=None, bias_ref=None):
    core = lax.axis_index("hidden")
    for target, side in ((theirs_ref, 1 - core), (mine_ref, core)):
        start = pl.multiple_of(side * plan.half, LANES)
        total = None
        for left, right_ref in pairs:
            term = jnp.dot(
                left, right_ref[:, pl.ds(start, plan.half)], preferred_element_type=F32
            )
            total = term if total is None else total + term
        if gain_ref is not None:
            once = jnp.where((lax.axis_index("latent") == 0) & (side == core), 1.0, 0.0)
            bias = bias_ref[:, pl.ds(start, plan.half)] * once
            total = (total + bias) * gain_ref[:, pl.ds(start, plan.half)]
        for tile in range(plan.tiles):
            target[tile * plan.rows : (tile + 1) * plan.rows, :] = total[
                :, tile * LANES : (tile + 1) * LANES
            ].astype(target.dtype)
        used = plan.tiles * plan.rows
        if used < plan.flat:
            target[used:, :] = jnp.zeros((plan.flat - used, LANES), target.dtype)


def encode_body(plan, own_ref, other_ref, dict_ref, bias_ref, decoder_ref, gain_ref, inputs_ref, latents_ref, mine_ref, theirs_ref, both):
    assemble(plan, False, own_ref, other_ref, both, inputs_ref)
    preact = (
        lax.dot_general(inputs_ref[...], dict_ref[...], ACROSS, preferred_element_type=F32)
        + bias_ref[...]
    )
    latents = jnp.maximum(preact, 0.0).astype(BF16)
    latents_ref[...] = latents
    halves_of_product(plan, [(latents, dict_ref)], mine_ref, theirs_ref, gain_ref, decoder_ref)


def encode(plan, own, other, dictionary, encoder_bias, decoder_bias, gain):
    latents = dictionary.shape[0]
    return call(
        functools.partial(encode_body, plan),
        [
            shaped(plan.rows, plan.width, dtype=BF16),
            shaped(plan.rows, latents, dtype=BF16),
            shaped(plan.flat, LANES),
            shaped(plan.flat, LANES),
        ],
        (own, other, dictionary, encoder_bias, decoder_bias, gain),
        (),
        [both_scratch(plan)],
        flops=4 * plan.rows * plan.width * latents,
        moved=dictionary.size * 2,
    )


def back_project_body(plan, own_ref, other_ref, down_hbm, grad_ref, down_ref, both, full, sems):
    (copy,) = copies([down_hbm], [down_ref], sems)
    assemble(plan, True, own_ref, other_ref, both, full)
    copy.wait()
    grad_ref[...] = lax.dot_general(
        full[...], down_ref[...], ACROSS, preferred_element_type=F32
    )


def back_project(plan, own, other, down_weight):
    units = down_weight.shape[0]
    return call(
        functools.partial(back_project_body, plan),
        shaped(plan.rows, units),
        (own, other),
        (down_weight,),
        [both_scratch(plan), pltpu.VMEM((plan.rows, plan.width), BF16), pltpu.SemaphoreType.DMA((1,))],
        flops=2 * plan.rows * plan.width * units,
        moved=down_weight.size * 2,
    )


def join_half(plan, source, first, full_ref):
    for tile in range(plan.tiles):
        column = pl.multiple_of(first + tile * LANES, LANES)
        row = 0
        while row < plan.rows:
            chip, place = divmod(tile * plan.rows + row, plan.chunk)
            count = min(plan.rows - row, plan.chunk - place)
            full_ref[row : row + count, pl.ds(column, LANES)] = source[
                chip, place : place + count, :
            ]
            row += count


def half_terms(plan, half, side, gate_ref, up_ref, gain_ref):
    span = pl.ds(pl.multiple_of(side * plan.half, LANES), plan.half)
    rebuilt = half.astype(F32) / gain_ref[:, span]
    squares = jnp.sum(rebuilt * rebuilt, axis=1, keepdims=True)
    gate = lax.dot_general(half, gate_ref[:, span], ACROSS, preferred_element_type=F32)
    up = lax.dot_general(half, up_ref[:, span], ACROSS, preferred_element_type=F32)
    return squares, gate, up


def mlp_first_body(plan, own_ref, gate_hbm, up_hbm, gain_hbm, grad_hbm, gate_ref, up_ref, gain_ref, grad_ref, half_ref, squares_ref, gate_part_ref, up_part_ref, sems):
    started = copies(
        [gain_hbm, gate_hbm, up_hbm, grad_hbm], [gain_ref, gate_ref, up_ref, grad_ref], sems
    )
    join_half(plan, own_ref, 0, half_ref)
    for copy in started:
        copy.wait()
    squares_ref[...], gate_part_ref[...], up_part_ref[...] = half_terms(
        plan, half_ref[...], lax.axis_index("hidden"), gate_ref, up_ref, gain_ref
    )


def mlp_first(plan, own, gain, hidden_grad, gate_weight, up_weight):
    units = gate_weight.shape[0]
    brought = (gate_weight, up_weight, gain, hidden_grad)
    outputs = [jax.ShapeDtypeStruct(one.shape, one.dtype) for one in brought] + [
        shaped(plan.rows, plan.half, dtype=BF16),
        shaped(plan.rows, 1),
        shaped(plan.rows, units),
        shaped(plan.rows, units),
    ]
    taken = sum(map(padded_bytes, [own, *outputs]))
    return pl.pallas_call(
        functools.partial(mlp_first_body, plan),
        out_shape=outputs,
        in_specs=[ONCHIP] + [HBM] * len(brought),
        out_specs=[ONCHIP] * len(outputs),
        scratch_shapes=[pltpu.SemaphoreType.DMA((len(brought),))],
        compiler_params=pltpu.CompilerParams(vmem_limit_bytes=VMEM_BYTES - taken),
        cost_estimate=pl.CostEstimate(
            flops=2 * plan.rows * plan.width * units,
            bytes_accessed=gate_weight.size * 8,
            transcendentals=0,
        ),
    )(own, *brought)


def mlp_body(plan, other_ref, gate_ref, up_ref, gain_ref, grad_ref, half_ref, squares_ref, gate_part_ref, up_part_ref, scaled_ref, inverse_ref, hidden_ref, mine_ref, theirs_ref):
    core = lax.axis_index("hidden")
    join_half(plan, other_ref, (1 - core) * plan.half, scaled_ref)
    other_span = pl.ds(pl.multiple_of((1 - core) * plan.half, LANES), plan.half)
    own_span = pl.ds(pl.multiple_of(core * plan.half, LANES), plan.half)
    scaled_ref[:, own_span] = half_ref[...]
    squares, gate, up = half_terms(
        plan, scaled_ref[:, other_span], 1 - core, gate_ref, up_ref, gain_ref
    )
    inverse = lax.rsqrt((squares + squares_ref[...]) / plan.width + NORM_EPSILON)
    inverse_ref[...] = inverse
    gate_proj = inverse * (gate + gate_part_ref[...])
    up_proj = inverse * (up + up_part_ref[...])
    gelu_value, gelu_slope = gelu_parts(gate_proj)
    hidden_ref[...] = (gelu_value * up_proj).astype(BF16)
    hidden_grad = grad_ref[...]
    gate_grad = (hidden_grad * up_proj * gelu_slope).astype(BF16)
    up_grad = (hidden_grad * gelu_value).astype(BF16)
    halves_of_product(plan, [(gate_grad, gate_ref), (up_grad, up_ref)], mine_ref, theirs_ref)


def mlp(plan, other, first):
    units = first[0].shape[0]
    return call(
        functools.partial(mlp_body, plan),
        [
            shaped(plan.rows, plan.width, dtype=BF16),
            shaped(plan.rows, 1),
            shaped(plan.rows, units, dtype=BF16),
            shaped(plan.flat, LANES),
            shaped(plan.flat, LANES),
        ],
        (other, *first),
        flops=6 * plan.rows * plan.width * units,
        moved=first[0].size * 4,
    )


def project_body(plan, hidden_ref, down_hbm, mine_ref, theirs_ref, down_ref, both, sems):
    (copy,) = copies([down_hbm], [down_ref], sems)
    core = lax.axis_index("hidden")
    copy.wait()
    terms = jnp.dot(hidden_ref[...], down_ref[...], preferred_element_type=F32)
    for chip in range(plan.chips):
        for side in range(plan.cores):
            start = (chip * plan.cores + side) * plan.own
            main, tail = pack_block(plan, terms[:, start : start + plan.own])
            both[side, chip, : plan.rows, :] = main
            both[side, chip, plan.rows :, :] = tail
    me = lax.axis_index("latent")
    for place, partner in enumerate(plan.order):
        chip = me ^ partner
        mine_ref[place] = both[core, chip]
        theirs_ref[place] = both[1 - core, chip]


def project(plan, hidden, down_weight):
    units = down_weight.shape[0]
    return call(
        functools.partial(project_body, plan),
        [shaped(plan.chips, plan.packed, LANES)] * 2,
        (hidden,),
        (down_weight,),
        [both_scratch(plan, F32), pltpu.SemaphoreType.DMA((1,))],
        flops=2 * plan.rows * plan.width * units,
        moved=down_weight.size * 2,
    )


def total_of(plan, terms_ref, start, count):
    total = terms_ref[0, start : start + count, :].astype(F32)
    for chip in range(1, plan.chips):
        total = total + terms_ref[chip, start : start + count, :].astype(F32)
    return total


def sum_body(plan, terms_ref, out_ref):
    total = total_of(plan, terms_ref, 0, plan.chunk).astype(BF16)
    for chip in range(plan.chips):
        out_ref[chip] = total


def sum_terms(plan, terms):
    return call(
        functools.partial(sum_body, plan),
        shaped(plan.chips, plan.chunk, LANES, dtype=BF16),
        (terms,),
        moved=terms.size * 4,
    )


def finish_output_body(plan, kept_ref, out_ref):
    out_ref[...] = unpack_block(plan, kept_ref[0]).astype(BF16)


def finish_output(plan, kept):
    return call(
        functools.partial(finish_output_body, plan),
        shaped(plan.rows, plan.own, dtype=BF16),
        (kept,),
        moved=kept.size * 4,
    )


def dictionary_body(plan, pieces, own_ref, other_ref, gain_ref, inverse_ref, scaled_ref, inputs_ref, latents_ref, dict_hbm, out_hbm, dict_ref, full, out_ref, sems, out_sems):
    (copy,) = copies([dict_hbm], [dict_ref], sems)
    core = lax.axis_index("hidden")
    join_half(plan, own_ref, core * plan.half, full)
    join_half(plan, other_ref, (1 - core) * plan.half, full)
    grad = full[...].astype(F32)
    gain = gain_ref[...]
    scaled_rebuilt = scaled_ref[...].astype(F32)
    rebuilt = scaled_rebuilt / gain
    inverse = inverse_ref[...]
    inner_row = jnp.sum(grad * scaled_rebuilt, axis=1, keepdims=True)
    inverse_cube = inverse * inverse * inverse
    inputs = inputs_ref[...]
    rebuilt_grad = (
        inverse * (grad * gain)
        - (inverse_cube * (inner_row / plan.width)) * rebuilt
        + (rebuilt - inputs.astype(F32))
    ).astype(BF16)
    copy.wait()
    size = dict_ref.shape[0] // pieces
    writes = []
    for piece in range(pieces):
        span = slice(piece * size, (piece + 1) * size)
        latents = latents_ref[:, span]
        latent_grad = lax.dot_general(
            rebuilt_grad, dict_ref[span, :], ACROSS, preferred_element_type=F32
        )
        preact_grad = jnp.where(latents.astype(F32) > 0.0, latent_grad, 0.0).astype(BF16)
        out_ref[span, :] = (
            lax.dot_general(latents, rebuilt_grad, DOWNWARD, preferred_element_type=F32)
            + lax.dot_general(preact_grad, inputs, DOWNWARD, preferred_element_type=F32)
        ).astype(BF16)
        one = pltpu.make_async_copy(
            out_ref.at[span, :], out_hbm.at[span, :], out_sems.at[piece]
        )
        one.start()
        writes.append(one)
    for one in writes:
        one.wait()


def dictionary_step(plan, own, other, gain, inverse, scaled, inputs, latents, dictionary):
    units = dictionary.shape[0]
    pieces = units // (2 * LANES) if units % (2 * LANES) == 0 else 1
    return call(
        functools.partial(dictionary_body, plan, pieces),
        shaped(*dictionary.shape, dtype=BF16),
        (own, other, gain, inverse, scaled, inputs, latents),
        (dictionary,),
        [
            pltpu.VMEM((plan.rows, plan.width), BF16),
            pltpu.VMEM(dictionary.shape, BF16),
            pltpu.SemaphoreType.DMA((1,)),
            pltpu.SemaphoreType.DMA((pieces,)),
        ],
        out_specs=HBM,
        flops=6 * plan.rows * plan.width * units,
        moved=dictionary.size * 4,
    )


def swap(value):
    size = lax.axis_size("hidden")
    return lax.ppermute(value, "hidden", [(i, (i + 1) % size) for i in range(size)])


def partner_swap(value, bit):
    size = lax.axis_size("latent")
    return lax.ppermute(value, "latent", [(i, i ^ bit) for i in range(size)])


def grow(stack, bit):
    return jnp.concatenate([stack, partner_swap(stack, bit)], axis=0)


def shrink(kept, sent, bit):
    return kept + partner_swap(sent, bit).astype(F32)


def halved(stack):
    middle = stack.shape[0] // 2
    return stack[:middle], stack[middle:].astype(BF16)


def trade(stack):
    return lax.all_to_all(stack, "latent", 0, 0, tiled=False)


def per_device(
    input_codes,
    cotangent_codes,
    dictionary,
    encoder_bias,
    decoder_bias,
    norm_gain,
    gate_weight,
    up_weight,
    down_weight,
):
    plan = Plan(
        lax.axis_size("latent"), lax.axis_size("hidden"), input_codes.shape[0], input_codes.shape[1]
    )
    if not plan.fits():
        return per_device_plain(
            input_codes,
            cotangent_codes,
            dictionary,
            encoder_bias,
            decoder_bias,
            norm_gain,
            gate_weight,
            up_weight,
            down_weight,
        )
    inputs_stack, cotangent = pack_codes(plan, input_codes, cotangent_codes)
    inputs_own = trade(inputs_stack)
    columns = plan.order[1 : plan.chips // 2]
    cotangent = jnp.concatenate(
        [cotangent] + [partner_swap(cotangent, bits) for bits in columns], axis=0
    )
    vectors = [one.reshape(1, -1) for one in (encoder_bias, decoder_bias, norm_gain)]
    inputs_own, cotangent, vectors = lax.optimization_barrier((inputs_own, cotangent, vectors))
    bias, decoder, gain = vectors
    inputs_own, late_dictionary = lax.optimization_barrier((inputs_own, dictionary))
    inputs, latents, mine, theirs = encode(
        plan, inputs_own, swap(inputs_own), *bring(late_dictionary, bias, decoder, gain)
    )
    half = (mine + swap(theirs)).astype(BF16)
    half, cotangent = lax.optimization_barrier((half, cotangent))
    terms = trade(half.reshape(plan.chips, plan.chunk, LANES))
    cotangent = grow(cotangent, plan.bits[-1])
    scaled_stack = sum_terms(plan, terms)
    scaled_stack, cotangent = lax.optimization_barrier((scaled_stack, cotangent))
    scaled_own = trade(scaled_stack)
    hidden_grad = back_project(plan, cotangent, swap(cotangent), down_weight)
    scaled_own, hidden_grad = lax.optimization_barrier((scaled_own, hidden_grad))
    first = mlp_first(plan, scaled_own, gain, hidden_grad, gate_weight, up_weight)
    scaled, inverse, hidden, mine, theirs = mlp(plan, swap(scaled_own), first)
    half = (mine + swap(theirs)).astype(BF16)
    out_mine, out_theirs = project(plan, hidden, down_weight)
    half, out_mine, out_theirs = lax.optimization_barrier((half, out_mine, out_theirs))
    terms = trade(half.reshape(plan.chips, plan.chunk, LANES))
    kept, sent = halved(out_mine + swap(out_theirs))
    kept = shrink(kept, sent, plan.bits[-1])
    grad_stack = sum_terms(plan, terms)
    grad_stack, kept = lax.optimization_barrier((grad_stack, kept))
    grad_own = trade(grad_stack)
    for bit in reversed(plan.bits[1:-1]):
        kept, sent = halved(kept)
        kept = shrink(kept, sent, bit)
    kept, sent = halved(kept)
    grad_own, kept, sent, *late = lax.optimization_barrier(
        (grad_own, kept, sent, gain, inverse, scaled, inputs, latents)
    )
    dictionary_grad = dictionary_step(plan, grad_own, swap(grad_own), *bring(*late), dictionary)
    dictionary_grad, kept = lax.optimization_barrier((dictionary_grad, kept))
    block_output = finish_output(plan, shrink(kept, sent, plan.bits[0]))
    return (block_output, dictionary_grad)


def per_device_plain(
    input_codes,
    cotangent_codes,
    dictionary,
    encoder_bias,
    decoder_bias,
    norm_gain,
    gate_weight,
    up_weight,
    down_weight,
):
    own_width = input_codes.shape[1]
    model_width = own_width * lax.axis_size(("latent", "hidden"))
    cotangent_local = (cotangent_codes.astype(jnp.float32) * CODE_STEP).astype(jnp.bfloat16)
    inputs_local = (input_codes.astype(jnp.float32) * CODE_STEP).astype(jnp.bfloat16)
    inputs = lax.all_gather(inputs_local, ("latent", "hidden"), axis=1, tiled=True)
    preact = (
        lax.dot_general(inputs, dictionary, ACROSS, preferred_element_type=jnp.float32)
        + encoder_bias
    )
    latents = jnp.maximum(preact, 0.0).astype(jnp.bfloat16)
    partial_value = jnp.dot(latents, dictionary, preferred_element_type=jnp.float32)
    rebuilt = lax.psum(partial_value, ("latent", "hidden")) + decoder_bias
    inverse = lax.rsqrt(
        jnp.sum(rebuilt * rebuilt, axis=1, keepdims=True) / model_width + NORM_EPSILON
    )
    normed = (rebuilt * inverse * norm_gain).astype(jnp.bfloat16)
    target = inputs.astype(jnp.float32)
    gate_proj = lax.dot_general(normed, gate_weight, ACROSS, preferred_element_type=jnp.float32)
    up_proj = lax.dot_general(normed, up_weight, ACROSS, preferred_element_type=jnp.float32)
    gelu_value, gelu_slope = gelu_parts(gate_proj)
    hidden = (gelu_value * up_proj).astype(jnp.bfloat16)
    output_terms = jnp.dot(hidden, down_weight, preferred_element_type=jnp.float32)
    block_output = lax.psum_scatter(
        output_terms, ("latent", "hidden"), scatter_dimension=1, tiled=True
    ).astype(jnp.bfloat16)
    hidden_grad = lax.dot_general(
        lax.all_gather(cotangent_local, ("latent", "hidden"), axis=1, tiled=True),
        down_weight,
        ACROSS,
        preferred_element_type=jnp.float32,
    )
    gate_grad = (hidden_grad * up_proj * gelu_slope).astype(jnp.bfloat16)
    up_grad = (hidden_grad * gelu_value).astype(jnp.bfloat16)
    partial_grad = jnp.dot(gate_grad, gate_weight, preferred_element_type=jnp.float32) + jnp.dot(
        up_grad, up_weight, preferred_element_type=jnp.float32
    )
    scaled = lax.psum(partial_grad, ("latent", "hidden")) * norm_gain
    inner_row = jnp.sum(scaled * rebuilt, axis=1, keepdims=True)
    inverse_cube = inverse * inverse * inverse
    rebuilt_grad = (
        inverse * scaled - inverse_cube * rebuilt * (inner_row / model_width) + (rebuilt - target)
    ).astype(jnp.bfloat16)
    latent_grad = lax.dot_general(
        rebuilt_grad, dictionary, ACROSS, preferred_element_type=jnp.float32
    )
    preact_grad = jnp.where(preact > 0.0, latent_grad, 0.0).astype(jnp.bfloat16)
    dictionary_grad = lax.dot_general(
        latents, rebuilt_grad, DOWNWARD, preferred_element_type=jnp.float32
    ) + lax.dot_general(preact_grad, inputs, DOWNWARD, preferred_element_type=jnp.float32)
    return (block_output, dictionary_grad.astype(jnp.bfloat16))


def solution(mesh):
    in_specs = (
        P("groups", ("latent", "hidden")),
        P("groups", ("latent", "hidden")),
        P(("latent", "hidden"), None),
        P(("latent", "hidden")),
        P(),
        P(),
        P(("latent", "hidden"), None),
        P(("latent", "hidden"), None),
        P(("latent", "hidden"), None),
    )
    out_specs = (P("groups", ("latent", "hidden")), P(("latent", "hidden"), "groups"))
    return jax.shard_map(
        per_device, mesh=mesh, in_specs=in_specs, out_specs=out_specs, check_vma=False
    )
```

```python
import functools
import math

import jax
import jax.numpy as jnp
from jax import lax
from jax.experimental import pallas as pl
from jax.experimental.pallas import tpu as pltpu
from jax.sharding import PartitionSpec as P

CODE_STEP = 2.0 ** (-6)
NORM_EPSILON = 1e-06
GELU_ROOT = 0.7978845608028654
GELU_CUBIC = 0.044715
ACROSS = (((1,), (1,)), ((), ()))
DOWNWARD = (((0,), (0,)), ((), ()))
LANES = 128
ROW_TILE = 16
VMEM_BYTES = 53 * 1024 * 1024
VMEM_LEAST = 32 * 1024 * 1024
VMEM_MOST = 60 * 1024 * 1024
F32 = jnp.float32
BF16 = jnp.bfloat16


def gelu_parts(values):
    argument = GELU_ROOT * (values + GELU_CUBIC * values * values * values)
    tanh_value = jnp.tanh(argument)
    result = 0.5 * values * (1.0 + tanh_value)
    derivative = 0.5 * (1.0 + tanh_value) + 0.5 * values * (
        1.0 - tanh_value * tanh_value
    ) * GELU_ROOT * (1.0 + 3.0 * GELU_CUBIC * values * values)
    return (result, derivative)


def up_to(value, unit):
    return -(-value // unit) * unit


class Plan:
    def __init__(self, chips, cores, rows, own):
        self.chips, self.cores, self.rows, self.own = chips, cores, rows, own
        self.width = own * chips * cores
        self.half = self.width // cores
        self.tiles = self.half // LANES
        self.chunk = up_to(-(-self.tiles * rows // chips), ROW_TILE)
        self.flat = self.chunk * chips
        self.tail = own - LANES
        if self.tail > 0:
            self.fold_rows = min(
                size
                for size in range(ROW_TILE, rows + ROW_TILE, ROW_TILE)
                if -(-rows // size) * self.tail <= LANES
            )
            self.packed = rows + self.fold_rows
        self.bits = [1 << k for k in reversed(range((chips - 1).bit_length()))]
        self.order = [0]
        for bit in self.bits:
            self.order = self.order + [place ^ bit for place in self.order]

    def fits(self):
        return (
            self.cores == 2
            and len(self.order) == self.chips
            and self.rows % ROW_TILE == 0
            and self.half % LANES == 0
            and 0 < self.tail < LANES
        )


HBM = pl.BlockSpec(memory_space=pltpu.HBM)
ONCHIP = pl.BlockSpec(memory_space=pltpu.VMEM)


def shaped(*dims, dtype=F32):
    return jax.ShapeDtypeStruct(dims, dtype)


def padded_bytes(array):
    *lead, rows, columns = array.shape
    item = jnp.dtype(array.dtype).itemsize
    return math.prod(lead) * up_to(rows, ROW_TILE) * up_to(columns, LANES) * item


def call(body, out_shapes, operands, fetched=(), scratch=(), out_specs=None, flops=0, moved=0, grant=VMEM_BYTES, keep_fetched=False):
    outputs = jax.tree.leaves(out_shapes) if out_specs is None else []
    taken = sum(padded_bytes(one) for one in list(operands) + outputs)
    return pl.pallas_call(
        body,
        out_shape=out_shapes,
        in_specs=[ONCHIP] * len(operands) + [HBM] * len(fetched),
        out_specs=jax.tree.map(lambda _: ONCHIP, out_shapes) if out_specs is None else out_specs,
        scratch_shapes=([] if keep_fetched else [pltpu.VMEM(one.shape, one.dtype) for one in fetched])
        + list(scratch),
        compiler_params=pltpu.CompilerParams(vmem_limit_bytes=grant - taken),
        cost_estimate=pl.CostEstimate(flops=flops, bytes_accessed=moved, transcendentals=0),
    )(*operands, *fetched)


def copies(sources, targets, sems, first=0):
    started = []
    for index, (source, target) in enumerate(zip(sources, targets)):
        one = pltpu.make_async_copy(source, target, sems.at[first + index])
        one.start()
        started.append(one)
    return started


def bring_body(count, *refs):
    sources, targets, sems = refs[:count], refs[count : 2 * count], refs[2 * count]
    for copy in copies(sources, targets, sems):
        copy.wait()


def bring(*arrays):
    return pl.pallas_call(
        functools.partial(bring_body, len(arrays)),
        out_shape=[jax.ShapeDtypeStruct(one.shape, one.dtype) for one in arrays],
        in_specs=[HBM] * len(arrays),
        out_specs=[ONCHIP] * len(arrays),
        scratch_shapes=[pltpu.SemaphoreType.DMA((len(arrays),))],
        compiler_params=pltpu.CompilerParams(
            vmem_limit_bytes=VMEM_BYTES - sum(map(padded_bytes, arrays))
        ),
        cost_estimate=pl.CostEstimate(
            flops=0, bytes_accessed=2 * sum(map(padded_bytes, arrays)), transcendentals=0
        ),
    )(*arrays)


def pack_block(plan, block):
    tail = block[:, LANES:]
    folded = []
    for start in range(0, plan.rows, plan.fold_rows):
        piece = tail[start : min(start + plan.fold_rows, plan.rows), :]
        short = plan.fold_rows - piece.shape[0]
        if short:
            piece = jnp.concatenate([piece, jnp.zeros((short, plan.tail), block.dtype)], axis=0)
        folded.append(piece)
    fill = LANES - len(folded) * plan.tail
    if fill:
        folded.append(jnp.zeros((plan.fold_rows, fill), block.dtype))
    return block[:, :LANES], jnp.concatenate(folded, axis=1)


def unpack_block(plan, packed):
    pieces = []
    for fold, start in enumerate(range(0, plan.rows, plan.fold_rows)):
        count = min(plan.fold_rows, plan.rows - start)
        pieces.append(
            packed[plan.rows : plan.rows + count, fold * plan.tail : (fold + 1) * plan.tail]
        )
    return jnp.concatenate([packed[: plan.rows, :], jnp.concatenate(pieces, axis=0)], axis=1)


def pack_codes_body(plan, input_hbm, cotangent_hbm, inputs_ref, cotangent_out_ref, input_ref, cotangent_ref, sems):
    for copy in copies([input_hbm, cotangent_hbm], [input_ref, cotangent_ref], sems):
        copy.wait()
    main, tail = pack_block(plan, input_ref[...].astype(F32) * CODE_STEP)
    for chip in range(plan.chips):
        inputs_ref[chip, : plan.rows, :] = main.astype(BF16)
        inputs_ref[chip, plan.rows :, :] = tail.astype(BF16)
    main, tail = pack_block(plan, cotangent_ref[...].astype(F32) * CODE_STEP)
    cotangent_out_ref[0, : plan.rows, :] = main.astype(BF16)
    cotangent_out_ref[0, plan.rows :, :] = tail.astype(BF16)


def pack_codes(plan, input_codes, cotangent_codes):
    return call(
        functools.partial(pack_codes_body, plan),
        [
            shaped(plan.chips, plan.packed, LANES, dtype=BF16),
            shaped(1, plan.packed, LANES, dtype=BF16),
        ],
        (),
        (input_codes, cotangent_codes),
        [pltpu.SemaphoreType.DMA((2,))],
        moved=plan.rows * plan.own * 8,
        grant=VMEM_MOST,
    )


def assemble(plan, relative, own_ref, other_ref, both, full_ref):
    core = lax.axis_index("hidden")
    if relative:
        me = lax.axis_index("latent")
        for place, partner in enumerate(plan.order):
            chip = me ^ partner
            both[core, chip] = own_ref[place]
            both[1 - core, chip] = other_ref[place]
    else:
        both[core] = own_ref[...]
        both[1 - core] = other_ref[...]
    for chip in range(plan.chips):
        for side in range(plan.cores):
            column = (chip * plan.cores + side) * plan.own
            block = unpack_block(plan, both[side, chip].astype(F32))
            full_ref[:, column : column + plan.own] = block.astype(BF16)


def both_scratch(plan, dtype=BF16):
    return pltpu.VMEM((plan.cores, plan.chips, plan.packed, LANES), dtype)


def write_chunks(plan, half, flat_ref):
    for tile in range(plan.tiles):
        flat_ref[tile * plan.rows : (tile + 1) * plan.rows, :] = half[
            :, tile * LANES : (tile + 1) * LANES
        ].astype(flat_ref.dtype)
    used = plan.tiles * plan.rows
    if used < plan.flat:
        flat_ref[used:, :] = jnp.zeros((plan.flat - used, LANES), flat_ref.dtype)


def own_half(plan):
    return pl.ds(pl.multiple_of(lax.axis_index("hidden") * plan.half, LANES), plan.half)


def other_half(plan):
    return pl.ds(pl.multiple_of((1 - lax.axis_index("hidden")) * plan.half, LANES), plan.half)


def cut_body(plan, count, *refs):
    sources, targets, sems = refs[:count], refs[count : 2 * count], refs[2 * count]
    for copy in copies([one.at[:, other_half(plan)] for one in sources], targets, sems):
        copy.wait()


def cut(plan, *weights):
    return pl.pallas_call(
        functools.partial(cut_body, plan, len(weights)),
        out_shape=[shaped(one.shape[0], plan.half, dtype=one.dtype) for one in weights],
        in_specs=[HBM] * len(weights),
        out_specs=[HBM] * len(weights),
        scratch_shapes=[pltpu.SemaphoreType.DMA((len(weights),))],
        compiler_params=pltpu.CompilerParams(vmem_limit_bytes=VMEM_LEAST),
        cost_estimate=pl.CostEstimate(
            flops=0, bytes_accessed=2 * sum(one.size for one in weights), transcendentals=0
        ),
    )(*weights)


def bring_encoder_body(dict_hbm, vectors_hbm, dict_ref, bias_ref, decoder_ref, gain_ref, sems):
    sources, targets = [dict_hbm], [dict_ref]
    start = 0
    for target in (bias_ref, decoder_ref, gain_ref):
        sources.append(vectors_hbm.at[:, start : start + target.shape[1]])
        targets.append(target)
        start += target.shape[1]
    for copy in copies(sources, targets, sems):
        copy.wait()


def bring_encoder(plan, dictionary, vectors):
    outputs = [
        shaped(*dictionary.shape, dtype=BF16),
        shaped(1, dictionary.shape[0]),
        shaped(1, plan.width),
        shaped(1, plan.width),
    ]
    return pl.pallas_call(
        bring_encoder_body,
        out_shape=outputs,
        in_specs=[HBM] * 2,
        out_specs=[ONCHIP] * len(outputs),
        scratch_shapes=[pltpu.SemaphoreType.DMA((len(outputs),))],
        compiler_params=pltpu.CompilerParams(
            vmem_limit_bytes=VMEM_BYTES - sum(map(padded_bytes, outputs))
        ),
        cost_estimate=pl.CostEstimate(
            flops=0, bytes_accessed=dictionary.size * 4, transcendentals=0
        ),
    )(dictionary, vectors)


def encode_body(plan, own_ref, other_ref, dict_ref, bias_ref, pair_hbm, inputs_ref, latents_ref, pair_ref, both, sems):
    (copy,) = copies([pair_hbm], [pair_ref], sems)
    assemble(plan, False, own_ref, other_ref, both, inputs_ref)
    preact = (
        lax.dot_general(inputs_ref[...], dict_ref[...], ACROSS, preferred_element_type=F32)
        + bias_ref[...]
    )
    latents_ref[...] = jnp.maximum(preact, 0.0).astype(BF16)
    copy.wait()


def encode(plan, own, other, dictionary, bias, pair_dictionary):
    latents = dictionary.shape[0]
    outputs = [
        shaped(plan.rows, plan.width, dtype=BF16),
        shaped(plan.rows, latents, dtype=BF16),
        shaped(*pair_dictionary.shape, dtype=BF16),
    ]
    return call(
        functools.partial(encode_body, plan),
        outputs,
        (own, other, dictionary, bias),
        (pair_dictionary,),
        [both_scratch(plan), pltpu.SemaphoreType.DMA((1,))],
        keep_fetched=True,
        grant=VMEM_LEAST,
        flops=2 * plan.rows * plan.width * latents,
        moved=dictionary.size * 2,
    )


def decode_body(plan, latents_ref, partner_ref, dict_ref, pair_ref, decoder_ref, gain_ref, flat_ref):
    span = own_half(plan)
    total = jnp.dot(latents_ref[...], dict_ref[:, span], preferred_element_type=F32) + jnp.dot(
        partner_ref[...], pair_ref[...], preferred_element_type=F32
    )
    once = jnp.where(lax.axis_index("latent") == 0, 1.0, 0.0)
    total = (total + decoder_ref[:, span] * once) * gain_ref[:, span]
    write_chunks(plan, total, flat_ref)


def decode(plan, latents, partner_latents, dictionary, pair_dictionary, decoder, gain):
    return call(
        functools.partial(decode_body, plan),
        shaped(plan.flat, LANES, dtype=BF16),
        (latents, partner_latents, dictionary, pair_dictionary, decoder, gain),
        grant=VMEM_LEAST,
        flops=2 * plan.rows * plan.width * dictionary.shape[0],
        moved=dictionary.size * 2,
    )


def back_project_body(plan, own_ref, other_ref, down_hbm, grad_ref, down_ref, both, full, sems):
    (copy,) = copies([down_hbm], [down_ref], sems)
    assemble(plan, True, own_ref, other_ref, both, full)
    copy.wait()
    grad_ref[...] = lax.dot_general(
        full[...], down_ref[...], ACROSS, preferred_element_type=F32
    )


def back_project(plan, own, other, down_weight):
    units = down_weight.shape[0]
    return call(
        functools.partial(back_project_body, plan),
        shaped(plan.rows, units),
        (own, other),
        (down_weight,),
        [both_scratch(plan), pltpu.VMEM((plan.rows, plan.width), BF16), pltpu.SemaphoreType.DMA((1,))],
        flops=2 * plan.rows * plan.width * units,
        moved=down_weight.size * 2,
    )


def join_half(plan, source, first, full_ref):
    for tile in range(plan.tiles):
        column = pl.multiple_of(first + tile * LANES, LANES)
        row = 0
        while row < plan.rows:
            chip, place = divmod(tile * plan.rows + row, plan.chunk)
            count = min(plan.rows - row, plan.chunk - place)
            full_ref[row : row + count, pl.ds(column, LANES)] = source[
                chip, place : place + count, :
            ]
            row += count


def half_squares(half, gain):
    rebuilt = half.astype(F32) / gain
    return jnp.sum(rebuilt * rebuilt, axis=1, keepdims=True)


def mlp_first_body(plan, own_ref, gate_hbm, up_hbm, gain_hbm, grad_hbm, gate_ref, up_ref, gain_ref, grad_ref, half_ref, squares_ref, gate_part_ref, up_part_ref, sems):
    mine, theirs = own_half(plan), other_half(plan)
    gain_copy, gate_copy, up_copy, *rest = copies(
        [gain_hbm, gate_hbm.at[:, mine], up_hbm.at[:, mine]]
        + [gate_hbm.at[:, theirs], up_hbm.at[:, theirs], grad_hbm],
        [gain_ref, gate_ref.at[:, mine], up_ref.at[:, mine]]
        + [gate_ref.at[:, theirs], up_ref.at[:, theirs], grad_ref],
        sems,
    )
    join_half(plan, own_ref, 0, half_ref)
    half = half_ref[...]
    gain_copy.wait()
    squares_ref[...] = half_squares(half, gain_ref[:, mine])
    gate_copy.wait()
    gate_part_ref[...] = lax.dot_general(
        half, gate_ref[:, mine], ACROSS, preferred_element_type=F32
    )
    up_copy.wait()
    up_part_ref[...] = lax.dot_general(half, up_ref[:, mine], ACROSS, preferred_element_type=F32)
    for copy in rest:
        copy.wait()


def mlp_first(plan, own, gain, hidden_grad, gate_weight, up_weight):
    units = gate_weight.shape[0]
    brought = (gate_weight, up_weight, gain, hidden_grad)
    outputs = [jax.ShapeDtypeStruct(one.shape, one.dtype) for one in brought] + [
        shaped(plan.rows, plan.half, dtype=BF16),
        shaped(plan.rows, 1),
        shaped(plan.rows, units),
        shaped(plan.rows, units),
    ]
    taken = sum(map(padded_bytes, [own, *outputs]))
    return pl.pallas_call(
        functools.partial(mlp_first_body, plan),
        out_shape=outputs,
        in_specs=[ONCHIP] + [HBM] * len(brought),
        out_specs=[ONCHIP] * len(outputs),
        scratch_shapes=[pltpu.SemaphoreType.DMA((len(brought) + 2,))],
        compiler_params=pltpu.CompilerParams(vmem_limit_bytes=VMEM_BYTES - taken),
        cost_estimate=pl.CostEstimate(
            flops=2 * plan.rows * plan.width * units,
            bytes_accessed=gate_weight.size * 8,
            transcendentals=0,
        ),
    )(own, *brought)


def mlp_body(plan, other_ref, gate_ref, up_ref, gain_ref, grad_ref, half_ref, squares_ref, gate_part_ref, up_part_ref, pair_gate_hbm, pair_up_hbm, scaled_ref, inverse_ref, hidden_ref, grads_ref, pair_gate_ref, pair_up_ref, sems):
    started = copies([pair_gate_hbm, pair_up_hbm], [pair_gate_ref, pair_up_ref], sems)
    core = lax.axis_index("hidden")
    mine, theirs = own_half(plan), other_half(plan)
    join_half(plan, other_ref, (1 - core) * plan.half, scaled_ref)
    scaled_ref[:, mine] = half_ref[...]
    half = scaled_ref[:, theirs]
    squares = half_squares(half, gain_ref[:, theirs]) + squares_ref[...]
    inverse = lax.rsqrt(squares / plan.width + NORM_EPSILON)
    inverse_ref[...] = inverse
    gate = lax.dot_general(half, gate_ref[:, theirs], ACROSS, preferred_element_type=F32)
    up = lax.dot_general(half, up_ref[:, theirs], ACROSS, preferred_element_type=F32)
    gate_proj = inverse * (gate + gate_part_ref[...])
    up_proj = inverse * (up + up_part_ref[...])
    gelu_value, gelu_slope = gelu_parts(gate_proj)
    hidden_ref[...] = (gelu_value * up_proj).astype(BF16)
    hidden_grad = grad_ref[...]
    grads_ref[0] = (hidden_grad * up_proj * gelu_slope).astype(BF16)
    grads_ref[1] = (hidden_grad * gelu_value).astype(BF16)
    for copy in started:
        copy.wait()


def mlp(plan, other, first, pair_gate, pair_up):
    units = first[0].shape[0]
    return call(
        functools.partial(mlp_body, plan),
        [
            shaped(plan.rows, plan.width, dtype=BF16),
            shaped(plan.rows, 1),
            shaped(plan.rows, units, dtype=BF16),
            shaped(2, plan.rows, units, dtype=BF16),
            shaped(*pair_gate.shape, dtype=BF16),
            shaped(*pair_up.shape, dtype=BF16),
        ],
        (other, *first),
        (pair_gate, pair_up),
        [pltpu.SemaphoreType.DMA((2,))],
        keep_fetched=True,
        grant=VMEM_LEAST,
        flops=2 * plan.rows * plan.width * units,
        moved=first[0].size * 4,
    )


def mlp_back_body(plan, grads_ref, partner_ref, gate_ref, up_ref, pair_gate_ref, pair_up_ref, flat_ref):
    span = own_half(plan)
    total = None
    for left, right in (
        (grads_ref[0], gate_ref[:, span]),
        (grads_ref[1], up_ref[:, span]),
        (partner_ref[0], pair_gate_ref[...]),
        (partner_ref[1], pair_up_ref[...]),
    ):
        term = jnp.dot(left, right, preferred_element_type=F32)
        total = term if total is None else total + term
    write_chunks(plan, total, flat_ref)


def mlp_back(plan, grads, partner_grads, gate, up, pair_gate, pair_up):
    return call(
        functools.partial(mlp_back_body, plan),
        shaped(plan.flat, LANES, dtype=BF16),
        (grads, partner_grads, gate, up, pair_gate, pair_up),
        grant=VMEM_LEAST,
        flops=4 * plan.rows * plan.width * gate.shape[0],
        moved=gate.size * 4,
    )


def project_body(plan, hidden_ref, down_hbm, mine_ref, theirs_ref, down_ref, both, sems):
    (copy,) = copies([down_hbm], [down_ref], sems)
    core = lax.axis_index("hidden")
    copy.wait()
    terms = jnp.dot(hidden_ref[...], down_ref[...], preferred_element_type=F32)
    for chip in range(plan.chips):
        for side in range(plan.cores):
            start = (chip * plan.cores + side) * plan.own
            main, tail = pack_block(plan, terms[:, start : start + plan.own])
            both[side, chip, : plan.rows, :] = main
            both[side, chip, plan.rows :, :] = tail
    me = lax.axis_index("latent")
    for place, partner in enumerate(plan.order):
        chip = me ^ partner
        mine_ref[place] = both[core, chip]
        theirs_ref[place] = both[1 - core, chip]


def project(plan, hidden, down_weight):
    units = down_weight.shape[0]
    return call(
        functools.partial(project_body, plan),
        [shaped(plan.chips, plan.packed, LANES)] * 2,
        (hidden,),
        (down_weight,),
        [both_scratch(plan, F32), pltpu.SemaphoreType.DMA((1,))],
        flops=2 * plan.rows * plan.width * units,
        moved=down_weight.size * 2,
    )


def total_of(plan, terms_ref, start, count):
    total = terms_ref[0, start : start + count, :].astype(F32)
    for chip in range(1, plan.chips):
        total = total + terms_ref[chip, start : start + count, :].astype(F32)
    return total


def sum_body(plan, terms_ref, out_ref):
    total = total_of(plan, terms_ref, 0, plan.chunk).astype(BF16)
    for chip in range(plan.chips):
        out_ref[chip] = total


def sum_terms(plan, terms):
    return call(
        functools.partial(sum_body, plan),
        shaped(plan.chips, plan.chunk, LANES, dtype=BF16),
        (terms,),
        moved=terms.size * 4,
    )


def finish_output_body(plan, kept_ref, out_ref):
    out_ref[...] = unpack_block(plan, kept_ref[0]).astype(BF16)


def finish_output(plan, kept):
    return call(
        functools.partial(finish_output_body, plan),
        shaped(plan.rows, plan.own, dtype=BF16),
        (kept,),
        moved=kept.size * 4,
    )


def dictionary_body(plan, pieces, own_ref, other_ref, gain_ref, inverse_ref, scaled_ref, inputs_ref, latents_ref, dict_hbm, out_hbm, dict_ref, full, out_ref, sems, out_sems):
    (copy,) = copies([dict_hbm], [dict_ref], sems)
    core = lax.axis_index("hidden")
    join_half(plan, own_ref, core * plan.half, full)
    join_half(plan, other_ref, (1 - core) * plan.half, full)
    grad = full[...].astype(F32)
    gain = gain_ref[...]
    scaled_rebuilt = scaled_ref[...].astype(F32)
    rebuilt = scaled_rebuilt / gain
    inverse = inverse_ref[...]
    inner_row = jnp.sum(grad * scaled_rebuilt, axis=1, keepdims=True)
    inverse_cube = inverse * inverse * inverse
    inputs = inputs_ref[...]
    rebuilt_grad = (
        inverse * (grad * gain)
        - (inverse_cube * (inner_row / plan.width)) * rebuilt
        + (rebuilt - inputs.astype(F32))
    ).astype(BF16)
    copy.wait()
    latents = latents_ref[...]
    latent_grad = lax.dot_general(
        rebuilt_grad, dict_ref[...], ACROSS, preferred_element_type=F32
    )
    preact_grad = jnp.where(latents.astype(F32) > 0.0, latent_grad, 0.0).astype(BF16)
    left = jnp.concatenate([latents, preact_grad], axis=0)
    right = jnp.concatenate([rebuilt_grad, inputs], axis=0)
    size = plan.width // pieces
    writes = []
    for piece in range(pieces):
        span = slice(piece * size, (piece + 1) * size)
        out_ref[:, span] = lax.dot_general(
            left, right[:, span], DOWNWARD, preferred_element_type=F32
        ).astype(BF16)
        one = pltpu.make_async_copy(
            out_ref.at[:, span], out_hbm.at[:, span], out_sems.at[piece]
        )
        one.start()
        writes.append(one)
    for one in writes:
        one.wait()


def dictionary_step(plan, own, other, gain, inverse, scaled, inputs, latents, dictionary):
    units = dictionary.shape[0]
    pieces = plan.cores
    return call(
        functools.partial(dictionary_body, plan, pieces),
        shaped(*dictionary.shape, dtype=BF16),
        (own, other, gain, inverse, scaled, inputs, latents),
        (dictionary,),
        [
            pltpu.VMEM((plan.rows, plan.width), BF16),
            pltpu.VMEM(dictionary.shape, BF16),
            pltpu.SemaphoreType.DMA((1,)),
            pltpu.SemaphoreType.DMA((pieces,)),
        ],
        out_specs=HBM,
        flops=6 * plan.rows * plan.width * units,
        moved=dictionary.size * 4,
    )


def swap(value):
    size = lax.axis_size("hidden")
    return lax.ppermute(value, "hidden", [(i, (i + 1) % size) for i in range(size)])


def partner_swap(value, bit):
    size = lax.axis_size("latent")
    return lax.ppermute(value, "latent", [(i, i ^ bit) for i in range(size)])


def grow(stack, bit):
    return jnp.concatenate([stack, partner_swap(stack, bit)], axis=0)


def shrink(kept, sent, bit):
    return kept + partner_swap(sent, bit).astype(F32)


def halved(stack):
    middle = stack.shape[0] // 2
    return stack[:middle], stack[middle:].astype(BF16)


def trade(stack):
    return lax.all_to_all(stack, "latent", 0, 0, tiled=False)


def per_device(
    input_codes,
    cotangent_codes,
    dictionary,
    encoder_bias,
    decoder_bias,
    norm_gain,
    gate_weight,
    up_weight,
    down_weight,
):
    plan = Plan(
        lax.axis_size("latent"), lax.axis_size("hidden"), input_codes.shape[0], input_codes.shape[1]
    )
    if not plan.fits():
        return per_device_plain(
            input_codes,
            cotangent_codes,
            dictionary,
            encoder_bias,
            decoder_bias,
            norm_gain,
            gate_weight,
            up_weight,
            down_weight,
        )
    inputs_stack, cotangent = pack_codes(plan, input_codes, cotangent_codes)
    inputs_stack, cotangent, weights = lax.optimization_barrier(
        (inputs_stack, cotangent, (dictionary, gate_weight, up_weight))
    )
    inputs_own = trade(inputs_stack)
    columns = plan.order[1 : plan.chips // 2]
    cotangent = jnp.concatenate(
        [cotangent] + [partner_swap(cotangent, bits) for bits in columns], axis=0
    )
    vectors = jnp.concatenate([encoder_bias, decoder_bias, norm_gain]).reshape(1, -1)
    pair_weights = [swap(one) for one in cut(plan, *weights)]
    inputs_own, cotangent, vectors, pair_weights = lax.optimization_barrier(
        (inputs_own, cotangent, vectors, pair_weights)
    )
    pair_dictionary, pair_gate, pair_up = pair_weights
    inputs_own, late_dictionary = lax.optimization_barrier((inputs_own, dictionary))
    brought_dictionary, bias, decoder, gain = bring_encoder(plan, late_dictionary, vectors)
    inputs, latents, pair_dictionary = encode(
        plan, inputs_own, swap(inputs_own), brought_dictionary, bias, pair_dictionary
    )
    flat = decode(
        plan, latents, swap(latents), brought_dictionary, pair_dictionary, decoder, gain
    )
    flat, cotangent = lax.optimization_barrier((flat, cotangent))
    terms = trade(flat.reshape(plan.chips, plan.chunk, LANES))
    cotangent = grow(cotangent, plan.bits[-1])
    scaled_stack = sum_terms(plan, terms)
    scaled_stack, cotangent = lax.optimization_barrier((scaled_stack, cotangent))
    scaled_own = trade(scaled_stack)
    hidden_grad = back_project(plan, cotangent, swap(cotangent), down_weight)
    scaled_own, hidden_grad = lax.optimization_barrier((scaled_own, hidden_grad))
    first = mlp_first(plan, scaled_own, gain, hidden_grad, gate_weight, up_weight)
    scaled, inverse, hidden, grads, pair_gate, pair_up = mlp(
        plan, swap(scaled_own), first, pair_gate, pair_up
    )
    flat = mlp_back(plan, grads, swap(grads), first[0], first[1], pair_gate, pair_up)
    flat, hidden = lax.optimization_barrier((flat, hidden))
    terms = trade(flat.reshape(plan.chips, plan.chunk, LANES))
    out_mine, out_theirs = project(plan, hidden, down_weight)
    kept, sent = halved(out_mine + swap(out_theirs))
    kept = shrink(kept, sent, plan.bits[-1])
    grad_own = trade(sum_terms(plan, terms))
    for bit in reversed(plan.bits[1:-1]):
        kept, sent = halved(kept)
        kept = shrink(kept, sent, bit)
    kept, sent = halved(kept)
    grad_own, kept, sent, *late = lax.optimization_barrier(
        (grad_own, kept, sent, gain, inverse, scaled, inputs, latents)
    )
    dictionary_grad = dictionary_step(plan, grad_own, swap(grad_own), *bring(*late), dictionary)
    dictionary_grad, kept = lax.optimization_barrier((dictionary_grad, kept))
    block_output = finish_output(plan, shrink(kept, sent, plan.bits[0]))
    return (block_output, dictionary_grad)


def per_device_plain(
    input_codes,
    cotangent_codes,
    dictionary,
    encoder_bias,
    decoder_bias,
    norm_gain,
    gate_weight,
    up_weight,
    down_weight,
):
    own_width = input_codes.shape[1]
    model_width = own_width * lax.axis_size(("latent", "hidden"))
    cotangent_local = (cotangent_codes.astype(jnp.float32) * CODE_STEP).astype(jnp.bfloat16)
    inputs_local = (input_codes.astype(jnp.float32) * CODE_STEP).astype(jnp.bfloat16)
    inputs = lax.all_gather(inputs_local, ("latent", "hidden"), axis=1, tiled=True)
    preact = (
        lax.dot_general(inputs, dictionary, ACROSS, preferred_element_type=jnp.float32)
        + encoder_bias
    )
    latents = jnp.maximum(preact, 0.0).astype(jnp.bfloat16)
    partial_value = jnp.dot(latents, dictionary, preferred_element_type=jnp.float32)
    rebuilt = lax.psum(partial_value, ("latent", "hidden")) + decoder_bias
    inverse = lax.rsqrt(
        jnp.sum(rebuilt * rebuilt, axis=1, keepdims=True) / model_width + NORM_EPSILON
    )
    normed = (rebuilt * inverse * norm_gain).astype(jnp.bfloat16)
    target = inputs.astype(jnp.float32)
    gate_proj = lax.dot_general(normed, gate_weight, ACROSS, preferred_element_type=jnp.float32)
    up_proj = lax.dot_general(normed, up_weight, ACROSS, preferred_element_type=jnp.float32)
    gelu_value, gelu_slope = gelu_parts(gate_proj)
    hidden = (gelu_value * up_proj).astype(jnp.bfloat16)
    output_terms = jnp.dot(hidden, down_weight, preferred_element_type=jnp.float32)
    block_output = lax.psum_scatter(
        output_terms, ("latent", "hidden"), scatter_dimension=1, tiled=True
    ).astype(jnp.bfloat16)
    hidden_grad = lax.dot_general(
        lax.all_gather(cotangent_local, ("latent", "hidden"), axis=1, tiled=True),
        down_weight,
        ACROSS,
        preferred_element_type=jnp.float32,
    )
    gate_grad = (hidden_grad * up_proj * gelu_slope).astype(jnp.bfloat16)
    up_grad = (hidden_grad * gelu_value).astype(jnp.bfloat16)
    partial_grad = jnp.dot(gate_grad, gate_weight, preferred_element_type=jnp.float32) + jnp.dot(
        up_grad, up_weight, preferred_element_type=jnp.float32
    )
    scaled = lax.psum(partial_grad, ("latent", "hidden")) * norm_gain
    inner_row = jnp.sum(scaled * rebuilt, axis=1, keepdims=True)
    inverse_cube = inverse * inverse * inverse
    rebuilt_grad = (
        inverse * scaled - inverse_cube * rebuilt * (inner_row / model_width) + (rebuilt - target)
    ).astype(jnp.bfloat16)
    latent_grad = lax.dot_general(
        rebuilt_grad, dictionary, ACROSS, preferred_element_type=jnp.float32
    )
    preact_grad = jnp.where(preact > 0.0, latent_grad, 0.0).astype(jnp.bfloat16)
    dictionary_grad = lax.dot_general(
        latents, rebuilt_grad, DOWNWARD, preferred_element_type=jnp.float32
    ) + lax.dot_general(preact_grad, inputs, DOWNWARD, preferred_element_type=jnp.float32)
    return (block_output, dictionary_grad.astype(jnp.bfloat16))


def solution(mesh):
    in_specs = (
        P("groups", ("latent", "hidden")),
        P("groups", ("latent", "hidden")),
        P(("latent", "hidden"), None),
        P(("latent", "hidden")),
        P(),
        P(),
        P(("latent", "hidden"), None),
        P(("latent", "hidden"), None),
        P(("latent", "hidden"), None),
    )
    out_specs = (P("groups", ("latent", "hidden")), P(("latent", "hidden"), "groups"))
    return jax.shard_map(
        per_device, mesh=mesh, in_specs=in_specs, out_specs=out_specs, check_vma=False
    )
```

```python
import functools
import math

import jax
import jax.numpy as jnp
from jax import lax
from jax.experimental import pallas as pl
from jax.experimental.pallas import tpu as pltpu
from jax.sharding import PartitionSpec as P

CODE_STEP = 2.0 ** (-6)
NORM_EPSILON = 1e-06
GELU_ROOT = 0.7978845608028654
GELU_CUBIC = 0.044715
ACROSS = (((1,), (1,)), ((), ()))
DOWNWARD = (((0,), (0,)), ((), ()))
LANES = 128
ROW_TILE = 16
VMEM_BYTES = 53 * 1024 * 1024
VMEM_LEAST = 32 * 1024 * 1024
VMEM_MOST = 60 * 1024 * 1024
F32 = jnp.float32
BF16 = jnp.bfloat16


def gelu_parts(values):
    argument = GELU_ROOT * (values + GELU_CUBIC * values * values * values)
    tanh_value = jnp.tanh(argument)
    result = 0.5 * values * (1.0 + tanh_value)
    derivative = 0.5 * (1.0 + tanh_value) + 0.5 * values * (
        1.0 - tanh_value * tanh_value
    ) * GELU_ROOT * (1.0 + 3.0 * GELU_CUBIC * values * values)
    return (result, derivative)


def up_to(value, unit):
    return -(-value // unit) * unit


class Plan:
    def __init__(self, chips, cores, rows, own):
        self.chips, self.cores, self.rows, self.own = chips, cores, rows, own
        self.width = own * chips * cores
        self.half = self.width // cores
        self.tiles = self.half // LANES
        self.chunk = up_to(-(-self.tiles * rows // chips), ROW_TILE)
        self.flat = self.chunk * chips
        self.tail = own - LANES
        if self.tail > 0:
            self.fold_rows = min(
                size
                for size in range(ROW_TILE, rows + ROW_TILE, ROW_TILE)
                if -(-rows // size) * self.tail <= LANES
            )
            self.packed = rows + self.fold_rows
        self.bits = [1 << k for k in reversed(range((chips - 1).bit_length()))]
        self.partners = [0] + list(range(chips - 1, 0, -1))
        self.order = [0]
        for bit in self.bits:
            self.order = self.order + [place ^ bit for place in self.order]

    def fits(self):
        return (
            self.cores == 2
            and len(self.order) == self.chips
            and self.rows % ROW_TILE == 0
            and self.half % LANES == 0
            and 0 < self.tail < LANES
        )


HBM = pl.BlockSpec(memory_space=pltpu.HBM)
ONCHIP = pl.BlockSpec(memory_space=pltpu.VMEM)


def shaped(*dims, dtype=F32):
    return jax.ShapeDtypeStruct(dims, dtype)


def padded_bytes(array):
    *lead, rows, columns = array.shape
    item = jnp.dtype(array.dtype).itemsize
    return math.prod(lead) * up_to(rows, ROW_TILE) * up_to(columns, LANES) * item


def call(body, out_shapes, operands, fetched=(), scratch=(), out_specs=None, flops=0, moved=0, grant=VMEM_BYTES):
    outputs = jax.tree.leaves(out_shapes) if out_specs is None else []
    taken = sum(padded_bytes(one) for one in list(operands) + outputs)
    return pl.pallas_call(
        body,
        out_shape=out_shapes,
        in_specs=[ONCHIP] * len(operands) + [HBM] * len(fetched),
        out_specs=jax.tree.map(lambda _: ONCHIP, out_shapes) if out_specs is None else out_specs,
        scratch_shapes=[pltpu.VMEM(one.shape, one.dtype) for one in fetched] + list(scratch),
        compiler_params=pltpu.CompilerParams(vmem_limit_bytes=grant - taken),
        cost_estimate=pl.CostEstimate(flops=flops, bytes_accessed=moved, transcendentals=0),
    )(*operands, *fetched)


def copies(sources, targets, sems, first=0):
    started = []
    for index, (source, target) in enumerate(zip(sources, targets)):
        one = pltpu.make_async_copy(source, target, sems.at[first + index])
        one.start()
        started.append(one)
    return started


def bring_body(count, *refs):
    sources, targets, sems = refs[:count], refs[count : 2 * count], refs[2 * count]
    for copy in copies(sources, targets, sems):
        copy.wait()


def bring(*arrays):
    return pl.pallas_call(
        functools.partial(bring_body, len(arrays)),
        out_shape=[jax.ShapeDtypeStruct(one.shape, one.dtype) for one in arrays],
        in_specs=[HBM] * len(arrays),
        out_specs=[ONCHIP] * len(arrays),
        scratch_shapes=[pltpu.SemaphoreType.DMA((len(arrays),))],
        compiler_params=pltpu.CompilerParams(
            vmem_limit_bytes=VMEM_BYTES - sum(map(padded_bytes, arrays))
        ),
        cost_estimate=pl.CostEstimate(
            flops=0, bytes_accessed=2 * sum(map(padded_bytes, arrays)), transcendentals=0
        ),
    )(*arrays)


def pack_block(plan, block):
    tail = block[:, LANES:]
    folded = []
    for start in range(0, plan.rows, plan.fold_rows):
        piece = tail[start : min(start + plan.fold_rows, plan.rows), :]
        short = plan.fold_rows - piece.shape[0]
        if short:
            piece = jnp.concatenate([piece, jnp.zeros((short, plan.tail), block.dtype)], axis=0)
        folded.append(piece)
    fill = LANES - len(folded) * plan.tail
    if fill:
        folded.append(jnp.zeros((plan.fold_rows, fill), block.dtype))
    return block[:, :LANES], jnp.concatenate(folded, axis=1)


def unpack_block(plan, packed):
    pieces = []
    for fold, start in enumerate(range(0, plan.rows, plan.fold_rows)):
        count = min(plan.fold_rows, plan.rows - start)
        pieces.append(
            packed[plan.rows : plan.rows + count, fold * plan.tail : (fold + 1) * plan.tail]
        )
    return jnp.concatenate([packed[: plan.rows, :], jnp.concatenate(pieces, axis=0)], axis=1)


def pack_codes_body(plan, input_hbm, cotangent_hbm, inputs_ref, cotangent_out_ref, input_ref, cotangent_ref, sems):
    for copy in copies([input_hbm, cotangent_hbm], [input_ref, cotangent_ref], sems):
        copy.wait()
    main, tail = pack_block(plan, input_ref[...].astype(F32) * CODE_STEP)
    for chip in range(plan.chips):
        inputs_ref[chip, : plan.rows, :] = main.astype(BF16)
        inputs_ref[chip, plan.rows :, :] = tail.astype(BF16)
    main, tail = pack_block(plan, cotangent_ref[...].astype(F32) * CODE_STEP)
    cotangent_out_ref[0, : plan.rows, :] = main.astype(BF16)
    cotangent_out_ref[0, plan.rows :, :] = tail.astype(BF16)


def pack_codes(plan, input_codes, cotangent_codes):
    return call(
        functools.partial(pack_codes_body, plan),
        [
            shaped(plan.chips, plan.packed, LANES, dtype=BF16),
            shaped(1, plan.packed, LANES, dtype=BF16),
        ],
        (),
        (input_codes, cotangent_codes),
        [pltpu.SemaphoreType.DMA((2,))],
        moved=plan.rows * plan.own * 8,
        grant=VMEM_MOST,
    )


def assemble(plan, relative, own_ref, other_ref, both, full_ref):
    core = lax.axis_index("hidden")
    if relative:
        me = lax.axis_index("latent")
        for place, partner in enumerate(plan.order):
            chip = me ^ partner
            both[core, chip] = own_ref[place]
            both[1 - core, chip] = other_ref[place]
    else:
        both[core] = own_ref[...]
        both[1 - core] = other_ref[...]
    for chip in range(plan.chips):
        for side in range(plan.cores):
            column = (chip * plan.cores + side) * plan.own
            block = unpack_block(plan, both[side, chip].astype(F32))
            full_ref[:, column : column + plan.own] = block.astype(BF16)


def both_scratch(plan, dtype=BF16):
    return pltpu.VMEM((plan.cores, plan.chips, plan.packed, LANES), dtype)


def halves_of_product(plan, pairs, mine_ref, theirs_ref, gain_ref=None, bias_ref=None):
    core = lax.axis_index("hidden")
    for target, side in ((theirs_ref, 1 - core), (mine_ref, core)):
        start = pl.multiple_of(side * plan.half, LANES)
        total = None
        for left, right_ref in pairs:
            term = jnp.dot(
                left, right_ref[:, pl.ds(start, plan.half)], preferred_element_type=F32
            )
            total = term if total is None else total + term
        if gain_ref is not None:
            once = jnp.where((lax.axis_index("latent") == 0) & (side == core), 1.0, 0.0)
            bias = bias_ref[:, pl.ds(start, plan.half)] * once
            total = (total + bias) * gain_ref[:, pl.ds(start, plan.half)]
        for tile in range(plan.tiles):
            target[tile * plan.rows : (tile + 1) * plan.rows, :] = total[
                :, tile * LANES : (tile + 1) * LANES
            ].astype(target.dtype)
        used = plan.tiles * plan.rows
        if used < plan.flat:
            target[used:, :] = jnp.zeros((plan.flat - used, LANES), target.dtype)


def bring_encoder_body(dict_hbm, vectors_hbm, dict_ref, bias_ref, decoder_ref, gain_ref, sems):
    sources, targets = [dict_hbm], [dict_ref]
    start = 0
    for target in (bias_ref, decoder_ref, gain_ref):
        sources.append(vectors_hbm.at[:, start : start + target.shape[1]])
        targets.append(target)
        start += target.shape[1]
    for copy in copies(sources, targets, sems):
        copy.wait()


def bring_encoder(plan, dictionary, vectors):
    outputs = [
        shaped(*dictionary.shape, dtype=BF16),
        shaped(1, dictionary.shape[0]),
        shaped(1, plan.width),
        shaped(1, plan.width),
    ]
    return pl.pallas_call(
        bring_encoder_body,
        out_shape=outputs,
        in_specs=[HBM] * 2,
        out_specs=[ONCHIP] * len(outputs),
        scratch_shapes=[pltpu.SemaphoreType.DMA((len(outputs),))],
        compiler_params=pltpu.CompilerParams(
            vmem_limit_bytes=VMEM_BYTES - sum(map(padded_bytes, outputs))
        ),
        cost_estimate=pl.CostEstimate(
            flops=0, bytes_accessed=dictionary.size * 4, transcendentals=0
        ),
    )(dictionary, vectors)


def encode_body(plan, own_ref, other_ref, dict_ref, bias_ref, decoder_ref, gain_ref, inputs_ref, latents_ref, mine_ref, theirs_ref, both):
    assemble(plan, False, own_ref, other_ref, both, inputs_ref)
    preact = (
        lax.dot_general(inputs_ref[...], dict_ref[...], ACROSS, preferred_element_type=F32)
        + bias_ref[...]
    )
    latents = jnp.maximum(preact, 0.0).astype(BF16)
    latents_ref[...] = latents
    halves_of_product(plan, [(latents, dict_ref)], mine_ref, theirs_ref, gain_ref, decoder_ref)


def encode(plan, own, other, dictionary, encoder_bias, decoder_bias, gain):
    latents = dictionary.shape[0]
    return call(
        functools.partial(encode_body, plan),
        [
            shaped(plan.rows, plan.width, dtype=BF16),
            shaped(plan.rows, latents, dtype=BF16),
            shaped(plan.flat, LANES),
            shaped(plan.flat, LANES),
        ],
        (own, other, dictionary, encoder_bias, decoder_bias, gain),
        (),
        [both_scratch(plan)],
        flops=4 * plan.rows * plan.width * latents,
        moved=dictionary.size * 2,
    )


def back_project_body(plan, own_ref, other_ref, down_hbm, grad_ref, down_ref, both, full, sems):
    (copy,) = copies([down_hbm], [down_ref], sems)
    assemble(plan, True, own_ref, other_ref, both, full)
    copy.wait()
    grad_ref[...] = lax.dot_general(
        full[...], down_ref[...], ACROSS, preferred_element_type=F32
    )


def back_project(plan, own, other, down_weight):
    units = down_weight.shape[0]
    return call(
        functools.partial(back_project_body, plan),
        shaped(plan.rows, units),
        (own, other),
        (down_weight,),
        [both_scratch(plan), pltpu.VMEM((plan.rows, plan.width), BF16), pltpu.SemaphoreType.DMA((1,))],
        flops=2 * plan.rows * plan.width * units,
        moved=down_weight.size * 2,
    )


def join_half(plan, source, first, full_ref):
    for tile in range(plan.tiles):
        column = pl.multiple_of(first + tile * LANES, LANES)
        row = 0
        while row < plan.rows:
            chip, place = divmod(tile * plan.rows + row, plan.chunk)
            count = min(plan.rows - row, plan.chunk - place)
            full_ref[row : row + count, pl.ds(column, LANES)] = source[
                chip, place : place + count, :
            ]
            row += count


def half_terms(plan, half, side, gate_ref, up_ref, gain_ref):
    span = pl.ds(pl.multiple_of(side * plan.half, LANES), plan.half)
    rebuilt = half.astype(F32) / gain_ref[:, span]
    squares = jnp.sum(rebuilt * rebuilt, axis=1, keepdims=True)
    gate = lax.dot_general(half, gate_ref[:, span], ACROSS, preferred_element_type=F32)
    up = lax.dot_general(half, up_ref[:, span], ACROSS, preferred_element_type=F32)
    return squares, gate, up


def mlp_first_body(plan, own_ref, gate_ref, up_ref, gain_ref, half_ref, squares_ref, gate_part_ref, up_part_ref):
    join_half(plan, own_ref, 0, half_ref)
    squares_ref[...], gate_part_ref[...], up_part_ref[...] = half_terms(
        plan, half_ref[...], lax.axis_index("hidden"), gate_ref, up_ref, gain_ref
    )


def mlp_first(plan, own, gate_weight, up_weight, gain):
    units = gate_weight.shape[0]
    return call(
        functools.partial(mlp_first_body, plan),
        [
            shaped(plan.rows, plan.half, dtype=BF16),
            shaped(plan.rows, 1),
            shaped(plan.rows, units),
            shaped(plan.rows, units),
        ],
        (own, gate_weight, up_weight, gain),
        grant=VMEM_LEAST,
        flops=2 * plan.rows * plan.width * units,
        moved=gate_weight.size * 4,
    )


def mlp_body(plan, other_ref, gate_ref, up_ref, gain_ref, grad_ref, half_ref, squares_ref, gate_part_ref, up_part_ref, scaled_ref, inverse_ref, hidden_ref, mine_ref, theirs_ref):
    core = lax.axis_index("hidden")
    join_half(plan, other_ref, (1 - core) * plan.half, scaled_ref)
    other_span = pl.ds(pl.multiple_of((1 - core) * plan.half, LANES), plan.half)
    own_span = pl.ds(pl.multiple_of(core * plan.half, LANES), plan.half)
    scaled_ref[:, own_span] = half_ref[...]
    squares, gate, up = half_terms(
        plan, scaled_ref[:, other_span], 1 - core, gate_ref, up_ref, gain_ref
    )
    inverse = lax.rsqrt((squares + squares_ref[...]) / plan.width + NORM_EPSILON)
    inverse_ref[...] = inverse
    gate_proj = inverse * (gate + gate_part_ref[...])
    up_proj = inverse * (up + up_part_ref[...])
    gelu_value, gelu_slope = gelu_parts(gate_proj)
    hidden_ref[...] = (gelu_value * up_proj).astype(BF16)
    hidden_grad = grad_ref[...]
    gate_grad = (hidden_grad * up_proj * gelu_slope).astype(BF16)
    up_grad = (hidden_grad * gelu_value).astype(BF16)
    halves_of_product(plan, [(gate_grad, gate_ref), (up_grad, up_ref)], mine_ref, theirs_ref)


def mlp(plan, other, gate_weight, up_weight, gain, hidden_grad, first):
    units = gate_weight.shape[0]
    return call(
        functools.partial(mlp_body, plan),
        [
            shaped(plan.rows, plan.width, dtype=BF16),
            shaped(plan.rows, 1),
            shaped(plan.rows, units, dtype=BF16),
            shaped(plan.flat, LANES),
            shaped(plan.flat, LANES),
        ],
        (other, gate_weight, up_weight, gain, hidden_grad, *first),
        grant=VMEM_LEAST,
        flops=6 * plan.rows * plan.width * units,
        moved=gate_weight.size * 4,
    )


def project_body(plan, hidden_ref, down_hbm, mine_ref, theirs_ref, down_ref, both, sems):
    (copy,) = copies([down_hbm], [down_ref], sems)
    core = lax.axis_index("hidden")
    copy.wait()
    terms = jnp.dot(hidden_ref[...], down_ref[...], preferred_element_type=F32)
    for chip in range(plan.chips):
        for side in range(plan.cores):
            start = (chip * plan.cores + side) * plan.own
            main, tail = pack_block(plan, terms[:, start : start + plan.own])
            both[side, chip, : plan.rows, :] = main
            both[side, chip, plan.rows :, :] = tail
    me = lax.axis_index("latent")
    for place, partner in enumerate(plan.order):
        chip = me ^ partner
        mine_ref[place] = both[core, chip]
        theirs_ref[place] = both[1 - core, chip]


def project(plan, hidden, down_weight):
    units = down_weight.shape[0]
    return call(
        functools.partial(project_body, plan),
        [shaped(plan.chips, plan.packed, LANES)] * 2,
        (hidden,),
        (down_weight,),
        [both_scratch(plan, F32), pltpu.SemaphoreType.DMA((1,))],
        flops=2 * plan.rows * plan.width * units,
        moved=down_weight.size * 2,
    )


def total_of(plan, terms_ref, start, count):
    total = terms_ref[0, start : start + count, :].astype(F32)
    for chip in range(1, plan.chips):
        total = total + terms_ref[chip, start : start + count, :].astype(F32)
    return total


def sum_body(plan, terms_ref, out_ref):
    total = total_of(plan, terms_ref, 0, plan.chunk).astype(BF16)
    for place in range(out_ref.shape[0]):
        out_ref[place] = total


def sum_terms(plan, terms, copies_of):
    return call(
        functools.partial(sum_body, plan),
        shaped(copies_of, plan.chunk, LANES, dtype=BF16),
        (terms,),
        grant=VMEM_LEAST,
        moved=terms.size * 4,
    )


def line_up_body(plan, *refs):
    me = lax.axis_index("latent")
    for place, partner in enumerate(plan.partners):
        refs[-1][me ^ partner] = refs[place][0]


def send_block(plan, block):
    return [block] + [partner_swap(block, partner) for partner in plan.partners[1:]]


def line_up(plan, blocks):
    return call(
        functools.partial(line_up_body, plan),
        shaped(plan.chips, plan.chunk, LANES, dtype=BF16),
        blocks,
        grant=VMEM_LEAST,
        moved=blocks[0].size * 4 * plan.chips,
    )


def finish_output_body(plan, kept_ref, out_ref):
    out_ref[...] = unpack_block(plan, kept_ref[0]).astype(BF16)


def finish_output(plan, kept):
    return call(
        functools.partial(finish_output_body, plan),
        shaped(plan.rows, plan.own, dtype=BF16),
        (kept,),
        moved=kept.size * 4,
    )


def dictionary_body(plan, pieces, own_ref, other_ref, gain_ref, inverse_ref, scaled_ref, inputs_ref, latents_ref, dict_hbm, out_hbm, dict_ref, full, out_ref, sems, out_sems):
    (copy,) = copies([dict_hbm], [dict_ref], sems)
    core = lax.axis_index("hidden")
    join_half(plan, own_ref, core * plan.half, full)
    join_half(plan, other_ref, (1 - core) * plan.half, full)
    grad = full[...].astype(F32)
    gain = gain_ref[...]
    scaled_rebuilt = scaled_ref[...].astype(F32)
    rebuilt = scaled_rebuilt / gain
    inverse = inverse_ref[...]
    inner_row = jnp.sum(grad * scaled_rebuilt, axis=1, keepdims=True)
    inverse_cube = inverse * inverse * inverse
    inputs = inputs_ref[...]
    rebuilt_grad = (
        inverse * (grad * gain)
        - (inverse_cube * (inner_row / plan.width)) * rebuilt
        + (rebuilt - inputs.astype(F32))
    ).astype(BF16)
    copy.wait()
    latents = latents_ref[...]
    latent_grad = lax.dot_general(
        rebuilt_grad, dict_ref[...], ACROSS, preferred_element_type=F32
    )
    preact_grad = jnp.where(latents.astype(F32) > 0.0, latent_grad, 0.0).astype(BF16)
    left = jnp.concatenate([latents, preact_grad], axis=0)
    right = jnp.concatenate([rebuilt_grad, inputs], axis=0)
    size = plan.width // pieces
    writes = []
    for piece in range(pieces):
        span = slice(piece * size, (piece + 1) * size)
        out_ref[:, span] = lax.dot_general(
            left, right[:, span], DOWNWARD, preferred_element_type=F32
        ).astype(BF16)
        one = pltpu.make_async_copy(
            out_ref.at[:, span], out_hbm.at[:, span], out_sems.at[piece]
        )
        one.start()
        writes.append(one)
    for one in writes:
        one.wait()


def dictionary_step(plan, own, other, gain, inverse, scaled, inputs, latents, dictionary):
    units = dictionary.shape[0]
    pieces = plan.cores
    return call(
        functools.partial(dictionary_body, plan, pieces),
        shaped(*dictionary.shape, dtype=BF16),
        (own, other, gain, inverse, scaled, inputs, latents),
        (dictionary,),
        [
            pltpu.VMEM((plan.rows, plan.width), BF16),
            pltpu.VMEM(dictionary.shape, BF16),
            pltpu.SemaphoreType.DMA((1,)),
            pltpu.SemaphoreType.DMA((pieces,)),
        ],
        out_specs=HBM,
        flops=6 * plan.rows * plan.width * units,
        moved=dictionary.size * 4,
    )


def swap(value):
    size = lax.axis_size("hidden")
    return lax.ppermute(value, "hidden", [(i, (i + 1) % size) for i in range(size)])


def partner_swap(value, bit):
    size = lax.axis_size("latent")
    return lax.ppermute(value, "latent", [(i, i ^ bit) for i in range(size)])


def grow(stack, bit):
    return jnp.concatenate([stack, partner_swap(stack, bit)], axis=0)


def shrink(kept, sent, bit):
    return kept + partner_swap(sent, bit).astype(F32)


def halved(stack):
    middle = stack.shape[0] // 2
    return stack[:middle], stack[middle:].astype(BF16)


def trade(stack):
    return lax.all_to_all(stack, "latent", 0, 0, tiled=False)


def per_device(
    input_codes,
    cotangent_codes,
    dictionary,
    encoder_bias,
    decoder_bias,
    norm_gain,
    gate_weight,
    up_weight,
    down_weight,
):
    plan = Plan(
        lax.axis_size("latent"), lax.axis_size("hidden"), input_codes.shape[0], input_codes.shape[1]
    )
    if not plan.fits():
        return per_device_plain(
            input_codes,
            cotangent_codes,
            dictionary,
            encoder_bias,
            decoder_bias,
            norm_gain,
            gate_weight,
            up_weight,
            down_weight,
        )
    inputs_stack, cotangent = pack_codes(plan, input_codes, cotangent_codes)
    inputs_own = trade(inputs_stack)
    columns = plan.order[1 : plan.chips // 2]
    cotangent = jnp.concatenate(
        [cotangent] + [partner_swap(cotangent, bits) for bits in columns], axis=0
    )
    vectors = jnp.concatenate([encoder_bias, decoder_bias, norm_gain]).reshape(1, -1)
    inputs_own, cotangent, vectors = lax.optimization_barrier((inputs_own, cotangent, vectors))
    inputs_own, late_dictionary = lax.optimization_barrier((inputs_own, dictionary))
    encoder = bring_encoder(plan, late_dictionary, vectors)
    gain = encoder[-1]
    inputs, latents, mine, theirs = encode(plan, inputs_own, swap(inputs_own), *encoder)
    half = (mine + swap(theirs)).astype(BF16)
    half, cotangent = lax.optimization_barrier((half, cotangent))
    terms = trade(half.reshape(plan.chips, plan.chunk, LANES))
    cotangent = grow(cotangent, plan.bits[-1])
    scaled_block = sum_terms(plan, terms, 1)
    scaled_block, cotangent, late = lax.optimization_barrier(
        (scaled_block, cotangent, (gate_weight, up_weight, gain))
    )
    blocks = send_block(plan, scaled_block)
    hidden_grad = back_project(plan, cotangent, swap(cotangent), down_weight)
    weights = bring(*late)
    blocks, hidden_grad, weights = lax.optimization_barrier((blocks, hidden_grad, weights))
    scaled_own = line_up(plan, blocks)
    first = mlp_first(plan, scaled_own, *weights)
    scaled, inverse, hidden, mine, theirs = mlp(
        plan, swap(scaled_own), *weights, hidden_grad, first
    )
    half = (mine + swap(theirs)).astype(BF16)
    out_mine, out_theirs = project(plan, hidden, down_weight)
    half, out_mine, out_theirs = lax.optimization_barrier((half, out_mine, out_theirs))
    terms = trade(half.reshape(plan.chips, plan.chunk, LANES))
    kept, sent = halved(out_mine + swap(out_theirs))
    kept = shrink(kept, sent, plan.bits[-1])
    grad_stack = sum_terms(plan, terms, plan.chips)
    grad_stack, kept = lax.optimization_barrier((grad_stack, kept))
    grad_own = trade(grad_stack)
    for bit in reversed(plan.bits[1:-1]):
        kept, sent = halved(kept)
        kept = shrink(kept, sent, bit)
    kept, sent = halved(kept)
    grad_own, kept, sent, *late = lax.optimization_barrier(
        (grad_own, kept, sent, gain, inverse, scaled, inputs, latents)
    )
    dictionary_grad = dictionary_step(plan, grad_own, swap(grad_own), *bring(*late), dictionary)
    dictionary_grad, kept = lax.optimization_barrier((dictionary_grad, kept))
    block_output = finish_output(plan, shrink(kept, sent, plan.bits[0]))
    return (block_output, dictionary_grad)


def per_device_plain(
    input_codes,
    cotangent_codes,
    dictionary,
    encoder_bias,
    decoder_bias,
    norm_gain,
    gate_weight,
    up_weight,
    down_weight,
):
    own_width = input_codes.shape[1]
    model_width = own_width * lax.axis_size(("latent", "hidden"))
    cotangent_local = (cotangent_codes.astype(jnp.float32) * CODE_STEP).astype(jnp.bfloat16)
    inputs_local = (input_codes.astype(jnp.float32) * CODE_STEP).astype(jnp.bfloat16)
    inputs = lax.all_gather(inputs_local, ("latent", "hidden"), axis=1, tiled=True)
    preact = (
        lax.dot_general(inputs, dictionary, ACROSS, preferred_element_type=jnp.float32)
        + encoder_bias
    )
    latents = jnp.maximum(preact, 0.0).astype(jnp.bfloat16)
    partial_value = jnp.dot(latents, dictionary, preferred_element_type=jnp.float32)
    rebuilt = lax.psum(partial_value, ("latent", "hidden")) + decoder_bias
    inverse = lax.rsqrt(
        jnp.sum(rebuilt * rebuilt, axis=1, keepdims=True) / model_width + NORM_EPSILON
    )
    normed = (rebuilt * inverse * norm_gain).astype(jnp.bfloat16)
    target = inputs.astype(jnp.float32)
    gate_proj = lax.dot_general(normed, gate_weight, ACROSS, preferred_element_type=jnp.float32)
    up_proj = lax.dot_general(normed, up_weight, ACROSS, preferred_element_type=jnp.float32)
    gelu_value, gelu_slope = gelu_parts(gate_proj)
    hidden = (gelu_value * up_proj).astype(jnp.bfloat16)
    output_terms = jnp.dot(hidden, down_weight, preferred_element_type=jnp.float32)
    block_output = lax.psum_scatter(
        output_terms, ("latent", "hidden"), scatter_dimension=1, tiled=True
    ).astype(jnp.bfloat16)
    hidden_grad = lax.dot_general(
        lax.all_gather(cotangent_local, ("latent", "hidden"), axis=1, tiled=True),
        down_weight,
        ACROSS,
        preferred_element_type=jnp.float32,
    )
    gate_grad = (hidden_grad * up_proj * gelu_slope).astype(jnp.bfloat16)
    up_grad = (hidden_grad * gelu_value).astype(jnp.bfloat16)
    partial_grad = jnp.dot(gate_grad, gate_weight, preferred_element_type=jnp.float32) + jnp.dot(
        up_grad, up_weight, preferred_element_type=jnp.float32
    )
    scaled = lax.psum(partial_grad, ("latent", "hidden")) * norm_gain
    inner_row = jnp.sum(scaled * rebuilt, axis=1, keepdims=True)
    inverse_cube = inverse * inverse * inverse
    rebuilt_grad = (
        inverse * scaled - inverse_cube * rebuilt * (inner_row / model_width) + (rebuilt - target)
    ).astype(jnp.bfloat16)
    latent_grad = lax.dot_general(
        rebuilt_grad, dictionary, ACROSS, preferred_element_type=jnp.float32
    )
    preact_grad = jnp.where(preact > 0.0, latent_grad, 0.0).astype(jnp.bfloat16)
    dictionary_grad = lax.dot_general(
        latents, rebuilt_grad, DOWNWARD, preferred_element_type=jnp.float32
    ) + lax.dot_general(preact_grad, inputs, DOWNWARD, preferred_element_type=jnp.float32)
    return (block_output, dictionary_grad.astype(jnp.bfloat16))


def solution(mesh):
    in_specs = (
        P("groups", ("latent", "hidden")),
        P("groups", ("latent", "hidden")),
        P(("latent", "hidden"), None),
        P(("latent", "hidden")),
        P(),
        P(),
        P(("latent", "hidden"), None),
        P(("latent", "hidden"), None),
        P(("latent", "hidden"), None),
    )
    out_specs = (P("groups", ("latent", "hidden")), P(("latent", "hidden"), "groups"))
    return jax.shard_map(
        per_device, mesh=mesh, in_specs=in_specs, out_specs=out_specs, check_vma=False
    )
```

```python
import functools
import math

import jax
import jax.numpy as jnp
from jax import lax
from jax.experimental import pallas as pl
from jax.experimental.pallas import tpu as pltpu
from jax.sharding import PartitionSpec as P

CODE_STEP = 2.0 ** (-6)
NORM_EPSILON = 1e-06
GELU_ROOT = 0.7978845608028654
GELU_CUBIC = 0.044715
ACROSS = (((1,), (1,)), ((), ()))
DOWNWARD = (((0,), (0,)), ((), ()))
LANES = 128
ROW_TILE = 16
DIRECT_LIMIT = 16
VMEM_BYTES = 24 * 1024 * 1024
F32 = jnp.float32
BF16 = jnp.bfloat16


def gelu_parts(values):
    argument = GELU_ROOT * (values + GELU_CUBIC * values * values * values)
    tanh_value = jnp.tanh(argument)
    result = 0.5 * values * (1.0 + tanh_value)
    derivative = 0.5 * (1.0 + tanh_value) + 0.5 * values * (
        1.0 - tanh_value * tanh_value
    ) * GELU_ROOT * (1.0 + 3.0 * GELU_CUBIC * values * values)
    return (result, derivative)


def up_to(value, unit):
    return -(-value // unit) * unit


def chips_fit(chips):
    return 2 <= chips <= DIRECT_LIMIT and chips & (chips - 1) == 0


class Plan:
    def __init__(self, chips, cores, rows, own):
        self.chips, self.cores, self.rows, self.own = chips, cores, rows, own
        self.width = own * chips * cores
        self.half = self.width // cores
        self.tiles = self.half // LANES
        self.chunk = up_to(-(-self.tiles * rows // chips), ROW_TILE)
        self.flat = self.chunk * chips
        self.tail = own - LANES
        if self.tail > 0:
            self.fold_rows = min(
                size
                for size in range(ROW_TILE, rows + ROW_TILE, ROW_TILE)
                if -(-rows // size) * self.tail <= LANES
            )
            self.packed = rows + self.fold_rows
        self.columns = list(range(0, chips, 2))

    def pieces(self):
        for tile in range(self.tiles):
            row = 0
            while row < self.rows:
                chip, place = divmod(tile * self.rows + row, self.chunk)
                count = min(self.rows - row, self.chunk - place)
                yield tile, chip, place, row, count
                row += count

    def fits(self):
        return (
            self.cores == 2
            and chips_fit(self.chips)
            and self.rows % ROW_TILE == 0
            and self.half % LANES == 0
            and 0 < self.tail < LANES
        )


HBM = pl.BlockSpec(memory_space=pltpu.HBM)
ONCHIP = pl.BlockSpec(memory_space=pltpu.VMEM)


def shaped(*dims, dtype=F32):
    return jax.ShapeDtypeStruct(dims, dtype)


HBM = pl.BlockSpec(memory_space=pltpu.HBM)
ONCHIP = pl.BlockSpec(memory_space=pltpu.VMEM)


def shaped(*dims, dtype=F32):
    return jax.ShapeDtypeStruct(dims, dtype)


def call(body, out_shapes, operands, scratch=(), out_specs=None, flops=0, moved=0):
    return pl.pallas_call(
        body,
        out_shape=out_shapes,
        in_specs=[ONCHIP] * len(operands),
        out_specs=jax.tree.map(lambda _: ONCHIP, out_shapes) if out_specs is None else out_specs,
        scratch_shapes=list(scratch),
        compiler_params=pltpu.CompilerParams(vmem_limit_bytes=VMEM_BYTES),
        cost_estimate=pl.CostEstimate(flops=flops, bytes_accessed=moved, transcendentals=0),
    )(*operands)


def pack_block(plan, block):
    tail = block[:, LANES:]
    folded = []
    for start in range(0, plan.rows, plan.fold_rows):
        piece = tail[start : min(start + plan.fold_rows, plan.rows), :]
        short = plan.fold_rows - piece.shape[0]
        if short:
            piece = jnp.concatenate([piece, jnp.zeros((short, plan.tail), block.dtype)], axis=0)
        folded.append(piece)
    fill = LANES - len(folded) * plan.tail
    if fill:
        folded.append(jnp.zeros((plan.fold_rows, fill), block.dtype))
    return block[:, :LANES], jnp.concatenate(folded, axis=1)


def unpack_block(plan, packed):
    pieces = []
    for fold, start in enumerate(range(0, plan.rows, plan.fold_rows)):
        count = min(plan.fold_rows, plan.rows - start)
        pieces.append(
            packed[plan.rows : plan.rows + count, fold * plan.tail : (fold + 1) * plan.tail]
        )
    return jnp.concatenate([packed[: plan.rows, :], jnp.concatenate(pieces, axis=0)], axis=1)


def pack_codes_body(plan, *refs):
    for codes_ref, out_ref in zip(refs[:2], refs[2:]):
        main, tail = pack_block(plan, codes_ref[...].astype(F32) * CODE_STEP)
        out_ref[0, : plan.rows, :] = main.astype(BF16)
        out_ref[0, plan.rows :, :] = tail.astype(BF16)


def pack_codes(plan, input_codes, cotangent_codes):
    return call(
        functools.partial(pack_codes_body, plan),
        [shaped(1, plan.packed, LANES, dtype=BF16)] * 2,
        (input_codes, cotangent_codes),
        moved=plan.rows * plan.own * 8,
    )


def assemble(plan, own_ref, other_ref, both, full_ref):
    core = lax.axis_index("hidden")
    both[core] = own_ref[...]
    both[1 - core] = other_ref[...]
    for chip in range(plan.chips):
        for side in range(plan.cores):
            column = (chip * plan.cores + side) * plan.own
            block = unpack_block(plan, both[side, chip].astype(F32))
            full_ref[:, column : column + plan.own] = block.astype(BF16)


def both_scratch(plan, dtype=BF16):
    return pltpu.VMEM((plan.cores, plan.chips, plan.packed, LANES), dtype)


def halves_of_product(plan, pairs, mine_ref, theirs_ref, gain_ref=None, bias_ref=None):
    core = lax.axis_index("hidden")
    for target, side in ((theirs_ref, 1 - core), (mine_ref, core)):
        start = pl.multiple_of(side * plan.half, LANES)
        total = None
        for left, right_ref in pairs:
            term = jnp.dot(
                left, right_ref[:, pl.ds(start, plan.half)], preferred_element_type=F32
            )
            total = term if total is None else total + term
        if gain_ref is not None:
            once = jnp.where((lax.axis_index("latent") == 0) & (side == core), 1.0, 0.0)
            bias = bias_ref[:, pl.ds(start, plan.half)] * once
            total = (total + bias) * gain_ref[:, pl.ds(start, plan.half)]
        for tile, chip, place, row, count in plan.pieces():
            target[chip, place : place + count, :] = total[
                row : row + count, tile * LANES : (tile + 1) * LANES
            ]
        used = plan.tiles * plan.rows
        while used < plan.flat:
            chip, place = divmod(used, plan.chunk)
            target[chip, place:, :] = jnp.zeros((plan.chunk - place, LANES), F32)
            used += plan.chunk - place


def encode_body(plan, own_ref, other_ref, dict_ref, bias_ref, decoder_ref, gain_ref, inputs_ref, latents_ref, mine_ref, theirs_ref, both):
    assemble(plan, own_ref, other_ref, both, inputs_ref)
    preact = (
        lax.dot_general(inputs_ref[...], dict_ref[...], ACROSS, preferred_element_type=F32)
        + bias_ref[...]
    )
    latents = jnp.maximum(preact, 0.0).astype(BF16)
    latents_ref[...] = latents
    halves_of_product(plan, [(latents, dict_ref)], mine_ref, theirs_ref, gain_ref, decoder_ref)


def encode(plan, own, other, dictionary, encoder_bias, decoder_bias, gain):
    latents = dictionary.shape[0]
    return call(
        functools.partial(encode_body, plan),
        [
            shaped(plan.rows, plan.width, dtype=BF16),
            shaped(plan.rows, latents, dtype=BF16),
            shaped(plan.chips, plan.chunk, LANES),
            shaped(plan.chips, plan.chunk, LANES),
        ],
        (own, other, dictionary, encoder_bias, decoder_bias, gain),
        [both_scratch(plan)],
        flops=4 * plan.rows * plan.width * latents,
        moved=dictionary.size * 2,
    )


def back_project_body(plan, own_ref, other_ref, down_ref, grad_ref, both, full):
    assemble(plan, own_ref, other_ref, both, full)
    grad_ref[...] = lax.dot_general(
        full[...], down_ref[...], ACROSS, preferred_element_type=F32
    )


def back_project(plan, own, other, down_weight):
    units = down_weight.shape[0]
    return call(
        functools.partial(back_project_body, plan),
        shaped(plan.rows, units),
        (own, other, down_weight),
        [both_scratch(plan), pltpu.VMEM((plan.rows, plan.width), BF16)],
        flops=2 * plan.rows * plan.width * units,
        moved=down_weight.size * 2,
    )


def join_half(plan, source, first, full_ref):
    for tile, chip, place, row, count in plan.pieces():
        column = pl.multiple_of(first + tile * LANES, LANES)
        full_ref[row : row + count, pl.ds(column, LANES)] = source[
            chip, place : place + count, :
        ]


def half_terms(plan, half, side, gate_ref, up_ref, gain_ref):
    span = pl.ds(pl.multiple_of(side * plan.half, LANES), plan.half)
    rebuilt = half.astype(F32) / gain_ref[:, span]
    squares = jnp.sum(rebuilt * rebuilt, axis=1, keepdims=True)
    gate = lax.dot_general(half, gate_ref[:, span], ACROSS, preferred_element_type=F32)
    up = lax.dot_general(half, up_ref[:, span], ACROSS, preferred_element_type=F32)
    return squares, gate, up


def mlp_first_body(plan, own_ref, gate_ref, up_ref, gain_ref, half_ref, squares_ref, gate_part_ref, up_part_ref):
    join_half(plan, own_ref, 0, half_ref)
    squares_ref[...], gate_part_ref[...], up_part_ref[...] = half_terms(
        plan, half_ref[...], lax.axis_index("hidden"), gate_ref, up_ref, gain_ref
    )


def mlp_first(plan, own, gate_weight, up_weight, gain):
    units = gate_weight.shape[0]
    return call(
        functools.partial(mlp_first_body, plan),
        [
            shaped(plan.rows, plan.half, dtype=BF16),
            shaped(plan.rows, 1),
            shaped(plan.rows, units),
            shaped(plan.rows, units),
        ],
        (own, gate_weight, up_weight, gain),
        flops=2 * plan.rows * plan.width * units,
        moved=gate_weight.size * 4,
    )


def mlp_body(plan, other_ref, gate_ref, up_ref, gain_ref, grad_ref, half_ref, squares_ref, gate_part_ref, up_part_ref, scaled_ref, inverse_ref, hidden_ref, mine_ref, theirs_ref):
    core = lax.axis_index("hidden")
    join_half(plan, other_ref, (1 - core) * plan.half, scaled_ref)
    other_span = pl.ds(pl.multiple_of((1 - core) * plan.half, LANES), plan.half)
    own_span = pl.ds(pl.multiple_of(core * plan.half, LANES), plan.half)
    scaled_ref[:, own_span] = half_ref[...]
    squares, gate, up = half_terms(
        plan, scaled_ref[:, other_span], 1 - core, gate_ref, up_ref, gain_ref
    )
    inverse = lax.rsqrt((squares + squares_ref[...]) / plan.width + NORM_EPSILON)
    inverse_ref[...] = inverse
    gate_proj = inverse * (gate + gate_part_ref[...])
    up_proj = inverse * (up + up_part_ref[...])
    gelu_value, gelu_slope = gelu_parts(gate_proj)
    hidden_ref[...] = (gelu_value * up_proj).astype(BF16)
    hidden_grad = grad_ref[...]
    gate_grad = (hidden_grad * up_proj * gelu_slope).astype(BF16)
    up_grad = (hidden_grad * gelu_value).astype(BF16)
    halves_of_product(plan, [(gate_grad, gate_ref), (up_grad, up_ref)], mine_ref, theirs_ref)


def mlp(plan, other, gate_weight, up_weight, gain, hidden_grad, first):
    units = gate_weight.shape[0]
    return call(
        functools.partial(mlp_body, plan),
        [
            shaped(plan.rows, plan.width, dtype=BF16),
            shaped(plan.rows, 1),
            shaped(plan.rows, units, dtype=BF16),
            shaped(plan.chips, plan.chunk, LANES),
            shaped(plan.chips, plan.chunk, LANES),
        ],
        (other, gate_weight, up_weight, gain, hidden_grad, *first),
        flops=6 * plan.rows * plan.width * units,
        moved=gate_weight.size * 4,
    )


def project_body(plan, hidden_ref, down_ref, mine_ref, theirs_ref, both):
    core = lax.axis_index("hidden")
    terms = jnp.dot(hidden_ref[...], down_ref[...], preferred_element_type=F32)
    for chip in range(plan.chips):
        for side in range(plan.cores):
            start = (chip * plan.cores + side) * plan.own
            main, tail = pack_block(plan, terms[:, start : start + plan.own])
            both[side, chip, : plan.rows, :] = main
            both[side, chip, plan.rows :, :] = tail
    mine_ref[...] = both[core]
    theirs_ref[...] = both[1 - core]


def project(plan, hidden, down_weight):
    units = down_weight.shape[0]
    shape = (plan.chips, plan.packed, LANES)
    return call(
        functools.partial(project_body, plan),
        [shaped(*shape)] * 2,
        (hidden, down_weight),
        [both_scratch(plan, F32)],
        flops=2 * plan.rows * plan.width * units,
        moved=down_weight.size * 2,
    )


def add_pair_body(plan, mine_ref, theirs_ref, kept_ref, sent_ref):
    me = lax.axis_index("latent")
    for place, column in enumerate(plan.columns):
        kept, sent = me ^ column, me ^ column ^ 1
        kept_ref[place] = mine_ref[kept] + theirs_ref[kept]
        sent_ref[place] = (mine_ref[sent] + theirs_ref[sent]).astype(BF16)


def add_pair(plan, mine, theirs):
    count, dims = len(plan.columns), mine.shape[1:]
    return call(
        functools.partial(add_pair_body, plan),
        [shaped(count, *dims), shaped(count, *dims, dtype=BF16)],
        (mine, theirs),
        moved=mine.size * 10,
    )


def add_across_body(plan, kept_ref, got_ref, own_ref, *sent_refs):
    own_ref[0] = kept_ref[0] + got_ref[0].astype(F32)
    for place, sent_ref in enumerate(sent_refs, 1):
        sent_ref[0] = (kept_ref[place] + got_ref[place].astype(F32)).astype(BF16)


def add_across(plan, kept, got):
    dims = kept.shape[1:]
    outs = [shaped(1, *dims, dtype=BF16)] * (len(plan.columns) - 1)
    own, *sent = call(
        functools.partial(add_across_body, plan),
        [shaped(1, *dims)] + outs,
        (kept, got),
        moved=kept.size * 6,
    )
    return own, sent


def column_total(refs):
    total = refs[0][0]
    for ref in refs[1:]:
        total = total + ref[0].astype(F32)
    return total


def add_column_body(*refs):
    refs[-1][0] = column_total(refs[:-1]).astype(BF16)


def add_column(plan, own, got):
    return call(
        add_column_body,
        shaped(*own.shape, dtype=BF16),
        (own, *got),
        moved=own.size * 8,
    )


def finish_output_body(plan, *refs):
    refs[-1][...] = unpack_block(plan, column_total(refs[:-1])).astype(BF16)


def finish_output(plan, own, got):
    return call(
        functools.partial(finish_output_body, plan),
        shaped(plan.rows, plan.own, dtype=BF16),
        (own, *got),
        moved=own.size * 8,
    )


def stack_body(*refs):
    for place, ref in enumerate(refs[:-1]):
        refs[-1][place] = ref[0]


def stack_up(plan, blocks):
    return call(
        stack_body,
        shaped(len(blocks), *blocks[0].shape[1:], dtype=BF16),
        blocks,
        moved=blocks[0].size * 16,
    )


def line_up_body(plan, stack_ref, crossed_ref, full_ref):
    me = lax.axis_index("latent")
    for place, column in enumerate(plan.columns):
        full_ref[me ^ column] = stack_ref[place]
        full_ref[me ^ column ^ 1] = crossed_ref[place]


def line_up(plan, stack, crossed):
    return call(
        functools.partial(line_up_body, plan),
        shaped(plan.chips, *stack.shape[1:], dtype=BF16),
        (stack, crossed),
        moved=stack.size * 8,
    )


def dictionary_body(plan, pieces, own_ref, other_ref, gain_ref, inverse_ref, scaled_ref, inputs_ref, latents_ref, dict_ref, out_hbm, full, out_ref, out_sems):
    core = lax.axis_index("hidden")
    join_half(plan, own_ref, core * plan.half, full)
    join_half(plan, other_ref, (1 - core) * plan.half, full)
    grad = full[...].astype(F32)
    gain = gain_ref[...]
    scaled_rebuilt = scaled_ref[...].astype(F32)
    rebuilt = scaled_rebuilt / gain
    inverse = inverse_ref[...]
    inner_row = jnp.sum(grad * scaled_rebuilt, axis=1, keepdims=True)
    inverse_cube = inverse * inverse * inverse
    inputs = inputs_ref[...]
    rebuilt_grad = (
        inverse * (grad * gain)
        - (inverse_cube * (inner_row / plan.width)) * rebuilt
        + (rebuilt - inputs.astype(F32))
    ).astype(BF16)
    latents = latents_ref[...]
    latent_grad = lax.dot_general(
        rebuilt_grad, dict_ref[...], ACROSS, preferred_element_type=F32
    )
    preact_grad = jnp.where(latents.astype(F32) > 0.0, latent_grad, 0.0).astype(BF16)
    left = jnp.concatenate([latents, preact_grad], axis=0)
    right = jnp.concatenate([rebuilt_grad, inputs], axis=0)
    size = plan.width // pieces
    writes = []
    for piece in range(pieces):
        span = slice(piece * size, (piece + 1) * size)
        out_ref[:, span] = lax.dot_general(
            left, right[:, span], DOWNWARD, preferred_element_type=F32
        ).astype(BF16)
        one = pltpu.make_async_copy(
            out_ref.at[:, span], out_hbm.at[:, span], out_sems.at[piece]
        )
        one.start()
        writes.append(one)
    for one in writes:
        one.wait()


def dictionary_step(plan, own, other, gain, inverse, scaled, inputs, latents, dictionary):
    units = dictionary.shape[0]
    pieces = plan.cores
    return call(
        functools.partial(dictionary_body, plan, pieces),
        shaped(*dictionary.shape, dtype=BF16),
        (own, other, gain, inverse, scaled, inputs, latents, dictionary),
        [
            pltpu.VMEM((plan.rows, plan.width), BF16),
            pltpu.VMEM(dictionary.shape, BF16),
            pltpu.SemaphoreType.DMA((pieces,)),
        ],
        out_specs=HBM,
        flops=6 * plan.rows * plan.width * units,
        moved=dictionary.size * 4,
    )


def swap(value):
    size = lax.axis_size("hidden")
    return lax.ppermute(value, "hidden", [(i, (i + 1) % size) for i in range(size)])


def partner_swap(value, bits):
    size = lax.axis_size("latent")
    return lax.ppermute(value, "latent", [(i, i ^ bits) for i in range(size)])


def cross(value):
    return partner_swap(value, 1)


def to_column(plan, blocks):
    return [partner_swap(one, bits) for one, bits in zip(blocks, plan.columns[1:])]


def tie(*values):
    return lax.optimization_barrier(values)


def per_device(
    input_codes,
    cotangent_codes,
    dictionary,
    encoder_bias,
    decoder_bias,
    norm_gain,
    gate_weight,
    up_weight,
    down_weight,
):
    plan = Plan(
        lax.axis_size("latent"), lax.axis_size("hidden"), input_codes.shape[0], input_codes.shape[1]
    )
    if not plan.fits():
        return per_device_plain(
            input_codes,
            cotangent_codes,
            dictionary,
            encoder_bias,
            decoder_bias,
            norm_gain,
            gate_weight,
            up_weight,
            down_weight,
        )
    fan = len(plan.columns) - 1
    bias, decoder, gain = (one.reshape(1, -1) for one in (encoder_bias, decoder_bias, norm_gain))
    block, cotangent = pack_codes(plan, input_codes, cotangent_codes)
    stack = stack_up(plan, [block] + to_column(plan, [block] * fan))
    inputs_own = line_up(plan, stack, cross(stack))
    inputs_own, cotangent = tie(inputs_own, cotangent)
    inputs, latents, mine, theirs = encode(
        plan, inputs_own, swap(inputs_own), dictionary, bias, decoder, gain
    )
    kept, sent = add_pair(plan, mine, swap(theirs))
    kept, sent, cotangent = tie(kept, sent, cotangent)
    got = cross(sent)
    cotangents = to_column(plan, [cotangent] * fan)
    own, sent = add_across(plan, kept, got)
    own, sent, cotangents = tie(own, sent, [cotangent] + cotangents)
    got = to_column(plan, sent)
    cotangent_stack = stack_up(plan, cotangents)
    cotangent_crossed = cross(cotangent_stack)
    block = add_column(plan, own, got)
    block, cotangent_stack, cotangent_crossed = tie(block, cotangent_stack, cotangent_crossed)
    stack = stack_up(plan, [block] + to_column(plan, [block] * fan))
    crossed = cross(stack)
    cotangent_own = line_up(plan, cotangent_stack, cotangent_crossed)
    hidden_grad = back_project(plan, cotangent_own, swap(cotangent_own), down_weight)
    stack, crossed, hidden_grad = tie(stack, crossed, hidden_grad)
    scaled_own = line_up(plan, stack, crossed)
    first = mlp_first(plan, scaled_own, gate_weight, up_weight, gain)
    scaled, inverse, hidden, mine, theirs = mlp(
        plan, swap(scaled_own), gate_weight, up_weight, gain, hidden_grad, first
    )
    kept, sent = add_pair(plan, mine, swap(theirs))
    kept, sent, hidden = tie(kept, sent, hidden)
    got = cross(sent)
    out_mine, out_theirs = project(plan, hidden, down_weight)
    out_kept, out_sent = add_pair(plan, out_mine, swap(out_theirs))
    own, sent = add_across(plan, kept, got)
    block = add_column(plan, own, to_column(plan, sent))
    block, out_kept, out_sent = tie(block, out_kept, out_sent)
    stack = stack_up(plan, [block] + to_column(plan, [block] * fan))
    out_own, out_sent = add_across(plan, out_kept, cross(out_sent))
    stack, out_own, out_sent = tie(stack, out_own, out_sent)
    crossed = cross(stack)
    out_got = to_column(plan, out_sent)
    grad_own = line_up(plan, stack, crossed)
    block_output = finish_output(plan, out_own, out_got)
    dictionary_grad = dictionary_step(
        plan, grad_own, swap(grad_own), gain, inverse, scaled, inputs, latents, dictionary
    )
    return (block_output, dictionary_grad)


def per_device_plain(
    input_codes,
    cotangent_codes,
    dictionary,
    encoder_bias,
    decoder_bias,
    norm_gain,
    gate_weight,
    up_weight,
    down_weight,
):
    own_width = input_codes.shape[1]
    model_width = own_width * lax.axis_size(("latent", "hidden"))
    cotangent_local = (cotangent_codes.astype(jnp.float32) * CODE_STEP).astype(jnp.bfloat16)
    inputs_local = (input_codes.astype(jnp.float32) * CODE_STEP).astype(jnp.bfloat16)
    inputs = lax.all_gather(inputs_local, ("latent", "hidden"), axis=1, tiled=True)
    preact = (
        lax.dot_general(inputs, dictionary, ACROSS, preferred_element_type=jnp.float32)
        + encoder_bias
    )
    latents = jnp.maximum(preact, 0.0).astype(jnp.bfloat16)
    partial_value = jnp.dot(latents, dictionary, preferred_element_type=jnp.float32)
    rebuilt = lax.psum(partial_value, ("latent", "hidden")) + decoder_bias
    inverse = lax.rsqrt(
        jnp.sum(rebuilt * rebuilt, axis=1, keepdims=True) / model_width + NORM_EPSILON
    )
    normed = (rebuilt * inverse * norm_gain).astype(jnp.bfloat16)
    target = inputs.astype(jnp.float32)
    gate_proj = lax.dot_general(normed, gate_weight, ACROSS, preferred_element_type=jnp.float32)
    up_proj = lax.dot_general(normed, up_weight, ACROSS, preferred_element_type=jnp.float32)
    gelu_value, gelu_slope = gelu_parts(gate_proj)
    hidden = (gelu_value * up_proj).astype(jnp.bfloat16)
    output_terms = jnp.dot(hidden, down_weight, preferred_element_type=jnp.float32)
    block_output = lax.psum_scatter(
        output_terms, ("latent", "hidden"), scatter_dimension=1, tiled=True
    ).astype(jnp.bfloat16)
    hidden_grad = lax.dot_general(
        lax.all_gather(cotangent_local, ("latent", "hidden"), axis=1, tiled=True),
        down_weight,
        ACROSS,
        preferred_element_type=jnp.float32,
    )
    gate_grad = (hidden_grad * up_proj * gelu_slope).astype(jnp.bfloat16)
    up_grad = (hidden_grad * gelu_value).astype(jnp.bfloat16)
    partial_grad = jnp.dot(gate_grad, gate_weight, preferred_element_type=jnp.float32) + jnp.dot(
        up_grad, up_weight, preferred_element_type=jnp.float32
    )
    scaled = lax.psum(partial_grad, ("latent", "hidden")) * norm_gain
    inner_row = jnp.sum(scaled * rebuilt, axis=1, keepdims=True)
    inverse_cube = inverse * inverse * inverse
    rebuilt_grad = (
        inverse * scaled - inverse_cube * rebuilt * (inner_row / model_width) + (rebuilt - target)
    ).astype(jnp.bfloat16)
    latent_grad = lax.dot_general(
        rebuilt_grad, dictionary, ACROSS, preferred_element_type=jnp.float32
    )
    preact_grad = jnp.where(preact > 0.0, latent_grad, 0.0).astype(jnp.bfloat16)
    dictionary_grad = lax.dot_general(
        latents, rebuilt_grad, DOWNWARD, preferred_element_type=jnp.float32
    ) + lax.dot_general(preact_grad, inputs, DOWNWARD, preferred_element_type=jnp.float32)
    return (block_output, dictionary_grad.astype(jnp.bfloat16))


def solution(mesh):
    in_specs = (
        P("groups", ("latent", "hidden")),
        P("groups", ("latent", "hidden")),
        P(("latent", "hidden"), None),
        P(("latent", "hidden")),
        P(),
        P(),
        P(("latent", "hidden"), None),
        P(("latent", "hidden"), None),
        P(("latent", "hidden"), None),
    )
    out_specs = (P("groups", ("latent", "hidden")), P(("latent", "hidden"), "groups"))
    return jax.shard_map(
        per_device, mesh=mesh, in_specs=in_specs, out_specs=out_specs, check_vma=False
    )
```

```python
import functools
import math

import jax
import jax.numpy as jnp
from jax import lax
from jax.experimental import pallas as pl
from jax.experimental.pallas import tpu as pltpu
from jax.sharding import PartitionSpec as P

CODE_STEP = 2.0 ** (-6)
NORM_EPSILON = 1e-06
GELU_ROOT = 0.7978845608028654
GELU_CUBIC = 0.044715
ACROSS = (((1,), (1,)), ((), ()))
DOWNWARD = (((0,), (0,)), ((), ()))
LANES = 128
ROW_TILE = 16
DIRECT_LIMIT = 16
VMEM_BYTES = 24 * 1024 * 1024
VMEM_BRING = 53 * 1024 * 1024
F32 = jnp.float32
BF16 = jnp.bfloat16


def gelu_parts(values):
    argument = GELU_ROOT * (values + GELU_CUBIC * values * values * values)
    tanh_value = jnp.tanh(argument)
    result = 0.5 * values * (1.0 + tanh_value)
    derivative = 0.5 * (1.0 + tanh_value) + 0.5 * values * (
        1.0 - tanh_value * tanh_value
    ) * GELU_ROOT * (1.0 + 3.0 * GELU_CUBIC * values * values)
    return (result, derivative)


def up_to(value, unit):
    return -(-value // unit) * unit


def chips_fit(chips):
    return 2 <= chips <= DIRECT_LIMIT and chips & (chips - 1) == 0


class Plan:
    def __init__(self, chips, cores, rows, own):
        self.chips, self.cores, self.rows, self.own = chips, cores, rows, own
        self.width = own * chips * cores
        self.half = self.width // cores
        self.tiles = self.half // LANES
        self.chunk = up_to(-(-self.tiles * rows // chips), ROW_TILE)
        self.flat = self.chunk * chips
        self.tail = own - LANES
        if self.tail > 0:
            self.fold_rows = min(
                size
                for size in range(ROW_TILE, rows + ROW_TILE, ROW_TILE)
                if -(-rows // size) * self.tail <= LANES
            )
            self.packed = rows + self.fold_rows
        self.columns = list(range(0, chips, 2))
        self.partners = list(range(chips - 1, 0, -1))

    def pieces(self):
        for tile in range(self.tiles):
            row = 0
            while row < self.rows:
                chip, place = divmod(tile * self.rows + row, self.chunk)
                count = min(self.rows - row, self.chunk - place)
                yield tile, chip, place, row, count
                row += count

    def fits(self):
        return (
            self.cores == 2
            and chips_fit(self.chips)
            and self.rows % ROW_TILE == 0
            and self.half % LANES == 0
            and 0 < self.tail < LANES
        )


HBM = pl.BlockSpec(memory_space=pltpu.HBM)
ONCHIP = pl.BlockSpec(memory_space=pltpu.VMEM)


def shaped(*dims, dtype=F32):
    return jax.ShapeDtypeStruct(dims, dtype)


HBM = pl.BlockSpec(memory_space=pltpu.HBM)
ONCHIP = pl.BlockSpec(memory_space=pltpu.VMEM)


def shaped(*dims, dtype=F32):
    return jax.ShapeDtypeStruct(dims, dtype)


def call(body, out_shapes, operands, scratch=(), out_specs=None, flops=0, moved=0):
    return pl.pallas_call(
        body,
        out_shape=out_shapes,
        in_specs=[ONCHIP] * len(operands),
        out_specs=jax.tree.map(lambda _: ONCHIP, out_shapes) if out_specs is None else out_specs,
        scratch_shapes=list(scratch),
        compiler_params=pltpu.CompilerParams(vmem_limit_bytes=VMEM_BYTES),
        cost_estimate=pl.CostEstimate(flops=flops, bytes_accessed=moved, transcendentals=0),
    )(*operands)


def padded_bytes(array):
    *lead, rows, columns = array.shape
    item = jnp.dtype(array.dtype).itemsize
    return math.prod(lead) * up_to(rows, ROW_TILE) * up_to(columns, LANES) * item


def copies(sources, targets, sems):
    started = []
    for index, (source, target) in enumerate(zip(sources, targets)):
        one = pltpu.make_async_copy(source, target, sems.at[index])
        one.start()
        started.append(one)
    return started


def pack_block(plan, block):
    tail = block[:, LANES:]
    folded = []
    for start in range(0, plan.rows, plan.fold_rows):
        piece = tail[start : min(start + plan.fold_rows, plan.rows), :]
        short = plan.fold_rows - piece.shape[0]
        if short:
            piece = jnp.concatenate([piece, jnp.zeros((short, plan.tail), block.dtype)], axis=0)
        folded.append(piece)
    fill = LANES - len(folded) * plan.tail
    if fill:
        folded.append(jnp.zeros((plan.fold_rows, fill), block.dtype))
    return block[:, :LANES], jnp.concatenate(folded, axis=1)


def unpack_block(plan, packed):
    pieces = []
    for fold, start in enumerate(range(0, plan.rows, plan.fold_rows)):
        count = min(plan.fold_rows, plan.rows - start)
        pieces.append(
            packed[plan.rows : plan.rows + count, fold * plan.tail : (fold + 1) * plan.tail]
        )
    return jnp.concatenate([packed[: plan.rows, :], jnp.concatenate(pieces, axis=0)], axis=1)


def pack_codes_body(plan, input_hbm, cotangent_hbm, block_ref, both_ref, input_ref, cotangent_ref, sems):
    for copy in copies([input_hbm, cotangent_hbm], [input_ref, cotangent_ref], sems):
        copy.wait()
    main, tail = pack_block(plan, input_ref[...].astype(F32) * CODE_STEP)
    for out_ref in (block_ref, both_ref):
        out_ref[0, : plan.rows, :] = main.astype(BF16)
        out_ref[0, plan.rows : plan.packed, :] = tail.astype(BF16)
    main, tail = pack_block(plan, cotangent_ref[...].astype(F32) * CODE_STEP)
    both_ref[0, plan.packed : plan.packed + plan.rows, :] = main.astype(BF16)
    both_ref[0, plan.packed + plan.rows :, :] = tail.astype(BF16)


def pack_codes(plan, input_codes, cotangent_codes):
    codes = (input_codes, cotangent_codes)
    return pl.pallas_call(
        functools.partial(pack_codes_body, plan),
        out_shape=[
            shaped(1, plan.packed, LANES, dtype=BF16),
            shaped(1, 2 * plan.packed, LANES, dtype=BF16),
        ],
        in_specs=[HBM] * 2,
        out_specs=[ONCHIP] * 2,
        scratch_shapes=[pltpu.VMEM(one.shape, one.dtype) for one in codes]
        + [pltpu.SemaphoreType.DMA((2,))],
        compiler_params=pltpu.CompilerParams(vmem_limit_bytes=55 * 1024 * 1024),
        cost_estimate=pl.CostEstimate(
            flops=0, bytes_accessed=plan.rows * plan.own * 16, transcendentals=0
        ),
    )(*codes)


def assemble(plan, own_ref, other_ref, both, full_ref):
    core = lax.axis_index("hidden")
    both[core] = own_ref[...]
    both[1 - core] = other_ref[...]
    for chip in range(plan.chips):
        for side in range(plan.cores):
            column = (chip * plan.cores + side) * plan.own
            block = unpack_block(plan, both[side, chip].astype(F32))
            full_ref[:, column : column + plan.own] = block.astype(BF16)


def both_scratch(plan, dtype=BF16):
    return pltpu.VMEM((plan.cores, plan.chips, plan.packed, LANES), dtype)


def half_product(plan, pairs, side, target, gain_ref=None, bias_ref=None):
    span = pl.ds(pl.multiple_of(side * plan.half, LANES), plan.half)
    total = None
    for left, right_ref in pairs:
        term = jnp.dot(left, right_ref[:, span], preferred_element_type=F32)
        total = term if total is None else total + term
    if bias_ref is not None:
        total = total + bias_ref[:, span] * jnp.where(lax.axis_index("latent") == 0, 1.0, 0.0)
    if gain_ref is not None:
        total = total * gain_ref[:, span]
    for tile, chip, place, row, count in plan.pieces():
        target[chip, place : place + count, :] = total[
            row : row + count, tile * LANES : (tile + 1) * LANES
        ]
    used = plan.tiles * plan.rows
    while used < plan.flat:
        chip, place = divmod(used, plan.chunk)
        target[chip, place:, :] = jnp.zeros((plan.chunk - place, LANES), F32)
        used += plan.chunk - place


def bring_encoder_body(dict_hbm, vectors_hbm, dict_ref, bias_ref, decoder_ref, gain_ref, sems):
    sources, targets = [dict_hbm], [dict_ref]
    start = 0
    for target in (bias_ref, decoder_ref, gain_ref):
        sources.append(vectors_hbm.at[:, start : start + target.shape[1]])
        targets.append(target)
        start += target.shape[1]
    for copy in copies(sources, targets, sems):
        copy.wait()


def bring_encoder(plan, dictionary, vectors):
    outputs = [
        shaped(*dictionary.shape, dtype=BF16),
        shaped(1, dictionary.shape[0]),
        shaped(1, plan.width),
        shaped(1, plan.width),
    ]
    return pl.pallas_call(
        bring_encoder_body,
        out_shape=outputs,
        in_specs=[HBM] * 2,
        out_specs=[ONCHIP] * len(outputs),
        scratch_shapes=[pltpu.SemaphoreType.DMA((len(outputs),))],
        compiler_params=pltpu.CompilerParams(
            vmem_limit_bytes=VMEM_BRING - sum(map(padded_bytes, outputs))
        ),
        cost_estimate=pl.CostEstimate(
            flops=0, bytes_accessed=dictionary.size * 4, transcendentals=0
        ),
    )(dictionary, vectors)


def encode_body(plan, own_ref, other_ref, dict_ref, bias_ref, gain_ref, inputs_ref, latents_ref, theirs_ref, both):
    assemble(plan, own_ref, other_ref, both, inputs_ref)
    preact = (
        lax.dot_general(inputs_ref[...], dict_ref[...], ACROSS, preferred_element_type=F32)
        + bias_ref[...]
    )
    latents = jnp.maximum(preact, 0.0).astype(BF16)
    latents_ref[...] = latents
    half_product(plan, [(latents, dict_ref)], 1 - lax.axis_index("hidden"), theirs_ref, gain_ref)


def encode(plan, own, other, dictionary, encoder_bias, gain):
    latents = dictionary.shape[0]
    return call(
        functools.partial(encode_body, plan),
        [
            shaped(plan.rows, plan.width, dtype=BF16),
            shaped(plan.rows, latents, dtype=BF16),
            shaped(plan.chips, plan.chunk, LANES),
        ],
        (own, other, dictionary, encoder_bias, gain),
        [both_scratch(plan)],
        flops=3 * plan.rows * plan.width * latents,
        moved=dictionary.size * 2,
    )


def decode_own_body(plan, latents_ref, dict_ref, decoder_ref, gain_ref, mine_ref):
    pairs = [(latents_ref[...], dict_ref)]
    half_product(plan, pairs, lax.axis_index("hidden"), mine_ref, gain_ref, decoder_ref)


def decode_own(plan, latents, dictionary, decoder_bias, gain):
    return call(
        functools.partial(decode_own_body, plan),
        shaped(plan.chips, plan.chunk, LANES),
        (latents, dictionary, decoder_bias, gain),
        flops=plan.rows * plan.width * dictionary.shape[0],
        moved=dictionary.size,
    )


def back_project_body(plan, own_ref, other_ref, down_ref, grad_ref, both, full):
    assemble(plan, own_ref, other_ref, both, full)
    grad_ref[...] = lax.dot_general(
        full[...], down_ref[...], ACROSS, preferred_element_type=F32
    )


def back_project(plan, own, other, down_weight):
    units = down_weight.shape[0]
    return call(
        functools.partial(back_project_body, plan),
        shaped(plan.rows, units),
        (own, other, down_weight),
        [both_scratch(plan), pltpu.VMEM((plan.rows, plan.width), BF16)],
        flops=2 * plan.rows * plan.width * units,
        moved=down_weight.size * 2,
    )


def join_half(plan, source, first, full_ref):
    for tile, chip, place, row, count in plan.pieces():
        column = pl.multiple_of(first + tile * LANES, LANES)
        full_ref[row : row + count, pl.ds(column, LANES)] = source[
            chip, place : place + count, :
        ]


def half_terms(plan, half, side, gate_ref, up_ref, gain_ref):
    span = pl.ds(pl.multiple_of(side * plan.half, LANES), plan.half)
    rebuilt = half.astype(F32) / gain_ref[:, span]
    squares = jnp.sum(rebuilt * rebuilt, axis=1, keepdims=True)
    gate = lax.dot_general(half, gate_ref[:, span], ACROSS, preferred_element_type=F32)
    up = lax.dot_general(half, up_ref[:, span], ACROSS, preferred_element_type=F32)
    return squares, gate, up


def mlp_first_body(plan, own_ref, gate_ref, up_ref, gain_ref, half_ref, squares_ref, gate_part_ref, up_part_ref):
    join_half(plan, own_ref, 0, half_ref)
    squares_ref[...], gate_part_ref[...], up_part_ref[...] = half_terms(
        plan, half_ref[...], lax.axis_index("hidden"), gate_ref, up_ref, gain_ref
    )


def mlp_first(plan, own, gate_weight, up_weight, gain):
    units = gate_weight.shape[0]
    return call(
        functools.partial(mlp_first_body, plan),
        [
            shaped(plan.rows, plan.half, dtype=BF16),
            shaped(plan.rows, 1),
            shaped(plan.rows, units),
            shaped(plan.rows, units),
        ],
        (own, gate_weight, up_weight, gain),
        flops=2 * plan.rows * plan.width * units,
        moved=gate_weight.size * 4,
    )


def mlp_body(plan, other_ref, gate_ref, up_ref, gain_ref, grad_ref, half_ref, squares_ref, gate_part_ref, up_part_ref, scaled_ref, inverse_ref, hidden_ref, gate_grad_ref, up_grad_ref, theirs_ref):
    core = lax.axis_index("hidden")
    join_half(plan, other_ref, (1 - core) * plan.half, scaled_ref)
    other_span = pl.ds(pl.multiple_of((1 - core) * plan.half, LANES), plan.half)
    own_span = pl.ds(pl.multiple_of(core * plan.half, LANES), plan.half)
    scaled_ref[:, own_span] = half_ref[...]
    squares, gate, up = half_terms(
        plan, scaled_ref[:, other_span], 1 - core, gate_ref, up_ref, gain_ref
    )
    inverse = lax.rsqrt((squares + squares_ref[...]) / plan.width + NORM_EPSILON)
    inverse_ref[...] = inverse
    gate_proj = inverse * (gate + gate_part_ref[...])
    up_proj = inverse * (up + up_part_ref[...])
    gelu_value, gelu_slope = gelu_parts(gate_proj)
    hidden_ref[...] = (gelu_value * up_proj).astype(BF16)
    hidden_grad = grad_ref[...]
    gate_grad = (hidden_grad * up_proj * gelu_slope).astype(BF16)
    up_grad = (hidden_grad * gelu_value).astype(BF16)
    gate_grad_ref[...] = gate_grad
    up_grad_ref[...] = up_grad
    half_product(plan, [(gate_grad, gate_ref), (up_grad, up_ref)], 1 - core, theirs_ref)


def mlp(plan, other, gate_weight, up_weight, gain, hidden_grad, first):
    units = gate_weight.shape[0]
    return call(
        functools.partial(mlp_body, plan),
        [
            shaped(plan.rows, plan.width, dtype=BF16),
            shaped(plan.rows, 1),
            shaped(plan.rows, units, dtype=BF16),
            shaped(plan.rows, units, dtype=BF16),
            shaped(plan.rows, units, dtype=BF16),
            shaped(plan.chips, plan.chunk, LANES),
        ],
        (other, gate_weight, up_weight, gain, hidden_grad, *first),
        flops=6 * plan.rows * plan.width * units,
        moved=gate_weight.size * 4,
    )


def mlp_own_body(plan, gate_grad_ref, up_grad_ref, gate_ref, up_ref, mine_ref):
    pairs = [(gate_grad_ref[...], gate_ref), (up_grad_ref[...], up_ref)]
    half_product(plan, pairs, lax.axis_index("hidden"), mine_ref)


def mlp_own(plan, gate_grad, up_grad, gate_weight, up_weight):
    return call(
        functools.partial(mlp_own_body, plan),
        shaped(plan.chips, plan.chunk, LANES),
        (gate_grad, up_grad, gate_weight, up_weight),
        flops=2 * plan.rows * plan.width * gate_weight.shape[0],
        moved=gate_weight.size * 2,
    )


def project_body(plan, hidden_ref, down_ref, mine_ref, theirs_ref, both):
    core = lax.axis_index("hidden")
    terms = jnp.dot(hidden_ref[...], down_ref[...], preferred_element_type=F32)
    for chip in range(plan.chips):
        for side in range(plan.cores):
            start = (chip * plan.cores + side) * plan.own
            main, tail = pack_block(plan, terms[:, start : start + plan.own])
            both[side, chip, : plan.rows, :] = main
            both[side, chip, plan.rows :, :] = tail
    mine_ref[...] = both[core]
    theirs_ref[...] = both[1 - core]


def project(plan, hidden, down_weight):
    units = down_weight.shape[0]
    shape = (plan.chips, plan.packed, LANES)
    return call(
        functools.partial(project_body, plan),
        [shaped(*shape)] * 2,
        (hidden, down_weight),
        [both_scratch(plan, F32)],
        flops=2 * plan.rows * plan.width * units,
        moved=down_weight.size * 2,
    )


def add_pair_body(plan, mine_ref, theirs_ref, kept_ref, sent_ref):
    me = lax.axis_index("latent")
    for place, column in enumerate(plan.columns):
        kept, sent = me ^ column, me ^ column ^ 1
        kept_ref[place] = mine_ref[kept] + theirs_ref[kept]
        sent_ref[place] = (mine_ref[sent] + theirs_ref[sent]).astype(BF16)


def add_pair(plan, mine, theirs):
    count, dims = len(plan.columns), mine.shape[1:]
    return call(
        functools.partial(add_pair_body, plan),
        [shaped(count, *dims), shaped(count, *dims, dtype=BF16)],
        (mine, theirs),
        moved=mine.size * 10,
    )


def split_pair_body(plan, mine_ref, theirs_ref, own_ref, *sent_refs):
    me = lax.axis_index("latent")
    own_ref[0] = mine_ref[me] + theirs_ref[me]
    for partner, sent_ref in zip(plan.partners, sent_refs):
        sent_ref[0] = (mine_ref[me ^ partner] + theirs_ref[me ^ partner]).astype(BF16)


def split_pair(plan, mine, theirs):
    dims = mine.shape[1:]
    own, *sent = call(
        functools.partial(split_pair_body, plan),
        [shaped(1, *dims)] + [shaped(1, *dims, dtype=BF16)] * len(plan.partners),
        (mine, theirs),
        moved=mine.size * 10,
    )
    return own, sent


def total_of(refs):
    total = refs[0][0]
    for ref in refs[1:]:
        total = total + ref[0].astype(F32)
    return total


def add_chunks_body(*refs):
    refs[-1][0] = total_of(refs[:-1]).astype(BF16)


def add_chunks(plan, own, got):
    return call(
        add_chunks_body,
        shaped(*own.shape, dtype=BF16),
        (own, *got),
        moved=own.size * 20,
    )


def add_with_output_body(plan, count, *refs):
    total = total_of(refs[:count]).astype(BF16)
    kept_ref, crossed_ref, block_ref, own_ref = refs[count : count + 4]
    block_ref[0] = total
    own_ref[0] = kept_ref[0] + crossed_ref[0].astype(F32)
    for place, both_ref in enumerate(refs[count + 4 :], 1):
        both_ref[0, : plan.chunk, :] = total
        both_ref[0, plan.chunk :, :] = (
            kept_ref[place] + crossed_ref[place].astype(F32)
        ).astype(BF16)


def add_with_output(plan, own, got, kept, crossed):
    both = shaped(1, plan.chunk + plan.packed, LANES, dtype=BF16)
    block, out_own, *messages = call(
        functools.partial(add_with_output_body, plan, 1 + len(got)),
        [shaped(*own.shape, dtype=BF16), shaped(1, plan.packed, LANES)]
        + [both] * (len(plan.columns) - 1),
        (own, *got, kept, crossed),
        moved=own.size * 30,
    )
    return block, out_own, messages


def line_up_body(plan, rows, *refs):
    me = lax.axis_index("latent")
    for partner, ref in zip([0] + plan.partners, refs):
        refs[-1][me ^ partner] = ref[0, :rows, :]


def line_up(plan, block, got):
    rows = block.shape[1]
    return call(
        functools.partial(line_up_body, plan, rows),
        shaped(plan.chips, rows, LANES, dtype=BF16),
        (block, *got),
        moved=block.size * 40,
    )


def stack_second_body(plan, rows, *refs):
    for place, ref in enumerate(refs[:-1]):
        refs[-1][place] = ref[0, rows:, :]


def stack_second(plan, rows, messages):
    return call(
        functools.partial(stack_second_body, plan, rows),
        shaped(len(messages), messages[0].shape[1] - rows, LANES, dtype=BF16),
        messages,
        moved=messages[0].size * 16,
    )


def line_up_sides_body(plan, stack_ref, crossed_ref, full_ref):
    me = lax.axis_index("latent")
    for place, column in enumerate(plan.columns):
        full_ref[me ^ column] = stack_ref[place]
        full_ref[me ^ column ^ 1] = crossed_ref[place]


def line_up_sides(plan, stack, crossed):
    return call(
        functools.partial(line_up_sides_body, plan),
        shaped(plan.chips, *stack.shape[1:], dtype=BF16),
        (stack, crossed),
        moved=stack.size * 8,
    )


def finish_output_body(plan, own_ref, *refs):
    total = own_ref[0]
    for ref in refs[:-1]:
        total = total + ref[0, plan.chunk :, :].astype(F32)
    refs[-1][...] = unpack_block(plan, total).astype(BF16)


def finish_output(plan, own, messages):
    return call(
        functools.partial(finish_output_body, plan),
        shaped(plan.rows, plan.own, dtype=BF16),
        (own, *messages),
        moved=own.size * 8,
    )


def dictionary_body(plan, pieces, own_ref, other_ref, gain_ref, inverse_ref, scaled_ref, inputs_ref, latents_ref, dict_ref, out_hbm, full, out_ref, out_sems):
    core = lax.axis_index("hidden")
    join_half(plan, own_ref, core * plan.half, full)
    join_half(plan, other_ref, (1 - core) * plan.half, full)
    grad = full[...].astype(F32)
    gain = gain_ref[...]
    scaled_rebuilt = scaled_ref[...].astype(F32)
    rebuilt = scaled_rebuilt / gain
    inverse = inverse_ref[...]
    inner_row = jnp.sum(grad * scaled_rebuilt, axis=1, keepdims=True)
    inverse_cube = inverse * inverse * inverse
    inputs = inputs_ref[...]
    rebuilt_grad = (
        inverse * (grad * gain)
        - (inverse_cube * (inner_row / plan.width)) * rebuilt
        + (rebuilt - inputs.astype(F32))
    ).astype(BF16)
    latents = latents_ref[...]
    latent_grad = lax.dot_general(
        rebuilt_grad, dict_ref[...], ACROSS, preferred_element_type=F32
    )
    preact_grad = jnp.where(latents.astype(F32) > 0.0, latent_grad, 0.0).astype(BF16)
    left = jnp.concatenate([latents, preact_grad], axis=0)
    right = jnp.concatenate([rebuilt_grad, inputs], axis=0)
    size = plan.width // pieces
    writes = []
    for piece in range(pieces):
        span = slice(piece * size, (piece + 1) * size)
        out_ref[:, span] = lax.dot_general(
            left, right[:, span], DOWNWARD, preferred_element_type=F32
        ).astype(BF16)
        one = pltpu.make_async_copy(
            out_ref.at[:, span], out_hbm.at[:, span], out_sems.at[piece]
        )
        one.start()
        writes.append(one)
    for one in writes:
        one.wait()


def dictionary_step(plan, own, other, gain, inverse, scaled, inputs, latents, dictionary):
    units = dictionary.shape[0]
    pieces = plan.cores
    return call(
        functools.partial(dictionary_body, plan, pieces),
        shaped(*dictionary.shape, dtype=BF16),
        (own, other, gain, inverse, scaled, inputs, latents, dictionary),
        [
            pltpu.VMEM((plan.rows, plan.width), BF16),
            pltpu.VMEM(dictionary.shape, BF16),
            pltpu.SemaphoreType.DMA((pieces,)),
        ],
        out_specs=HBM,
        flops=6 * plan.rows * plan.width * units,
        moved=dictionary.size * 4,
    )


def swap(value):
    size = lax.axis_size("hidden")
    return lax.ppermute(value, "hidden", [(i, (i + 1) % size) for i in range(size)])


def partner_swap(value, bits):
    size = lax.axis_size("latent")
    return lax.ppermute(value, "latent", [(i, i ^ bits) for i in range(size)])


def cross(value):
    return partner_swap(value, 1)


def send_all(plan, values):
    return [partner_swap(one, partner) for one, partner in zip(values, plan.partners)]


def send_blocks(plan, block, messages):
    by_column = dict(zip(plan.columns[1:], messages))
    return send_all(plan, [by_column.get(partner, block) for partner in plan.partners])


def of_column(plan, got):
    by_partner = dict(zip(plan.partners, got))
    return [by_partner[column] for column in plan.columns[1:]]


def tie(*values):
    return lax.optimization_barrier(values)


def per_device(
    input_codes,
    cotangent_codes,
    dictionary,
    encoder_bias,
    decoder_bias,
    norm_gain,
    gate_weight,
    up_weight,
    down_weight,
):
    plan = Plan(
        lax.axis_size("latent"), lax.axis_size("hidden"), input_codes.shape[0], input_codes.shape[1]
    )
    if not plan.fits():
        return per_device_plain(
            input_codes,
            cotangent_codes,
            dictionary,
            encoder_bias,
            decoder_bias,
            norm_gain,
            gate_weight,
            up_weight,
            down_weight,
        )
    fan = len(plan.columns) - 1
    block, both = pack_codes(plan, input_codes, cotangent_codes)
    got = send_blocks(plan, block, [both] * fan)
    vectors = jnp.concatenate([encoder_bias, decoder_bias, norm_gain]).reshape(1, -1)
    got, vectors, late_dictionary = tie(got, vectors, dictionary)
    inputs_own = line_up(plan, block, got)
    cotangent = stack_second(plan, plan.packed, [both] + of_column(plan, got))
    brought, bias, decoder, gain = bring_encoder(plan, late_dictionary, vectors)
    inputs, latents, theirs = encode(plan, inputs_own, swap(inputs_own), brought, bias, gain)
    theirs = swap(theirs)
    mine = decode_own(plan, latents, brought, decoder, gain)
    own, sent = split_pair(plan, mine, theirs)
    own, sent, cotangent = tie(own, sent, cotangent)
    got = send_all(plan, sent)
    cotangent_own = line_up_sides(plan, cotangent, cross(cotangent))
    block = add_chunks(plan, own, got)
    block, cotangent_own = tie(block, cotangent_own)
    got = send_all(plan, [block] * len(plan.partners))
    hidden_grad = back_project(plan, cotangent_own, swap(cotangent_own), down_weight)
    scaled_own = line_up(plan, block, got)
    first = mlp_first(plan, scaled_own, gate_weight, up_weight, gain)
    scaled, inverse, hidden, gate_grad, up_grad, theirs = mlp(
        plan, swap(scaled_own), gate_weight, up_weight, gain, hidden_grad, first
    )
    theirs = swap(theirs)
    mine = mlp_own(plan, gate_grad, up_grad, gate_weight, up_weight)
    out_mine, out_theirs = project(plan, hidden, down_weight)
    own, sent = split_pair(plan, mine, theirs)
    got = send_all(plan, sent)
    out_kept, out_sent = add_pair(plan, out_mine, swap(out_theirs))
    out_crossed = cross(out_sent)
    block, out_own, messages = add_with_output(plan, own, got, out_kept, out_crossed)
    got = send_blocks(plan, block, messages)
    grad_own = line_up(plan, block, got)
    block_output = finish_output(plan, out_own, of_column(plan, got))
    dictionary_grad = dictionary_step(
        plan, grad_own, swap(grad_own), gain, inverse, scaled, inputs, latents, dictionary
    )
    return (block_output, dictionary_grad)


def per_device_plain(
    input_codes,
    cotangent_codes,
    dictionary,
    encoder_bias,
    decoder_bias,
    norm_gain,
    gate_weight,
    up_weight,
    down_weight,
):
    own_width = input_codes.shape[1]
    model_width = own_width * lax.axis_size(("latent", "hidden"))
    cotangent_local = (cotangent_codes.astype(jnp.float32) * CODE_STEP).astype(jnp.bfloat16)
    inputs_local = (input_codes.astype(jnp.float32) * CODE_STEP).astype(jnp.bfloat16)
    inputs = lax.all_gather(inputs_local, ("latent", "hidden"), axis=1, tiled=True)
    preact = (
        lax.dot_general(inputs, dictionary, ACROSS, preferred_element_type=jnp.float32)
        + encoder_bias
    )
    latents = jnp.maximum(preact, 0.0).astype(jnp.bfloat16)
    partial_value = jnp.dot(latents, dictionary, preferred_element_type=jnp.float32)
    rebuilt = lax.psum(partial_value, ("latent", "hidden")) + decoder_bias
    inverse = lax.rsqrt(
        jnp.sum(rebuilt * rebuilt, axis=1, keepdims=True) / model_width + NORM_EPSILON
    )
    normed = (rebuilt * inverse * norm_gain).astype(jnp.bfloat16)
    target = inputs.astype(jnp.float32)
    gate_proj = lax.dot_general(normed, gate_weight, ACROSS, preferred_element_type=jnp.float32)
    up_proj = lax.dot_general(normed, up_weight, ACROSS, preferred_element_type=jnp.float32)
    gelu_value, gelu_slope = gelu_parts(gate_proj)
    hidden = (gelu_value * up_proj).astype(jnp.bfloat16)
    output_terms = jnp.dot(hidden, down_weight, preferred_element_type=jnp.float32)
    block_output = lax.psum_scatter(
        output_terms, ("latent", "hidden"), scatter_dimension=1, tiled=True
    ).astype(jnp.bfloat16)
    hidden_grad = lax.dot_general(
        lax.all_gather(cotangent_local, ("latent", "hidden"), axis=1, tiled=True),
        down_weight,
        ACROSS,
        preferred_element_type=jnp.float32,
    )
    gate_grad = (hidden_grad * up_proj * gelu_slope).astype(jnp.bfloat16)
    up_grad = (hidden_grad * gelu_value).astype(jnp.bfloat16)
    partial_grad = jnp.dot(gate_grad, gate_weight, preferred_element_type=jnp.float32) + jnp.dot(
        up_grad, up_weight, preferred_element_type=jnp.float32
    )
    scaled = lax.psum(partial_grad, ("latent", "hidden")) * norm_gain
    inner_row = jnp.sum(scaled * rebuilt, axis=1, keepdims=True)
    inverse_cube = inverse * inverse * inverse
    rebuilt_grad = (
        inverse * scaled - inverse_cube * rebuilt * (inner_row / model_width) + (rebuilt - target)
    ).astype(jnp.bfloat16)
    latent_grad = lax.dot_general(
        rebuilt_grad, dictionary, ACROSS, preferred_element_type=jnp.float32
    )
    preact_grad = jnp.where(preact > 0.0, latent_grad, 0.0).astype(jnp.bfloat16)
    dictionary_grad = lax.dot_general(
        latents, rebuilt_grad, DOWNWARD, preferred_element_type=jnp.float32
    ) + lax.dot_general(preact_grad, inputs, DOWNWARD, preferred_element_type=jnp.float32)
    return (block_output, dictionary_grad.astype(jnp.bfloat16))


def solution(mesh):
    in_specs = (
        P("groups", ("latent", "hidden")),
        P("groups", ("latent", "hidden")),
        P(("latent", "hidden"), None),
        P(("latent", "hidden")),
        P(),
        P(),
        P(("latent", "hidden"), None),
        P(("latent", "hidden"), None),
        P(("latent", "hidden"), None),
    )
    out_specs = (P("groups", ("latent", "hidden")), P(("latent", "hidden"), "groups"))
    return jax.shard_map(
        per_device, mesh=mesh, in_specs=in_specs, out_specs=out_specs, check_vma=False
    )
```

```python
import functools
import math

import jax
import jax.numpy as jnp
from jax import lax
from jax.experimental import pallas as pl
from jax.experimental.pallas import tpu as pltpu
from jax.sharding import PartitionSpec as P

CODE_STEP = 2.0 ** (-6)
NORM_EPSILON = 1e-06
GELU_ROOT = 0.7978845608028654
GELU_CUBIC = 0.044715
ACROSS = (((1,), (1,)), ((), ()))
DOWNWARD = (((0,), (0,)), ((), ()))
LANES = 128
ROW_TILE = 16
DIRECT_LIMIT = 16
VMEM_BYTES = 24 * 1024 * 1024
VMEM_BRING = 53 * 1024 * 1024
F32 = jnp.float32
BF16 = jnp.bfloat16


def gelu_parts(values):
    argument = GELU_ROOT * (values + GELU_CUBIC * values * values * values)
    tanh_value = jnp.tanh(argument)
    result = 0.5 * values * (1.0 + tanh_value)
    derivative = 0.5 * (1.0 + tanh_value) + 0.5 * values * (
        1.0 - tanh_value * tanh_value
    ) * GELU_ROOT * (1.0 + 3.0 * GELU_CUBIC * values * values)
    return (result, derivative)


def up_to(value, unit):
    return -(-value // unit) * unit


def chips_fit(chips):
    return 2 <= chips <= DIRECT_LIMIT and chips & (chips - 1) == 0


class Plan:
    def __init__(self, chips, cores, rows, own):
        self.chips, self.cores, self.rows, self.own = chips, cores, rows, own
        self.width = own * chips * cores
        self.half = self.width // cores
        self.tiles = self.half // LANES
        self.chunk = up_to(-(-self.tiles * rows // chips), ROW_TILE)
        self.flat = self.chunk * chips
        self.tail = own - LANES
        if self.tail > 0:
            self.fold_rows = min(
                size
                for size in range(ROW_TILE, rows + ROW_TILE, ROW_TILE)
                if -(-rows // size) * self.tail <= LANES
            )
            self.packed = rows + self.fold_rows
        self.columns = list(range(0, chips, 2))

    def pieces(self):
        for tile in range(self.tiles):
            row = 0
            while row < self.rows:
                chip, place = divmod(tile * self.rows + row, self.chunk)
                count = min(self.rows - row, self.chunk - place)
                yield tile, chip, place, row, count
                row += count

    def fits(self):
        return (
            self.cores == 2
            and chips_fit(self.chips)
            and self.rows % ROW_TILE == 0
            and self.half % LANES == 0
            and 0 < self.tail < LANES
        )


HBM = pl.BlockSpec(memory_space=pltpu.HBM)
ONCHIP = pl.BlockSpec(memory_space=pltpu.VMEM)


def shaped(*dims, dtype=F32):
    return jax.ShapeDtypeStruct(dims, dtype)


HBM = pl.BlockSpec(memory_space=pltpu.HBM)
ONCHIP = pl.BlockSpec(memory_space=pltpu.VMEM)


def shaped(*dims, dtype=F32):
    return jax.ShapeDtypeStruct(dims, dtype)


def call(body, out_shapes, operands, scratch=(), out_specs=None, flops=0, moved=0):
    return pl.pallas_call(
        body,
        out_shape=out_shapes,
        in_specs=[ONCHIP] * len(operands),
        out_specs=jax.tree.map(lambda _: ONCHIP, out_shapes) if out_specs is None else out_specs,
        scratch_shapes=list(scratch),
        compiler_params=pltpu.CompilerParams(vmem_limit_bytes=VMEM_BYTES),
        cost_estimate=pl.CostEstimate(flops=flops, bytes_accessed=moved, transcendentals=0),
    )(*operands)


def padded_bytes(array):
    *lead, rows, columns = array.shape
    item = jnp.dtype(array.dtype).itemsize
    return math.prod(lead) * up_to(rows, ROW_TILE) * up_to(columns, LANES) * item


def copies(sources, targets, sems):
    started = []
    for index, (source, target) in enumerate(zip(sources, targets)):
        one = pltpu.make_async_copy(source, target, sems.at[index])
        one.start()
        started.append(one)
    return started


def pack_block(plan, block):
    tail = block[:, LANES:]
    folded = []
    for start in range(0, plan.rows, plan.fold_rows):
        piece = tail[start : min(start + plan.fold_rows, plan.rows), :]
        short = plan.fold_rows - piece.shape[0]
        if short:
            piece = jnp.concatenate([piece, jnp.zeros((short, plan.tail), block.dtype)], axis=0)
        folded.append(piece)
    fill = LANES - len(folded) * plan.tail
    if fill:
        folded.append(jnp.zeros((plan.fold_rows, fill), block.dtype))
    return block[:, :LANES], jnp.concatenate(folded, axis=1)


def unpack_block(plan, packed):
    pieces = []
    for fold, start in enumerate(range(0, plan.rows, plan.fold_rows)):
        count = min(plan.fold_rows, plan.rows - start)
        pieces.append(
            packed[plan.rows : plan.rows + count, fold * plan.tail : (fold + 1) * plan.tail]
        )
    return jnp.concatenate([packed[: plan.rows, :], jnp.concatenate(pieces, axis=0)], axis=1)


def pack_codes_body(plan, *refs):
    for codes_ref, out_ref in zip(refs[:2], refs[2:]):
        main, tail = pack_block(plan, codes_ref[...].astype(F32) * CODE_STEP)
        out_ref[0, : plan.rows, :] = main.astype(BF16)
        out_ref[0, plan.rows :, :] = tail.astype(BF16)


def pack_codes(plan, input_codes, cotangent_codes):
    return call(
        functools.partial(pack_codes_body, plan),
        [shaped(1, plan.packed, LANES, dtype=BF16)] * 2,
        (input_codes, cotangent_codes),
        moved=plan.rows * plan.own * 8,
    )


def assemble(plan, own_refs, other_refs, both, full_ref):
    core, me = lax.axis_index("hidden"), lax.axis_index("latent")
    for side, refs in ((core, own_refs), (1 - core, other_refs)):
        for across, ref in enumerate(refs):
            for place, column in enumerate(plan.columns):
                both[side, me ^ column ^ across] = ref[place]
    for chip in range(plan.chips):
        for side in range(plan.cores):
            column = (chip * plan.cores + side) * plan.own
            block = unpack_block(plan, both[side, chip].astype(F32))
            full_ref[:, column : column + plan.own] = block.astype(BF16)


def both_scratch(plan, dtype=BF16):
    return pltpu.VMEM((plan.cores, plan.chips, plan.packed, LANES), dtype)


def chunk_scratch(plan):
    return pltpu.VMEM((plan.chips, plan.chunk, LANES), F32)


def side_shapes(plan, dtype=F32):
    return [shaped(len(plan.columns), plan.chunk, LANES, dtype=dtype)] * 2


def half_product(plan, pairs, side, kept_ref, sent_ref, target, gain_ref=None, bias_ref=None):
    span = pl.ds(pl.multiple_of(side * plan.half, LANES), plan.half)
    total = None
    for left, right_ref in pairs:
        term = jnp.dot(left, right_ref[:, span], preferred_element_type=F32)
        total = term if total is None else total + term
    if bias_ref is not None:
        total = total + bias_ref[:, span] * jnp.where(lax.axis_index("latent") == 0, 1.0, 0.0)
    if gain_ref is not None:
        total = total * gain_ref[:, span]
    for tile, chip, place, row, count in plan.pieces():
        target[chip, place : place + count, :] = total[
            row : row + count, tile * LANES : (tile + 1) * LANES
        ]
    used = plan.tiles * plan.rows
    while used < plan.flat:
        chip, place = divmod(used, plan.chunk)
        target[chip, place:, :] = jnp.zeros((plan.chunk - place, LANES), F32)
        used += plan.chunk - place
    me = lax.axis_index("latent")
    for place, column in enumerate(plan.columns):
        kept_ref[place] = target[me ^ column]
        sent_ref[place] = target[me ^ column ^ 1]


def bring_encoder_body(dict_hbm, vectors_hbm, dict_ref, bias_ref, decoder_ref, gain_ref, sems):
    sources, targets = [dict_hbm], [dict_ref]
    start = 0
    for target in (bias_ref, decoder_ref, gain_ref):
        sources.append(vectors_hbm.at[:, start : start + target.shape[1]])
        targets.append(target)
        start += target.shape[1]
    for copy in copies(sources, targets, sems):
        copy.wait()


def bring_encoder(plan, dictionary, vectors):
    outputs = [
        shaped(*dictionary.shape, dtype=BF16),
        shaped(1, dictionary.shape[0]),
        shaped(1, plan.width),
        shaped(1, plan.width),
    ]
    return pl.pallas_call(
        bring_encoder_body,
        out_shape=outputs,
        in_specs=[HBM] * 2,
        out_specs=[ONCHIP] * len(outputs),
        scratch_shapes=[pltpu.SemaphoreType.DMA((len(outputs),))],
        compiler_params=pltpu.CompilerParams(
            vmem_limit_bytes=VMEM_BRING - sum(map(padded_bytes, outputs))
        ),
        cost_estimate=pl.CostEstimate(
            flops=0, bytes_accessed=dictionary.size * 4, transcendentals=0
        ),
    )(dictionary, vectors)


def encode_body(plan, *refs):
    own, other, (dict_ref, bias_ref, gain_ref) = refs[:2], refs[2:4], refs[4:7]
    inputs_ref, latents_ref, kept_ref, sent_ref, both, target = refs[7:]
    assemble(plan, own, other, both, inputs_ref)
    preact = (
        lax.dot_general(inputs_ref[...], dict_ref[...], ACROSS, preferred_element_type=F32)
        + bias_ref[...]
    )
    latents = jnp.maximum(preact, 0.0).astype(BF16)
    latents_ref[...] = latents
    theirs = 1 - lax.axis_index("hidden")
    half_product(plan, [(latents, dict_ref)], theirs, kept_ref, sent_ref, target, gain_ref)


def encode(plan, own, other, dictionary, encoder_bias, gain):
    latents = dictionary.shape[0]
    return call(
        functools.partial(encode_body, plan),
        [
            shaped(plan.rows, plan.width, dtype=BF16),
            shaped(plan.rows, latents, dtype=BF16),
            *side_shapes(plan),
        ],
        (*own, *other, dictionary, encoder_bias, gain),
        [both_scratch(plan), chunk_scratch(plan)],
        flops=3 * plan.rows * plan.width * latents,
        moved=dictionary.size * 2,
    )


def decode_own_body(plan, latents_ref, dict_ref, decoder_ref, gain_ref, kept_ref, sent_ref, target):
    pairs = [(latents_ref[...], dict_ref)]
    mine = lax.axis_index("hidden")
    half_product(plan, pairs, mine, kept_ref, sent_ref, target, gain_ref, decoder_ref)


def decode_own(plan, latents, dictionary, decoder_bias, gain):
    return call(
        functools.partial(decode_own_body, plan),
        side_shapes(plan),
        (latents, dictionary, decoder_bias, gain),
        [chunk_scratch(plan)],
        flops=plan.rows * plan.width * dictionary.shape[0],
        moved=dictionary.size,
    )


def back_project_body(plan, *refs):
    own, other, (down_ref, grad_ref, both, full) = refs[:2], refs[2:4], refs[4:]
    assemble(plan, own, other, both, full)
    grad_ref[...] = lax.dot_general(
        full[...], down_ref[...], ACROSS, preferred_element_type=F32
    )


def back_project(plan, own, other, down_weight):
    units = down_weight.shape[0]
    return call(
        functools.partial(back_project_body, plan),
        shaped(plan.rows, units),
        (*own, *other, down_weight),
        [both_scratch(plan), pltpu.VMEM((plan.rows, plan.width), BF16)],
        flops=2 * plan.rows * plan.width * units,
        moved=down_weight.size * 2,
    )


def join_half(plan, source, first, full_ref):
    for tile, chip, place, row, count in plan.pieces():
        column = pl.multiple_of(first + tile * LANES, LANES)
        full_ref[row : row + count, pl.ds(column, LANES)] = source[
            chip, place : place + count, :
        ]


def half_terms(plan, half, side, gate_ref, up_ref, gain_ref):
    span = pl.ds(pl.multiple_of(side * plan.half, LANES), plan.half)
    rebuilt = half.astype(F32) / gain_ref[:, span]
    squares = jnp.sum(rebuilt * rebuilt, axis=1, keepdims=True)
    gate = lax.dot_general(half, gate_ref[:, span], ACROSS, preferred_element_type=F32)
    up = lax.dot_general(half, up_ref[:, span], ACROSS, preferred_element_type=F32)
    return squares, gate, up


def mlp_first_body(plan, own_ref, gate_ref, up_ref, gain_ref, half_ref, squares_ref, gate_part_ref, up_part_ref):
    join_half(plan, own_ref, 0, half_ref)
    squares_ref[...], gate_part_ref[...], up_part_ref[...] = half_terms(
        plan, half_ref[...], lax.axis_index("hidden"), gate_ref, up_ref, gain_ref
    )


def mlp_first(plan, own, gate_weight, up_weight, gain):
    units = gate_weight.shape[0]
    return call(
        functools.partial(mlp_first_body, plan),
        [
            shaped(plan.rows, plan.half, dtype=BF16),
            shaped(plan.rows, 1),
            shaped(plan.rows, units),
            shaped(plan.rows, units),
        ],
        (own, gate_weight, up_weight, gain),
        flops=2 * plan.rows * plan.width * units,
        moved=gate_weight.size * 4,
    )


def mlp_body(plan, other_ref, gate_ref, up_ref, gain_ref, grad_ref, half_ref, squares_ref, gate_part_ref, up_part_ref, scaled_ref, inverse_ref, hidden_ref, gate_grad_ref, up_grad_ref, kept_ref, sent_ref, target):
    core = lax.axis_index("hidden")
    join_half(plan, other_ref, (1 - core) * plan.half, scaled_ref)
    other_span = pl.ds(pl.multiple_of((1 - core) * plan.half, LANES), plan.half)
    own_span = pl.ds(pl.multiple_of(core * plan.half, LANES), plan.half)
    scaled_ref[:, own_span] = half_ref[...]
    squares, gate, up = half_terms(
        plan, scaled_ref[:, other_span], 1 - core, gate_ref, up_ref, gain_ref
    )
    inverse = lax.rsqrt((squares + squares_ref[...]) / plan.width + NORM_EPSILON)
    inverse_ref[...] = inverse
    gate_proj = inverse * (gate + gate_part_ref[...])
    up_proj = inverse * (up + up_part_ref[...])
    gelu_value, gelu_slope = gelu_parts(gate_proj)
    hidden_ref[...] = (gelu_value * up_proj).astype(BF16)
    hidden_grad = grad_ref[...]
    gate_grad = (hidden_grad * up_proj * gelu_slope).astype(BF16)
    up_grad = (hidden_grad * gelu_value).astype(BF16)
    gate_grad_ref[...] = gate_grad
    up_grad_ref[...] = up_grad
    pairs = [(gate_grad, gate_ref), (up_grad, up_ref)]
    half_product(plan, pairs, 1 - core, kept_ref, sent_ref, target)


def mlp(plan, other, gate_weight, up_weight, gain, hidden_grad, first):
    units = gate_weight.shape[0]
    return call(
        functools.partial(mlp_body, plan),
        [
            shaped(plan.rows, plan.width, dtype=BF16),
            shaped(plan.rows, 1),
            shaped(plan.rows, units, dtype=BF16),
            shaped(plan.rows, units, dtype=BF16),
            shaped(plan.rows, units, dtype=BF16),
            *side_shapes(plan),
        ],
        (other, gate_weight, up_weight, gain, hidden_grad, *first),
        [chunk_scratch(plan)],
        flops=6 * plan.rows * plan.width * units,
        moved=gate_weight.size * 4,
    )


def mlp_own_body(plan, gate_grad_ref, up_grad_ref, gate_ref, up_ref, kept_ref, sent_ref, target):
    pairs = [(gate_grad_ref[...], gate_ref), (up_grad_ref[...], up_ref)]
    half_product(plan, pairs, lax.axis_index("hidden"), kept_ref, sent_ref, target)


def mlp_own(plan, gate_grad, up_grad, gate_weight, up_weight):
    return call(
        functools.partial(mlp_own_body, plan),
        side_shapes(plan),
        (gate_grad, up_grad, gate_weight, up_weight),
        [chunk_scratch(plan)],
        flops=2 * plan.rows * plan.width * gate_weight.shape[0],
        moved=gate_weight.size * 2,
    )


def project_body(plan, hidden_ref, down_ref, mine_ref, theirs_ref, both):
    core = lax.axis_index("hidden")
    terms = jnp.dot(hidden_ref[...], down_ref[...], preferred_element_type=F32)
    for chip in range(plan.chips):
        for side in range(plan.cores):
            start = (chip * plan.cores + side) * plan.own
            main, tail = pack_block(plan, terms[:, start : start + plan.own])
            both[side, chip, : plan.rows, :] = main
            both[side, chip, plan.rows :, :] = tail
    mine_ref[...] = both[core]
    theirs_ref[...] = both[1 - core]


def project(plan, hidden, down_weight):
    units = down_weight.shape[0]
    shape = (plan.chips, plan.packed, LANES)
    return call(
        functools.partial(project_body, plan),
        [shaped(*shape)] * 2,
        (hidden, down_weight),
        [both_scratch(plan, F32)],
        flops=2 * plan.rows * plan.width * units,
        moved=down_weight.size * 2,
    )


def add_pair_body(plan, mine_ref, theirs_ref, kept_ref, sent_ref):
    me = lax.axis_index("latent")
    for place, column in enumerate(plan.columns):
        kept, sent = me ^ column, me ^ column ^ 1
        kept_ref[place] = mine_ref[kept] + theirs_ref[kept]
        sent_ref[place] = (mine_ref[sent] + theirs_ref[sent]).astype(BF16)


def add_pair(plan, mine, theirs):
    count, dims = len(plan.columns), mine.shape[1:]
    return call(
        functools.partial(add_pair_body, plan),
        [shaped(count, *dims), shaped(count, *dims, dtype=BF16)],
        (mine, theirs),
        moved=mine.size * 10,
    )


def add_sent_body(mine_ref, theirs_ref, sent_ref):
    sent_ref[...] = (mine_ref[...] + theirs_ref[...]).astype(BF16)


def add_sent(plan, mine, theirs):
    return call(
        add_sent_body, shaped(*mine.shape, dtype=BF16), (mine, theirs), moved=mine.size * 10
    )


def add_across_body(plan, mine_ref, theirs_ref, got_ref, own_ref, *sent_refs):
    for place, out_ref in enumerate((own_ref, *sent_refs)):
        total = mine_ref[place] + theirs_ref[place] + got_ref[place].astype(F32)
        out_ref[0] = total.astype(out_ref.dtype)


def add_across(plan, mine, theirs, got):
    dims = mine.shape[1:]
    own, *sent = call(
        functools.partial(add_across_body, plan),
        [shaped(1, *dims)] + [shaped(1, *dims, dtype=BF16)] * (len(plan.columns) - 1),
        (mine, theirs, got),
        moved=mine.size * 10,
    )
    return own, sent


def total_of(refs):
    total = refs[0][0]
    for ref in refs[1:]:
        total = total + ref[0].astype(F32)
    return total


def add_column_body(*refs):
    refs[-1][0] = total_of(refs[:-1]).astype(BF16)


def add_column(plan, own, got):
    return call(
        add_column_body, shaped(*own.shape, dtype=BF16), (own, *got), moved=own.size * 8
    )


def add_with_output_body(plan, count, *refs):
    total = total_of(refs[:count]).astype(BF16)
    kept_ref, crossed_ref, block_ref, own_ref = refs[count : count + 4]
    block_ref[0] = total
    own_ref[0] = kept_ref[0] + crossed_ref[0].astype(F32)
    for place, both_ref in enumerate(refs[count + 4 :], 1):
        both_ref[0, : plan.chunk, :] = total
        both_ref[0, plan.chunk :, :] = (
            kept_ref[place] + crossed_ref[place].astype(F32)
        ).astype(BF16)


def add_with_output(plan, own, got, kept, crossed):
    both = shaped(1, plan.chunk + plan.packed, LANES, dtype=BF16)
    block, out_own, *messages = call(
        functools.partial(add_with_output_body, plan, 1 + len(got)),
        [shaped(*own.shape, dtype=BF16), shaped(1, plan.packed, LANES)]
        + [both] * (len(plan.columns) - 1),
        (own, *got, kept, crossed),
        moved=own.size * 30,
    )
    return block, out_own, messages


def stack_body(*refs):
    rows = refs[-1].shape[1]
    for place, ref in enumerate(refs[:-1]):
        refs[-1][place] = ref[0, :rows, :]


def stack_up(plan, block, got):
    return call(
        stack_body,
        shaped(1 + len(got), *block.shape[1:], dtype=BF16),
        (block, *got),
        moved=block.size * 16,
    )


def line_up_body(plan, stack_ref, crossed_ref, full_ref):
    me = lax.axis_index("latent")
    for place, column in enumerate(plan.columns):
        full_ref[me ^ column] = stack_ref[place]
        full_ref[me ^ column ^ 1] = crossed_ref[place]


def line_up(plan, stack, crossed):
    return call(
        functools.partial(line_up_body, plan),
        shaped(plan.chips, *stack.shape[1:], dtype=BF16),
        (stack, crossed),
        moved=stack.size * 8,
    )


def finish_output_body(plan, own_ref, *refs):
    total = own_ref[0]
    for ref in refs[:-1]:
        total = total + ref[0, plan.chunk :, :].astype(F32)
    refs[-1][...] = unpack_block(plan, total).astype(BF16)


def finish_output(plan, own, messages):
    return call(
        functools.partial(finish_output_body, plan),
        shaped(plan.rows, plan.own, dtype=BF16),
        (own, *messages),
        moved=own.size * 8,
    )


def dictionary_body(plan, pieces, own_ref, other_ref, gain_ref, inverse_ref, scaled_ref, inputs_ref, latents_ref, dict_ref, out_hbm, full, out_ref, out_sems):
    core = lax.axis_index("hidden")
    join_half(plan, own_ref, core * plan.half, full)
    join_half(plan, other_ref, (1 - core) * plan.half, full)
    grad = full[...].astype(F32)
    gain = gain_ref[...]
    scaled_rebuilt = scaled_ref[...].astype(F32)
    rebuilt = scaled_rebuilt / gain
    inverse = inverse_ref[...]
    inner_row = jnp.sum(grad * scaled_rebuilt, axis=1, keepdims=True)
    inverse_cube = inverse * inverse * inverse
    inputs = inputs_ref[...]
    rebuilt_grad = (
        inverse * (grad * gain)
        - (inverse_cube * (inner_row / plan.width)) * rebuilt
        + (rebuilt - inputs.astype(F32))
    ).astype(BF16)
    latents = latents_ref[...]
    latent_grad = lax.dot_general(
        rebuilt_grad, dict_ref[...], ACROSS, preferred_element_type=F32
    )
    preact_grad = jnp.where(latents.astype(F32) > 0.0, latent_grad, 0.0).astype(BF16)
    left = jnp.concatenate([latents, preact_grad], axis=0)
    right = jnp.concatenate([rebuilt_grad, inputs], axis=0)
    size = plan.width // pieces
    writes = []
    for piece in range(pieces):
        span = slice(piece * size, (piece + 1) * size)
        out_ref[:, span] = lax.dot_general(
            left, right[:, span], DOWNWARD, preferred_element_type=F32
        ).astype(BF16)
        one = pltpu.make_async_copy(
            out_ref.at[:, span], out_hbm.at[:, span], out_sems.at[piece]
        )
        one.start()
        writes.append(one)
    for one in writes:
        one.wait()


def dictionary_step(plan, own, other, gain, inverse, scaled, inputs, latents, dictionary):
    units = dictionary.shape[0]
    pieces = plan.tiles
    return call(
        functools.partial(dictionary_body, plan, pieces),
        shaped(*dictionary.shape, dtype=BF16),
        (own, other, gain, inverse, scaled, inputs, latents, dictionary),
        [
            pltpu.VMEM((plan.rows, plan.width), BF16),
            pltpu.VMEM(dictionary.shape, BF16),
            pltpu.SemaphoreType.DMA((pieces,)),
        ],
        out_specs=HBM,
        flops=6 * plan.rows * plan.width * units,
        moved=dictionary.size * 4,
    )


def swap(value):
    size = lax.axis_size("hidden")
    return lax.ppermute(value, "hidden", [(i, (i + 1) % size) for i in range(size)])


def partner_swap(value, bits):
    size = lax.axis_size("latent")
    return lax.ppermute(value, "latent", [(i, i ^ bits) for i in range(size)])


def cross(value):
    return partner_swap(value, 1)


def to_column(plan, blocks):
    return [partner_swap(one, column) for one, column in zip(blocks, plan.columns[1:])]


def tie(*values):
    return lax.optimization_barrier(values)


def per_device(
    input_codes,
    cotangent_codes,
    dictionary,
    encoder_bias,
    decoder_bias,
    norm_gain,
    gate_weight,
    up_weight,
    down_weight,
):
    plan = Plan(
        lax.axis_size("latent"), lax.axis_size("hidden"), input_codes.shape[0], input_codes.shape[1]
    )
    if not plan.fits():
        return per_device_plain(
            input_codes,
            cotangent_codes,
            dictionary,
            encoder_bias,
            decoder_bias,
            norm_gain,
            gate_weight,
            up_weight,
            down_weight,
        )
    fan = len(plan.columns) - 1
    vectors = jnp.concatenate([encoder_bias, decoder_bias, norm_gain]).reshape(1, -1)
    block, cotangent = pack_codes(plan, input_codes, cotangent_codes)
    stack = stack_up(plan, block, to_column(plan, [block] * fan))
    stack, vectors, late_dictionary = tie(stack, vectors, dictionary)
    crossed, stack_other = cross(stack), swap(stack)
    encoder = bring_encoder(plan, late_dictionary, vectors)
    crossed, stack_other, encoder, cotangent = tie(crossed, stack_other, encoder, cotangent)
    brought, bias, decoder, gain = encoder
    inputs, latents, kept, sent = encode(
        plan, (stack, crossed), (stack_other, swap(crossed)), brought, bias, gain
    )
    sent, kept = swap(sent), swap(kept)
    own_kept, own_sent = decode_own(plan, latents, brought, decoder, gain)
    sent, cotangent = tie(add_sent(plan, own_sent, sent), cotangent)
    crossed = cross(sent)
    got = to_column(plan, [cotangent] * fan)
    own, sent = add_across(plan, own_kept, kept, crossed)
    own, sent, got = tie(own, sent, got)
    cotangent_stack = stack_up(plan, cotangent, got)
    cotangent_crossed = cross(cotangent_stack)
    block = add_column(plan, own, to_column(plan, sent))
    block, cotangent_stack, cotangent_crossed = tie(block, cotangent_stack, cotangent_crossed)
    stack = stack_up(plan, block, to_column(plan, [block] * fan))
    crossed, stack_other = cross(stack), swap(stack)
    hidden_grad = back_project(
        plan,
        (cotangent_stack, cotangent_crossed),
        (swap(cotangent_stack), swap(cotangent_crossed)),
        down_weight,
    )
    crossed, stack_other, hidden_grad = tie(crossed, stack_other, hidden_grad)
    first = mlp_first(plan, line_up(plan, stack, crossed), gate_weight, up_weight, gain)
    scaled_other = line_up(plan, stack_other, swap(crossed))
    scaled, inverse, hidden, gate_grad, up_grad, kept, sent = mlp(
        plan, scaled_other, gate_weight, up_weight, gain, hidden_grad, first
    )
    sent, kept = swap(sent), swap(kept)
    own_kept, own_sent = mlp_own(plan, gate_grad, up_grad, gate_weight, up_weight)
    out_mine, out_theirs = project(plan, hidden, down_weight)
    sent, out_mine, out_theirs = tie(add_sent(plan, own_sent, sent), out_mine, out_theirs)
    crossed = cross(sent)
    out_kept, out_sent = add_pair(plan, out_mine, swap(out_theirs))
    own, sent = add_across(plan, own_kept, kept, crossed)
    own, sent, out_kept, out_sent = tie(own, sent, out_kept, out_sent)
    got = to_column(plan, sent)
    out_crossed = cross(out_sent)
    block, out_own, messages = add_with_output(plan, own, got, out_kept, out_crossed)
    got = to_column(plan, messages)
    stack = stack_up(plan, block, got)
    crossed, stack_other = cross(stack), swap(stack)
    block_output = finish_output(plan, out_own, got)
    grad_own = line_up(plan, stack, crossed)
    grad_other = line_up(plan, stack_other, swap(crossed))
    dictionary_grad = dictionary_step(
        plan, grad_own, grad_other, gain, inverse, scaled, inputs, latents, brought
    )
    return (block_output, dictionary_grad)


def per_device_plain(
    input_codes,
    cotangent_codes,
    dictionary,
    encoder_bias,
    decoder_bias,
    norm_gain,
    gate_weight,
    up_weight,
    down_weight,
):
    own_width = input_codes.shape[1]
    model_width = own_width * lax.axis_size(("latent", "hidden"))
    cotangent_local = (cotangent_codes.astype(jnp.float32) * CODE_STEP).astype(jnp.bfloat16)
    inputs_local = (input_codes.astype(jnp.float32) * CODE_STEP).astype(jnp.bfloat16)
    inputs = lax.all_gather(inputs_local, ("latent", "hidden"), axis=1, tiled=True)
    preact = (
        lax.dot_general(inputs, dictionary, ACROSS, preferred_element_type=jnp.float32)
        + encoder_bias
    )
    latents = jnp.maximum(preact, 0.0).astype(jnp.bfloat16)
    partial_value = jnp.dot(latents, dictionary, preferred_element_type=jnp.float32)
    rebuilt = lax.psum(partial_value, ("latent", "hidden")) + decoder_bias
    inverse = lax.rsqrt(
        jnp.sum(rebuilt * rebuilt, axis=1, keepdims=True) / model_width + NORM_EPSILON
    )
    normed = (rebuilt * inverse * norm_gain).astype(jnp.bfloat16)
    target = inputs.astype(jnp.float32)
    gate_proj = lax.dot_general(normed, gate_weight, ACROSS, preferred_element_type=jnp.float32)
    up_proj = lax.dot_general(normed, up_weight, ACROSS, preferred_element_type=jnp.float32)
    gelu_value, gelu_slope = gelu_parts(gate_proj)
    hidden = (gelu_value * up_proj).astype(jnp.bfloat16)
    output_terms = jnp.dot(hidden, down_weight, preferred_element_type=jnp.float32)
    block_output = lax.psum_scatter(
        output_terms, ("latent", "hidden"), scatter_dimension=1, tiled=True
    ).astype(jnp.bfloat16)
    hidden_grad = lax.dot_general(
        lax.all_gather(cotangent_local, ("latent", "hidden"), axis=1, tiled=True),
        down_weight,
        ACROSS,
        preferred_element_type=jnp.float32,
    )
    gate_grad = (hidden_grad * up_proj * gelu_slope).astype(jnp.bfloat16)
    up_grad = (hidden_grad * gelu_value).astype(jnp.bfloat16)
    partial_grad = jnp.dot(gate_grad, gate_weight, preferred_element_type=jnp.float32) + jnp.dot(
        up_grad, up_weight, preferred_element_type=jnp.float32
    )
    scaled = lax.psum(partial_grad, ("latent", "hidden")) * norm_gain
    inner_row = jnp.sum(scaled * rebuilt, axis=1, keepdims=True)
    inverse_cube = inverse * inverse * inverse
    rebuilt_grad = (
        inverse * scaled - inverse_cube * rebuilt * (inner_row / model_width) + (rebuilt - target)
    ).astype(jnp.bfloat16)
    latent_grad = lax.dot_general(
        rebuilt_grad, dictionary, ACROSS, preferred_element_type=jnp.float32
    )
    preact_grad = jnp.where(preact > 0.0, latent_grad, 0.0).astype(jnp.bfloat16)
    dictionary_grad = lax.dot_general(
        latents, rebuilt_grad, DOWNWARD, preferred_element_type=jnp.float32
    ) + lax.dot_general(preact_grad, inputs, DOWNWARD, preferred_element_type=jnp.float32)
    return (block_output, dictionary_grad.astype(jnp.bfloat16))


def solution(mesh):
    in_specs = (
        P("groups", ("latent", "hidden")),
        P("groups", ("latent", "hidden")),
        P(("latent", "hidden"), None),
        P(("latent", "hidden")),
        P(),
        P(),
        P(("latent", "hidden"), None),
        P(("latent", "hidden"), None),
        P(("latent", "hidden"), None),
    )
    out_specs = (P("groups", ("latent", "hidden")), P(("latent", "hidden"), "groups"))
    return jax.shard_map(
        per_device, mesh=mesh, in_specs=in_specs, out_specs=out_specs, check_vma=False
    )
```

```python
import functools
import math

import jax
import jax.numpy as jnp
from jax import lax
from jax.experimental import pallas as pl
from jax.experimental.pallas import tpu as pltpu
from jax.sharding import PartitionSpec as P

CODE_STEP = 2.0 ** (-6)
NORM_EPSILON = 1e-06
GELU_ROOT = 0.7978845608028654
GELU_CUBIC = 0.044715
ACROSS = (((1,), (1,)), ((), ()))
DOWNWARD = (((0,), (0,)), ((), ()))
LANES = 128
ROW_TILE = 16
DIRECT_LIMIT = 16
VMEM_BYTES = 24 * 1024 * 1024
VMEM_BRING = 53 * 1024 * 1024
F32 = jnp.float32
BF16 = jnp.bfloat16


def gelu_parts(values):
    argument = GELU_ROOT * (values + GELU_CUBIC * values * values * values)
    tanh_value = jnp.tanh(argument)
    result = 0.5 * values * (1.0 + tanh_value)
    derivative = 0.5 * (1.0 + tanh_value) + 0.5 * values * (
        1.0 - tanh_value * tanh_value
    ) * GELU_ROOT * (1.0 + 3.0 * GELU_CUBIC * values * values)
    return (result, derivative)


def up_to(value, unit):
    return -(-value // unit) * unit


def chips_fit(chips):
    return 2 <= chips <= DIRECT_LIMIT and chips & (chips - 1) == 0


class Plan:
    def __init__(self, chips, cores, rows, own):
        self.chips, self.cores, self.rows, self.own = chips, cores, rows, own
        self.width = own * chips * cores
        self.half = self.width // cores
        self.tiles = self.half // LANES
        self.chunk = up_to(-(-self.tiles * rows // chips), ROW_TILE)
        self.flat = self.chunk * chips
        self.tail = own - LANES
        if self.tail > 0:
            self.fold_rows = min(
                size
                for size in range(ROW_TILE, rows + ROW_TILE, ROW_TILE)
                if -(-rows // size) * self.tail <= LANES
            )
            self.packed = rows + self.fold_rows
        self.columns = list(range(0, chips, 2))

    def side_blocks(self, refs):
        me = lax.axis_index("latent")
        stack_ref, *crossed_refs = refs
        for place, column in enumerate(self.columns):
            yield me ^ column, stack_ref[place]
        places = iter(self.columns)
        for ref in crossed_refs:
            for place in range(ref.shape[0]):
                yield me ^ next(places) ^ 1, ref[place]

    def pieces(self):
        for tile in range(self.tiles):
            row = 0
            while row < self.rows:
                chip, place = divmod(tile * self.rows + row, self.chunk)
                count = min(self.rows - row, self.chunk - place)
                yield tile, chip, place, row, count
                row += count

    def fits(self):
        return (
            self.cores == 2
            and chips_fit(self.chips)
            and self.rows % ROW_TILE == 0
            and self.half % LANES == 0
            and 0 < self.tail < LANES
        )


HBM = pl.BlockSpec(memory_space=pltpu.HBM)
ONCHIP = pl.BlockSpec(memory_space=pltpu.VMEM)


def shaped(*dims, dtype=F32):
    return jax.ShapeDtypeStruct(dims, dtype)


HBM = pl.BlockSpec(memory_space=pltpu.HBM)
ONCHIP = pl.BlockSpec(memory_space=pltpu.VMEM)


def shaped(*dims, dtype=F32):
    return jax.ShapeDtypeStruct(dims, dtype)


def call(body, out_shapes, operands, scratch=(), out_specs=None, flops=0, moved=0):
    return pl.pallas_call(
        body,
        out_shape=out_shapes,
        in_specs=[ONCHIP] * len(operands),
        out_specs=jax.tree.map(lambda _: ONCHIP, out_shapes) if out_specs is None else out_specs,
        scratch_shapes=list(scratch),
        compiler_params=pltpu.CompilerParams(vmem_limit_bytes=VMEM_BYTES),
        cost_estimate=pl.CostEstimate(flops=flops, bytes_accessed=moved, transcendentals=0),
    )(*operands)


def padded_bytes(array):
    *lead, rows, columns = array.shape
    item = jnp.dtype(array.dtype).itemsize
    return math.prod(lead) * up_to(rows, ROW_TILE) * up_to(columns, LANES) * item


def copies(sources, targets, sems):
    started = []
    for index, (source, target) in enumerate(zip(sources, targets)):
        one = pltpu.make_async_copy(source, target, sems.at[index])
        one.start()
        started.append(one)
    return started


def pack_block(plan, block):
    tail = block[:, LANES:]
    folded = []
    for start in range(0, plan.rows, plan.fold_rows):
        piece = tail[start : min(start + plan.fold_rows, plan.rows), :]
        short = plan.fold_rows - piece.shape[0]
        if short:
            piece = jnp.concatenate([piece, jnp.zeros((short, plan.tail), block.dtype)], axis=0)
        folded.append(piece)
    fill = LANES - len(folded) * plan.tail
    if fill:
        folded.append(jnp.zeros((plan.fold_rows, fill), block.dtype))
    return block[:, :LANES], jnp.concatenate(folded, axis=1)


def unpack_block(plan, packed):
    pieces = []
    for fold, start in enumerate(range(0, plan.rows, plan.fold_rows)):
        count = min(plan.fold_rows, plan.rows - start)
        pieces.append(
            packed[plan.rows : plan.rows + count, fold * plan.tail : (fold + 1) * plan.tail]
        )
    return jnp.concatenate([packed[: plan.rows, :], jnp.concatenate(pieces, axis=0)], axis=1)


def pack_codes_body(plan, codes_ref, out_ref):
    main, tail = pack_block(plan, codes_ref[...].astype(F32) * CODE_STEP)
    out_ref[0, : plan.rows, :] = main.astype(BF16)
    out_ref[0, plan.rows :, :] = tail.astype(BF16)


def pack_codes(plan, codes):
    return call(
        functools.partial(pack_codes_body, plan),
        shaped(1, plan.packed, LANES, dtype=BF16),
        (codes,),
        moved=plan.rows * plan.own * 8,
    )


def assemble(plan, own_refs, other_refs, both, full_ref):
    core = lax.axis_index("hidden")
    for side, refs in ((core, own_refs), (1 - core, other_refs)):
        for chip, block in plan.side_blocks(refs):
            both[side, chip] = block
    for chip in range(plan.chips):
        for side in range(plan.cores):
            column = (chip * plan.cores + side) * plan.own
            block = unpack_block(plan, both[side, chip].astype(F32))
            full_ref[:, column : column + plan.own] = block.astype(BF16)


def both_scratch(plan, dtype=BF16):
    return pltpu.VMEM((plan.cores, plan.chips, plan.packed, LANES), dtype)


def chunk_scratch(plan):
    return pltpu.VMEM((plan.chips, plan.chunk, LANES), F32)


def side_shapes(plan, dtype=F32):
    return [shaped(len(plan.columns), plan.chunk, LANES, dtype=dtype)] * 2


def half_product(plan, pairs, side, kept_ref, sent_ref, target, gain_ref=None, bias_ref=None):
    span = pl.ds(pl.multiple_of(side * plan.half, LANES), plan.half)
    total = None
    for left, right_ref in pairs:
        term = jnp.dot(left, right_ref[:, span], preferred_element_type=F32)
        total = term if total is None else total + term
    if bias_ref is not None:
        total = total + bias_ref[:, span] * jnp.where(lax.axis_index("latent") == 0, 1.0, 0.0)
    if gain_ref is not None:
        total = total * gain_ref[:, span]
    for tile, chip, place, row, count in plan.pieces():
        target[chip, place : place + count, :] = total[
            row : row + count, tile * LANES : (tile + 1) * LANES
        ]
    used = plan.tiles * plan.rows
    while used < plan.flat:
        chip, place = divmod(used, plan.chunk)
        target[chip, place:, :] = jnp.zeros((plan.chunk - place, LANES), F32)
        used += plan.chunk - place
    me = lax.axis_index("latent")
    for place, column in enumerate(plan.columns):
        kept_ref[place] = target[me ^ column]
        sent_ref[place] = target[me ^ column ^ 1]


def bring_encoder_body(dict_hbm, vectors_hbm, dict_ref, bias_ref, decoder_ref, gain_ref, sems):
    sources, targets = [dict_hbm], [dict_ref]
    start = 0
    for target in (bias_ref, decoder_ref, gain_ref):
        sources.append(vectors_hbm.at[:, start : start + target.shape[1]])
        targets.append(target)
        start += target.shape[1]
    for copy in copies(sources, targets, sems):
        copy.wait()


def bring_encoder(plan, dictionary, vectors):
    outputs = [
        shaped(*dictionary.shape, dtype=BF16),
        shaped(1, dictionary.shape[0]),
        shaped(1, plan.width),
        shaped(1, plan.width),
    ]
    return pl.pallas_call(
        bring_encoder_body,
        out_shape=outputs,
        in_specs=[HBM] * 2,
        out_specs=[ONCHIP] * len(outputs),
        scratch_shapes=[pltpu.SemaphoreType.DMA((len(outputs),))],
        compiler_params=pltpu.CompilerParams(
            vmem_limit_bytes=VMEM_BRING - sum(map(padded_bytes, outputs))
        ),
        cost_estimate=pl.CostEstimate(
            flops=0, bytes_accessed=dictionary.size * 4, transcendentals=0
        ),
    )(dictionary, vectors)


def encode_body(plan, *refs):
    own, other, (dict_ref, bias_ref, gain_ref) = refs[:3], refs[3:6], refs[6:9]
    inputs_ref, latents_ref, kept_ref, sent_ref, both, target = refs[9:]
    assemble(plan, own, other, both, inputs_ref)
    preact = (
        lax.dot_general(inputs_ref[...], dict_ref[...], ACROSS, preferred_element_type=F32)
        + bias_ref[...]
    )
    latents = jnp.maximum(preact, 0.0).astype(BF16)
    latents_ref[...] = latents
    theirs = 1 - lax.axis_index("hidden")
    half_product(plan, [(latents, dict_ref)], theirs, kept_ref, sent_ref, target, gain_ref)


def encode(plan, own, other, dictionary, encoder_bias, gain):
    latents = dictionary.shape[0]
    return call(
        functools.partial(encode_body, plan),
        [
            shaped(plan.rows, plan.width, dtype=BF16),
            shaped(plan.rows, latents, dtype=BF16),
            *side_shapes(plan),
        ],
        (*own, *other, dictionary, encoder_bias, gain),
        [both_scratch(plan), chunk_scratch(plan)],
        flops=3 * plan.rows * plan.width * latents,
        moved=dictionary.size * 2,
    )


def decode_own_body(plan, latents_ref, dict_ref, decoder_ref, gain_ref, kept_ref, sent_ref, target):
    pairs = [(latents_ref[...], dict_ref)]
    mine = lax.axis_index("hidden")
    half_product(plan, pairs, mine, kept_ref, sent_ref, target, gain_ref, decoder_ref)


def decode_own(plan, latents, dictionary, decoder_bias, gain):
    return call(
        functools.partial(decode_own_body, plan),
        side_shapes(plan),
        (latents, dictionary, decoder_bias, gain),
        [chunk_scratch(plan)],
        flops=plan.rows * plan.width * dictionary.shape[0],
        moved=dictionary.size,
    )


def back_project_body(plan, *refs):
    own, other, (down_ref, grad_ref, both, full) = refs[:2], refs[2:4], refs[4:]
    assemble(plan, own, other, both, full)
    grad_ref[...] = lax.dot_general(
        full[...], down_ref[...], ACROSS, preferred_element_type=F32
    )


def back_project(plan, own, other, down_weight):
    units = down_weight.shape[0]
    return call(
        functools.partial(back_project_body, plan),
        shaped(plan.rows, units),
        (*own, *other, down_weight),
        [both_scratch(plan), pltpu.VMEM((plan.rows, plan.width), BF16)],
        flops=2 * plan.rows * plan.width * units,
        moved=down_weight.size * 2,
    )


def join_half(plan, source, first, full_ref):
    for tile, chip, place, row, count in plan.pieces():
        column = pl.multiple_of(first + tile * LANES, LANES)
        full_ref[row : row + count, pl.ds(column, LANES)] = source[
            chip, place : place + count, :
        ]


def half_terms(plan, half, side, gate_ref, up_ref, gain_ref):
    span = pl.ds(pl.multiple_of(side * plan.half, LANES), plan.half)
    rebuilt = half.astype(F32) / gain_ref[:, span]
    squares = jnp.sum(rebuilt * rebuilt, axis=1, keepdims=True)
    gate = lax.dot_general(half, gate_ref[:, span], ACROSS, preferred_element_type=F32)
    up = lax.dot_general(half, up_ref[:, span], ACROSS, preferred_element_type=F32)
    return squares, gate, up


def mlp_first_body(plan, own_ref, gate_ref, up_ref, gain_ref, half_ref, squares_ref, gate_part_ref, up_part_ref):
    join_half(plan, own_ref, 0, half_ref)
    squares_ref[...], gate_part_ref[...], up_part_ref[...] = half_terms(
        plan, half_ref[...], lax.axis_index("hidden"), gate_ref, up_ref, gain_ref
    )


def mlp_first(plan, own, gate_weight, up_weight, gain):
    units = gate_weight.shape[0]
    return call(
        functools.partial(mlp_first_body, plan),
        [
            shaped(plan.rows, plan.half, dtype=BF16),
            shaped(plan.rows, 1),
            shaped(plan.rows, units),
            shaped(plan.rows, units),
        ],
        (own, gate_weight, up_weight, gain),
        flops=2 * plan.rows * plan.width * units,
        moved=gate_weight.size * 4,
    )


def mlp_body(plan, other_ref, gate_ref, up_ref, gain_ref, grad_ref, half_ref, squares_ref, gate_part_ref, up_part_ref, scaled_ref, inverse_ref, hidden_ref, gate_grad_ref, up_grad_ref, kept_ref, sent_ref, target):
    core = lax.axis_index("hidden")
    join_half(plan, other_ref, (1 - core) * plan.half, scaled_ref)
    other_span = pl.ds(pl.multiple_of((1 - core) * plan.half, LANES), plan.half)
    own_span = pl.ds(pl.multiple_of(core * plan.half, LANES), plan.half)
    scaled_ref[:, own_span] = half_ref[...]
    squares, gate, up = half_terms(
        plan, scaled_ref[:, other_span], 1 - core, gate_ref, up_ref, gain_ref
    )
    inverse = lax.rsqrt((squares + squares_ref[...]) / plan.width + NORM_EPSILON)
    inverse_ref[...] = inverse
    gate_proj = inverse * (gate + gate_part_ref[...])
    up_proj = inverse * (up + up_part_ref[...])
    gelu_value, gelu_slope = gelu_parts(gate_proj)
    hidden_ref[...] = (gelu_value * up_proj).astype(BF16)
    hidden_grad = grad_ref[...]
    gate_grad = (hidden_grad * up_proj * gelu_slope).astype(BF16)
    up_grad = (hidden_grad * gelu_value).astype(BF16)
    gate_grad_ref[...] = gate_grad
    up_grad_ref[...] = up_grad
    pairs = [(gate_grad, gate_ref), (up_grad, up_ref)]
    half_product(plan, pairs, 1 - core, kept_ref, sent_ref, target)


def mlp(plan, other, gate_weight, up_weight, gain, hidden_grad, first):
    units = gate_weight.shape[0]
    return call(
        functools.partial(mlp_body, plan),
        [
            shaped(plan.rows, plan.width, dtype=BF16),
            shaped(plan.rows, 1),
            shaped(plan.rows, units, dtype=BF16),
            shaped(plan.rows, units, dtype=BF16),
            shaped(plan.rows, units, dtype=BF16),
            *side_shapes(plan),
        ],
        (other, gate_weight, up_weight, gain, hidden_grad, *first),
        [chunk_scratch(plan)],
        flops=6 * plan.rows * plan.width * units,
        moved=gate_weight.size * 4,
    )


def mlp_own_body(plan, gate_grad_ref, up_grad_ref, gate_ref, up_ref, kept_ref, sent_ref, target):
    pairs = [(gate_grad_ref[...], gate_ref), (up_grad_ref[...], up_ref)]
    half_product(plan, pairs, lax.axis_index("hidden"), kept_ref, sent_ref, target)


def mlp_own(plan, gate_grad, up_grad, gate_weight, up_weight):
    return call(
        functools.partial(mlp_own_body, plan),
        side_shapes(plan),
        (gate_grad, up_grad, gate_weight, up_weight),
        [chunk_scratch(plan)],
        flops=2 * plan.rows * plan.width * gate_weight.shape[0],
        moved=gate_weight.size * 2,
    )


def project_body(plan, hidden_ref, down_ref, mine_ref, theirs_ref, both):
    core = lax.axis_index("hidden")
    terms = jnp.dot(hidden_ref[...], down_ref[...], preferred_element_type=F32)
    for chip in range(plan.chips):
        for side in range(plan.cores):
            start = (chip * plan.cores + side) * plan.own
            main, tail = pack_block(plan, terms[:, start : start + plan.own])
            both[side, chip, : plan.rows, :] = main
            both[side, chip, plan.rows :, :] = tail
    mine_ref[...] = both[core]
    theirs_ref[...] = both[1 - core]


def project(plan, hidden, down_weight):
    units = down_weight.shape[0]
    shape = (plan.chips, plan.packed, LANES)
    return call(
        functools.partial(project_body, plan),
        [shaped(*shape)] * 2,
        (hidden, down_weight),
        [both_scratch(plan, F32)],
        flops=2 * plan.rows * plan.width * units,
        moved=down_weight.size * 2,
    )


def add_pair_body(plan, mine_ref, theirs_ref, kept_ref, sent_ref):
    me = lax.axis_index("latent")
    for place, column in enumerate(plan.columns):
        kept, sent = me ^ column, me ^ column ^ 1
        kept_ref[place] = mine_ref[kept] + theirs_ref[kept]
        sent_ref[place] = (mine_ref[sent] + theirs_ref[sent]).astype(BF16)


def add_pair(plan, mine, theirs):
    count, dims = len(plan.columns), mine.shape[1:]
    return call(
        functools.partial(add_pair_body, plan),
        [shaped(count, *dims), shaped(count, *dims, dtype=BF16)],
        (mine, theirs),
        moved=mine.size * 10,
    )


def add_sent_body(mine_ref, theirs_ref, first_ref, rest_ref):
    total = (mine_ref[...] + theirs_ref[...]).astype(BF16)
    first_ref[...] = total[:1]
    rest_ref[...] = total[1:]


def add_sent(plan, mine, theirs):
    count, *dims = mine.shape
    return call(
        add_sent_body,
        [shaped(1, *dims, dtype=BF16), shaped(count - 1, *dims, dtype=BF16)],
        (mine, theirs),
        moved=mine.size * 10,
    )


def add_across_body(mine_ref, theirs_ref, got_ref, *sent_refs):
    for place, out_ref in enumerate(sent_refs):
        total = mine_ref[1 + place] + theirs_ref[1 + place] + got_ref[place].astype(F32)
        out_ref[0] = total.astype(BF16)


def add_across(plan, mine, theirs, got):
    return call(
        add_across_body,
        [shaped(1, *mine.shape[1:], dtype=BF16)] * got.shape[0],
        (mine, theirs, got),
        moved=mine.size * 10,
    )


def column_total(mine_ref, theirs_ref, first_ref, *refs):
    total = mine_ref[0] + theirs_ref[0] + first_ref[0].astype(F32)
    for ref in refs:
        total = total + ref[0].astype(F32)
    return total.astype(BF16)


def add_column_body(*refs):
    refs[-1][0] = column_total(*refs[:-1])


def add_column(plan, mine, theirs, first, got):
    return call(
        add_column_body,
        shaped(1, *mine.shape[1:], dtype=BF16),
        (mine, theirs, first, *reversed(got)),
        moved=mine.size * 8,
    )


def add_with_output_body(plan, count, *refs):
    total = column_total(*refs[:count])
    kept_ref, crossed_ref, block_ref, own_ref = refs[count : count + 4]
    block_ref[0] = total
    own_ref[0] = kept_ref[0] + crossed_ref[0].astype(F32)
    for place, both_ref in enumerate(refs[count + 4 :], 1):
        both_ref[0, : plan.chunk, :] = total
        both_ref[0, plan.chunk :, :] = (
            kept_ref[place] + crossed_ref[place].astype(F32)
        ).astype(BF16)


def add_with_output(plan, mine, theirs, first, got, kept, crossed):
    both = shaped(1, plan.chunk + plan.packed, LANES, dtype=BF16)
    block, out_own, *messages = call(
        functools.partial(add_with_output_body, plan, 3 + len(got)),
        [shaped(1, plan.chunk, LANES, dtype=BF16), shaped(1, plan.packed, LANES)]
        + [both] * (len(plan.columns) - 1),
        (mine, theirs, first, *reversed(got), kept, crossed),
        moved=mine.size * 12,
    )
    return block, out_own, messages


def stack_body(places, *refs):
    *sources, stack_ref, rest_ref = refs
    rows = stack_ref.shape[1]
    for place, ref in zip(places, sources):
        stack_ref[place] = ref[0, :rows, :]
        if place:
            rest_ref[place - 1] = ref[0, :rows, :]


def stack_up(plan, block, got, backwards=False):
    dims = block.shape[1:]
    operands = [block, *got]
    places = list(range(len(operands)))
    if backwards:
        operands, places = operands[::-1], places[::-1]
    return call(
        functools.partial(stack_body, places),
        [shaped(1 + len(got), *dims, dtype=BF16), shaped(len(got), *dims, dtype=BF16)],
        operands,
        moved=block.size * 16,
    )


def line_up_body(plan, *refs):
    for chip, block in plan.side_blocks(refs[:3]):
        refs[3][chip] = block


def line_up(plan, stack, first, rest):
    return call(
        functools.partial(line_up_body, plan),
        shaped(plan.chips, *stack.shape[1:], dtype=BF16),
        (stack, first, rest),
        moved=stack.size * 8,
    )


def finish_output_body(plan, own_ref, *refs):
    total = own_ref[0]
    for ref in refs[:-1]:
        total = total + ref[0, plan.chunk :, :].astype(F32)
    refs[-1][...] = unpack_block(plan, total).astype(BF16)


def finish_output(plan, own, messages):
    return call(
        functools.partial(finish_output_body, plan),
        shaped(plan.rows, plan.own, dtype=BF16),
        (own, *reversed(messages)),
        moved=own.size * 8,
    )


def dictionary_body(plan, pieces, own_ref, other_ref, gain_ref, inverse_ref, scaled_ref, inputs_ref, latents_ref, dict_ref, out_hbm, full, out_ref, out_sems):
    core = lax.axis_index("hidden")
    join_half(plan, own_ref, core * plan.half, full)
    join_half(plan, other_ref, (1 - core) * plan.half, full)
    grad = full[...].astype(F32)
    gain = gain_ref[...]
    scaled_rebuilt = scaled_ref[...].astype(F32)
    rebuilt = scaled_rebuilt / gain
    inverse = inverse_ref[...]
    inner_row = jnp.sum(grad * scaled_rebuilt, axis=1, keepdims=True)
    inverse_cube = inverse * inverse * inverse
    inputs = inputs_ref[...]
    rebuilt_grad = (
        inverse * (grad * gain)
        - (inverse_cube * (inner_row / plan.width)) * rebuilt
        + (rebuilt - inputs.astype(F32))
    ).astype(BF16)
    latents = latents_ref[...]
    latent_grad = lax.dot_general(
        rebuilt_grad, dict_ref[...], ACROSS, preferred_element_type=F32
    )
    preact_grad = jnp.where(latents.astype(F32) > 0.0, latent_grad, 0.0).astype(BF16)
    left = jnp.concatenate([latents, preact_grad], axis=0)
    right = jnp.concatenate([rebuilt_grad, inputs], axis=0)
    size = plan.width // pieces
    writes = []
    for piece in range(pieces):
        span = slice(piece * size, (piece + 1) * size)
        out_ref[:, span] = lax.dot_general(
            left, right[:, span], DOWNWARD, preferred_element_type=F32
        ).astype(BF16)
        one = pltpu.make_async_copy(
            out_ref.at[:, span], out_hbm.at[:, span], out_sems.at[piece]
        )
        one.start()
        writes.append(one)
    for one in writes:
        one.wait()


def dictionary_step(plan, own, other, gain, inverse, scaled, inputs, latents, dictionary):
    units = dictionary.shape[0]
    pieces = plan.tiles
    return call(
        functools.partial(dictionary_body, plan, pieces),
        shaped(*dictionary.shape, dtype=BF16),
        (own, other, gain, inverse, scaled, inputs, latents, dictionary),
        [
            pltpu.VMEM((plan.rows, plan.width), BF16),
            pltpu.VMEM(dictionary.shape, BF16),
            pltpu.SemaphoreType.DMA((pieces,)),
        ],
        out_specs=HBM,
        flops=6 * plan.rows * plan.width * units,
        moved=dictionary.size * 4,
    )


def swap(value):
    size = lax.axis_size("hidden")
    return lax.ppermute(value, "hidden", [(i, (i + 1) % size) for i in range(size)])


def partner_swap(value, bits):
    size = lax.axis_size("latent")
    return lax.ppermute(value, "latent", [(i, i ^ bits) for i in range(size)])


def cross(value):
    return partner_swap(value, 1)


def to_column(plan, blocks):
    pairs = list(zip(blocks, plan.columns[1:]))
    got = [partner_swap(one, column) for one, column in reversed(pairs)]
    return got[::-1]


def to_all_columns(plan, block):
    return [partner_swap(block, column) for column in plan.columns[1:]]


def tie(*values):
    return lax.optimization_barrier(values)


def per_device(
    input_codes,
    cotangent_codes,
    dictionary,
    encoder_bias,
    decoder_bias,
    norm_gain,
    gate_weight,
    up_weight,
    down_weight,
):
    plan = Plan(
        lax.axis_size("latent"), lax.axis_size("hidden"), input_codes.shape[0], input_codes.shape[1]
    )
    if not plan.fits():
        return per_device_plain(
            input_codes,
            cotangent_codes,
            dictionary,
            encoder_bias,
            decoder_bias,
            norm_gain,
            gate_weight,
            up_weight,
            down_weight,
        )
    vectors = jnp.concatenate([encoder_bias, decoder_bias, norm_gain]).reshape(1, -1)
    block = pack_codes(plan, input_codes)
    got, first = tie(to_all_columns(plan, block), cross(block))
    stack, rest = stack_up(plan, block, got)
    stack, rest, vectors, late_dictionary, cotangent_codes = tie(
        stack, rest, vectors, dictionary, cotangent_codes
    )
    rest, stack_other, first_other = cross(rest), swap(stack), swap(first)
    cotangent = pack_codes(plan, cotangent_codes)
    cotangent_got = to_all_columns(plan, cotangent)
    encoder = bring_encoder(plan, late_dictionary, vectors)
    rest, stack_other, first_other, encoder, cotangent_got = tie(
        rest, stack_other, first_other, encoder, cotangent_got
    )
    brought, bias, decoder, gain = encoder
    inputs, latents, kept, sent = encode(
        plan, (stack, first, rest), (stack_other, first_other, swap(rest)), brought, bias, gain
    )
    sent, kept = swap(sent), swap(kept)
    own_kept, own_sent = decode_own(plan, latents, brought, decoder, gain)
    sent_first, sent_rest = add_sent(plan, own_sent, sent)
    sent = add_across(plan, own_kept, kept, cross(sent_rest))
    sent, sent_first, cotangent_got = tie(sent, sent_first, cotangent_got)
    cotangent_stack, _ = stack_up(plan, cotangent, cotangent_got)
    cotangent_crossed = cross(cotangent_stack)
    block = add_column(plan, own_kept, kept, cross(sent_first), to_column(plan, sent))
    block, *cotangent_own = tie(block, cotangent_stack, cotangent_crossed)
    got, first = tie(to_all_columns(plan, block), cross(block))
    hidden_grad = back_project(
        plan, cotangent_own, [swap(one) for one in cotangent_own], down_weight
    )
    stack, rest = stack_up(plan, block, got)
    rest, stack_other, first_other = cross(rest), swap(stack), swap(first)
    rest, stack_other, first_other, hidden_grad = tie(rest, stack_other, first_other, hidden_grad)
    terms = mlp_first(plan, line_up(plan, stack, first, rest), gate_weight, up_weight, gain)
    scaled_other = line_up(plan, stack_other, first_other, swap(rest))
    scaled, inverse, hidden, gate_grad, up_grad, kept, sent = mlp(
        plan, scaled_other, gate_weight, up_weight, gain, hidden_grad, terms
    )
    sent, kept = swap(sent), swap(kept)
    own_kept, own_sent = mlp_own(plan, gate_grad, up_grad, gate_weight, up_weight)
    out_mine, out_theirs = project(plan, hidden, down_weight)
    sent_first, sent_rest = add_sent(plan, own_sent, sent)
    sent_first, sent_rest, out_mine, out_theirs = tie(sent_first, sent_rest, out_mine, out_theirs)
    crossed = cross(sent_rest)
    out_kept, out_sent = add_pair(plan, out_mine, swap(out_theirs))
    sent = add_across(plan, own_kept, kept, crossed)
    sent, sent_first, out_kept, out_sent = tie(sent, sent_first, out_kept, out_sent)
    got = to_column(plan, sent)
    first = cross(sent_first)
    out_crossed = cross(out_sent)
    block, out_own, messages = add_with_output(
        plan, own_kept, kept, first, got, out_kept, out_crossed
    )
    got, first = tie(to_column(plan, messages), cross(block))
    stack, rest = stack_up(plan, block, got, backwards=True)
    rest, stack_other, first_other = cross(rest), swap(stack), swap(first)
    block_output = finish_output(plan, out_own, got)
    grad_own = line_up(plan, stack, first, rest)
    grad_other = line_up(plan, stack_other, first_other, swap(rest))
    dictionary_grad = dictionary_step(
        plan, grad_own, grad_other, gain, inverse, scaled, inputs, latents, brought
    )
    return (block_output, dictionary_grad)


def per_device_plain(
    input_codes,
    cotangent_codes,
    dictionary,
    encoder_bias,
    decoder_bias,
    norm_gain,
    gate_weight,
    up_weight,
    down_weight,
):
    own_width = input_codes.shape[1]
    model_width = own_width * lax.axis_size(("latent", "hidden"))
    cotangent_local = (cotangent_codes.astype(jnp.float32) * CODE_STEP).astype(jnp.bfloat16)
    inputs_local = (input_codes.astype(jnp.float32) * CODE_STEP).astype(jnp.bfloat16)
    inputs = lax.all_gather(inputs_local, ("latent", "hidden"), axis=1, tiled=True)
    preact = (
        lax.dot_general(inputs, dictionary, ACROSS, preferred_element_type=jnp.float32)
        + encoder_bias
    )
    latents = jnp.maximum(preact, 0.0).astype(jnp.bfloat16)
    partial_value = jnp.dot(latents, dictionary, preferred_element_type=jnp.float32)
    rebuilt = lax.psum(partial_value, ("latent", "hidden")) + decoder_bias
    inverse = lax.rsqrt(
        jnp.sum(rebuilt * rebuilt, axis=1, keepdims=True) / model_width + NORM_EPSILON
    )
    normed = (rebuilt * inverse * norm_gain).astype(jnp.bfloat16)
    target = inputs.astype(jnp.float32)
    gate_proj = lax.dot_general(normed, gate_weight, ACROSS, preferred_element_type=jnp.float32)
    up_proj = lax.dot_general(normed, up_weight, ACROSS, preferred_element_type=jnp.float32)
    gelu_value, gelu_slope = gelu_parts(gate_proj)
    hidden = (gelu_value * up_proj).astype(jnp.bfloat16)
    output_terms = jnp.dot(hidden, down_weight, preferred_element_type=jnp.float32)
    block_output = lax.psum_scatter(
        output_terms, ("latent", "hidden"), scatter_dimension=1, tiled=True
    ).astype(jnp.bfloat16)
    hidden_grad = lax.dot_general(
        lax.all_gather(cotangent_local, ("latent", "hidden"), axis=1, tiled=True),
        down_weight,
        ACROSS,
        preferred_element_type=jnp.float32,
    )
    gate_grad = (hidden_grad * up_proj * gelu_slope).astype(jnp.bfloat16)
    up_grad = (hidden_grad * gelu_value).astype(jnp.bfloat16)
    partial_grad = jnp.dot(gate_grad, gate_weight, preferred_element_type=jnp.float32) + jnp.dot(
        up_grad, up_weight, preferred_element_type=jnp.float32
    )
    scaled = lax.psum(partial_grad, ("latent", "hidden")) * norm_gain
    inner_row = jnp.sum(scaled * rebuilt, axis=1, keepdims=True)
    inverse_cube = inverse * inverse * inverse
    rebuilt_grad = (
        inverse * scaled - inverse_cube * rebuilt * (inner_row / model_width) + (rebuilt - target)
    ).astype(jnp.bfloat16)
    latent_grad = lax.dot_general(
        rebuilt_grad, dictionary, ACROSS, preferred_element_type=jnp.float32
    )
    preact_grad = jnp.where(preact > 0.0, latent_grad, 0.0).astype(jnp.bfloat16)
    dictionary_grad = lax.dot_general(
        latents, rebuilt_grad, DOWNWARD, preferred_element_type=jnp.float32
    ) + lax.dot_general(preact_grad, inputs, DOWNWARD, preferred_element_type=jnp.float32)
    return (block_output, dictionary_grad.astype(jnp.bfloat16))


def solution(mesh):
    in_specs = (
        P("groups", ("latent", "hidden")),
        P("groups", ("latent", "hidden")),
        P(("latent", "hidden"), None),
        P(("latent", "hidden")),
        P(),
        P(),
        P(("latent", "hidden"), None),
        P(("latent", "hidden"), None),
        P(("latent", "hidden"), None),
    )
    out_specs = (P("groups", ("latent", "hidden")), P(("latent", "hidden"), "groups"))
    return jax.shard_map(
        per_device, mesh=mesh, in_specs=in_specs, out_specs=out_specs, check_vma=False
    )
```

```python
import functools
import math

import jax
import jax.numpy as jnp
from jax import lax
from jax.experimental import pallas as pl
from jax.experimental.pallas import tpu as pltpu
from jax.sharding import PartitionSpec as P

CODE_STEP = 2.0 ** (-6)
NORM_EPSILON = 1e-06
GELU_ROOT = 0.7978845608028654
GELU_CUBIC = 0.044715
ACROSS = (((1,), (1,)), ((), ()))
DOWNWARD = (((0,), (0,)), ((), ()))
LANES = 128
ROW_TILE = 16
DIRECT_LIMIT = 16
VMEM_BYTES = 24 * 1024 * 1024
VMEM_BRING = 53 * 1024 * 1024
F32 = jnp.float32
BF16 = jnp.bfloat16


def gelu_parts(values):
    argument = GELU_ROOT * (values + GELU_CUBIC * values * values * values)
    tanh_value = jnp.tanh(argument)
    result = 0.5 * values * (1.0 + tanh_value)
    derivative = 0.5 * (1.0 + tanh_value) + 0.5 * values * (
        1.0 - tanh_value * tanh_value
    ) * GELU_ROOT * (1.0 + 3.0 * GELU_CUBIC * values * values)
    return (result, derivative)


def up_to(value, unit):
    return -(-value // unit) * unit


def chips_fit(chips):
    return 2 <= chips <= DIRECT_LIMIT and chips & (chips - 1) == 0


class Plan:
    def __init__(self, chips, cores, rows, own):
        self.chips, self.cores, self.rows, self.own = chips, cores, rows, own
        self.width = own * chips * cores
        self.half = self.width // cores
        self.tiles = self.half // LANES
        self.chunk = up_to(-(-self.tiles * rows // chips), ROW_TILE)
        self.flat = self.chunk * chips
        self.tail = own - LANES
        if self.tail > 0:
            self.fold_rows = min(
                size
                for size in range(ROW_TILE, rows + ROW_TILE, ROW_TILE)
                if -(-rows // size) * self.tail <= LANES
            )
            self.packed = rows + self.fold_rows
        self.columns = list(range(0, chips, 2))

    def side_blocks(self, refs):
        me = lax.axis_index("latent")
        stack_ref, *crossed_refs = refs
        for place, column in enumerate(self.columns):
            yield me ^ column, stack_ref[place]
        places = iter(self.columns)
        for ref in crossed_refs:
            for place in range(ref.shape[0]):
                yield me ^ next(places) ^ 1, ref[place]

    def pieces(self):
        for tile in range(self.tiles):
            row = 0
            while row < self.rows:
                chip, place = divmod(tile * self.rows + row, self.chunk)
                count = min(self.rows - row, self.chunk - place)
                yield tile, chip, place, row, count
                row += count

    def fits(self):
        return (
            self.cores == 2
            and chips_fit(self.chips)
            and self.rows % ROW_TILE == 0
            and self.half % LANES == 0
            and 0 < self.tail < LANES
        )


HBM = pl.BlockSpec(memory_space=pltpu.HBM)
ONCHIP = pl.BlockSpec(memory_space=pltpu.VMEM)


def shaped(*dims, dtype=F32):
    return jax.ShapeDtypeStruct(dims, dtype)


HBM = pl.BlockSpec(memory_space=pltpu.HBM)
ONCHIP = pl.BlockSpec(memory_space=pltpu.VMEM)


def shaped(*dims, dtype=F32):
    return jax.ShapeDtypeStruct(dims, dtype)


def call(body, out_shapes, operands, scratch=(), out_specs=None, flops=0, moved=0):
    return pl.pallas_call(
        body,
        out_shape=out_shapes,
        in_specs=[ONCHIP] * len(operands),
        out_specs=jax.tree.map(lambda _: ONCHIP, out_shapes) if out_specs is None else out_specs,
        scratch_shapes=list(scratch),
        compiler_params=pltpu.CompilerParams(vmem_limit_bytes=VMEM_BYTES),
        cost_estimate=pl.CostEstimate(flops=flops, bytes_accessed=moved, transcendentals=0),
    )(*operands)


def padded_bytes(array):
    *lead, rows, columns = array.shape
    item = jnp.dtype(array.dtype).itemsize
    return math.prod(lead) * up_to(rows, ROW_TILE) * up_to(columns, LANES) * item


def copies(sources, targets, sems):
    started = []
    for index, (source, target) in enumerate(zip(sources, targets)):
        one = pltpu.make_async_copy(source, target, sems.at[index])
        one.start()
        started.append(one)
    return started


def pack_block(plan, block):
    tail = block[:, LANES:]
    folded = []
    for start in range(0, plan.rows, plan.fold_rows):
        piece = tail[start : min(start + plan.fold_rows, plan.rows), :]
        short = plan.fold_rows - piece.shape[0]
        if short:
            piece = jnp.concatenate([piece, jnp.zeros((short, plan.tail), block.dtype)], axis=0)
        folded.append(piece)
    fill = LANES - len(folded) * plan.tail
    if fill:
        folded.append(jnp.zeros((plan.fold_rows, fill), block.dtype))
    return block[:, :LANES], jnp.concatenate(folded, axis=1)


def unpack_block(plan, packed):
    pieces = []
    for fold, start in enumerate(range(0, plan.rows, plan.fold_rows)):
        count = min(plan.fold_rows, plan.rows - start)
        pieces.append(
            packed[plan.rows : plan.rows + count, fold * plan.tail : (fold + 1) * plan.tail]
        )
    return jnp.concatenate([packed[: plan.rows, :], jnp.concatenate(pieces, axis=0)], axis=1)


def pack_values_body(plan, values_ref, block_ref, both_ref):
    for index in range(values_ref.shape[0]):
        main, tail = pack_block(plan, values_ref[index].astype(F32))
        start = index * plan.packed
        both_ref[0, start : start + plan.rows, :] = main.astype(BF16)
        both_ref[0, start + plan.rows : start + plan.packed, :] = tail.astype(BF16)
    block_ref[...] = both_ref[:, : plan.packed, :]


def pack_values(plan, values):
    count = values.shape[0]
    return call(
        functools.partial(pack_values_body, plan),
        [
            shaped(1, plan.packed, LANES, dtype=BF16),
            shaped(1, count * plan.packed, LANES, dtype=BF16),
        ],
        (values,),
        moved=values.size * 6,
    )


def assemble(plan, own_refs, other_refs, both, full_ref):
    core = lax.axis_index("hidden")
    for side, refs in ((core, own_refs), (1 - core, other_refs)):
        for chip, block in plan.side_blocks(refs):
            both[side, chip] = block
    for chip in range(plan.chips):
        for side in range(plan.cores):
            column = (chip * plan.cores + side) * plan.own
            block = unpack_block(plan, both[side, chip].astype(F32))
            full_ref[:, column : column + plan.own] = block.astype(BF16)


def both_scratch(plan, dtype=BF16):
    return pltpu.VMEM((plan.cores, plan.chips, plan.packed, LANES), dtype)


def chunk_scratch(plan):
    return pltpu.VMEM((plan.chips, plan.chunk, LANES), F32)


def side_shapes(plan, dtype=F32):
    return [shaped(len(plan.columns), plan.chunk, LANES, dtype=dtype)] * 2


def half_product(plan, pairs, side, kept_ref, sent_ref, target, gain_ref=None, bias_ref=None):
    span = pl.ds(pl.multiple_of(side * plan.half, LANES), plan.half)
    total = None
    for left, right_ref in pairs:
        term = jnp.dot(left, right_ref[:, span], preferred_element_type=F32)
        total = term if total is None else total + term
    if bias_ref is not None:
        total = total + bias_ref[:, span] * jnp.where(lax.axis_index("latent") == 0, 1.0, 0.0)
    if gain_ref is not None:
        total = total * gain_ref[:, span]
    for tile, chip, place, row, count in plan.pieces():
        target[chip, place : place + count, :] = total[
            row : row + count, tile * LANES : (tile + 1) * LANES
        ]
    used = plan.tiles * plan.rows
    while used < plan.flat:
        chip, place = divmod(used, plan.chunk)
        target[chip, place:, :] = jnp.zeros((plan.chunk - place, LANES), F32)
        used += plan.chunk - place
    me = lax.axis_index("latent")
    for place, column in enumerate(plan.columns):
        kept_ref[place] = target[me ^ column]
        sent_ref[place] = target[me ^ column ^ 1]


def bring_encoder_body(dict_hbm, vectors_hbm, dict_ref, bias_ref, decoder_ref, gain_ref, sems):
    sources, targets = [dict_hbm], [dict_ref]
    start = 0
    for target in (bias_ref, decoder_ref, gain_ref):
        sources.append(vectors_hbm.at[:, start : start + target.shape[1]])
        targets.append(target)
        start += target.shape[1]
    for copy in copies(sources, targets, sems):
        copy.wait()


def bring_encoder(plan, dictionary, vectors):
    outputs = [
        shaped(*dictionary.shape, dtype=BF16),
        shaped(1, dictionary.shape[0]),
        shaped(1, plan.width),
        shaped(1, plan.width),
    ]
    return pl.pallas_call(
        bring_encoder_body,
        out_shape=outputs,
        in_specs=[HBM] * 2,
        out_specs=[ONCHIP] * len(outputs),
        scratch_shapes=[pltpu.SemaphoreType.DMA((len(outputs),))],
        compiler_params=pltpu.CompilerParams(
            vmem_limit_bytes=VMEM_BRING - sum(map(padded_bytes, outputs))
        ),
        cost_estimate=pl.CostEstimate(
            flops=0, bytes_accessed=dictionary.size * 4, transcendentals=0
        ),
    )(dictionary, vectors)


def encode_body(plan, *refs):
    own, other, (dict_ref, bias_ref, gain_ref) = refs[:2], refs[2:4], refs[4:7]
    inputs_ref, latents_ref, kept_ref, sent_ref, both, target = refs[7:]
    assemble(plan, own, other, both, inputs_ref)
    preact = (
        lax.dot_general(inputs_ref[...], dict_ref[...], ACROSS, preferred_element_type=F32)
        + bias_ref[...]
    )
    latents = jnp.maximum(preact, 0.0).astype(BF16)
    latents_ref[...] = latents
    theirs = 1 - lax.axis_index("hidden")
    half_product(plan, [(latents, dict_ref)], theirs, kept_ref, sent_ref, target, gain_ref)


def encode(plan, own, other, dictionary, encoder_bias, gain):
    latents = dictionary.shape[0]
    return call(
        functools.partial(encode_body, plan),
        [
            shaped(plan.rows, plan.width, dtype=BF16),
            shaped(plan.rows, latents, dtype=BF16),
            *side_shapes(plan),
        ],
        (*own, *other, dictionary, encoder_bias, gain),
        [both_scratch(plan), chunk_scratch(plan)],
        flops=3 * plan.rows * plan.width * latents,
        moved=dictionary.size * 2,
    )


def decode_own_body(plan, latents_ref, dict_ref, decoder_ref, gain_ref, kept_ref, sent_ref, target):
    pairs = [(latents_ref[...], dict_ref)]
    mine = lax.axis_index("hidden")
    half_product(plan, pairs, mine, kept_ref, sent_ref, target, gain_ref, decoder_ref)


def decode_own(plan, latents, dictionary, decoder_bias, gain):
    return call(
        functools.partial(decode_own_body, plan),
        side_shapes(plan),
        (latents, dictionary, decoder_bias, gain),
        [chunk_scratch(plan)],
        flops=plan.rows * plan.width * dictionary.shape[0],
        moved=dictionary.size,
    )


def back_project_body(plan, *refs):
    own, other, (down_ref, grad_ref, both, full) = refs[:2], refs[2:4], refs[4:]
    assemble(plan, own, other, both, full)
    grad_ref[...] = lax.dot_general(
        full[...], down_ref[...], ACROSS, preferred_element_type=F32
    )


def back_project(plan, own, other, down_weight):
    units = down_weight.shape[0]
    return call(
        functools.partial(back_project_body, plan),
        shaped(plan.rows, units),
        (*own, *other, down_weight),
        [both_scratch(plan), pltpu.VMEM((plan.rows, plan.width), BF16)],
        flops=2 * plan.rows * plan.width * units,
        moved=down_weight.size * 2,
    )


def join_half(plan, source, first, full_ref):
    for tile, chip, place, row, count in plan.pieces():
        column = pl.multiple_of(first + tile * LANES, LANES)
        full_ref[row : row + count, pl.ds(column, LANES)] = source[
            chip, place : place + count, :
        ]


def half_terms(plan, half, side, gate_ref, up_ref, gain_ref):
    span = pl.ds(pl.multiple_of(side * plan.half, LANES), plan.half)
    rebuilt = half.astype(F32) / gain_ref[:, span]
    squares = jnp.sum(rebuilt * rebuilt, axis=1, keepdims=True)
    gate = lax.dot_general(half, gate_ref[:, span], ACROSS, preferred_element_type=F32)
    up = lax.dot_general(half, up_ref[:, span], ACROSS, preferred_element_type=F32)
    return squares, gate, up


def mlp_first_body(plan, own_ref, gate_ref, up_ref, gain_ref, half_ref, squares_ref, gate_part_ref, up_part_ref):
    join_half(plan, own_ref, 0, half_ref)
    squares_ref[...], gate_part_ref[...], up_part_ref[...] = half_terms(
        plan, half_ref[...], lax.axis_index("hidden"), gate_ref, up_ref, gain_ref
    )


def mlp_first(plan, own, gate_weight, up_weight, gain):
    units = gate_weight.shape[0]
    return call(
        functools.partial(mlp_first_body, plan),
        [
            shaped(plan.rows, plan.half, dtype=BF16),
            shaped(plan.rows, 1),
            shaped(plan.rows, units),
            shaped(plan.rows, units),
        ],
        (own, gate_weight, up_weight, gain),
        flops=2 * plan.rows * plan.width * units,
        moved=gate_weight.size * 4,
    )


def mlp_body(plan, other_ref, gate_ref, up_ref, gain_ref, grad_ref, half_ref, squares_ref, gate_part_ref, up_part_ref, scaled_ref, inverse_ref, hidden_ref, gate_grad_ref, up_grad_ref, kept_ref, sent_ref, target):
    core = lax.axis_index("hidden")
    join_half(plan, other_ref, (1 - core) * plan.half, scaled_ref)
    other_span = pl.ds(pl.multiple_of((1 - core) * plan.half, LANES), plan.half)
    own_span = pl.ds(pl.multiple_of(core * plan.half, LANES), plan.half)
    scaled_ref[:, own_span] = half_ref[...]
    squares, gate, up = half_terms(
        plan, scaled_ref[:, other_span], 1 - core, gate_ref, up_ref, gain_ref
    )
    inverse = lax.rsqrt((squares + squares_ref[...]) / plan.width + NORM_EPSILON)
    inverse_ref[...] = inverse
    gate_proj = inverse * (gate + gate_part_ref[...])
    up_proj = inverse * (up + up_part_ref[...])
    gelu_value, gelu_slope = gelu_parts(gate_proj)
    hidden_ref[...] = (gelu_value * up_proj).astype(BF16)
    hidden_grad = grad_ref[...]
    gate_grad = (hidden_grad * up_proj * gelu_slope).astype(BF16)
    up_grad = (hidden_grad * gelu_value).astype(BF16)
    gate_grad_ref[...] = gate_grad
    up_grad_ref[...] = up_grad
    pairs = [(gate_grad, gate_ref), (up_grad, up_ref)]
    half_product(plan, pairs, 1 - core, kept_ref, sent_ref, target)


def mlp(plan, other, gate_weight, up_weight, gain, hidden_grad, first):
    units = gate_weight.shape[0]
    return call(
        functools.partial(mlp_body, plan),
        [
            shaped(plan.rows, plan.width, dtype=BF16),
            shaped(plan.rows, 1),
            shaped(plan.rows, units, dtype=BF16),
            shaped(plan.rows, units, dtype=BF16),
            shaped(plan.rows, units, dtype=BF16),
            *side_shapes(plan),
        ],
        (other, gate_weight, up_weight, gain, hidden_grad, *first),
        [chunk_scratch(plan)],
        flops=6 * plan.rows * plan.width * units,
        moved=gate_weight.size * 4,
    )


def mlp_own_body(plan, gate_grad_ref, up_grad_ref, gate_ref, up_ref, kept_ref, sent_ref, target):
    pairs = [(gate_grad_ref[...], gate_ref), (up_grad_ref[...], up_ref)]
    half_product(plan, pairs, lax.axis_index("hidden"), kept_ref, sent_ref, target)


def mlp_own(plan, gate_grad, up_grad, gate_weight, up_weight):
    return call(
        functools.partial(mlp_own_body, plan),
        side_shapes(plan),
        (gate_grad, up_grad, gate_weight, up_weight),
        [chunk_scratch(plan)],
        flops=2 * plan.rows * plan.width * gate_weight.shape[0],
        moved=gate_weight.size * 2,
    )


def project_body(plan, hidden_ref, down_ref, mine_ref, theirs_ref, both):
    core = lax.axis_index("hidden")
    terms = jnp.dot(hidden_ref[...], down_ref[...], preferred_element_type=F32)
    for chip in range(plan.chips):
        for side in range(plan.cores):
            start = (chip * plan.cores + side) * plan.own
            main, tail = pack_block(plan, terms[:, start : start + plan.own])
            both[side, chip, : plan.rows, :] = main
            both[side, chip, plan.rows :, :] = tail
    mine_ref[...] = both[core]
    theirs_ref[...] = both[1 - core]


def project(plan, hidden, down_weight):
    units = down_weight.shape[0]
    shape = (plan.chips, plan.packed, LANES)
    return call(
        functools.partial(project_body, plan),
        [shaped(*shape)] * 2,
        (hidden, down_weight),
        [both_scratch(plan, F32)],
        flops=2 * plan.rows * plan.width * units,
        moved=down_weight.size * 2,
    )


def add_pair_body(plan, mine_ref, theirs_ref, kept_ref, sent_ref):
    me = lax.axis_index("latent")
    for place, column in enumerate(plan.columns):
        kept, sent = me ^ column, me ^ column ^ 1
        kept_ref[place] = mine_ref[kept] + theirs_ref[kept]
        sent_ref[place] = (mine_ref[sent] + theirs_ref[sent]).astype(BF16)


def add_pair(plan, mine, theirs):
    count, dims = len(plan.columns), mine.shape[1:]
    return call(
        functools.partial(add_pair_body, plan),
        [shaped(count, *dims), shaped(count, *dims, dtype=BF16)],
        (mine, theirs),
        moved=mine.size * 10,
    )


def add_sent_body(mine_ref, theirs_ref, first_ref, rest_ref):
    total = (mine_ref[...] + theirs_ref[...]).astype(BF16)
    first_ref[...] = total[:1]
    rest_ref[...] = total[1:]


def add_sent(plan, mine, theirs):
    count, *dims = mine.shape
    return call(
        add_sent_body,
        [shaped(1, *dims, dtype=BF16), shaped(count - 1, *dims, dtype=BF16)],
        (mine, theirs),
        moved=mine.size * 10,
    )


def add_across_body(mine_ref, theirs_ref, got_ref, *sent_refs):
    for place, out_ref in enumerate(sent_refs):
        total = mine_ref[1 + place] + theirs_ref[1 + place] + got_ref[place].astype(F32)
        out_ref[0] = total.astype(BF16)


def add_across(plan, mine, theirs, got):
    return call(
        add_across_body,
        [shaped(1, *mine.shape[1:], dtype=BF16)] * got.shape[0],
        (mine, theirs, got),
        moved=mine.size * 10,
    )


def column_total(mine_ref, theirs_ref, *refs):
    total = mine_ref[0] + theirs_ref[0]
    for ref in refs:
        total = total + ref[0].astype(F32)
    return total.astype(BF16)


def add_column_body(*refs):
    refs[-1][0] = column_total(*refs[:-1])


def add_column(plan, mine, theirs, first, got):
    return call(
        add_column_body,
        shaped(1, *mine.shape[1:], dtype=BF16),
        (mine, theirs, *reversed(got), first),
        moved=mine.size * 8,
    )


def add_with_output_body(plan, count, *refs):
    total = column_total(*refs[:count])
    kept_ref, crossed_ref, block_ref, own_ref = refs[count : count + 4]
    block_ref[0] = total
    own_ref[0] = kept_ref[0] + crossed_ref[0].astype(F32)
    for place, both_ref in enumerate(refs[count + 4 :], 1):
        both_ref[0, : plan.chunk, :] = total
        both_ref[0, plan.chunk :, :] = (
            kept_ref[place] + crossed_ref[place].astype(F32)
        ).astype(BF16)


def add_with_output(plan, mine, theirs, first, got, kept, crossed):
    both = shaped(1, plan.chunk + plan.packed, LANES, dtype=BF16)
    block, out_own, *messages = call(
        functools.partial(add_with_output_body, plan, 3 + len(got)),
        [shaped(1, plan.chunk, LANES, dtype=BF16), shaped(1, plan.packed, LANES)]
        + [both] * (len(plan.columns) - 1),
        (mine, theirs, *reversed(got), first, kept, crossed),
        moved=mine.size * 12,
    )
    return block, out_own, messages


def stack_body(places, *refs):
    *sources, stack_ref, rest_ref = refs
    rows = stack_ref.shape[1]
    for place, ref in zip(places, sources):
        stack_ref[place] = ref[0, :rows, :]
        if place:
            rest_ref[place - 1] = ref[0, :rows, :]


def stack_up(plan, block, got, backwards=False):
    dims = block.shape[1:]
    operands = [block, *got]
    places = list(range(len(operands)))
    if backwards:
        operands, places = operands[::-1], places[::-1]
    return call(
        functools.partial(stack_body, places),
        [shaped(1 + len(got), *dims, dtype=BF16), shaped(len(got), *dims, dtype=BF16)],
        operands,
        moved=block.size * 16,
    )


def stack_second_body(rows, *refs):
    for place, ref in enumerate(refs[:-1]):
        refs[-1][place] = ref[0, rows:, :]


def stack_second(plan, rows, messages):
    return call(
        functools.partial(stack_second_body, rows),
        shaped(len(messages), messages[0].shape[1] - rows, LANES, dtype=BF16),
        messages,
        moved=messages[0].size * 16,
    )


def line_up_body(plan, *refs):
    for chip, block in plan.side_blocks(refs[:-1]):
        refs[-1][chip] = block


def line_up(plan, stack, *crossed):
    return call(
        functools.partial(line_up_body, plan),
        shaped(plan.chips, *stack.shape[1:], dtype=BF16),
        (stack, *crossed),
        moved=stack.size * 8,
    )


def finish_output_body(plan, own_ref, *refs):
    total = own_ref[0]
    for ref in refs[:-1]:
        total = total + ref[0, plan.chunk :, :].astype(F32)
    refs[-1][...] = unpack_block(plan, total).astype(BF16)


def finish_output(plan, own, messages):
    return call(
        functools.partial(finish_output_body, plan),
        shaped(plan.rows, plan.own, dtype=BF16),
        (own, *reversed(messages)),
        moved=own.size * 8,
    )


def dictionary_body(plan, pieces, own_ref, other_ref, gain_ref, inverse_ref, scaled_ref, inputs_ref, latents_ref, dict_ref, out_hbm, full, out_ref, out_sems):
    core = lax.axis_index("hidden")
    join_half(plan, own_ref, core * plan.half, full)
    join_half(plan, other_ref, (1 - core) * plan.half, full)
    grad = full[...].astype(F32)
    gain = gain_ref[...]
    scaled_rebuilt = scaled_ref[...].astype(F32)
    rebuilt = scaled_rebuilt / gain
    inverse = inverse_ref[...]
    inner_row = jnp.sum(grad * scaled_rebuilt, axis=1, keepdims=True)
    inverse_cube = inverse * inverse * inverse
    inputs = inputs_ref[...]
    rebuilt_grad = (
        inverse * (grad * gain)
        - (inverse_cube * (inner_row / plan.width)) * rebuilt
        + (rebuilt - inputs.astype(F32))
    ).astype(BF16)
    latents = latents_ref[...]
    latent_grad = lax.dot_general(
        rebuilt_grad, dict_ref[...], ACROSS, preferred_element_type=F32
    )
    preact_grad = jnp.where(latents.astype(F32) > 0.0, latent_grad, 0.0).astype(BF16)
    left = jnp.concatenate([latents, preact_grad], axis=0)
    right = jnp.concatenate([rebuilt_grad, inputs], axis=0)
    size = plan.width // pieces
    writes = []
    for piece in range(pieces):
        span = slice(piece * size, (piece + 1) * size)
        out_ref[:, span] = lax.dot_general(
            left, right[:, span], DOWNWARD, preferred_element_type=F32
        ).astype(BF16)
        one = pltpu.make_async_copy(
            out_ref.at[:, span], out_hbm.at[:, span], out_sems.at[piece]
        )
        one.start()
        writes.append(one)
    for one in writes:
        one.wait()


def dictionary_step(plan, own, other, gain, inverse, scaled, inputs, latents, dictionary):
    units = dictionary.shape[0]
    pieces = plan.tiles
    return call(
        functools.partial(dictionary_body, plan, pieces),
        shaped(*dictionary.shape, dtype=BF16),
        (own, other, gain, inverse, scaled, inputs, latents, dictionary),
        [
            pltpu.VMEM((plan.rows, plan.width), BF16),
            pltpu.VMEM(dictionary.shape, BF16),
            pltpu.SemaphoreType.DMA((pieces,)),
        ],
        out_specs=HBM,
        flops=6 * plan.rows * plan.width * units,
        moved=dictionary.size * 4,
    )


def swap(value):
    size = lax.axis_size("hidden")
    return lax.ppermute(value, "hidden", [(i, (i + 1) % size) for i in range(size)])


def partner_swap(value, bits):
    size = lax.axis_size("latent")
    return lax.ppermute(value, "latent", [(i, i ^ bits) for i in range(size)])


def cross(value):
    return partner_swap(value, 1)


def to_column(plan, blocks):
    pairs = list(zip(blocks, plan.columns[1:]))
    got = [partner_swap(one, column) for one, column in reversed(pairs)]
    return got[::-1]


def to_all_columns(plan, block):
    return [partner_swap(block, column) for column in plan.columns[1:]]


def tie(*values):
    return lax.optimization_barrier(values)


def per_device(
    input_codes,
    cotangent_codes,
    dictionary,
    encoder_bias,
    decoder_bias,
    norm_gain,
    gate_weight,
    up_weight,
    down_weight,
):
    plan = Plan(
        lax.axis_size("latent"), lax.axis_size("hidden"), input_codes.shape[0], input_codes.shape[1]
    )
    if not plan.fits():
        return per_device_plain(
            input_codes,
            cotangent_codes,
            dictionary,
            encoder_bias,
            decoder_bias,
            norm_gain,
            gate_weight,
            up_weight,
            down_weight,
        )
    vectors = jnp.concatenate([encoder_bias, decoder_bias, norm_gain]).reshape(1, -1)
    codes = jnp.stack([input_codes, cotangent_codes])
    values = (codes.astype(F32) * CODE_STEP).astype(BF16)
    block, both = pack_values(plan, values)
    got = to_all_columns(plan, both)
    stack, _ = stack_up(plan, block, got)
    stack, vectors, late_dictionary = tie(stack, vectors, dictionary)
    crossed, stack_other = cross(stack), swap(stack)
    encoder = bring_encoder(plan, late_dictionary, vectors)
    cotangent = stack_second(plan, plan.packed, [both, *got])
    crossed, stack_other, encoder, cotangent = tie(crossed, stack_other, encoder, cotangent)
    brought, bias, decoder, gain = encoder
    inputs, latents, kept, sent = encode(
        plan, (stack, crossed), (stack_other, swap(crossed)), brought, bias, gain
    )
    sent, kept = swap(sent), swap(kept)
    own_kept, own_sent = decode_own(plan, latents, brought, decoder, gain)
    sent_first, sent_rest = add_sent(plan, own_sent, sent)
    sent = add_across(plan, own_kept, kept, cross(sent_rest))
    sent, sent_first, cotangent = tie(sent, sent_first, cotangent)
    cotangent_crossed = cross(cotangent)
    block = add_column(plan, own_kept, kept, cross(sent_first), to_column(plan, sent))
    block, *cotangent_own = tie(block, cotangent, cotangent_crossed)
    hidden_grad = back_project(
        plan, cotangent_own, [swap(one) for one in cotangent_own], down_weight
    )
    stack, _ = stack_up(plan, block, to_all_columns(plan, block))
    crossed, stack_other = cross(stack), swap(stack)
    crossed, stack_other, hidden_grad = tie(crossed, stack_other, hidden_grad)
    terms = mlp_first(plan, line_up(plan, stack, crossed), gate_weight, up_weight, gain)
    scaled_other = line_up(plan, stack_other, swap(crossed))
    scaled, inverse, hidden, gate_grad, up_grad, kept, sent = mlp(
        plan, scaled_other, gate_weight, up_weight, gain, hidden_grad, terms
    )
    sent, kept = swap(sent), swap(kept)
    own_kept, own_sent = mlp_own(plan, gate_grad, up_grad, gate_weight, up_weight)
    out_mine, out_theirs = project(plan, hidden, down_weight)
    sent_first, sent_rest = add_sent(plan, own_sent, sent)
    sent_first, sent_rest, out_mine, out_theirs = tie(sent_first, sent_rest, out_mine, out_theirs)
    crossed = cross(sent_rest)
    out_kept, out_sent = add_pair(plan, out_mine, swap(out_theirs))
    sent = add_across(plan, own_kept, kept, crossed)
    sent, sent_first, out_kept, out_sent = tie(sent, sent_first, out_kept, out_sent)
    got = to_column(plan, sent)
    first = cross(sent_first)
    out_crossed = cross(out_sent)
    block, out_own, messages = add_with_output(
        plan, own_kept, kept, first, got, out_kept, out_crossed
    )
    got, first = tie(to_column(plan, messages), cross(block))
    stack, rest = stack_up(plan, block, got, backwards=True)
    rest, stack_other, first_other = cross(rest), swap(stack), swap(first)
    block_output = finish_output(plan, out_own, got)
    grad_own = line_up(plan, stack, first, rest)
    grad_other = line_up(plan, stack_other, first_other, swap(rest))
    dictionary_grad = dictionary_step(
        plan, grad_own, grad_other, gain, inverse, scaled, inputs, latents, brought
    )
    return (block_output, dictionary_grad)


def per_device_plain(
    input_codes,
    cotangent_codes,
    dictionary,
    encoder_bias,
    decoder_bias,
    norm_gain,
    gate_weight,
    up_weight,
    down_weight,
):
    own_width = input_codes.shape[1]
    model_width = own_width * lax.axis_size(("latent", "hidden"))
    cotangent_local = (cotangent_codes.astype(jnp.float32) * CODE_STEP).astype(jnp.bfloat16)
    inputs_local = (input_codes.astype(jnp.float32) * CODE_STEP).astype(jnp.bfloat16)
    inputs = lax.all_gather(inputs_local, ("latent", "hidden"), axis=1, tiled=True)
    preact = (
        lax.dot_general(inputs, dictionary, ACROSS, preferred_element_type=jnp.float32)
        + encoder_bias
    )
    latents = jnp.maximum(preact, 0.0).astype(jnp.bfloat16)
    partial_value = jnp.dot(latents, dictionary, preferred_element_type=jnp.float32)
    rebuilt = lax.psum(partial_value, ("latent", "hidden")) + decoder_bias
    inverse = lax.rsqrt(
        jnp.sum(rebuilt * rebuilt, axis=1, keepdims=True) / model_width + NORM_EPSILON
    )
    normed = (rebuilt * inverse * norm_gain).astype(jnp.bfloat16)
    target = inputs.astype(jnp.float32)
    gate_proj = lax.dot_general(normed, gate_weight, ACROSS, preferred_element_type=jnp.float32)
    up_proj = lax.dot_general(normed, up_weight, ACROSS, preferred_element_type=jnp.float32)
    gelu_value, gelu_slope = gelu_parts(gate_proj)
    hidden = (gelu_value * up_proj).astype(jnp.bfloat16)
    output_terms = jnp.dot(hidden, down_weight, preferred_element_type=jnp.float32)
    block_output = lax.psum_scatter(
        output_terms, ("latent", "hidden"), scatter_dimension=1, tiled=True
    ).astype(jnp.bfloat16)
    hidden_grad = lax.dot_general(
        lax.all_gather(cotangent_local, ("latent", "hidden"), axis=1, tiled=True),
        down_weight,
        ACROSS,
        preferred_element_type=jnp.float32,
    )
    gate_grad = (hidden_grad * up_proj * gelu_slope).astype(jnp.bfloat16)
    up_grad = (hidden_grad * gelu_value).astype(jnp.bfloat16)
    partial_grad = jnp.dot(gate_grad, gate_weight, preferred_element_type=jnp.float32) + jnp.dot(
        up_grad, up_weight, preferred_element_type=jnp.float32
    )
    scaled = lax.psum(partial_grad, ("latent", "hidden")) * norm_gain
    inner_row = jnp.sum(scaled * rebuilt, axis=1, keepdims=True)
    inverse_cube = inverse * inverse * inverse
    rebuilt_grad = (
        inverse * scaled - inverse_cube * rebuilt * (inner_row / model_width) + (rebuilt - target)
    ).astype(jnp.bfloat16)
    latent_grad = lax.dot_general(
        rebuilt_grad, dictionary, ACROSS, preferred_element_type=jnp.float32
    )
    preact_grad = jnp.where(preact > 0.0, latent_grad, 0.0).astype(jnp.bfloat16)
    dictionary_grad = lax.dot_general(
        latents, rebuilt_grad, DOWNWARD, preferred_element_type=jnp.float32
    ) + lax.dot_general(preact_grad, inputs, DOWNWARD, preferred_element_type=jnp.float32)
    return (block_output, dictionary_grad.astype(jnp.bfloat16))


def solution(mesh):
    in_specs = (
        P("groups", ("latent", "hidden")),
        P("groups", ("latent", "hidden")),
        P(("latent", "hidden"), None),
        P(("latent", "hidden")),
        P(),
        P(),
        P(("latent", "hidden"), None),
        P(("latent", "hidden"), None),
        P(("latent", "hidden"), None),
    )
    out_specs = (P("groups", ("latent", "hidden")), P(("latent", "hidden"), "groups"))
    return jax.shard_map(
        per_device, mesh=mesh, in_specs=in_specs, out_specs=out_specs, check_vma=False
    )
```

```python
import functools
import math

import jax
import jax.numpy as jnp
from jax import lax
from jax.experimental import pallas as pl
from jax.experimental.pallas import tpu as pltpu
from jax.sharding import PartitionSpec as P

CODE_STEP = 2.0 ** (-6)
NORM_EPSILON = 1e-06
GELU_ROOT = 0.7978845608028654
GELU_CUBIC = 0.044715
ACROSS = (((1,), (1,)), ((), ()))
DOWNWARD = (((0,), (0,)), ((), ()))
LANES = 128
ROW_TILE = 16
DIRECT_LIMIT = 16
VMEM_BYTES = 24 * 1024 * 1024
VMEM_BRING = 53 * 1024 * 1024
F32 = jnp.float32
BF16 = jnp.bfloat16


def gelu_parts(values):
    argument = GELU_ROOT * (values + GELU_CUBIC * values * values * values)
    tanh_value = jnp.tanh(argument)
    result = 0.5 * values * (1.0 + tanh_value)
    derivative = 0.5 * (1.0 + tanh_value) + 0.5 * values * (
        1.0 - tanh_value * tanh_value
    ) * GELU_ROOT * (1.0 + 3.0 * GELU_CUBIC * values * values)
    return (result, derivative)


def up_to(value, unit):
    return -(-value // unit) * unit


def chips_fit(chips):
    return 2 <= chips <= DIRECT_LIMIT and chips & (chips - 1) == 0


class Plan:
    def __init__(self, chips, cores, rows, own):
        self.chips, self.cores, self.rows, self.own = chips, cores, rows, own
        self.width = own * chips * cores
        self.half = self.width // cores
        self.tiles = self.half // LANES
        self.chunk = up_to(-(-self.tiles * rows // chips), ROW_TILE)
        self.flat = self.chunk * chips
        self.tail = own - LANES
        if self.tail > 0:
            self.fold_rows = min(
                size
                for size in range(ROW_TILE, rows + ROW_TILE, ROW_TILE)
                if -(-rows // size) * self.tail <= LANES
            )
            self.packed = rows + self.fold_rows
        self.columns = list(range(0, chips, 2))

    def side_blocks(self, refs):
        me = lax.axis_index("latent")
        stack_ref, *crossed_refs = refs
        for place, column in enumerate(self.columns):
            yield me ^ column, stack_ref[place]
        places = iter(self.columns)
        for ref in crossed_refs:
            for place in range(ref.shape[0]):
                yield me ^ next(places) ^ 1, ref[place]

    def pieces(self):
        for tile in range(self.tiles):
            row = 0
            while row < self.rows:
                chip, place = divmod(tile * self.rows + row, self.chunk)
                count = min(self.rows - row, self.chunk - place)
                yield tile, chip, place, row, count
                row += count

    def fits(self):
        return (
            self.cores == 2
            and chips_fit(self.chips)
            and self.rows % ROW_TILE == 0
            and self.half % LANES == 0
            and 0 < self.tail < LANES
        )


HBM = pl.BlockSpec(memory_space=pltpu.HBM)
ONCHIP = pl.BlockSpec(memory_space=pltpu.VMEM)


def shaped(*dims, dtype=F32):
    return jax.ShapeDtypeStruct(dims, dtype)


HBM = pl.BlockSpec(memory_space=pltpu.HBM)
ONCHIP = pl.BlockSpec(memory_space=pltpu.VMEM)


def shaped(*dims, dtype=F32):
    return jax.ShapeDtypeStruct(dims, dtype)


def call(body, out_shapes, operands, scratch=(), out_specs=None, flops=0, moved=0):
    return pl.pallas_call(
        body,
        out_shape=out_shapes,
        in_specs=[ONCHIP] * len(operands),
        out_specs=jax.tree.map(lambda _: ONCHIP, out_shapes) if out_specs is None else out_specs,
        scratch_shapes=list(scratch),
        compiler_params=pltpu.CompilerParams(vmem_limit_bytes=VMEM_BYTES),
        cost_estimate=pl.CostEstimate(flops=flops, bytes_accessed=moved, transcendentals=0),
    )(*operands)


def padded_bytes(array):
    *lead, rows, columns = array.shape
    item = jnp.dtype(array.dtype).itemsize
    return math.prod(lead) * up_to(rows, ROW_TILE) * up_to(columns, LANES) * item


def copies(sources, targets, sems):
    started = []
    for index, (source, target) in enumerate(zip(sources, targets)):
        one = pltpu.make_async_copy(source, target, sems.at[index])
        one.start()
        started.append(one)
    return started


def pack_block(plan, block):
    tail = block[:, LANES:]
    folded = []
    for start in range(0, plan.rows, plan.fold_rows):
        piece = tail[start : min(start + plan.fold_rows, plan.rows), :]
        short = plan.fold_rows - piece.shape[0]
        if short:
            piece = jnp.concatenate([piece, jnp.zeros((short, plan.tail), block.dtype)], axis=0)
        folded.append(piece)
    fill = LANES - len(folded) * plan.tail
    if fill:
        folded.append(jnp.zeros((plan.fold_rows, fill), block.dtype))
    return block[:, :LANES], jnp.concatenate(folded, axis=1)


def unpack_block(plan, packed):
    pieces = []
    for fold, start in enumerate(range(0, plan.rows, plan.fold_rows)):
        count = min(plan.fold_rows, plan.rows - start)
        pieces.append(
            packed[plan.rows : plan.rows + count, fold * plan.tail : (fold + 1) * plan.tail]
        )
    return jnp.concatenate([packed[: plan.rows, :], jnp.concatenate(pieces, axis=0)], axis=1)


def pack_values_body(plan, values_ref, block_ref, both_ref):
    for index in range(values_ref.shape[0]):
        main, tail = pack_block(plan, values_ref[index].astype(F32))
        start = index * plan.packed
        both_ref[0, start : start + plan.rows, :] = main.astype(BF16)
        both_ref[0, start + plan.rows : start + plan.packed, :] = tail.astype(BF16)
    block_ref[...] = both_ref[:, : plan.packed, :]


def pack_values(plan, values):
    count = values.shape[0]
    return call(
        functools.partial(pack_values_body, plan),
        [
            shaped(1, plan.packed, LANES, dtype=BF16),
            shaped(1, count * plan.packed, LANES, dtype=BF16),
        ],
        (values,),
        moved=values.size * 6,
    )


def assemble(plan, own_refs, other_refs, both, full_ref):
    core = lax.axis_index("hidden")
    for side, refs in ((core, own_refs), (1 - core, other_refs)):
        for chip, block in plan.side_blocks(refs):
            both[side, chip] = block
    for chip in range(plan.chips):
        for side in range(plan.cores):
            column = (chip * plan.cores + side) * plan.own
            block = unpack_block(plan, both[side, chip].astype(F32))
            full_ref[:, column : column + plan.own] = block.astype(BF16)


def both_scratch(plan, dtype=BF16):
    return pltpu.VMEM((plan.cores, plan.chips, plan.packed, LANES), dtype)


def chunk_scratch(plan):
    return pltpu.VMEM((plan.chips, plan.chunk, LANES), F32)


def side_shapes(plan, dtype=F32):
    return [shaped(len(plan.columns), plan.chunk, LANES, dtype=dtype)] * 2


def half_product(plan, pairs, side, kept_ref, sent_ref, target, gain_ref=None, bias_ref=None):
    span = pl.ds(pl.multiple_of(side * plan.half, LANES), plan.half)
    total = None
    for left, right_ref in pairs:
        term = jnp.dot(left, right_ref[:, span], preferred_element_type=F32)
        total = term if total is None else total + term
    if bias_ref is not None:
        total = total + bias_ref[:, span] * jnp.where(lax.axis_index("latent") == 0, 1.0, 0.0)
    if gain_ref is not None:
        total = total * gain_ref[:, span]
    for tile, chip, place, row, count in plan.pieces():
        target[chip, place : place + count, :] = total[
            row : row + count, tile * LANES : (tile + 1) * LANES
        ]
    used = plan.tiles * plan.rows
    while used < plan.flat:
        chip, place = divmod(used, plan.chunk)
        target[chip, place:, :] = jnp.zeros((plan.chunk - place, LANES), F32)
        used += plan.chunk - place
    me = lax.axis_index("latent")
    for place, column in enumerate(plan.columns):
        kept_ref[place] = target[me ^ column]
        sent_ref[place] = target[me ^ column ^ 1]


def bring_encoder_body(dict_hbm, vectors_hbm, dict_ref, bias_ref, decoder_ref, gain_ref, sems):
    sources, targets = [dict_hbm], [dict_ref]
    start = 0
    for target in (bias_ref, decoder_ref, gain_ref):
        sources.append(vectors_hbm.at[:, start : start + target.shape[1]])
        targets.append(target)
        start += target.shape[1]
    for copy in copies(sources, targets, sems):
        copy.wait()


def bring_encoder(plan, dictionary, vectors):
    outputs = [
        shaped(*dictionary.shape, dtype=BF16),
        shaped(1, dictionary.shape[0]),
        shaped(1, plan.width),
        shaped(1, plan.width),
    ]
    return pl.pallas_call(
        bring_encoder_body,
        out_shape=outputs,
        in_specs=[HBM] * 2,
        out_specs=[ONCHIP] * len(outputs),
        scratch_shapes=[pltpu.SemaphoreType.DMA((len(outputs),))],
        compiler_params=pltpu.CompilerParams(
            vmem_limit_bytes=VMEM_BRING - sum(map(padded_bytes, outputs))
        ),
        cost_estimate=pl.CostEstimate(
            flops=0, bytes_accessed=dictionary.size * 4, transcendentals=0
        ),
    )(dictionary, vectors)


def encode_body(plan, *refs):
    own, other, (dict_ref, bias_ref, gain_ref) = refs[:2], refs[2:4], refs[4:7]
    inputs_ref, latents_ref, kept_ref, sent_ref, both, target = refs[7:]
    assemble(plan, own, other, both, inputs_ref)
    preact = (
        lax.dot_general(inputs_ref[...], dict_ref[...], ACROSS, preferred_element_type=F32)
        + bias_ref[...]
    )
    latents = jnp.maximum(preact, 0.0).astype(BF16)
    latents_ref[...] = latents
    theirs = 1 - lax.axis_index("hidden")
    half_product(plan, [(latents, dict_ref)], theirs, kept_ref, sent_ref, target, gain_ref)


def encode(plan, own, other, dictionary, encoder_bias, gain):
    latents = dictionary.shape[0]
    return call(
        functools.partial(encode_body, plan),
        [
            shaped(plan.rows, plan.width, dtype=BF16),
            shaped(plan.rows, latents, dtype=BF16),
            *side_shapes(plan),
        ],
        (*own, *other, dictionary, encoder_bias, gain),
        [both_scratch(plan), chunk_scratch(plan)],
        flops=3 * plan.rows * plan.width * latents,
        moved=dictionary.size * 2,
    )


def decode_own_body(plan, latents_ref, dict_ref, decoder_ref, gain_ref, kept_ref, sent_ref, target):
    pairs = [(latents_ref[...], dict_ref)]
    mine = lax.axis_index("hidden")
    half_product(plan, pairs, mine, kept_ref, sent_ref, target, gain_ref, decoder_ref)


def decode_own(plan, latents, dictionary, decoder_bias, gain):
    return call(
        functools.partial(decode_own_body, plan),
        side_shapes(plan),
        (latents, dictionary, decoder_bias, gain),
        [chunk_scratch(plan)],
        flops=plan.rows * plan.width * dictionary.shape[0],
        moved=dictionary.size,
    )


def back_project_body(plan, *refs):
    own, other, (down_ref, grad_ref, both, full) = refs[:2], refs[2:4], refs[4:]
    assemble(plan, own, other, both, full)
    grad_ref[...] = lax.dot_general(
        full[...], down_ref[...], ACROSS, preferred_element_type=F32
    )


def back_project(plan, own, other, down_weight):
    units = down_weight.shape[0]
    return call(
        functools.partial(back_project_body, plan),
        shaped(plan.rows, units),
        (*own, *other, down_weight),
        [both_scratch(plan), pltpu.VMEM((plan.rows, plan.width), BF16)],
        flops=2 * plan.rows * plan.width * units,
        moved=down_weight.size * 2,
    )


def join_half(plan, source, first, full_ref):
    for tile, chip, place, row, count in plan.pieces():
        column = pl.multiple_of(first + tile * LANES, LANES)
        full_ref[row : row + count, pl.ds(column, LANES)] = source[
            chip, place : place + count, :
        ]


def half_terms(plan, half, side, gate_ref, up_ref, gain_ref):
    span = pl.ds(pl.multiple_of(side * plan.half, LANES), plan.half)
    rebuilt = half.astype(F32) / gain_ref[:, span]
    squares = jnp.sum(rebuilt * rebuilt, axis=1, keepdims=True)
    gate = lax.dot_general(half, gate_ref[:, span], ACROSS, preferred_element_type=F32)
    up = lax.dot_general(half, up_ref[:, span], ACROSS, preferred_element_type=F32)
    return squares, gate, up


def mlp_first_body(plan, own_ref, gate_ref, up_ref, gain_ref, half_ref, squares_ref, gate_part_ref, up_part_ref):
    join_half(plan, own_ref, 0, half_ref)
    squares_ref[...], gate_part_ref[...], up_part_ref[...] = half_terms(
        plan, half_ref[...], lax.axis_index("hidden"), gate_ref, up_ref, gain_ref
    )


def mlp_first(plan, own, gate_weight, up_weight, gain):
    units = gate_weight.shape[0]
    return call(
        functools.partial(mlp_first_body, plan),
        [
            shaped(plan.rows, plan.half, dtype=BF16),
            shaped(plan.rows, 1),
            shaped(plan.rows, units),
            shaped(plan.rows, units),
        ],
        (own, gate_weight, up_weight, gain),
        flops=2 * plan.rows * plan.width * units,
        moved=gate_weight.size * 4,
    )


def mlp_body(plan, other_ref, gate_ref, up_ref, gain_ref, grad_ref, half_ref, squares_ref, gate_part_ref, up_part_ref, scaled_ref, inverse_ref, hidden_ref, gate_grad_ref, up_grad_ref, kept_ref, sent_ref, target):
    core = lax.axis_index("hidden")
    join_half(plan, other_ref, (1 - core) * plan.half, scaled_ref)
    other_span = pl.ds(pl.multiple_of((1 - core) * plan.half, LANES), plan.half)
    own_span = pl.ds(pl.multiple_of(core * plan.half, LANES), plan.half)
    scaled_ref[:, own_span] = half_ref[...]
    squares, gate, up = half_terms(
        plan, scaled_ref[:, other_span], 1 - core, gate_ref, up_ref, gain_ref
    )
    inverse = lax.rsqrt((squares + squares_ref[...]) / plan.width + NORM_EPSILON)
    inverse_ref[...] = inverse
    gate_proj = inverse * (gate + gate_part_ref[...])
    up_proj = inverse * (up + up_part_ref[...])
    gelu_value, gelu_slope = gelu_parts(gate_proj)
    hidden_ref[...] = (gelu_value * up_proj).astype(BF16)
    hidden_grad = grad_ref[...]
    gate_grad = (hidden_grad * up_proj * gelu_slope).astype(BF16)
    up_grad = (hidden_grad * gelu_value).astype(BF16)
    gate_grad_ref[...] = gate_grad
    up_grad_ref[...] = up_grad
    pairs = [(gate_grad, gate_ref), (up_grad, up_ref)]
    half_product(plan, pairs, 1 - core, kept_ref, sent_ref, target)


def mlp(plan, other, gate_weight, up_weight, gain, hidden_grad, first):
    units = gate_weight.shape[0]
    return call(
        functools.partial(mlp_body, plan),
        [
            shaped(plan.rows, plan.width, dtype=BF16),
            shaped(plan.rows, 1),
            shaped(plan.rows, units, dtype=BF16),
            shaped(plan.rows, units, dtype=BF16),
            shaped(plan.rows, units, dtype=BF16),
            *side_shapes(plan),
        ],
        (other, gate_weight, up_weight, gain, hidden_grad, *first),
        [chunk_scratch(plan)],
        flops=6 * plan.rows * plan.width * units,
        moved=gate_weight.size * 4,
    )


def mlp_own_body(plan, gate_grad_ref, up_grad_ref, gate_ref, up_ref, kept_ref, sent_ref, target):
    pairs = [(gate_grad_ref[...], gate_ref), (up_grad_ref[...], up_ref)]
    half_product(plan, pairs, lax.axis_index("hidden"), kept_ref, sent_ref, target)


def mlp_own(plan, gate_grad, up_grad, gate_weight, up_weight):
    return call(
        functools.partial(mlp_own_body, plan),
        side_shapes(plan),
        (gate_grad, up_grad, gate_weight, up_weight),
        [chunk_scratch(plan)],
        flops=2 * plan.rows * plan.width * gate_weight.shape[0],
        moved=gate_weight.size * 2,
    )


def project_body(plan, hidden_ref, down_ref, mine_ref, theirs_ref, both):
    core = lax.axis_index("hidden")
    terms = jnp.dot(hidden_ref[...], down_ref[...], preferred_element_type=F32)
    for chip in range(plan.chips):
        for side in range(plan.cores):
            start = (chip * plan.cores + side) * plan.own
            main, tail = pack_block(plan, terms[:, start : start + plan.own])
            both[side, chip, : plan.rows, :] = main
            both[side, chip, plan.rows :, :] = tail
    mine_ref[...] = both[core]
    theirs_ref[...] = both[1 - core]


def project(plan, hidden, down_weight):
    units = down_weight.shape[0]
    shape = (plan.chips, plan.packed, LANES)
    return call(
        functools.partial(project_body, plan),
        [shaped(*shape)] * 2,
        (hidden, down_weight),
        [both_scratch(plan, F32)],
        flops=2 * plan.rows * plan.width * units,
        moved=down_weight.size * 2,
    )


def add_pair_body(plan, first_ref, mine_ref, theirs_ref, kept_ref, sent_ref):
    me = lax.axis_index("latent")
    sent_ref[0] = first_ref[0]
    for place, column in enumerate(plan.columns):
        kept, sent = me ^ column, me ^ column ^ 1
        kept_ref[place] = mine_ref[kept] + theirs_ref[kept]
        sent_ref[1 + place] = (mine_ref[sent] + theirs_ref[sent]).astype(BF16)


def add_pair(plan, first, mine, theirs):
    count, dims = len(plan.columns), mine.shape[1:]
    return call(
        functools.partial(add_pair_body, plan),
        [shaped(count, *dims), shaped(1 + count, *dims, dtype=BF16)],
        (first, mine, theirs),
        moved=mine.size * 10,
    )


def add_sent_body(mine_ref, theirs_ref, *refs):
    *more_refs, first_ref, rest_ref = refs
    total = (mine_ref[...] + theirs_ref[...]).astype(BF16)
    first_ref[:1] = total[:1]
    for more_ref in more_refs:
        first_ref[1:] = more_ref[...]
    rest_ref[...] = total[1:]


def add_sent(plan, mine, theirs, *more):
    count, *dims = mine.shape
    first = 1 + sum(one.shape[0] for one in more)
    return call(
        add_sent_body,
        [shaped(first, *dims, dtype=BF16), shaped(count - 1, *dims, dtype=BF16)],
        (mine, theirs, *more),
        moved=mine.size * 10,
    )


def add_across_body(mine_ref, theirs_ref, got_ref, *sent_refs):
    for place, out_ref in enumerate(sent_refs):
        total = mine_ref[1 + place] + theirs_ref[1 + place] + got_ref[place].astype(F32)
        out_ref[0] = total.astype(BF16)


def add_across(plan, mine, theirs, got):
    return call(
        add_across_body,
        [shaped(1, *mine.shape[1:], dtype=BF16)] * got.shape[0],
        (mine, theirs, got),
        moved=mine.size * 10,
    )


def column_total(mine_ref, theirs_ref, *refs):
    total = mine_ref[0] + theirs_ref[0]
    for ref in refs:
        total = total + ref[0].astype(F32)
    return total.astype(BF16)


def add_column_body(*refs):
    *sources, block_ref, more_ref = refs
    block_ref[0] = column_total(*sources)
    more_ref[...] = sources[-1][1:]


def add_column(plan, mine, theirs, got, first):
    dims = mine.shape[1:]
    return call(
        add_column_body,
        [shaped(1, *dims, dtype=BF16), shaped(first.shape[0] - 1, *dims, dtype=BF16)],
        (mine, theirs, *reversed(got), first),
        moved=mine.size * 8,
    )


def add_with_output_body(plan, count, *refs):
    total = column_total(*refs[:count])
    first_ref, kept_ref, block_ref, own_ref = refs[count - 1 : count + 3]
    block_ref[0] = total
    own_ref[0] = kept_ref[0] + first_ref[1].astype(F32)
    for place, both_ref in enumerate(refs[count + 3 :], 1):
        both_ref[0, : plan.chunk, :] = total
        both_ref[0, plan.chunk :, :] = (
            kept_ref[place] + first_ref[1 + place].astype(F32)
        ).astype(BF16)


def add_with_output(plan, mine, theirs, got, first, kept):
    both = shaped(1, plan.chunk + plan.packed, LANES, dtype=BF16)
    block, out_own, *messages = call(
        functools.partial(add_with_output_body, plan, 3 + len(got)),
        [shaped(1, plan.chunk, LANES, dtype=BF16), shaped(1, plan.packed, LANES)]
        + [both] * (len(plan.columns) - 1),
        (mine, theirs, *reversed(got), first, kept),
        moved=mine.size * 12,
    )
    return block, out_own, messages


def stack_body(places, *refs):
    count = len(places)
    stack_ref, *rest_refs = refs[count:]
    rows = stack_ref.shape[1]
    for place, ref in zip(places, refs):
        stack_ref[place] = ref[0, :rows, :]
        for rest_ref in rest_refs:
            if place:
                rest_ref[place - 1] = ref[0, :rows, :]


def stack_up(plan, block, got, with_rest=False):
    dims = block.shape[1:]
    operands = [block, *got]
    places = list(range(len(operands)))
    if with_rest:
        operands, places = operands[::-1], places[::-1]
    outs = [shaped(1 + len(got), *dims, dtype=BF16), shaped(len(got), *dims, dtype=BF16)]
    return call(
        functools.partial(stack_body, places),
        outs if with_rest else outs[0],
        operands,
        moved=block.size * 16,
    )


def stack_second_body(rows, *refs):
    for place, ref in enumerate(refs[:-1]):
        refs[-1][place] = ref[0, rows:, :]


def stack_second(plan, rows, messages):
    return call(
        functools.partial(stack_second_body, rows),
        shaped(len(messages), messages[0].shape[1] - rows, LANES, dtype=BF16),
        messages,
        moved=messages[0].size * 16,
    )


def line_up_body(plan, *refs):
    for chip, block in plan.side_blocks(refs[:-1]):
        refs[-1][chip] = block


def line_up(plan, stack, *crossed):
    return call(
        functools.partial(line_up_body, plan),
        shaped(plan.chips, *stack.shape[1:], dtype=BF16),
        (stack, *crossed),
        moved=stack.size * 8,
    )


def finish_output_body(plan, own_ref, *refs):
    total = own_ref[0]
    for ref in refs[:-1]:
        total = total + ref[0, plan.chunk :, :].astype(F32)
    refs[-1][...] = unpack_block(plan, total).astype(BF16)


def finish_output(plan, own, messages):
    return call(
        functools.partial(finish_output_body, plan),
        shaped(plan.rows, plan.own, dtype=BF16),
        (own, *reversed(messages)),
        moved=own.size * 8,
    )


def dictionary_body(plan, pieces, own_ref, other_ref, gain_ref, inverse_ref, scaled_ref, inputs_ref, latents_ref, dict_ref, out_hbm, full, out_ref, out_sems):
    core = lax.axis_index("hidden")
    join_half(plan, own_ref, core * plan.half, full)
    join_half(plan, other_ref, (1 - core) * plan.half, full)
    grad = full[...].astype(F32)
    gain = gain_ref[...]
    scaled_rebuilt = scaled_ref[...].astype(F32)
    rebuilt = scaled_rebuilt / gain
    inverse = inverse_ref[...]
    inner_row = jnp.sum(grad * scaled_rebuilt, axis=1, keepdims=True)
    inverse_cube = inverse * inverse * inverse
    inputs = inputs_ref[...]
    rebuilt_grad = (
        inverse * (grad * gain)
        - (inverse_cube * (inner_row / plan.width)) * rebuilt
        + (rebuilt - inputs.astype(F32))
    ).astype(BF16)
    latents = latents_ref[...]
    latent_grad = lax.dot_general(
        rebuilt_grad, dict_ref[...], ACROSS, preferred_element_type=F32
    )
    preact_grad = jnp.where(latents.astype(F32) > 0.0, latent_grad, 0.0).astype(BF16)
    left = jnp.concatenate([latents, preact_grad], axis=0)
    right = jnp.concatenate([rebuilt_grad, inputs], axis=0)
    size = plan.width // pieces
    writes = []
    for piece in range(pieces):
        span = slice(piece * size, (piece + 1) * size)
        out_ref[:, span] = lax.dot_general(
            left, right[:, span], DOWNWARD, preferred_element_type=F32
        ).astype(BF16)
        one = pltpu.make_async_copy(
            out_ref.at[:, span], out_hbm.at[:, span], out_sems.at[piece]
        )
        one.start()
        writes.append(one)
    for one in writes:
        one.wait()


def dictionary_step(plan, own, other, gain, inverse, scaled, inputs, latents, dictionary):
    units = dictionary.shape[0]
    pieces = plan.tiles
    return call(
        functools.partial(dictionary_body, plan, pieces),
        shaped(*dictionary.shape, dtype=BF16),
        (own, other, gain, inverse, scaled, inputs, latents, dictionary),
        [
            pltpu.VMEM((plan.rows, plan.width), BF16),
            pltpu.VMEM(dictionary.shape, BF16),
            pltpu.SemaphoreType.DMA((pieces,)),
        ],
        out_specs=HBM,
        flops=6 * plan.rows * plan.width * units,
        moved=dictionary.size * 4,
    )


def swap(value):
    size = lax.axis_size("hidden")
    return lax.ppermute(value, "hidden", [(i, (i + 1) % size) for i in range(size)])


def partner_swap(value, bits):
    size = lax.axis_size("latent")
    return lax.ppermute(value, "latent", [(i, i ^ bits) for i in range(size)])


def cross(value):
    return partner_swap(value, 1)


def to_column(plan, blocks):
    pairs = list(zip(blocks, plan.columns[1:]))
    got = [partner_swap(one, column) for one, column in reversed(pairs)]
    return got[::-1]


def to_all_columns(plan, block):
    return [partner_swap(block, column) for column in plan.columns[1:]]


def tie(*values):
    return lax.optimization_barrier(values)


def per_device(
    input_codes,
    cotangent_codes,
    dictionary,
    encoder_bias,
    decoder_bias,
    norm_gain,
    gate_weight,
    up_weight,
    down_weight,
):
    plan = Plan(
        lax.axis_size("latent"), lax.axis_size("hidden"), input_codes.shape[0], input_codes.shape[1]
    )
    if not plan.fits():
        return per_device_plain(
            input_codes,
            cotangent_codes,
            dictionary,
            encoder_bias,
            decoder_bias,
            norm_gain,
            gate_weight,
            up_weight,
            down_weight,
        )
    vectors = jnp.concatenate([encoder_bias, decoder_bias, norm_gain]).reshape(1, -1)
    codes = jnp.stack([input_codes, cotangent_codes])
    values = (codes.astype(F32) * CODE_STEP).astype(BF16)
    block, both = pack_values(plan, values)
    got = to_all_columns(plan, both)
    stack = stack_up(plan, block, got)
    stack, vectors, late_dictionary = tie(stack, vectors, dictionary)
    stack_other, crossed = swap(stack), cross(stack)
    encoder = bring_encoder(plan, late_dictionary, vectors)
    cotangent = stack_second(plan, plan.packed, [both, *got])
    stack_other, crossed, encoder, cotangent = tie(stack_other, crossed, encoder, cotangent)
    brought, bias, decoder, gain = encoder
    inputs, latents, kept, sent = encode(
        plan, (stack, crossed), (stack_other, swap(crossed)), brought, bias, gain
    )
    sent, kept = swap(sent), swap(kept)
    own_kept, own_sent = decode_own(plan, latents, brought, decoder, gain)
    sent_first, sent_rest = add_sent(plan, own_sent, sent, cotangent)
    sent = add_across(plan, own_kept, kept, cross(sent_rest))
    sent, sent_first = tie(sent, sent_first)
    got, first = to_column(plan, sent), cross(sent_first)
    block, crossed = add_column(plan, own_kept, kept, got, first)
    cotangent_own = (cotangent, crossed)
    hidden_grad = back_project(
        plan, cotangent_own, [swap(one) for one in cotangent_own], down_weight
    )
    stack = stack_up(plan, block, to_all_columns(plan, block))
    stack_other, crossed = swap(stack), cross(stack)
    stack_other, crossed, hidden_grad = tie(stack_other, crossed, hidden_grad)
    terms = mlp_first(plan, line_up(plan, stack, crossed), gate_weight, up_weight, gain)
    scaled_other = line_up(plan, stack_other, swap(crossed))
    scaled, inverse, hidden, gate_grad, up_grad, kept, sent = mlp(
        plan, scaled_other, gate_weight, up_weight, gain, hidden_grad, terms
    )
    sent, kept = swap(sent), swap(kept)
    own_kept, own_sent = mlp_own(plan, gate_grad, up_grad, gate_weight, up_weight)
    out_mine, out_theirs = project(plan, hidden, down_weight)
    sent_first, sent_rest = add_sent(plan, own_sent, sent)
    sent_first, sent_rest, out_mine, out_theirs = tie(sent_first, sent_rest, out_mine, out_theirs)
    crossed = cross(sent_rest)
    out_kept, sent_first = add_pair(plan, sent_first, out_mine, swap(out_theirs))
    sent = add_across(plan, own_kept, kept, crossed)
    sent, sent_first, out_kept = tie(sent, sent_first, out_kept)
    got = to_column(plan, sent)
    first = cross(sent_first)
    block, out_own, messages = add_with_output(plan, own_kept, kept, got, first, out_kept)
    got, first = tie(to_column(plan, messages), cross(block))
    stack, rest = stack_up(plan, block, got, with_rest=True)
    rest, stack_other, first_other = cross(rest), swap(stack), swap(first)
    block_output = finish_output(plan, out_own, got)
    grad_own = line_up(plan, stack, first, rest)
    grad_other = line_up(plan, stack_other, first_other, swap(rest))
    dictionary_grad = dictionary_step(
        plan, grad_own, grad_other, gain, inverse, scaled, inputs, latents, brought
    )
    return (block_output, dictionary_grad)


def per_device_plain(
    input_codes,
    cotangent_codes,
    dictionary,
    encoder_bias,
    decoder_bias,
    norm_gain,
    gate_weight,
    up_weight,
    down_weight,
):
    own_width = input_codes.shape[1]
    model_width = own_width * lax.axis_size(("latent", "hidden"))
    cotangent_local = (cotangent_codes.astype(jnp.float32) * CODE_STEP).astype(jnp.bfloat16)
    inputs_local = (input_codes.astype(jnp.float32) * CODE_STEP).astype(jnp.bfloat16)
    inputs = lax.all_gather(inputs_local, ("latent", "hidden"), axis=1, tiled=True)
    preact = (
        lax.dot_general(inputs, dictionary, ACROSS, preferred_element_type=jnp.float32)
        + encoder_bias
    )
    latents = jnp.maximum(preact, 0.0).astype(jnp.bfloat16)
    partial_value = jnp.dot(latents, dictionary, preferred_element_type=jnp.float32)
    rebuilt = lax.psum(partial_value, ("latent", "hidden")) + decoder_bias
    inverse = lax.rsqrt(
        jnp.sum(rebuilt * rebuilt, axis=1, keepdims=True) / model_width + NORM_EPSILON
    )
    normed = (rebuilt * inverse * norm_gain).astype(jnp.bfloat16)
    target = inputs.astype(jnp.float32)
    gate_proj = lax.dot_general(normed, gate_weight, ACROSS, preferred_element_type=jnp.float32)
    up_proj = lax.dot_general(normed, up_weight, ACROSS, preferred_element_type=jnp.float32)
    gelu_value, gelu_slope = gelu_parts(gate_proj)
    hidden = (gelu_value * up_proj).astype(jnp.bfloat16)
    output_terms = jnp.dot(hidden, down_weight, preferred_element_type=jnp.float32)
    block_output = lax.psum_scatter(
        output_terms, ("latent", "hidden"), scatter_dimension=1, tiled=True
    ).astype(jnp.bfloat16)
    hidden_grad = lax.dot_general(
        lax.all_gather(cotangent_local, ("latent", "hidden"), axis=1, tiled=True),
        down_weight,
        ACROSS,
        preferred_element_type=jnp.float32,
    )
    gate_grad = (hidden_grad * up_proj * gelu_slope).astype(jnp.bfloat16)
    up_grad = (hidden_grad * gelu_value).astype(jnp.bfloat16)
    partial_grad = jnp.dot(gate_grad, gate_weight, preferred_element_type=jnp.float32) + jnp.dot(
        up_grad, up_weight, preferred_element_type=jnp.float32
    )
    scaled = lax.psum(partial_grad, ("latent", "hidden")) * norm_gain
    inner_row = jnp.sum(scaled * rebuilt, axis=1, keepdims=True)
    inverse_cube = inverse * inverse * inverse
    rebuilt_grad = (
        inverse * scaled - inverse_cube * rebuilt * (inner_row / model_width) + (rebuilt - target)
    ).astype(jnp.bfloat16)
    latent_grad = lax.dot_general(
        rebuilt_grad, dictionary, ACROSS, preferred_element_type=jnp.float32
    )
    preact_grad = jnp.where(preact > 0.0, latent_grad, 0.0).astype(jnp.bfloat16)
    dictionary_grad = lax.dot_general(
        latents, rebuilt_grad, DOWNWARD, preferred_element_type=jnp.float32
    ) + lax.dot_general(preact_grad, inputs, DOWNWARD, preferred_element_type=jnp.float32)
    return (block_output, dictionary_grad.astype(jnp.bfloat16))


def solution(mesh):
    in_specs = (
        P("groups", ("latent", "hidden")),
        P("groups", ("latent", "hidden")),
        P(("latent", "hidden"), None),
        P(("latent", "hidden")),
        P(),
        P(),
        P(("latent", "hidden"), None),
        P(("latent", "hidden"), None),
        P(("latent", "hidden"), None),
    )
    out_specs = (P("groups", ("latent", "hidden")), P(("latent", "hidden"), "groups"))
    return jax.shard_map(
        per_device, mesh=mesh, in_specs=in_specs, out_specs=out_specs, check_vma=False
    )
```

```python
import functools
import math

import jax
import jax.numpy as jnp
from jax import lax
from jax.experimental import pallas as pl
from jax.experimental.pallas import tpu as pltpu
from jax.sharding import PartitionSpec as P

CODE_STEP = 2.0 ** (-6)
NORM_EPSILON = 1e-06
GELU_ROOT = 0.7978845608028654
GELU_CUBIC = 0.044715
ACROSS = (((1,), (1,)), ((), ()))
DOWNWARD = (((0,), (0,)), ((), ()))
LANES = 128
ROW_TILE = 16
DIRECT_LIMIT = 16
VMEM_BYTES = 24 * 1024 * 1024
VMEM_BRING = 53 * 1024 * 1024
F32 = jnp.float32
BF16 = jnp.bfloat16


def gelu_parts(values):
    argument = GELU_ROOT * (values + GELU_CUBIC * values * values * values)
    tanh_value = jnp.tanh(argument)
    result = 0.5 * values * (1.0 + tanh_value)
    derivative = 0.5 * (1.0 + tanh_value) + 0.5 * values * (
        1.0 - tanh_value * tanh_value
    ) * GELU_ROOT * (1.0 + 3.0 * GELU_CUBIC * values * values)
    return (result, derivative)


def up_to(value, unit):
    return -(-value // unit) * unit


def chips_fit(chips):
    return 2 <= chips <= DIRECT_LIMIT and chips & (chips - 1) == 0


class Plan:
    def __init__(self, chips, cores, rows, own):
        self.chips, self.cores, self.rows, self.own = chips, cores, rows, own
        self.width = own * chips * cores
        self.half = self.width // cores
        self.tiles = self.half // LANES
        self.chunk = up_to(-(-self.tiles * rows // chips), ROW_TILE)
        self.flat = self.chunk * chips
        self.tail = own - LANES
        if self.tail > 0:
            self.fold_rows = min(
                size
                for size in range(ROW_TILE, rows + ROW_TILE, ROW_TILE)
                if -(-rows // size) * self.tail <= LANES
            )
            self.packed = rows + self.fold_rows
        self.columns = list(range(0, chips, 2))

    def side_blocks(self, stack_ref, crossed_ref):
        me = lax.axis_index("latent")
        for place, column in enumerate(self.columns):
            yield me ^ column, stack_ref[place]
            yield me ^ column ^ 1, crossed_ref[place]

    def pieces(self):
        for tile in range(self.tiles):
            row = 0
            while row < self.rows:
                chip, place = divmod(tile * self.rows + row, self.chunk)
                count = min(self.rows - row, self.chunk - place)
                yield tile, chip, place, row, count
                row += count

    def fits(self):
        return (
            self.cores == 2
            and chips_fit(self.chips)
            and self.rows % ROW_TILE == 0
            and self.half % LANES == 0
            and 0 < self.tail < LANES
        )


HBM = pl.BlockSpec(memory_space=pltpu.HBM)
ONCHIP = pl.BlockSpec(memory_space=pltpu.VMEM)


def shaped(*dims, dtype=F32):
    return jax.ShapeDtypeStruct(dims, dtype)


HBM = pl.BlockSpec(memory_space=pltpu.HBM)
ONCHIP = pl.BlockSpec(memory_space=pltpu.VMEM)


def shaped(*dims, dtype=F32):
    return jax.ShapeDtypeStruct(dims, dtype)


def call(body, out_shapes, operands, scratch=(), out_specs=None, flops=0, moved=0):
    return pl.pallas_call(
        body,
        out_shape=out_shapes,
        in_specs=[ONCHIP] * len(operands),
        out_specs=jax.tree.map(lambda _: ONCHIP, out_shapes) if out_specs is None else out_specs,
        scratch_shapes=list(scratch),
        compiler_params=pltpu.CompilerParams(vmem_limit_bytes=VMEM_BYTES),
        cost_estimate=pl.CostEstimate(flops=flops, bytes_accessed=moved, transcendentals=0),
    )(*operands)


def padded_bytes(array):
    *lead, rows, columns = array.shape
    item = jnp.dtype(array.dtype).itemsize
    return math.prod(lead) * up_to(rows, ROW_TILE) * up_to(columns, LANES) * item


def copies(sources, targets, sems):
    started = []
    for index, (source, target) in enumerate(zip(sources, targets)):
        one = pltpu.make_async_copy(source, target, sems.at[index])
        one.start()
        started.append(one)
    return started


def pack_block(plan, block):
    tail = block[:, LANES:]
    folded = []
    for start in range(0, plan.rows, plan.fold_rows):
        piece = tail[start : min(start + plan.fold_rows, plan.rows), :]
        short = plan.fold_rows - piece.shape[0]
        if short:
            piece = jnp.concatenate([piece, jnp.zeros((short, plan.tail), block.dtype)], axis=0)
        folded.append(piece)
    fill = LANES - len(folded) * plan.tail
    if fill:
        folded.append(jnp.zeros((plan.fold_rows, fill), block.dtype))
    return block[:, :LANES], jnp.concatenate(folded, axis=1)


def unpack_block(plan, packed):
    pieces = []
    for fold, start in enumerate(range(0, plan.rows, plan.fold_rows)):
        count = min(plan.fold_rows, plan.rows - start)
        pieces.append(
            packed[plan.rows : plan.rows + count, fold * plan.tail : (fold + 1) * plan.tail]
        )
    return jnp.concatenate([packed[: plan.rows, :], jnp.concatenate(pieces, axis=0)], axis=1)


def pack_values_body(plan, values_ref, *block_refs):
    for index, block_ref in enumerate(block_refs):
        main, tail = pack_block(plan, values_ref[index].astype(F32))
        block_ref[0, : plan.rows, :] = main.astype(BF16)
        block_ref[0, plan.rows :, :] = tail.astype(BF16)


def pack_values(plan, values):
    return call(
        functools.partial(pack_values_body, plan),
        [shaped(1, plan.packed, LANES, dtype=BF16)] * values.shape[0],
        (values,),
        moved=values.size * 6,
    )


def assemble(plan, own_refs, other_refs, both, full_ref):
    core = lax.axis_index("hidden")
    for side, refs in ((core, own_refs), (1 - core, other_refs)):
        if len(refs) == 1:
            both[side] = refs[0][...]
        else:
            for chip, block in plan.side_blocks(*refs):
                both[side, chip] = block
    for chip in range(plan.chips):
        for side in range(plan.cores):
            column = (chip * plan.cores + side) * plan.own
            block = unpack_block(plan, both[side, chip].astype(F32))
            full_ref[:, column : column + plan.own] = block.astype(BF16)


def both_scratch(plan, dtype=BF16):
    return pltpu.VMEM((plan.cores, plan.chips, plan.packed, LANES), dtype)


def chunk_scratch(plan):
    return pltpu.VMEM((plan.chips, plan.chunk, LANES), F32)


def side_shapes(plan):
    far = plan.chips - 2
    return [shaped(2, plan.chunk, LANES), shaped(far, plan.chunk, LANES)]


def half_product(plan, pairs, side, near_ref, far_ref, target, gain_ref=None, bias_ref=None):
    span = pl.ds(pl.multiple_of(side * plan.half, LANES), plan.half)
    total = None
    for left, right_ref in pairs:
        term = jnp.dot(left, right_ref[:, span], preferred_element_type=F32)
        total = term if total is None else total + term
    if bias_ref is not None:
        total = total + bias_ref[:, span] * jnp.where(lax.axis_index("latent") == 0, 1.0, 0.0)
    if gain_ref is not None:
        total = total * gain_ref[:, span]
    for tile, chip, place, row, count in plan.pieces():
        target[chip, place : place + count, :] = total[
            row : row + count, tile * LANES : (tile + 1) * LANES
        ]
    used = plan.tiles * plan.rows
    while used < plan.flat:
        chip, place = divmod(used, plan.chunk)
        target[chip, place:, :] = jnp.zeros((plan.chunk - place, LANES), F32)
        used += plan.chunk - place
    me = lax.axis_index("latent")
    for across in range(2):
        near_ref[across] = target[me ^ across]
        for place, column in enumerate(plan.columns[1:]):
            far_ref[2 * place + across] = target[me ^ column ^ across]


def bring_encoder_body(dict_hbm, vectors_hbm, dict_ref, bias_ref, decoder_ref, gain_ref, sems):
    sources, targets = [dict_hbm], [dict_ref]
    start = 0
    for target in (bias_ref, decoder_ref, gain_ref):
        sources.append(vectors_hbm.at[:, start : start + target.shape[1]])
        targets.append(target)
        start += target.shape[1]
    for copy in copies(sources, targets, sems):
        copy.wait()


def bring_encoder(plan, dictionary, vectors):
    outputs = [
        shaped(*dictionary.shape, dtype=BF16),
        shaped(1, dictionary.shape[0]),
        shaped(1, plan.width),
        shaped(1, plan.width),
    ]
    return pl.pallas_call(
        bring_encoder_body,
        out_shape=outputs,
        in_specs=[HBM] * 2,
        out_specs=[ONCHIP] * len(outputs),
        scratch_shapes=[pltpu.SemaphoreType.DMA((len(outputs),))],
        compiler_params=pltpu.CompilerParams(
            vmem_limit_bytes=VMEM_BRING - sum(map(padded_bytes, outputs))
        ),
        cost_estimate=pl.CostEstimate(
            flops=0, bytes_accessed=dictionary.size * 4, transcendentals=0
        ),
    )(dictionary, vectors)


def encode_body(plan, *refs):
    own, other, (dict_ref, bias_ref, gain_ref) = refs[:1], refs[1:2], refs[2:5]
    inputs_ref, latents_ref, near_ref, far_ref, both, target = refs[5:]
    assemble(plan, own, other, both, inputs_ref)
    preact = (
        lax.dot_general(inputs_ref[...], dict_ref[...], ACROSS, preferred_element_type=F32)
        + bias_ref[...]
    )
    latents = jnp.maximum(preact, 0.0).astype(BF16)
    latents_ref[...] = latents
    theirs = 1 - lax.axis_index("hidden")
    half_product(plan, [(latents, dict_ref)], theirs, near_ref, far_ref, target, gain_ref)


def encode(plan, own, other, dictionary, encoder_bias, gain):
    latents = dictionary.shape[0]
    return call(
        functools.partial(encode_body, plan),
        [
            shaped(plan.rows, plan.width, dtype=BF16),
            shaped(plan.rows, latents, dtype=BF16),
            *side_shapes(plan),
        ],
        (own, other, dictionary, encoder_bias, gain),
        [both_scratch(plan), chunk_scratch(plan)],
        flops=3 * plan.rows * plan.width * latents,
        moved=dictionary.size * 2,
    )


def decode_own_body(plan, latents_ref, dict_ref, decoder_ref, gain_ref, near_ref, far_ref, target):
    pairs = [(latents_ref[...], dict_ref)]
    mine = lax.axis_index("hidden")
    half_product(plan, pairs, mine, near_ref, far_ref, target, gain_ref, decoder_ref)


def decode_own(plan, latents, dictionary, decoder_bias, gain):
    return call(
        functools.partial(decode_own_body, plan),
        side_shapes(plan),
        (latents, dictionary, decoder_bias, gain),
        [chunk_scratch(plan)],
        flops=plan.rows * plan.width * dictionary.shape[0],
        moved=dictionary.size,
    )


def back_project_body(plan, *refs):
    own, other, (down_ref, grad_ref, both, full) = refs[:2], refs[2:4], refs[4:]
    assemble(plan, own, other, both, full)
    grad_ref[...] = lax.dot_general(
        full[...], down_ref[...], ACROSS, preferred_element_type=F32
    )


def back_project(plan, own, other, down_weight):
    units = down_weight.shape[0]
    return call(
        functools.partial(back_project_body, plan),
        shaped(plan.rows, units),
        (*own, *other, down_weight),
        [both_scratch(plan), pltpu.VMEM((plan.rows, plan.width), BF16)],
        flops=2 * plan.rows * plan.width * units,
        moved=down_weight.size * 2,
    )


def join_half(plan, source, first, full_ref):
    for tile, chip, place, row, count in plan.pieces():
        column = pl.multiple_of(first + tile * LANES, LANES)
        full_ref[row : row + count, pl.ds(column, LANES)] = source[
            chip, place : place + count, :
        ]


def half_terms(plan, half, side, gate_ref, up_ref, gain_ref):
    span = pl.ds(pl.multiple_of(side * plan.half, LANES), plan.half)
    rebuilt = half.astype(F32) / gain_ref[:, span]
    squares = jnp.sum(rebuilt * rebuilt, axis=1, keepdims=True)
    gate = lax.dot_general(half, gate_ref[:, span], ACROSS, preferred_element_type=F32)
    up = lax.dot_general(half, up_ref[:, span], ACROSS, preferred_element_type=F32)
    return squares, gate, up


def mlp_first_body(plan, own_ref, gate_ref, up_ref, gain_ref, half_ref, squares_ref, gate_part_ref, up_part_ref):
    join_half(plan, own_ref, 0, half_ref)
    squares_ref[...], gate_part_ref[...], up_part_ref[...] = half_terms(
        plan, half_ref[...], lax.axis_index("hidden"), gate_ref, up_ref, gain_ref
    )


def mlp_first(plan, own, gate_weight, up_weight, gain):
    units = gate_weight.shape[0]
    return call(
        functools.partial(mlp_first_body, plan),
        [
            shaped(plan.rows, plan.half, dtype=BF16),
            shaped(plan.rows, 1),
            shaped(plan.rows, units),
            shaped(plan.rows, units),
        ],
        (own, gate_weight, up_weight, gain),
        flops=2 * plan.rows * plan.width * units,
        moved=gate_weight.size * 4,
    )


def mlp_body(plan, other_ref, gate_ref, up_ref, gain_ref, grad_ref, half_ref, squares_ref, gate_part_ref, up_part_ref, scaled_ref, inverse_ref, hidden_ref, gate_grad_ref, up_grad_ref, near_ref, far_ref, target):
    core = lax.axis_index("hidden")
    join_half(plan, other_ref, (1 - core) * plan.half, scaled_ref)
    other_span = pl.ds(pl.multiple_of((1 - core) * plan.half, LANES), plan.half)
    own_span = pl.ds(pl.multiple_of(core * plan.half, LANES), plan.half)
    scaled_ref[:, own_span] = half_ref[...]
    squares, gate, up = half_terms(
        plan, scaled_ref[:, other_span], 1 - core, gate_ref, up_ref, gain_ref
    )
    inverse = lax.rsqrt((squares + squares_ref[...]) / plan.width + NORM_EPSILON)
    inverse_ref[...] = inverse
    gate_proj = inverse * (gate + gate_part_ref[...])
    up_proj = inverse * (up + up_part_ref[...])
    gelu_value, gelu_slope = gelu_parts(gate_proj)
    hidden_ref[...] = (gelu_value * up_proj).astype(BF16)
    hidden_grad = grad_ref[...]
    gate_grad = (hidden_grad * up_proj * gelu_slope).astype(BF16)
    up_grad = (hidden_grad * gelu_value).astype(BF16)
    gate_grad_ref[...] = gate_grad
    up_grad_ref[...] = up_grad
    pairs = [(gate_grad, gate_ref), (up_grad, up_ref)]
    half_product(plan, pairs, 1 - core, near_ref, far_ref, target)


def mlp(plan, other, gate_weight, up_weight, gain, hidden_grad, first):
    units = gate_weight.shape[0]
    return call(
        functools.partial(mlp_body, plan),
        [
            shaped(plan.rows, plan.width, dtype=BF16),
            shaped(plan.rows, 1),
            shaped(plan.rows, units, dtype=BF16),
            shaped(plan.rows, units, dtype=BF16),
            shaped(plan.rows, units, dtype=BF16),
            *side_shapes(plan),
        ],
        (other, gate_weight, up_weight, gain, hidden_grad, *first),
        [chunk_scratch(plan)],
        flops=6 * plan.rows * plan.width * units,
        moved=gate_weight.size * 4,
    )


def mlp_own_body(plan, gate_grad_ref, up_grad_ref, gate_ref, up_ref, near_ref, far_ref, target):
    pairs = [(gate_grad_ref[...], gate_ref), (up_grad_ref[...], up_ref)]
    half_product(plan, pairs, lax.axis_index("hidden"), near_ref, far_ref, target)


def mlp_own(plan, gate_grad, up_grad, gate_weight, up_weight):
    return call(
        functools.partial(mlp_own_body, plan),
        side_shapes(plan),
        (gate_grad, up_grad, gate_weight, up_weight),
        [chunk_scratch(plan)],
        flops=2 * plan.rows * plan.width * gate_weight.shape[0],
        moved=gate_weight.size * 2,
    )


def project_body(plan, hidden_ref, down_ref, mine_ref, theirs_ref, both):
    core = lax.axis_index("hidden")
    terms = jnp.dot(hidden_ref[...], down_ref[...], preferred_element_type=F32)
    for chip in range(plan.chips):
        for side in range(plan.cores):
            start = (chip * plan.cores + side) * plan.own
            main, tail = pack_block(plan, terms[:, start : start + plan.own])
            both[side, chip, : plan.rows, :] = main
            both[side, chip, plan.rows :, :] = tail
    mine_ref[...] = both[core]
    theirs_ref[...] = both[1 - core]


def project(plan, hidden, down_weight):
    units = down_weight.shape[0]
    shape = (plan.chips, plan.packed, LANES)
    return call(
        functools.partial(project_body, plan),
        [shaped(*shape)] * 2,
        (hidden, down_weight),
        [both_scratch(plan, F32)],
        flops=2 * plan.rows * plan.width * units,
        moved=down_weight.size * 2,
    )


def add_pair_body(plan, mine_ref, theirs_ref, kept_ref, sent_ref):
    me = lax.axis_index("latent")
    for place, column in enumerate(plan.columns):
        kept, sent = me ^ column, me ^ column ^ 1
        kept_ref[place] = mine_ref[kept] + theirs_ref[kept]
        sent_ref[place] = (mine_ref[sent] + theirs_ref[sent]).astype(BF16)


def add_pair(plan, mine, theirs):
    count, dims = len(plan.columns), mine.shape[1:]
    return call(
        functools.partial(add_pair_body, plan),
        [shaped(count, *dims), shaped(count, *dims, dtype=BF16)],
        (mine, theirs),
        moved=mine.size * 10,
    )


def add_far_body(mine_ref, theirs_ref, *message_refs):
    rows = mine_ref.shape[1]
    for place, message_ref in enumerate(message_refs):
        for across in range(2):
            index = 2 * place + across
            message_ref[0, across * rows : (across + 1) * rows, :] = (
                mine_ref[index] + theirs_ref[index]
            ).astype(BF16)


def add_far(plan, mine, theirs):
    message = shaped(1, 2 * plan.chunk, LANES, dtype=BF16)
    return call(
        add_far_body,
        [message] * (len(plan.columns) - 1),
        (mine, theirs),
        moved=mine.size * 10,
    )


def add_near_body(*refs):
    mine_ref, theirs_ref, *got_refs, message_ref = refs
    rows = mine_ref.shape[1]
    for across in range(2):
        total = mine_ref[across] + theirs_ref[across]
        span = slice(across * rows, (across + 1) * rows)
        for ref in got_refs:
            total = total + ref[0, span, :].astype(F32)
        message_ref[0, span, :] = total.astype(BF16)


def add_near(plan, mine, theirs, got):
    return call(
        add_near_body,
        shaped(1, 2 * plan.chunk, LANES, dtype=BF16),
        (mine, theirs, *reversed(got)),
        moved=mine.size * 20,
    )


def sums_across(message_ref, got_ref):
    rows = message_ref.shape[1] // 2
    first, second = slice(0, rows), slice(rows, 2 * rows)
    for here, there in ((first, second), (second, first)):
        yield here, (
            message_ref[0, here, :].astype(F32) + got_ref[0, there, :].astype(F32)
        ).astype(BF16)


def add_across_body(message_ref, got_ref, sum_ref):
    for span, total in sums_across(message_ref, got_ref):
        sum_ref[0, span, :] = total


def add_across(plan, message, got):
    return call(
        add_across_body,
        shaped(*message.shape, dtype=BF16),
        (message, got),
        moved=message.size * 8,
    )


def message_body(*refs):
    *sources, message_ref = refs
    start = 0
    for ref in sources:
        message_ref[0, start : start + ref.shape[1], :] = ref[0]
        start += ref.shape[1]


def message_of(plan, *blocks):
    return call(
        message_body,
        shaped(1, sum(one.shape[1] for one in blocks), LANES, dtype=BF16),
        blocks,
        moved=blocks[0].size * 12,
    )


def add_with_output_body(plan, message_ref, got_ref, kept_ref, out_got_ref, own_ref, *sum_refs):
    own_ref[0] = kept_ref[0] + out_got_ref[0].astype(F32)
    for span, total in sums_across(message_ref, got_ref):
        for sum_ref in sum_refs:
            sum_ref[0, span, :] = total
    for place, sum_ref in enumerate(sum_refs[1:], 1):
        sum_ref[0, 2 * plan.chunk :, :] = (
            kept_ref[place] + out_got_ref[place].astype(F32)
        ).astype(BF16)


def add_with_output(plan, message, got, kept, out_got):
    longer = shaped(1, 2 * plan.chunk + plan.packed, LANES, dtype=BF16)
    own, *sums = call(
        functools.partial(add_with_output_body, plan),
        [shaped(1, plan.packed, LANES), shaped(*message.shape, dtype=BF16)]
        + [longer] * (len(plan.columns) - 1),
        (message, got, kept, out_got),
        moved=message.size * 20,
    )
    return own, sums


def line_up_body(plan, rows, *refs):
    me = lax.axis_index("latent")
    for column, ref in zip(plan.columns, refs):
        refs[-1][me ^ column] = ref[0, :rows, :]
        refs[-1][me ^ column ^ 1] = ref[0, rows : 2 * rows, :]


def line_up(plan, rows, messages):
    return call(
        functools.partial(line_up_body, plan, rows),
        shaped(plan.chips, rows, LANES, dtype=BF16),
        messages,
        moved=messages[0].size * 16,
    )


def third_body(rows, *refs):
    for place, ref in enumerate(refs[:-1]):
        refs[-1][place] = ref[0, 2 * rows :, :]


def third_of(plan, rows, messages):
    return call(
        functools.partial(third_body, rows),
        shaped(len(messages), messages[0].shape[1] - 2 * rows, LANES, dtype=BF16),
        messages,
        moved=messages[0].size * 16,
    )


def finish_output_body(plan, own_ref, *refs):
    total = own_ref[0]
    for ref in refs[:-1]:
        total = total + ref[0, 2 * plan.chunk :, :].astype(F32)
    refs[-1][...] = unpack_block(plan, total).astype(BF16)


def finish_output(plan, own, messages):
    return call(
        functools.partial(finish_output_body, plan),
        shaped(plan.rows, plan.own, dtype=BF16),
        (own, *reversed(messages)),
        moved=own.size * 8,
    )


def dictionary_body(plan, pieces, own_ref, other_ref, gain_ref, inverse_ref, scaled_ref, inputs_ref, latents_ref, dict_ref, out_hbm, full, out_ref, out_sems):
    core = lax.axis_index("hidden")
    join_half(plan, own_ref, core * plan.half, full)
    join_half(plan, other_ref, (1 - core) * plan.half, full)
    grad = full[...].astype(F32)
    gain = gain_ref[...]
    scaled_rebuilt = scaled_ref[...].astype(F32)
    rebuilt = scaled_rebuilt / gain
    inverse = inverse_ref[...]
    inner_row = jnp.sum(grad * scaled_rebuilt, axis=1, keepdims=True)
    inverse_cube = inverse * inverse * inverse
    inputs = inputs_ref[...]
    rebuilt_grad = (
        inverse * (grad * gain)
        - (inverse_cube * (inner_row / plan.width)) * rebuilt
        + (rebuilt - inputs.astype(F32))
    ).astype(BF16)
    latents = latents_ref[...]
    latent_grad = lax.dot_general(
        rebuilt_grad, dict_ref[...], ACROSS, preferred_element_type=F32
    )
    preact_grad = jnp.where(latents.astype(F32) > 0.0, latent_grad, 0.0).astype(BF16)
    left = jnp.concatenate([latents, preact_grad], axis=0)
    right = jnp.concatenate([rebuilt_grad, inputs], axis=0)
    size = plan.width // pieces
    writes = []
    for piece in range(pieces):
        span = slice(piece * size, (piece + 1) * size)
        out_ref[:, span] = lax.dot_general(
            left, right[:, span], DOWNWARD, preferred_element_type=F32
        ).astype(BF16)
        one = pltpu.make_async_copy(
            out_ref.at[:, span], out_hbm.at[:, span], out_sems.at[piece]
        )
        one.start()
        writes.append(one)
    for one in writes:
        one.wait()


def dictionary_step(plan, own, other, gain, inverse, scaled, inputs, latents, dictionary):
    units = dictionary.shape[0]
    pieces = plan.tiles
    return call(
        functools.partial(dictionary_body, plan, pieces),
        shaped(*dictionary.shape, dtype=BF16),
        (own, other, gain, inverse, scaled, inputs, latents, dictionary),
        [
            pltpu.VMEM((plan.rows, plan.width), BF16),
            pltpu.VMEM(dictionary.shape, BF16),
            pltpu.SemaphoreType.DMA((pieces,)),
        ],
        out_specs=HBM,
        flops=6 * plan.rows * plan.width * units,
        moved=dictionary.size * 4,
    )


def swap(value):
    size = lax.axis_size("hidden")
    return lax.ppermute(value, "hidden", [(i, (i + 1) % size) for i in range(size)])


def partner_swap(value, bits):
    size = lax.axis_size("latent")
    return lax.ppermute(value, "latent", [(i, i ^ bits) for i in range(size)])


def cross(value):
    return partner_swap(value, 1)


def to_column(plan, blocks):
    pairs = list(zip(blocks, plan.columns[1:]))
    got = [partner_swap(one, column) for one, column in reversed(pairs)]
    return got[::-1]


def to_all_columns(plan, block):
    return [partner_swap(block, column) for column in plan.columns[1:]]


def tie(*values):
    return lax.optimization_barrier(values)


def per_device(
    input_codes,
    cotangent_codes,
    dictionary,
    encoder_bias,
    decoder_bias,
    norm_gain,
    gate_weight,
    up_weight,
    down_weight,
):
    plan = Plan(
        lax.axis_size("latent"), lax.axis_size("hidden"), input_codes.shape[0], input_codes.shape[1]
    )
    if not plan.fits():
        return per_device_plain(
            input_codes,
            cotangent_codes,
            dictionary,
            encoder_bias,
            decoder_bias,
            norm_gain,
            gate_weight,
            up_weight,
            down_weight,
        )
    vectors = jnp.concatenate([encoder_bias, decoder_bias, norm_gain]).reshape(1, -1)
    codes = jnp.stack([input_codes, cotangent_codes])
    values = (codes.astype(F32) * CODE_STEP).astype(BF16)
    block, cotangent = pack_values(plan, values)
    message = message_of(plan, block, cross(block), cotangent)
    got = to_all_columns(plan, message)
    got, vectors, late_dictionary = tie(got, vectors, dictionary)
    inputs_own = line_up(plan, plan.packed, [message, *got])
    cotangent = third_of(plan, plan.packed, [message, *got])
    brought, bias, decoder, gain = bring_encoder(plan, late_dictionary, vectors)
    inputs, latents, near, far = encode(
        plan, inputs_own, swap(inputs_own), brought, bias, gain
    )
    far, near = swap(far), swap(near)
    own_near, own_far = decode_own(plan, latents, brought, decoder, gain)
    messages, cotangent = tie(add_far(plan, own_far, far), cotangent)
    got = to_column(plan, messages)
    cotangent_crossed = cross(cotangent)
    message = add_near(plan, own_near, near, got)
    message, cotangent_crossed = tie(message, cotangent_crossed)
    message = add_across(plan, message, cross(message))
    cotangent_own = (cotangent, cotangent_crossed)
    hidden_grad = back_project(
        plan, cotangent_own, [swap(one) for one in cotangent_own], down_weight
    )
    got, hidden_grad = tie(to_all_columns(plan, message), hidden_grad)
    scaled_own = line_up(plan, plan.chunk, [message, *got])
    terms = mlp_first(plan, scaled_own, gate_weight, up_weight, gain)
    scaled, inverse, hidden, gate_grad, up_grad, near, far = mlp(
        plan, swap(scaled_own), gate_weight, up_weight, gain, hidden_grad, terms
    )
    far, near = swap(far), swap(near)
    own_near, own_far = mlp_own(plan, gate_grad, up_grad, gate_weight, up_weight)
    out_mine, out_theirs = project(plan, hidden, down_weight)
    messages, out_mine, out_theirs = tie(add_far(plan, own_far, far), out_mine, out_theirs)
    got = to_column(plan, messages)
    out_kept, out_sent = add_pair(plan, out_mine, swap(out_theirs))
    out_crossed = cross(out_sent)
    message = add_near(plan, own_near, near, got)
    out_own, (message, *messages) = add_with_output(
        plan, message, cross(message), out_kept, out_crossed
    )
    got = to_column(plan, messages)
    block_output = finish_output(plan, out_own, got)
    grad_own = line_up(plan, plan.chunk, [message, *got])
    dictionary_grad = dictionary_step(
        plan, grad_own, swap(grad_own), gain, inverse, scaled, inputs, latents, brought
    )
    return (block_output, dictionary_grad)


def per_device_plain(
    input_codes,
    cotangent_codes,
    dictionary,
    encoder_bias,
    decoder_bias,
    norm_gain,
    gate_weight,
    up_weight,
    down_weight,
):
    own_width = input_codes.shape[1]
    model_width = own_width * lax.axis_size(("latent", "hidden"))
    cotangent_local = (cotangent_codes.astype(jnp.float32) * CODE_STEP).astype(jnp.bfloat16)
    inputs_local = (input_codes.astype(jnp.float32) * CODE_STEP).astype(jnp.bfloat16)
    inputs = lax.all_gather(inputs_local, ("latent", "hidden"), axis=1, tiled=True)
    preact = (
        lax.dot_general(inputs, dictionary, ACROSS, preferred_element_type=jnp.float32)
        + encoder_bias
    )
    latents = jnp.maximum(preact, 0.0).astype(jnp.bfloat16)
    partial_value = jnp.dot(latents, dictionary, preferred_element_type=jnp.float32)
    rebuilt = lax.psum(partial_value, ("latent", "hidden")) + decoder_bias
    inverse = lax.rsqrt(
        jnp.sum(rebuilt * rebuilt, axis=1, keepdims=True) / model_width + NORM_EPSILON
    )
    normed = (rebuilt * inverse * norm_gain).astype(jnp.bfloat16)
    target = inputs.astype(jnp.float32)
    gate_proj = lax.dot_general(normed, gate_weight, ACROSS, preferred_element_type=jnp.float32)
    up_proj = lax.dot_general(normed, up_weight, ACROSS, preferred_element_type=jnp.float32)
    gelu_value, gelu_slope = gelu_parts(gate_proj)
    hidden = (gelu_value * up_proj).astype(jnp.bfloat16)
    output_terms = jnp.dot(hidden, down_weight, preferred_element_type=jnp.float32)
    block_output = lax.psum_scatter(
        output_terms, ("latent", "hidden"), scatter_dimension=1, tiled=True
    ).astype(jnp.bfloat16)
    hidden_grad = lax.dot_general(
        lax.all_gather(cotangent_local, ("latent", "hidden"), axis=1, tiled=True),
        down_weight,
        ACROSS,
        preferred_element_type=jnp.float32,
    )
    gate_grad = (hidden_grad * up_proj * gelu_slope).astype(jnp.bfloat16)
    up_grad = (hidden_grad * gelu_value).astype(jnp.bfloat16)
    partial_grad = jnp.dot(gate_grad, gate_weight, preferred_element_type=jnp.float32) + jnp.dot(
        up_grad, up_weight, preferred_element_type=jnp.float32
    )
    scaled = lax.psum(partial_grad, ("latent", "hidden")) * norm_gain
    inner_row = jnp.sum(scaled * rebuilt, axis=1, keepdims=True)
    inverse_cube = inverse * inverse * inverse
    rebuilt_grad = (
        inverse * scaled - inverse_cube * rebuilt * (inner_row / model_width) + (rebuilt - target)
    ).astype(jnp.bfloat16)
    latent_grad = lax.dot_general(
        rebuilt_grad, dictionary, ACROSS, preferred_element_type=jnp.float32
    )
    preact_grad = jnp.where(preact > 0.0, latent_grad, 0.0).astype(jnp.bfloat16)
    dictionary_grad = lax.dot_general(
        latents, rebuilt_grad, DOWNWARD, preferred_element_type=jnp.float32
    ) + lax.dot_general(preact_grad, inputs, DOWNWARD, preferred_element_type=jnp.float32)
    return (block_output, dictionary_grad.astype(jnp.bfloat16))


def solution(mesh):
    in_specs = (
        P("groups", ("latent", "hidden")),
        P("groups", ("latent", "hidden")),
        P(("latent", "hidden"), None),
        P(("latent", "hidden")),
        P(),
        P(),
        P(("latent", "hidden"), None),
        P(("latent", "hidden"), None),
        P(("latent", "hidden"), None),
    )
    out_specs = (P("groups", ("latent", "hidden")), P(("latent", "hidden"), "groups"))
    return jax.shard_map(
        per_device, mesh=mesh, in_specs=in_specs, out_specs=out_specs, check_vma=False
    )
```

```python
import functools
import math

import jax
import jax.numpy as jnp
from jax import lax
from jax.experimental import pallas as pl
from jax.experimental.pallas import tpu as pltpu
from jax.sharding import PartitionSpec as P

CODE_STEP = 2.0 ** (-6)
NORM_EPSILON = 1e-06
GELU_ROOT = 0.7978845608028654
GELU_CUBIC = 0.044715
ACROSS = (((1,), (1,)), ((), ()))
DOWNWARD = (((0,), (0,)), ((), ()))
LANES = 128
ROW_TILE = 16
DIRECT_LIMIT = 16
VMEM_BYTES = 24 * 1024 * 1024
VMEM_BRING = 53 * 1024 * 1024
F32 = jnp.float32
BF16 = jnp.bfloat16


def gelu_parts(values):
    argument = GELU_ROOT * (values + GELU_CUBIC * values * values * values)
    tanh_value = jnp.tanh(argument)
    result = 0.5 * values * (1.0 + tanh_value)
    derivative = 0.5 * (1.0 + tanh_value) + 0.5 * values * (
        1.0 - tanh_value * tanh_value
    ) * GELU_ROOT * (1.0 + 3.0 * GELU_CUBIC * values * values)
    return (result, derivative)


def up_to(value, unit):
    return -(-value // unit) * unit


def chips_fit(chips):
    return 2 <= chips <= DIRECT_LIMIT and chips & (chips - 1) == 0


class Plan:
    def __init__(self, chips, cores, rows, own):
        self.chips, self.cores, self.rows, self.own = chips, cores, rows, own
        self.width = own * chips * cores
        self.half = self.width // cores
        self.tiles = self.half // LANES
        self.chunk = up_to(-(-self.tiles * rows // chips), ROW_TILE)
        self.flat = self.chunk * chips
        self.tail = own - LANES
        if self.tail > 0:
            self.fold_rows = min(
                size
                for size in range(ROW_TILE, rows + ROW_TILE, ROW_TILE)
                if -(-rows // size) * self.tail <= LANES
            )
            self.packed = rows + self.fold_rows
        self.columns = list(range(0, chips, 2))

    def side_blocks(self, refs):
        me = lax.axis_index("latent")
        stack_ref, *crossed_refs = refs
        for place, column in enumerate(self.columns):
            yield me ^ column, stack_ref[place]
        places = iter(self.columns)
        for ref in crossed_refs:
            for place in range(ref.shape[0]):
                yield me ^ next(places) ^ 1, ref[place]

    def pieces(self):
        for tile in range(self.tiles):
            row = 0
            while row < self.rows:
                chip, place = divmod(tile * self.rows + row, self.chunk)
                count = min(self.rows - row, self.chunk - place)
                yield tile, chip, place, row, count
                row += count

    def fits(self):
        return (
            self.cores == 2
            and chips_fit(self.chips)
            and self.rows % ROW_TILE == 0
            and self.half % LANES == 0
            and 0 < self.tail < LANES
        )


HBM = pl.BlockSpec(memory_space=pltpu.HBM)
ONCHIP = pl.BlockSpec(memory_space=pltpu.VMEM)


def shaped(*dims, dtype=F32):
    return jax.ShapeDtypeStruct(dims, dtype)


HBM = pl.BlockSpec(memory_space=pltpu.HBM)
ONCHIP = pl.BlockSpec(memory_space=pltpu.VMEM)


def shaped(*dims, dtype=F32):
    return jax.ShapeDtypeStruct(dims, dtype)


def call(body, out_shapes, operands, scratch=(), out_specs=None, flops=0, moved=0):
    return pl.pallas_call(
        body,
        out_shape=out_shapes,
        in_specs=[ONCHIP] * len(operands),
        out_specs=jax.tree.map(lambda _: ONCHIP, out_shapes) if out_specs is None else out_specs,
        scratch_shapes=list(scratch),
        compiler_params=pltpu.CompilerParams(vmem_limit_bytes=VMEM_BYTES),
        cost_estimate=pl.CostEstimate(flops=flops, bytes_accessed=moved, transcendentals=0),
    )(*operands)


def padded_bytes(array):
    *lead, rows, columns = array.shape
    item = jnp.dtype(array.dtype).itemsize
    return math.prod(lead) * up_to(rows, ROW_TILE) * up_to(columns, LANES) * item


def copies(sources, targets, sems):
    started = []
    for index, (source, target) in enumerate(zip(sources, targets)):
        one = pltpu.make_async_copy(source, target, sems.at[index])
        one.start()
        started.append(one)
    return started


def pack_block(plan, block):
    tail = block[:, LANES:]
    folded = []
    for start in range(0, plan.rows, plan.fold_rows):
        piece = tail[start : min(start + plan.fold_rows, plan.rows), :]
        short = plan.fold_rows - piece.shape[0]
        if short:
            piece = jnp.concatenate([piece, jnp.zeros((short, plan.tail), block.dtype)], axis=0)
        folded.append(piece)
    fill = LANES - len(folded) * plan.tail
    if fill:
        folded.append(jnp.zeros((plan.fold_rows, fill), block.dtype))
    return block[:, :LANES], jnp.concatenate(folded, axis=1)


def unpack_block(plan, packed):
    pieces = []
    for fold, start in enumerate(range(0, plan.rows, plan.fold_rows)):
        count = min(plan.fold_rows, plan.rows - start)
        pieces.append(
            packed[plan.rows : plan.rows + count, fold * plan.tail : (fold + 1) * plan.tail]
        )
    return jnp.concatenate([packed[: plan.rows, :], jnp.concatenate(pieces, axis=0)], axis=1)


def pack_values_body(plan, values_ref, block_ref, both_ref):
    for index in range(values_ref.shape[0]):
        main, tail = pack_block(plan, values_ref[index].astype(F32))
        start = index * plan.packed
        both_ref[0, start : start + plan.rows, :] = main.astype(BF16)
        both_ref[0, start + plan.rows : start + plan.packed, :] = tail.astype(BF16)
    block_ref[...] = both_ref[:, : plan.packed, :]


def pack_values(plan, values):
    count = values.shape[0]
    return call(
        functools.partial(pack_values_body, plan),
        [
            shaped(1, plan.packed, LANES, dtype=BF16),
            shaped(1, count * plan.packed, LANES, dtype=BF16),
        ],
        (values,),
        moved=values.size * 6,
    )


def assemble(plan, own_refs, other_refs, both, full_ref):
    core = lax.axis_index("hidden")
    for side, refs in ((core, own_refs), (1 - core, other_refs)):
        for chip, block in plan.side_blocks(refs):
            both[side, chip] = block
    for chip in range(plan.chips):
        for side in range(plan.cores):
            column = (chip * plan.cores + side) * plan.own
            full_ref[:, column : column + plan.own] = unpack_block(plan, both[side, chip])


def both_scratch(plan, dtype=BF16):
    return pltpu.VMEM((plan.cores, plan.chips, plan.packed, LANES), dtype)


def chunk_scratch(plan):
    return pltpu.VMEM((plan.chips, plan.chunk, LANES), F32)


def side_shapes(plan, dtype=F32):
    return [shaped(len(plan.columns), plan.chunk, LANES, dtype=dtype)] * 2


def half_product(plan, pairs, side, kept_ref, sent_ref, target, gain_ref=None, bias_ref=None):
    span = pl.ds(pl.multiple_of(side * plan.half, LANES), plan.half)
    total = None
    for left, right_ref in pairs:
        term = jnp.dot(left, right_ref[:, span], preferred_element_type=F32)
        total = term if total is None else total + term
    if bias_ref is not None:
        total = total + bias_ref[:, span] * jnp.where(lax.axis_index("latent") == 0, 1.0, 0.0)
    if gain_ref is not None:
        total = total * gain_ref[:, span]
    for tile, chip, place, row, count in plan.pieces():
        target[chip, place : place + count, :] = total[
            row : row + count, tile * LANES : (tile + 1) * LANES
        ]
    used = plan.tiles * plan.rows
    while used < plan.flat:
        chip, place = divmod(used, plan.chunk)
        target[chip, place:, :] = jnp.zeros((plan.chunk - place, LANES), F32)
        used += plan.chunk - place
    me = lax.axis_index("latent")
    for place, column in enumerate(plan.columns):
        kept_ref[place] = target[me ^ column]
        sent_ref[place] = target[me ^ column ^ 1]


def bring_encoder_body(dict_hbm, vectors_hbm, dict_ref, bias_ref, decoder_ref, gain_ref, sems):
    sources, targets = [dict_hbm], [dict_ref]
    start = 0
    for target in (bias_ref, decoder_ref, gain_ref):
        sources.append(vectors_hbm.at[:, start : start + target.shape[1]])
        targets.append(target)
        start += target.shape[1]
    for copy in copies(sources, targets, sems):
        copy.wait()


def bring_encoder(plan, dictionary, vectors):
    outputs = [
        shaped(*dictionary.shape, dtype=BF16),
        shaped(1, dictionary.shape[0]),
        shaped(1, plan.width),
        shaped(1, plan.width),
    ]
    return pl.pallas_call(
        bring_encoder_body,
        out_shape=outputs,
        in_specs=[HBM] * 2,
        out_specs=[ONCHIP] * len(outputs),
        scratch_shapes=[pltpu.SemaphoreType.DMA((len(outputs),))],
        compiler_params=pltpu.CompilerParams(
            vmem_limit_bytes=VMEM_BRING - sum(map(padded_bytes, outputs))
        ),
        cost_estimate=pl.CostEstimate(
            flops=0, bytes_accessed=dictionary.size * 4, transcendentals=0
        ),
    )(dictionary, vectors)


def encode_body(plan, *refs):
    own, other, (dict_ref, bias_ref, gain_ref) = refs[:2], refs[2:4], refs[4:7]
    inputs_ref, latents_ref, kept_ref, sent_ref, both, target = refs[7:]
    assemble(plan, own, other, both, inputs_ref)
    preact = (
        lax.dot_general(inputs_ref[...], dict_ref[...], ACROSS, preferred_element_type=F32)
        + bias_ref[...]
    )
    latents = jnp.maximum(preact, 0.0).astype(BF16)
    latents_ref[...] = latents
    theirs = 1 - lax.axis_index("hidden")
    half_product(plan, [(latents, dict_ref)], theirs, kept_ref, sent_ref, target, gain_ref)


def encode(plan, own, other, dictionary, encoder_bias, gain):
    latents = dictionary.shape[0]
    return call(
        functools.partial(encode_body, plan),
        [
            shaped(plan.rows, plan.width, dtype=BF16),
            shaped(plan.rows, latents, dtype=BF16),
            *side_shapes(plan),
        ],
        (*own, *other, dictionary, encoder_bias, gain),
        [both_scratch(plan), chunk_scratch(plan)],
        flops=3 * plan.rows * plan.width * latents,
        moved=dictionary.size * 2,
    )


def decode_own_body(plan, latents_ref, dict_ref, decoder_ref, gain_ref, kept_ref, sent_ref, target):
    pairs = [(latents_ref[...], dict_ref)]
    mine = lax.axis_index("hidden")
    half_product(plan, pairs, mine, kept_ref, sent_ref, target, gain_ref, decoder_ref)


def decode_own(plan, latents, dictionary, decoder_bias, gain):
    return call(
        functools.partial(decode_own_body, plan),
        side_shapes(plan),
        (latents, dictionary, decoder_bias, gain),
        [chunk_scratch(plan)],
        flops=plan.rows * plan.width * dictionary.shape[0],
        moved=dictionary.size,
    )


def back_project_body(plan, *refs):
    own, other, (down_ref, grad_ref, both, full) = refs[:2], refs[2:4], refs[4:]
    assemble(plan, own, other, both, full)
    grad_ref[...] = lax.dot_general(
        full[...], down_ref[...], ACROSS, preferred_element_type=F32
    )


def back_project(plan, own, other, down_weight):
    units = down_weight.shape[0]
    return call(
        functools.partial(back_project_body, plan),
        shaped(plan.rows, units),
        (*own, *other, down_weight),
        [both_scratch(plan), pltpu.VMEM((plan.rows, plan.width), BF16)],
        flops=2 * plan.rows * plan.width * units,
        moved=down_weight.size * 2,
    )


def join_half(plan, source, first, full_ref):
    for tile, chip, place, row, count in plan.pieces():
        column = pl.multiple_of(first + tile * LANES, LANES)
        full_ref[row : row + count, pl.ds(column, LANES)] = source[
            chip, place : place + count, :
        ]


def half_terms(plan, half, side, gate_ref, up_ref, gain_ref):
    span = pl.ds(pl.multiple_of(side * plan.half, LANES), plan.half)
    rebuilt = half.astype(F32) / gain_ref[:, span]
    squares = jnp.sum(rebuilt * rebuilt, axis=1, keepdims=True)
    gate = lax.dot_general(half, gate_ref[:, span], ACROSS, preferred_element_type=F32)
    up = lax.dot_general(half, up_ref[:, span], ACROSS, preferred_element_type=F32)
    return squares, gate, up


def mlp_first_body(plan, own_ref, gate_ref, up_ref, gain_ref, half_ref, squares_ref, gate_part_ref, up_part_ref):
    join_half(plan, own_ref, 0, half_ref)
    squares_ref[...], gate_part_ref[...], up_part_ref[...] = half_terms(
        plan, half_ref[...], lax.axis_index("hidden"), gate_ref, up_ref, gain_ref
    )


def mlp_first(plan, own, gate_weight, up_weight, gain):
    units = gate_weight.shape[0]
    return call(
        functools.partial(mlp_first_body, plan),
        [
            shaped(plan.rows, plan.half, dtype=BF16),
            shaped(plan.rows, 1),
            shaped(plan.rows, units),
            shaped(plan.rows, units),
        ],
        (own, gate_weight, up_weight, gain),
        flops=2 * plan.rows * plan.width * units,
        moved=gate_weight.size * 4,
    )


def mlp_body(plan, other_ref, gate_ref, up_ref, gain_ref, grad_ref, half_ref, squares_ref, gate_part_ref, up_part_ref, scaled_ref, inverse_ref, hidden_ref, gate_grad_ref, up_grad_ref, kept_ref, sent_ref, target):
    core = lax.axis_index("hidden")
    join_half(plan, other_ref, (1 - core) * plan.half, scaled_ref)
    other_span = pl.ds(pl.multiple_of((1 - core) * plan.half, LANES), plan.half)
    own_span = pl.ds(pl.multiple_of(core * plan.half, LANES), plan.half)
    scaled_ref[:, own_span] = half_ref[...]
    squares, gate, up = half_terms(
        plan, scaled_ref[:, other_span], 1 - core, gate_ref, up_ref, gain_ref
    )
    inverse = lax.rsqrt((squares + squares_ref[...]) / plan.width + NORM_EPSILON)
    inverse_ref[...] = inverse
    gate_proj = inverse * (gate + gate_part_ref[...])
    up_proj = inverse * (up + up_part_ref[...])
    gelu_value, gelu_slope = gelu_parts(gate_proj)
    hidden_ref[...] = (gelu_value * up_proj).astype(BF16)
    hidden_grad = grad_ref[...]
    gate_grad = (hidden_grad * up_proj * gelu_slope).astype(BF16)
    up_grad = (hidden_grad * gelu_value).astype(BF16)
    gate_grad_ref[...] = gate_grad
    up_grad_ref[...] = up_grad
    pairs = [(gate_grad, gate_ref), (up_grad, up_ref)]
    half_product(plan, pairs, 1 - core, kept_ref, sent_ref, target)


def mlp(plan, other, gate_weight, up_weight, gain, hidden_grad, first):
    units = gate_weight.shape[0]
    return call(
        functools.partial(mlp_body, plan),
        [
            shaped(plan.rows, plan.width, dtype=BF16),
            shaped(plan.rows, 1),
            shaped(plan.rows, units, dtype=BF16),
            shaped(plan.rows, units, dtype=BF16),
            shaped(plan.rows, units, dtype=BF16),
            *side_shapes(plan),
        ],
        (other, gate_weight, up_weight, gain, hidden_grad, *first),
        [chunk_scratch(plan)],
        flops=6 * plan.rows * plan.width * units,
        moved=gate_weight.size * 4,
    )


def mlp_own_body(plan, gate_grad_ref, up_grad_ref, gate_ref, up_ref, kept_ref, sent_ref, target):
    pairs = [(gate_grad_ref[...], gate_ref), (up_grad_ref[...], up_ref)]
    half_product(plan, pairs, lax.axis_index("hidden"), kept_ref, sent_ref, target)


def mlp_own(plan, gate_grad, up_grad, gate_weight, up_weight):
    return call(
        functools.partial(mlp_own_body, plan),
        side_shapes(plan),
        (gate_grad, up_grad, gate_weight, up_weight),
        [chunk_scratch(plan)],
        flops=2 * plan.rows * plan.width * gate_weight.shape[0],
        moved=gate_weight.size * 2,
    )


def project_body(plan, hidden_ref, down_ref, mine_ref, theirs_ref, both):
    core = lax.axis_index("hidden")
    terms = jnp.dot(hidden_ref[...], down_ref[...], preferred_element_type=F32)
    for chip in range(plan.chips):
        for side in range(plan.cores):
            start = (chip * plan.cores + side) * plan.own
            main, tail = pack_block(plan, terms[:, start : start + plan.own])
            both[side, chip, : plan.rows, :] = main
            both[side, chip, plan.rows :, :] = tail
    mine_ref[...] = both[core]
    theirs_ref[...] = both[1 - core]


def project(plan, hidden, down_weight):
    units = down_weight.shape[0]
    shape = (plan.chips, plan.packed, LANES)
    return call(
        functools.partial(project_body, plan),
        [shaped(*shape)] * 2,
        (hidden, down_weight),
        [both_scratch(plan, F32)],
        flops=2 * plan.rows * plan.width * units,
        moved=down_weight.size * 2,
    )


def add_pair_body(plan, first_ref, mine_ref, theirs_ref, kept_ref, sent_ref):
    me = lax.axis_index("latent")
    sent_ref[0] = first_ref[0]
    for place, column in enumerate(plan.columns):
        kept, sent = me ^ column, me ^ column ^ 1
        kept_ref[place] = mine_ref[kept] + theirs_ref[kept]
        sent_ref[1 + place] = (mine_ref[sent] + theirs_ref[sent]).astype(BF16)


def add_pair(plan, first, mine, theirs):
    count, dims = len(plan.columns), mine.shape[1:]
    return call(
        functools.partial(add_pair_body, plan),
        [shaped(count, *dims), shaped(1 + count, *dims, dtype=BF16)],
        (first, mine, theirs),
        moved=mine.size * 10,
    )


def add_sent_body(mine_ref, theirs_ref, *refs):
    *more_refs, first_ref, rest_ref = refs
    total = (mine_ref[...] + theirs_ref[...]).astype(BF16)
    first_ref[:1] = total[:1]
    for more_ref in more_refs:
        first_ref[1:] = more_ref[...]
    rest_ref[...] = total[1:]


def add_sent(plan, mine, theirs, *more):
    count, *dims = mine.shape
    first = 1 + sum(one.shape[0] for one in more)
    return call(
        add_sent_body,
        [shaped(first, *dims, dtype=BF16), shaped(count - 1, *dims, dtype=BF16)],
        (mine, theirs, *more),
        moved=mine.size * 10,
    )


def add_across_body(mine_ref, theirs_ref, got_ref, *sent_refs):
    for place, out_ref in enumerate(sent_refs):
        total = mine_ref[1 + place] + theirs_ref[1 + place] + got_ref[place].astype(F32)
        out_ref[0] = total.astype(BF16)


def add_across(plan, mine, theirs, got):
    return call(
        add_across_body,
        [shaped(1, *mine.shape[1:], dtype=BF16)] * got.shape[0],
        (mine, theirs, got),
        moved=mine.size * 10,
    )


def column_total(mine_ref, theirs_ref, *refs):
    total = mine_ref[0] + theirs_ref[0]
    for ref in refs:
        total = total + ref[0].astype(F32)
    return total.astype(BF16)


def add_column_body(*refs):
    *sources, block_ref, more_ref = refs
    block_ref[0] = column_total(*sources)
    more_ref[...] = sources[-1][1:]


def add_column(plan, mine, theirs, got, first):
    dims = mine.shape[1:]
    return call(
        add_column_body,
        [shaped(1, *dims, dtype=BF16), shaped(first.shape[0] - 1, *dims, dtype=BF16)],
        (mine, theirs, *reversed(got), first),
        moved=mine.size * 8,
    )


def add_with_output_body(plan, count, *refs):
    total = column_total(*refs[:count])
    first_ref, kept_ref, block_ref, own_ref = refs[count - 1 : count + 3]
    block_ref[0] = total
    own_ref[0] = kept_ref[0] + first_ref[1].astype(F32)
    for place, both_ref in enumerate(refs[count + 3 :], 1):
        both_ref[0, : plan.chunk, :] = total
        both_ref[0, plan.chunk :, :] = (
            kept_ref[place] + first_ref[1 + place].astype(F32)
        ).astype(BF16)


def add_with_output(plan, mine, theirs, got, first, kept):
    both = shaped(1, plan.chunk + plan.packed, LANES, dtype=BF16)
    block, out_own, *messages = call(
        functools.partial(add_with_output_body, plan, 3 + len(got)),
        [shaped(1, plan.chunk, LANES, dtype=BF16), shaped(1, plan.packed, LANES)]
        + [both] * (len(plan.columns) - 1),
        (mine, theirs, *reversed(got), first, kept),
        moved=mine.size * 12,
    )
    return block, out_own, messages


def stack_body(places, *refs):
    count = len(places)
    stack_ref, *rest_refs = refs[count:]
    rows = stack_ref.shape[1]
    for place, ref in zip(places, refs):
        stack_ref[place] = ref[0, :rows, :]
        for rest_ref in rest_refs:
            if place:
                rest_ref[place - 1] = ref[0, :rows, :]


def stack_up(plan, block, got, with_rest=False):
    dims = block.shape[1:]
    operands = [block, *got]
    places = list(range(len(operands)))
    if with_rest:
        operands, places = operands[::-1], places[::-1]
    outs = [shaped(1 + len(got), *dims, dtype=BF16), shaped(len(got), *dims, dtype=BF16)]
    return call(
        functools.partial(stack_body, places),
        outs if with_rest else outs[0],
        operands,
        moved=block.size * 16,
    )


def stack_second_body(rows, *refs):
    for place, ref in enumerate(refs[:-1]):
        refs[-1][place] = ref[0, rows:, :]


def stack_second(plan, rows, messages):
    return call(
        functools.partial(stack_second_body, rows),
        shaped(len(messages), messages[0].shape[1] - rows, LANES, dtype=BF16),
        messages,
        moved=messages[0].size * 16,
    )


def line_up_body(plan, *refs):
    for chip, block in plan.side_blocks(refs[:-1]):
        refs[-1][chip] = block


def line_up(plan, stack, *crossed):
    return call(
        functools.partial(line_up_body, plan),
        shaped(plan.chips, *stack.shape[1:], dtype=BF16),
        (stack, *crossed),
        moved=stack.size * 8,
    )


def finish_output_body(plan, own_ref, *refs):
    total = own_ref[0]
    for ref in refs[:-1]:
        total = total + ref[0, plan.chunk :, :].astype(F32)
    refs[-1][...] = unpack_block(plan, total).astype(BF16)


def finish_output(plan, own, messages):
    return call(
        functools.partial(finish_output_body, plan),
        shaped(plan.rows, plan.own, dtype=BF16),
        (own, *reversed(messages)),
        moved=own.size * 8,
    )


def prepare_body(plan, scaled_ref, inputs_ref, gain_ref, inverse_ref, factor_ref, slope_ref, base_ref):
    gain = gain_ref[...]
    inverse = inverse_ref[...]
    rebuilt = scaled_ref[...].astype(F32) / gain
    factor_ref[...] = inverse * gain
    slope_ref[...] = rebuilt * (inverse * inverse * inverse / plan.width)
    base_ref[...] = rebuilt - inputs_ref[...].astype(F32)


def prepare(plan, scaled, inputs, gain, inverse):
    return call(
        functools.partial(prepare_body, plan),
        [shaped(plan.rows, plan.width)] * 3,
        (scaled, inputs, gain, inverse),
        moved=scaled.size * 16,
    )


def dictionary_body(plan, pieces, own_ref, other_ref, scaled_ref, factor_ref, slope_ref, base_ref, inputs_ref, latents_ref, dict_ref, out_hbm, full, out_ref, out_sems):
    core = lax.axis_index("hidden")
    join_half(plan, own_ref, core * plan.half, full)
    join_half(plan, other_ref, (1 - core) * plan.half, full)
    grad = full[...].astype(F32)
    inner_row = jnp.sum(grad * scaled_ref[...].astype(F32), axis=1, keepdims=True)
    inputs = inputs_ref[...]
    rebuilt_grad = (
        grad * factor_ref[...] - inner_row * slope_ref[...] + base_ref[...]
    ).astype(BF16)
    latents = latents_ref[...]
    latent_grad = lax.dot_general(
        rebuilt_grad, dict_ref[...], ACROSS, preferred_element_type=F32
    )
    preact_grad = jnp.where(latents.astype(F32) > 0.0, latent_grad, 0.0).astype(BF16)
    left = jnp.concatenate([latents, preact_grad], axis=0)
    right = jnp.concatenate([rebuilt_grad, inputs], axis=0)
    size = plan.width // pieces
    writes = []
    for piece in range(pieces):
        span = slice(piece * size, (piece + 1) * size)
        out_ref[:, span] = lax.dot_general(
            left, right[:, span], DOWNWARD, preferred_element_type=F32
        ).astype(BF16)
        one = pltpu.make_async_copy(
            out_ref.at[:, span], out_hbm.at[:, span], out_sems.at[piece]
        )
        one.start()
        writes.append(one)
    for one in writes:
        one.wait()


def dictionary_step(plan, own, other, scaled, prepared, inputs, latents, dictionary):
    units = dictionary.shape[0]
    pieces = plan.tiles
    return call(
        functools.partial(dictionary_body, plan, pieces),
        shaped(*dictionary.shape, dtype=BF16),
        (own, other, scaled, *prepared, inputs, latents, dictionary),
        [
            pltpu.VMEM((plan.rows, plan.width), BF16),
            pltpu.VMEM(dictionary.shape, BF16),
            pltpu.SemaphoreType.DMA((pieces,)),
        ],
        out_specs=HBM,
        flops=6 * plan.rows * plan.width * units,
        moved=dictionary.size * 4,
    )


def swap(value):
    size = lax.axis_size("hidden")
    return lax.ppermute(value, "hidden", [(i, (i + 1) % size) for i in range(size)])


def partner_swap(value, bits):
    size = lax.axis_size("latent")
    return lax.ppermute(value, "latent", [(i, i ^ bits) for i in range(size)])


def cross(value):
    return partner_swap(value, 1)


def to_column(plan, blocks):
    pairs = list(zip(blocks, plan.columns[1:]))
    got = [partner_swap(one, column) for one, column in reversed(pairs)]
    return got[::-1]


def to_all_columns(plan, block):
    return [partner_swap(block, column) for column in plan.columns[1:]]


def tie(*values):
    return lax.optimization_barrier(values)


def per_device(
    input_codes,
    cotangent_codes,
    dictionary,
    encoder_bias,
    decoder_bias,
    norm_gain,
    gate_weight,
    up_weight,
    down_weight,
):
    plan = Plan(
        lax.axis_size("latent"), lax.axis_size("hidden"), input_codes.shape[0], input_codes.shape[1]
    )
    if not plan.fits():
        return per_device_plain(
            input_codes,
            cotangent_codes,
            dictionary,
            encoder_bias,
            decoder_bias,
            norm_gain,
            gate_weight,
            up_weight,
            down_weight,
        )
    vectors = jnp.concatenate([encoder_bias, decoder_bias, norm_gain]).reshape(1, -1)
    codes = jnp.stack([input_codes, cotangent_codes])
    values = (codes.astype(F32) * CODE_STEP).astype(BF16)
    block, both = pack_values(plan, values)
    got = to_all_columns(plan, both)
    stack = stack_up(plan, block, got)
    stack, vectors, late_dictionary = tie(stack, vectors, dictionary)
    stack_other, crossed = swap(stack), cross(stack)
    encoder = bring_encoder(plan, late_dictionary, vectors)
    cotangent = stack_second(plan, plan.packed, [both, *got])
    stack_other, crossed, encoder, cotangent = tie(stack_other, crossed, encoder, cotangent)
    brought, bias, decoder, gain = encoder
    inputs, latents, kept, sent = encode(
        plan, (stack, crossed), (stack_other, swap(crossed)), brought, bias, gain
    )
    sent, kept = swap(sent), swap(kept)
    own_kept, own_sent = decode_own(plan, latents, brought, decoder, gain)
    sent_first, sent_rest = add_sent(plan, own_sent, sent, cotangent)
    sent = add_across(plan, own_kept, kept, cross(sent_rest))
    sent, sent_first = tie(sent, sent_first)
    got, first = to_column(plan, sent), cross(sent_first)
    block, crossed = add_column(plan, own_kept, kept, got, first)
    cotangent_own = (cotangent, crossed)
    hidden_grad = back_project(
        plan, cotangent_own, [swap(one) for one in cotangent_own], down_weight
    )
    stack = stack_up(plan, block, to_all_columns(plan, block))
    stack_other, crossed = swap(stack), cross(stack)
    stack_other, crossed, hidden_grad = tie(stack_other, crossed, hidden_grad)
    terms = mlp_first(plan, line_up(plan, stack, crossed), gate_weight, up_weight, gain)
    scaled_other = line_up(plan, stack_other, swap(crossed))
    scaled, inverse, hidden, gate_grad, up_grad, kept, sent = mlp(
        plan, scaled_other, gate_weight, up_weight, gain, hidden_grad, terms
    )
    sent, kept = swap(sent), swap(kept)
    own_kept, own_sent = mlp_own(plan, gate_grad, up_grad, gate_weight, up_weight)
    out_mine, out_theirs = project(plan, hidden, down_weight)
    sent_first, sent_rest = add_sent(plan, own_sent, sent)
    sent_first, sent_rest, out_mine, out_theirs = tie(sent_first, sent_rest, out_mine, out_theirs)
    crossed = cross(sent_rest)
    out_kept, sent_first = add_pair(plan, sent_first, out_mine, swap(out_theirs))
    sent = add_across(plan, own_kept, kept, crossed)
    sent, sent_first, out_kept = tie(sent, sent_first, out_kept)
    got = to_column(plan, sent)
    first = cross(sent_first)
    block, out_own, messages = add_with_output(plan, own_kept, kept, got, first, out_kept)
    got = list(tie(*reversed(to_column(plan, messages))))[::-1]
    stack = stack_up(plan, block, got)
    stack, scaled_late, inputs_late = tie(stack, scaled, inputs)
    crossed, stack_other = cross(stack), swap(stack)
    prepared = prepare(plan, scaled_late, inputs_late, gain, inverse)
    block_output = finish_output(plan, out_own, got)
    grad_own = line_up(plan, stack, crossed)
    grad_other = line_up(plan, stack_other, swap(crossed))
    dictionary_grad = dictionary_step(
        plan, grad_own, grad_other, scaled, prepared, inputs, latents, brought
    )
    return (block_output, dictionary_grad)


def per_device_plain(
    input_codes,
    cotangent_codes,
    dictionary,
    encoder_bias,
    decoder_bias,
    norm_gain,
    gate_weight,
    up_weight,
    down_weight,
):
    own_width = input_codes.shape[1]
    model_width = own_width * lax.axis_size(("latent", "hidden"))
    cotangent_local = (cotangent_codes.astype(jnp.float32) * CODE_STEP).astype(jnp.bfloat16)
    inputs_local = (input_codes.astype(jnp.float32) * CODE_STEP).astype(jnp.bfloat16)
    inputs = lax.all_gather(inputs_local, ("latent", "hidden"), axis=1, tiled=True)
    preact = (
        lax.dot_general(inputs, dictionary, ACROSS, preferred_element_type=jnp.float32)
        + encoder_bias
    )
    latents = jnp.maximum(preact, 0.0).astype(jnp.bfloat16)
    partial_value = jnp.dot(latents, dictionary, preferred_element_type=jnp.float32)
    rebuilt = lax.psum(partial_value, ("latent", "hidden")) + decoder_bias
    inverse = lax.rsqrt(
        jnp.sum(rebuilt * rebuilt, axis=1, keepdims=True) / model_width + NORM_EPSILON
    )
    normed = (rebuilt * inverse * norm_gain).astype(jnp.bfloat16)
    target = inputs.astype(jnp.float32)
    gate_proj = lax.dot_general(normed, gate_weight, ACROSS, preferred_element_type=jnp.float32)
    up_proj = lax.dot_general(normed, up_weight, ACROSS, preferred_element_type=jnp.float32)
    gelu_value, gelu_slope = gelu_parts(gate_proj)
    hidden = (gelu_value * up_proj).astype(jnp.bfloat16)
    output_terms = jnp.dot(hidden, down_weight, preferred_element_type=jnp.float32)
    block_output = lax.psum_scatter(
        output_terms, ("latent", "hidden"), scatter_dimension=1, tiled=True
    ).astype(jnp.bfloat16)
    hidden_grad = lax.dot_general(
        lax.all_gather(cotangent_local, ("latent", "hidden"), axis=1, tiled=True),
        down_weight,
        ACROSS,
        preferred_element_type=jnp.float32,
    )
    gate_grad = (hidden_grad * up_proj * gelu_slope).astype(jnp.bfloat16)
    up_grad = (hidden_grad * gelu_value).astype(jnp.bfloat16)
    partial_grad = jnp.dot(gate_grad, gate_weight, preferred_element_type=jnp.float32) + jnp.dot(
        up_grad, up_weight, preferred_element_type=jnp.float32
    )
    scaled = lax.psum(partial_grad, ("latent", "hidden")) * norm_gain
    inner_row = jnp.sum(scaled * rebuilt, axis=1, keepdims=True)
    inverse_cube = inverse * inverse * inverse
    rebuilt_grad = (
        inverse * scaled - inverse_cube * rebuilt * (inner_row / model_width) + (rebuilt - target)
    ).astype(jnp.bfloat16)
    latent_grad = lax.dot_general(
        rebuilt_grad, dictionary, ACROSS, preferred_element_type=jnp.float32
    )
    preact_grad = jnp.where(preact > 0.0, latent_grad, 0.0).astype(jnp.bfloat16)
    dictionary_grad = lax.dot_general(
        latents, rebuilt_grad, DOWNWARD, preferred_element_type=jnp.float32
    ) + lax.dot_general(preact_grad, inputs, DOWNWARD, preferred_element_type=jnp.float32)
    return (block_output, dictionary_grad.astype(jnp.bfloat16))


def solution(mesh):
    in_specs = (
        P("groups", ("latent", "hidden")),
        P("groups", ("latent", "hidden")),
        P(("latent", "hidden"), None),
        P(("latent", "hidden")),
        P(),
        P(),
        P(("latent", "hidden"), None),
        P(("latent", "hidden"), None),
        P(("latent", "hidden"), None),
    )
    out_specs = (P("groups", ("latent", "hidden")), P(("latent", "hidden"), "groups"))
    return jax.shard_map(
        per_device, mesh=mesh, in_specs=in_specs, out_specs=out_specs, check_vma=False
    )
```

```python
import functools
import math

import jax
import jax.numpy as jnp
from jax import lax
from jax.experimental import pallas as pl
from jax.experimental.pallas import tpu as pltpu
from jax.sharding import PartitionSpec as P

CODE_STEP = 2.0 ** (-6)
NORM_EPSILON = 1e-06
GELU_ROOT = 0.7978845608028654
GELU_CUBIC = 0.044715
ACROSS = (((1,), (1,)), ((), ()))
DOWNWARD = (((0,), (0,)), ((), ()))
LANES = 128
ROW_TILE = 16
DIRECT_LIMIT = 16
VMEM_BYTES = 24 * 1024 * 1024
VMEM_BRING = 53 * 1024 * 1024
F32 = jnp.float32
BF16 = jnp.bfloat16


def gelu_parts(values):
    argument = GELU_ROOT * (values + GELU_CUBIC * values * values * values)
    tanh_value = jnp.tanh(argument)
    result = 0.5 * values * (1.0 + tanh_value)
    derivative = 0.5 * (1.0 + tanh_value) + 0.5 * values * (
        1.0 - tanh_value * tanh_value
    ) * GELU_ROOT * (1.0 + 3.0 * GELU_CUBIC * values * values)
    return (result, derivative)


def up_to(value, unit):
    return -(-value // unit) * unit


def chips_fit(chips):
    return 2 <= chips <= DIRECT_LIMIT and chips & (chips - 1) == 0


class Plan:
    def __init__(self, chips, cores, rows, own):
        self.chips, self.cores, self.rows, self.own = chips, cores, rows, own
        self.width = own * chips * cores
        self.half = self.width // cores
        self.tiles = self.half // LANES
        self.chunk = up_to(-(-self.tiles * rows // chips), ROW_TILE)
        self.flat = self.chunk * chips
        self.tail = own - LANES
        if self.tail > 0:
            self.fold_rows = min(
                size
                for size in range(ROW_TILE, rows + ROW_TILE, ROW_TILE)
                if -(-rows // size) * self.tail <= LANES
            )
            self.packed = rows + self.fold_rows
        self.columns = list(range(0, chips, 2))

    def side_blocks(self, refs):
        me = lax.axis_index("latent")
        stack_ref, *crossed_refs = refs
        for place, column in enumerate(self.columns):
            yield me ^ column, stack_ref[place]
        places = iter(self.columns)
        for ref in crossed_refs:
            for place in range(ref.shape[0]):
                yield me ^ next(places) ^ 1, ref[place]

    def pieces(self):
        for tile in range(self.tiles):
            row = 0
            while row < self.rows:
                chip, place = divmod(tile * self.rows + row, self.chunk)
                count = min(self.rows - row, self.chunk - place)
                yield tile, chip, place, row, count
                row += count

    def fits(self):
        return (
            self.cores == 2
            and chips_fit(self.chips)
            and self.rows % ROW_TILE == 0
            and self.half % LANES == 0
            and 0 < self.tail < LANES
        )


HBM = pl.BlockSpec(memory_space=pltpu.HBM)
ONCHIP = pl.BlockSpec(memory_space=pltpu.VMEM)


def shaped(*dims, dtype=F32):
    return jax.ShapeDtypeStruct(dims, dtype)


HBM = pl.BlockSpec(memory_space=pltpu.HBM)
ONCHIP = pl.BlockSpec(memory_space=pltpu.VMEM)


def shaped(*dims, dtype=F32):
    return jax.ShapeDtypeStruct(dims, dtype)


def call(body, out_shapes, operands, scratch=(), out_specs=None, flops=0, moved=0):
    return pl.pallas_call(
        body,
        out_shape=out_shapes,
        in_specs=[ONCHIP] * len(operands),
        out_specs=jax.tree.map(lambda _: ONCHIP, out_shapes) if out_specs is None else out_specs,
        scratch_shapes=list(scratch),
        compiler_params=pltpu.CompilerParams(vmem_limit_bytes=VMEM_BYTES),
        cost_estimate=pl.CostEstimate(flops=flops, bytes_accessed=moved, transcendentals=0),
    )(*operands)


def padded_bytes(array):
    *lead, rows, columns = array.shape
    item = jnp.dtype(array.dtype).itemsize
    return math.prod(lead) * up_to(rows, ROW_TILE) * up_to(columns, LANES) * item


def copies(sources, targets, sems):
    started = []
    for index, (source, target) in enumerate(zip(sources, targets)):
        one = pltpu.make_async_copy(source, target, sems.at[index])
        one.start()
        started.append(one)
    return started


def pack_block(plan, block):
    tail = block[:, LANES:]
    folded = []
    for start in range(0, plan.rows, plan.fold_rows):
        piece = tail[start : min(start + plan.fold_rows, plan.rows), :]
        short = plan.fold_rows - piece.shape[0]
        if short:
            piece = jnp.concatenate([piece, jnp.zeros((short, plan.tail), block.dtype)], axis=0)
        folded.append(piece)
    fill = LANES - len(folded) * plan.tail
    if fill:
        folded.append(jnp.zeros((plan.fold_rows, fill), block.dtype))
    return block[:, :LANES], jnp.concatenate(folded, axis=1)


def unpack_block(plan, packed):
    pieces = []
    for fold, start in enumerate(range(0, plan.rows, plan.fold_rows)):
        count = min(plan.fold_rows, plan.rows - start)
        pieces.append(
            packed[plan.rows : plan.rows + count, fold * plan.tail : (fold + 1) * plan.tail]
        )
    return jnp.concatenate([packed[: plan.rows, :], jnp.concatenate(pieces, axis=0)], axis=1)


def pack_values_body(plan, values_ref, block_ref, both_ref):
    for index in range(values_ref.shape[0]):
        main, tail = pack_block(plan, values_ref[index].astype(F32))
        start = index * plan.packed
        both_ref[0, start : start + plan.rows, :] = main.astype(BF16)
        both_ref[0, start + plan.rows : start + plan.packed, :] = tail.astype(BF16)
    block_ref[...] = both_ref[:, : plan.packed, :]


def pack_values(plan, values):
    count = values.shape[0]
    return call(
        functools.partial(pack_values_body, plan),
        [
            shaped(1, plan.packed, LANES, dtype=BF16),
            shaped(1, count * plan.packed, LANES, dtype=BF16),
        ],
        (values,),
        moved=values.size * 6,
    )


def assemble(plan, own_refs, other_refs, both, full_ref):
    core = lax.axis_index("hidden")
    for side, refs in ((core, own_refs), (1 - core, other_refs)):
        for chip, block in plan.side_blocks(refs):
            both[side, chip] = block
    for chip in range(plan.chips):
        for side in range(plan.cores):
            column = (chip * plan.cores + side) * plan.own
            full_ref[:, column : column + plan.own] = unpack_block(plan, both[side, chip])


def both_scratch(plan, dtype=BF16):
    return pltpu.VMEM((plan.cores, plan.chips, plan.packed, LANES), dtype)


def chunk_scratch(plan):
    return pltpu.VMEM((plan.chips, plan.chunk, LANES), F32)


def side_shapes(plan, dtype=F32):
    return [shaped(len(plan.columns), plan.chunk, LANES, dtype=dtype)] * 2


def half_product(plan, pairs, side, kept_ref, sent_ref, target, gain_ref=None, bias_ref=None):
    span = pl.ds(pl.multiple_of(side * plan.half, LANES), plan.half)
    total = None
    for left, right_ref in pairs:
        term = jnp.dot(left, right_ref[:, span], preferred_element_type=F32)
        total = term if total is None else total + term
    if bias_ref is not None:
        total = total + bias_ref[:, span] * jnp.where(lax.axis_index("latent") == 0, 1.0, 0.0)
    if gain_ref is not None:
        total = total * gain_ref[:, span]
    for tile, chip, place, row, count in plan.pieces():
        target[chip, place : place + count, :] = total[
            row : row + count, tile * LANES : (tile + 1) * LANES
        ]
    used = plan.tiles * plan.rows
    while used < plan.flat:
        chip, place = divmod(used, plan.chunk)
        target[chip, place:, :] = jnp.zeros((plan.chunk - place, LANES), F32)
        used += plan.chunk - place
    me = lax.axis_index("latent")
    for place, column in enumerate(plan.columns):
        kept_ref[place] = target[me ^ column]
        sent_ref[place] = target[me ^ column ^ 1]


def bring_encoder_body(dict_hbm, vectors_hbm, dict_ref, bias_ref, decoder_ref, gain_ref, sems):
    sources, targets = [dict_hbm], [dict_ref]
    start = 0
    for target in (bias_ref, decoder_ref, gain_ref):
        sources.append(vectors_hbm.at[:, start : start + target.shape[1]])
        targets.append(target)
        start += target.shape[1]
    for copy in copies(sources, targets, sems):
        copy.wait()


def bring_encoder(plan, dictionary, vectors):
    outputs = [
        shaped(*dictionary.shape, dtype=BF16),
        shaped(1, dictionary.shape[0]),
        shaped(1, plan.width),
        shaped(1, plan.width),
    ]
    return pl.pallas_call(
        bring_encoder_body,
        out_shape=outputs,
        in_specs=[HBM] * 2,
        out_specs=[ONCHIP] * len(outputs),
        scratch_shapes=[pltpu.SemaphoreType.DMA((len(outputs),))],
        compiler_params=pltpu.CompilerParams(
            vmem_limit_bytes=VMEM_BRING - sum(map(padded_bytes, outputs))
        ),
        cost_estimate=pl.CostEstimate(
            flops=0, bytes_accessed=dictionary.size * 4, transcendentals=0
        ),
    )(dictionary, vectors)


def encode_body(plan, *refs):
    own, other, (dict_ref, bias_ref, gain_ref) = refs[:2], refs[2:4], refs[4:7]
    inputs_ref, latents_ref, kept_ref, sent_ref, both, target = refs[7:]
    assemble(plan, own, other, both, inputs_ref)
    preact = (
        lax.dot_general(inputs_ref[...], dict_ref[...], ACROSS, preferred_element_type=F32)
        + bias_ref[...]
    )
    latents = jnp.maximum(preact, 0.0).astype(BF16)
    latents_ref[...] = latents
    theirs = 1 - lax.axis_index("hidden")
    half_product(plan, [(latents, dict_ref)], theirs, kept_ref, sent_ref, target, gain_ref)


def encode(plan, own, other, dictionary, encoder_bias, gain):
    latents = dictionary.shape[0]
    return call(
        functools.partial(encode_body, plan),
        [
            shaped(plan.rows, plan.width, dtype=BF16),
            shaped(plan.rows, latents, dtype=BF16),
            *side_shapes(plan),
        ],
        (*own, *other, dictionary, encoder_bias, gain),
        [both_scratch(plan), chunk_scratch(plan)],
        flops=3 * plan.rows * plan.width * latents,
        moved=dictionary.size * 2,
    )


def decode_own_body(plan, latents_ref, dict_ref, decoder_ref, gain_ref, kept_ref, sent_ref, target):
    pairs = [(latents_ref[...], dict_ref)]
    mine = lax.axis_index("hidden")
    half_product(plan, pairs, mine, kept_ref, sent_ref, target, gain_ref, decoder_ref)


def decode_own(plan, latents, dictionary, decoder_bias, gain):
    return call(
        functools.partial(decode_own_body, plan),
        side_shapes(plan),
        (latents, dictionary, decoder_bias, gain),
        [chunk_scratch(plan)],
        flops=plan.rows * plan.width * dictionary.shape[0],
        moved=dictionary.size,
    )


def back_project_body(plan, *refs):
    own, other, (down_ref, grad_ref, both, full) = refs[:2], refs[2:4], refs[4:]
    assemble(plan, own, other, both, full)
    grad_ref[...] = lax.dot_general(
        full[...], down_ref[...], ACROSS, preferred_element_type=F32
    )


def back_project(plan, own, other, down_weight):
    units = down_weight.shape[0]
    return call(
        functools.partial(back_project_body, plan),
        shaped(plan.rows, units),
        (*own, *other, down_weight),
        [both_scratch(plan), pltpu.VMEM((plan.rows, plan.width), BF16)],
        flops=2 * plan.rows * plan.width * units,
        moved=down_weight.size * 2,
    )


def join_half(plan, source, first, full_ref):
    for tile, chip, place, row, count in plan.pieces():
        column = pl.multiple_of(first + tile * LANES, LANES)
        full_ref[row : row + count, pl.ds(column, LANES)] = source[
            chip, place : place + count, :
        ]


def half_terms(plan, half, side, gate_ref, up_ref, gain_ref):
    span = pl.ds(pl.multiple_of(side * plan.half, LANES), plan.half)
    rebuilt = half.astype(F32) / gain_ref[:, span]
    squares = jnp.sum(rebuilt * rebuilt, axis=1, keepdims=True)
    gate = lax.dot_general(half, gate_ref[:, span], ACROSS, preferred_element_type=F32)
    up = lax.dot_general(half, up_ref[:, span], ACROSS, preferred_element_type=F32)
    return squares, gate, up


def mlp_first_body(plan, own_ref, gate_ref, up_ref, gain_ref, half_ref, squares_ref, gate_part_ref, up_part_ref):
    join_half(plan, own_ref, 0, half_ref)
    squares_ref[...], gate_part_ref[...], up_part_ref[...] = half_terms(
        plan, half_ref[...], lax.axis_index("hidden"), gate_ref, up_ref, gain_ref
    )


def mlp_first(plan, own, gate_weight, up_weight, gain):
    units = gate_weight.shape[0]
    return call(
        functools.partial(mlp_first_body, plan),
        [
            shaped(plan.rows, plan.half, dtype=BF16),
            shaped(plan.rows, 1),
            shaped(plan.rows, units),
            shaped(plan.rows, units),
        ],
        (own, gate_weight, up_weight, gain),
        flops=2 * plan.rows * plan.width * units,
        moved=gate_weight.size * 4,
    )


def mlp_body(plan, other_ref, gate_ref, up_ref, gain_ref, grad_ref, half_ref, squares_ref, gate_part_ref, up_part_ref, scaled_ref, inverse_ref, hidden_ref, gate_grad_ref, up_grad_ref, kept_ref, sent_ref, target):
    core = lax.axis_index("hidden")
    join_half(plan, other_ref, (1 - core) * plan.half, scaled_ref)
    other_span = pl.ds(pl.multiple_of((1 - core) * plan.half, LANES), plan.half)
    own_span = pl.ds(pl.multiple_of(core * plan.half, LANES), plan.half)
    scaled_ref[:, own_span] = half_ref[...]
    squares, gate, up = half_terms(
        plan, scaled_ref[:, other_span], 1 - core, gate_ref, up_ref, gain_ref
    )
    inverse = lax.rsqrt((squares + squares_ref[...]) / plan.width + NORM_EPSILON)
    inverse_ref[...] = inverse
    gate_proj = inverse * (gate + gate_part_ref[...])
    up_proj = inverse * (up + up_part_ref[...])
    gelu_value, gelu_slope = gelu_parts(gate_proj)
    hidden_ref[...] = (gelu_value * up_proj).astype(BF16)
    hidden_grad = grad_ref[...]
    gate_grad = (hidden_grad * up_proj * gelu_slope).astype(BF16)
    up_grad = (hidden_grad * gelu_value).astype(BF16)
    gate_grad_ref[...] = gate_grad
    up_grad_ref[...] = up_grad
    pairs = [(gate_grad, gate_ref), (up_grad, up_ref)]
    half_product(plan, pairs, 1 - core, kept_ref, sent_ref, target)


def mlp(plan, other, gate_weight, up_weight, gain, hidden_grad, first):
    units = gate_weight.shape[0]
    return call(
        functools.partial(mlp_body, plan),
        [
            shaped(plan.rows, plan.width, dtype=BF16),
            shaped(plan.rows, 1),
            shaped(plan.rows, units, dtype=BF16),
            shaped(plan.rows, units, dtype=BF16),
            shaped(plan.rows, units, dtype=BF16),
            *side_shapes(plan),
        ],
        (other, gate_weight, up_weight, gain, hidden_grad, *first),
        [chunk_scratch(plan)],
        flops=6 * plan.rows * plan.width * units,
        moved=gate_weight.size * 4,
    )


def mlp_own_body(plan, gate_grad_ref, up_grad_ref, gate_ref, up_ref, kept_ref, sent_ref, target):
    pairs = [(gate_grad_ref[...], gate_ref), (up_grad_ref[...], up_ref)]
    half_product(plan, pairs, lax.axis_index("hidden"), kept_ref, sent_ref, target)


def mlp_own(plan, gate_grad, up_grad, gate_weight, up_weight):
    return call(
        functools.partial(mlp_own_body, plan),
        side_shapes(plan),
        (gate_grad, up_grad, gate_weight, up_weight),
        [chunk_scratch(plan)],
        flops=2 * plan.rows * plan.width * gate_weight.shape[0],
        moved=gate_weight.size * 2,
    )


def project_body(plan, hidden_ref, down_ref, mine_ref, theirs_ref, both):
    core = lax.axis_index("hidden")
    terms = jnp.dot(hidden_ref[...], down_ref[...], preferred_element_type=F32).astype(BF16)
    for chip in range(plan.chips):
        for side in range(plan.cores):
            start = (chip * plan.cores + side) * plan.own
            main, tail = pack_block(plan, terms[:, start : start + plan.own])
            both[side, chip, : plan.rows, :] = main
            both[side, chip, plan.rows :, :] = tail
    mine_ref[...] = both[core]
    theirs_ref[...] = both[1 - core]


def project(plan, hidden, down_weight):
    units = down_weight.shape[0]
    shape = (plan.chips, plan.packed, LANES)
    return call(
        functools.partial(project_body, plan),
        [shaped(*shape, dtype=BF16)] * 2,
        (hidden, down_weight),
        [both_scratch(plan)],
        flops=2 * plan.rows * plan.width * units,
        moved=down_weight.size * 2,
    )


def add_pair_body(plan, first_ref, mine_ref, theirs_ref, kept_ref, sent_ref):
    me = lax.axis_index("latent")
    sent_ref[0] = first_ref[0]
    for place, column in enumerate(plan.columns):
        kept, sent = me ^ column, me ^ column ^ 1
        kept_ref[place] = mine_ref[kept].astype(F32) + theirs_ref[kept].astype(F32)
        sent_ref[1 + place] = (
            mine_ref[sent].astype(F32) + theirs_ref[sent].astype(F32)
        ).astype(BF16)


def add_pair(plan, first, mine, theirs):
    count, dims = len(plan.columns), mine.shape[1:]
    return call(
        functools.partial(add_pair_body, plan),
        [shaped(count, *dims), shaped(1 + count, *dims, dtype=BF16)],
        (first, mine, theirs),
        moved=mine.size * 10,
    )


def add_sent_body(mine_ref, theirs_ref, *refs):
    *more_refs, first_ref, rest_ref = refs
    total = (mine_ref[...] + theirs_ref[...]).astype(BF16)
    first_ref[:1] = total[:1]
    for more_ref in more_refs:
        first_ref[1:] = more_ref[...]
    rest_ref[...] = total[1:]


def add_sent(plan, mine, theirs, *more):
    count, *dims = mine.shape
    first = 1 + sum(one.shape[0] for one in more)
    return call(
        add_sent_body,
        [shaped(first, *dims, dtype=BF16), shaped(count - 1, *dims, dtype=BF16)],
        (mine, theirs, *more),
        moved=mine.size * 10,
    )


def add_across_body(mine_ref, theirs_ref, got_ref, *sent_refs):
    for place, out_ref in enumerate(sent_refs):
        total = mine_ref[1 + place] + theirs_ref[1 + place] + got_ref[place].astype(F32)
        out_ref[0] = total.astype(BF16)


def add_across(plan, mine, theirs, got):
    return call(
        add_across_body,
        [shaped(1, *mine.shape[1:], dtype=BF16)] * got.shape[0],
        (mine, theirs, got),
        moved=mine.size * 10,
    )


def column_total(mine_ref, theirs_ref, *refs):
    total = mine_ref[0] + theirs_ref[0]
    for ref in refs:
        total = total + ref[0].astype(F32)
    return total.astype(BF16)


def add_column_body(*refs):
    *sources, block_ref, more_ref = refs
    block_ref[0] = column_total(*sources)
    more_ref[...] = sources[-1][1:]


def add_column(plan, mine, theirs, got, first):
    dims = mine.shape[1:]
    return call(
        add_column_body,
        [shaped(1, *dims, dtype=BF16), shaped(first.shape[0] - 1, *dims, dtype=BF16)],
        (mine, theirs, *reversed(got), first),
        moved=mine.size * 8,
    )


def add_with_output_body(plan, count, *refs):
    total = column_total(*refs[:count])
    first_ref, kept_ref, block_ref, own_ref = refs[count - 1 : count + 3]
    block_ref[0] = total
    own_ref[0] = kept_ref[0] + first_ref[1].astype(F32)
    for place, both_ref in enumerate(refs[count + 3 :], 1):
        both_ref[0, : plan.chunk, :] = total
        both_ref[0, plan.chunk :, :] = (
            kept_ref[place] + first_ref[1 + place].astype(F32)
        ).astype(BF16)


def add_with_output(plan, mine, theirs, got, first, kept):
    both = shaped(1, plan.chunk + plan.packed, LANES, dtype=BF16)
    block, out_own, *messages = call(
        functools.partial(add_with_output_body, plan, 3 + len(got)),
        [shaped(1, plan.chunk, LANES, dtype=BF16), shaped(1, plan.packed, LANES)]
        + [both] * (len(plan.columns) - 1),
        (mine, theirs, *reversed(got), first, kept),
        moved=mine.size * 12,
    )
    return block, out_own, messages


def stack_body(places, *refs):
    count = len(places)
    stack_ref, *rest_refs = refs[count:]
    rows = stack_ref.shape[1]
    for place, ref in zip(places, refs):
        stack_ref[place] = ref[0, :rows, :]
        for rest_ref in rest_refs:
            if place:
                rest_ref[place - 1] = ref[0, :rows, :]


def stack_up(plan, block, got, with_rest=False):
    dims = block.shape[1:]
    operands = [block, *got]
    places = list(range(len(operands)))
    if with_rest:
        operands, places = operands[::-1], places[::-1]
    outs = [shaped(1 + len(got), *dims, dtype=BF16), shaped(len(got), *dims, dtype=BF16)]
    return call(
        functools.partial(stack_body, places),
        outs if with_rest else outs[0],
        operands,
        moved=block.size * 16,
    )


def stack_second_body(rows, *refs):
    for place, ref in enumerate(refs[:-1]):
        refs[-1][place] = ref[0, rows:, :]


def stack_second(plan, rows, messages):
    return call(
        functools.partial(stack_second_body, rows),
        shaped(len(messages), messages[0].shape[1] - rows, LANES, dtype=BF16),
        messages,
        moved=messages[0].size * 16,
    )


def line_up_body(plan, *refs):
    for chip, block in plan.side_blocks(refs[:-1]):
        refs[-1][chip] = block


def line_up(plan, stack, *crossed):
    return call(
        functools.partial(line_up_body, plan),
        shaped(plan.chips, *stack.shape[1:], dtype=BF16),
        (stack, *crossed),
        moved=stack.size * 8,
    )


def finish_output_body(plan, own_ref, *refs):
    total = own_ref[0]
    for ref in refs[:-1]:
        total = total + ref[0, plan.chunk :, :].astype(F32)
    refs[-1][...] = unpack_block(plan, total).astype(BF16)


def finish_output(plan, own, messages):
    return call(
        functools.partial(finish_output_body, plan),
        shaped(plan.rows, plan.own, dtype=BF16),
        (own, *reversed(messages)),
        moved=own.size * 8,
    )


def prepare_body(plan, scaled_ref, inputs_ref, gain_ref, inverse_ref, factor_ref, slope_ref, base_ref):
    gain = gain_ref[...]
    inverse = inverse_ref[...]
    rebuilt = scaled_ref[...].astype(F32) / gain
    factor_ref[...] = inverse * gain
    slope_ref[...] = rebuilt * (inverse * inverse * inverse / plan.width)
    base_ref[...] = rebuilt - inputs_ref[...].astype(F32)


def prepare(plan, scaled, inputs, gain, inverse):
    return call(
        functools.partial(prepare_body, plan),
        [shaped(plan.rows, plan.width)] * 3,
        (scaled, inputs, gain, inverse),
        moved=scaled.size * 16,
    )


def dictionary_body(plan, pieces, own_ref, other_ref, scaled_ref, factor_ref, slope_ref, base_ref, inputs_ref, latents_ref, dict_ref, out_hbm, full, out_ref, out_sems):
    core = lax.axis_index("hidden")
    join_half(plan, own_ref, core * plan.half, full)
    join_half(plan, other_ref, (1 - core) * plan.half, full)
    grad = full[...].astype(F32)
    inner_row = jnp.sum(grad * scaled_ref[...].astype(F32), axis=1, keepdims=True)
    inputs = inputs_ref[...]
    rebuilt_grad = (
        grad * factor_ref[...] - inner_row * slope_ref[...] + base_ref[...]
    ).astype(BF16)
    latents = latents_ref[...]
    latent_grad = lax.dot_general(
        rebuilt_grad, dict_ref[...], ACROSS, preferred_element_type=F32
    )
    preact_grad = jnp.where(latents.astype(F32) > 0.0, latent_grad, 0.0).astype(BF16)
    left = jnp.concatenate([latents, preact_grad], axis=0)
    right = jnp.concatenate([rebuilt_grad, inputs], axis=0)
    size = plan.width // pieces
    writes = []
    for piece in range(pieces):
        span = slice(piece * size, (piece + 1) * size)
        out_ref[:, span] = lax.dot_general(
            left, right[:, span], DOWNWARD, preferred_element_type=F32
        ).astype(BF16)
        one = pltpu.make_async_copy(
            out_ref.at[:, span], out_hbm.at[:, span], out_sems.at[piece]
        )
        one.start()
        writes.append(one)
    for one in writes:
        one.wait()


def dictionary_step(plan, own, other, scaled, prepared, inputs, latents, dictionary):
    units = dictionary.shape[0]
    pieces = plan.tiles
    return call(
        functools.partial(dictionary_body, plan, pieces),
        shaped(*dictionary.shape, dtype=BF16),
        (own, other, scaled, *prepared, inputs, latents, dictionary),
        [
            pltpu.VMEM((plan.rows, plan.width), BF16),
            pltpu.VMEM(dictionary.shape, BF16),
            pltpu.SemaphoreType.DMA((pieces,)),
        ],
        out_specs=HBM,
        flops=6 * plan.rows * plan.width * units,
        moved=dictionary.size * 4,
    )


def swap(value):
    size = lax.axis_size("hidden")
    return lax.ppermute(value, "hidden", [(i, (i + 1) % size) for i in range(size)])


def partner_swap(value, bits):
    size = lax.axis_size("latent")
    return lax.ppermute(value, "latent", [(i, i ^ bits) for i in range(size)])


def cross(value):
    return partner_swap(value, 1)


def to_column(plan, blocks):
    pairs = list(zip(blocks, plan.columns[1:]))
    got = [partner_swap(one, column) for one, column in reversed(pairs)]
    return got[::-1]


def to_all_columns(plan, block):
    return [partner_swap(block, column) for column in plan.columns[1:]]


def tie(*values):
    return lax.optimization_barrier(values)


def per_device(
    input_codes,
    cotangent_codes,
    dictionary,
    encoder_bias,
    decoder_bias,
    norm_gain,
    gate_weight,
    up_weight,
    down_weight,
):
    plan = Plan(
        lax.axis_size("latent"), lax.axis_size("hidden"), input_codes.shape[0], input_codes.shape[1]
    )
    if not plan.fits():
        return per_device_plain(
            input_codes,
            cotangent_codes,
            dictionary,
            encoder_bias,
            decoder_bias,
            norm_gain,
            gate_weight,
            up_weight,
            down_weight,
        )
    vectors = jnp.concatenate([encoder_bias, decoder_bias, norm_gain]).reshape(1, -1)
    codes = jnp.stack([input_codes, cotangent_codes])
    values = (codes.astype(F32) * CODE_STEP).astype(BF16)
    block, both = pack_values(plan, values)
    got = list(tie(*reversed(to_all_columns(plan, both))))[::-1]
    stack = stack_up(plan, block, got)
    stack, vectors, late_dictionary = tie(stack, vectors, dictionary)
    stack_other, crossed = swap(stack), cross(stack)
    encoder = bring_encoder(plan, late_dictionary, vectors)
    cotangent = stack_second(plan, plan.packed, [both, *got])
    stack_other, crossed, encoder, cotangent = tie(stack_other, crossed, encoder, cotangent)
    brought, bias, decoder, gain = encoder
    inputs, latents, kept, sent = encode(
        plan, (stack, crossed), (stack_other, swap(crossed)), brought, bias, gain
    )
    sent, kept = swap(sent), swap(kept)
    own_kept, own_sent = decode_own(plan, latents, brought, decoder, gain)
    sent_first, sent_rest = add_sent(plan, own_sent, sent, cotangent)
    sent = add_across(plan, own_kept, kept, cross(sent_rest))
    sent, sent_first = tie(sent, sent_first)
    got, first = to_column(plan, sent), cross(sent_first)
    block, crossed = add_column(plan, own_kept, kept, got, first)
    cotangent_own = (cotangent, crossed)
    hidden_grad = back_project(
        plan, cotangent_own, [swap(one) for one in cotangent_own], down_weight
    )
    stack = stack_up(plan, block, to_all_columns(plan, block))
    stack_other, crossed = swap(stack), cross(stack)
    stack_other, crossed, hidden_grad = tie(stack_other, crossed, hidden_grad)
    terms = mlp_first(plan, line_up(plan, stack, crossed), gate_weight, up_weight, gain)
    scaled_other = line_up(plan, stack_other, swap(crossed))
    scaled, inverse, hidden, gate_grad, up_grad, kept, sent = mlp(
        plan, scaled_other, gate_weight, up_weight, gain, hidden_grad, terms
    )
    sent, kept = swap(sent), swap(kept)
    own_kept, own_sent = mlp_own(plan, gate_grad, up_grad, gate_weight, up_weight)
    out_mine, out_theirs = project(plan, hidden, down_weight)
    sent_first, sent_rest = add_sent(plan, own_sent, sent)
    sent_first, sent_rest, out_mine, out_theirs = tie(sent_first, sent_rest, out_mine, out_theirs)
    crossed = cross(sent_rest)
    out_kept, sent_first = add_pair(plan, sent_first, out_mine, swap(out_theirs))
    sent = add_across(plan, own_kept, kept, crossed)
    sent, sent_first, out_kept = tie(sent, sent_first, out_kept)
    got = to_column(plan, sent)
    first = cross(sent_first)
    block, out_own, messages = add_with_output(plan, own_kept, kept, got, first, out_kept)
    got = list(tie(*to_column(plan, messages)))
    stack = stack_up(plan, block, got)
    stack, scaled_late, inputs_late = tie(stack, scaled, inputs)
    crossed, stack_other = cross(stack), swap(stack)
    prepared = prepare(plan, scaled_late, inputs_late, gain, inverse)
    block_output = finish_output(plan, out_own, got)
    grad_own = line_up(plan, stack, crossed)
    grad_other = line_up(plan, stack_other, swap(crossed))
    dictionary_grad = dictionary_step(
        plan, grad_own, grad_other, scaled, prepared, inputs, latents, brought
    )
    return (block_output, dictionary_grad)


def per_device_plain(
    input_codes,
    cotangent_codes,
    dictionary,
    encoder_bias,
    decoder_bias,
    norm_gain,
    gate_weight,
    up_weight,
    down_weight,
):
    own_width = input_codes.shape[1]
    model_width = own_width * lax.axis_size(("latent", "hidden"))
    cotangent_local = (cotangent_codes.astype(jnp.float32) * CODE_STEP).astype(jnp.bfloat16)
    inputs_local = (input_codes.astype(jnp.float32) * CODE_STEP).astype(jnp.bfloat16)
    inputs = lax.all_gather(inputs_local, ("latent", "hidden"), axis=1, tiled=True)
    preact = (
        lax.dot_general(inputs, dictionary, ACROSS, preferred_element_type=jnp.float32)
        + encoder_bias
    )
    latents = jnp.maximum(preact, 0.0).astype(jnp.bfloat16)
    partial_value = jnp.dot(latents, dictionary, preferred_element_type=jnp.float32)
    rebuilt = lax.psum(partial_value, ("latent", "hidden")) + decoder_bias
    inverse = lax.rsqrt(
        jnp.sum(rebuilt * rebuilt, axis=1, keepdims=True) / model_width + NORM_EPSILON
    )
    normed = (rebuilt * inverse * norm_gain).astype(jnp.bfloat16)
    target = inputs.astype(jnp.float32)
    gate_proj = lax.dot_general(normed, gate_weight, ACROSS, preferred_element_type=jnp.float32)
    up_proj = lax.dot_general(normed, up_weight, ACROSS, preferred_element_type=jnp.float32)
    gelu_value, gelu_slope = gelu_parts(gate_proj)
    hidden = (gelu_value * up_proj).astype(jnp.bfloat16)
    output_terms = jnp.dot(hidden, down_weight, preferred_element_type=jnp.float32)
    block_output = lax.psum_scatter(
        output_terms, ("latent", "hidden"), scatter_dimension=1, tiled=True
    ).astype(jnp.bfloat16)
    hidden_grad = lax.dot_general(
        lax.all_gather(cotangent_local, ("latent", "hidden"), axis=1, tiled=True),
        down_weight,
        ACROSS,
        preferred_element_type=jnp.float32,
    )
    gate_grad = (hidden_grad * up_proj * gelu_slope).astype(jnp.bfloat16)
    up_grad = (hidden_grad * gelu_value).astype(jnp.bfloat16)
    partial_grad = jnp.dot(gate_grad, gate_weight, preferred_element_type=jnp.float32) + jnp.dot(
        up_grad, up_weight, preferred_element_type=jnp.float32
    )
    scaled = lax.psum(partial_grad, ("latent", "hidden")) * norm_gain
    inner_row = jnp.sum(scaled * rebuilt, axis=1, keepdims=True)
    inverse_cube = inverse * inverse * inverse
    rebuilt_grad = (
        inverse * scaled - inverse_cube * rebuilt * (inner_row / model_width) + (rebuilt - target)
    ).astype(jnp.bfloat16)
    latent_grad = lax.dot_general(
        rebuilt_grad, dictionary, ACROSS, preferred_element_type=jnp.float32
    )
    preact_grad = jnp.where(preact > 0.0, latent_grad, 0.0).astype(jnp.bfloat16)
    dictionary_grad = lax.dot_general(
        latents, rebuilt_grad, DOWNWARD, preferred_element_type=jnp.float32
    ) + lax.dot_general(preact_grad, inputs, DOWNWARD, preferred_element_type=jnp.float32)
    return (block_output, dictionary_grad.astype(jnp.bfloat16))


def solution(mesh):
    in_specs = (
        P("groups", ("latent", "hidden")),
        P("groups", ("latent", "hidden")),
        P(("latent", "hidden"), None),
        P(("latent", "hidden")),
        P(),
        P(),
        P(("latent", "hidden"), None),
        P(("latent", "hidden"), None),
        P(("latent", "hidden"), None),
    )
    out_specs = (P("groups", ("latent", "hidden")), P(("latent", "hidden"), "groups"))
    return jax.shard_map(
        per_device, mesh=mesh, in_specs=in_specs, out_specs=out_specs, check_vma=False
    )
```

```python
import functools
import math

import jax
import jax.numpy as jnp
from jax import lax
from jax.experimental import pallas as pl
from jax.experimental.pallas import tpu as pltpu
from jax.sharding import PartitionSpec as P

CODE_STEP = 2.0 ** (-6)
NORM_EPSILON = 1e-06
GELU_ROOT = 0.7978845608028654
GELU_CUBIC = 0.044715
ACROSS = (((1,), (1,)), ((), ()))
DOWNWARD = (((0,), (0,)), ((), ()))
LANES = 128
ROW_TILE = 16
DIRECT_LIMIT = 16
VMEM_BYTES = 24 * 1024 * 1024
VMEM_BRING = 53 * 1024 * 1024
F32 = jnp.float32
BF16 = jnp.bfloat16


def gelu_parts(values):
    argument = GELU_ROOT * (values + GELU_CUBIC * values * values * values)
    tanh_value = jnp.tanh(argument)
    result = 0.5 * values * (1.0 + tanh_value)
    derivative = 0.5 * (1.0 + tanh_value) + 0.5 * values * (
        1.0 - tanh_value * tanh_value
    ) * GELU_ROOT * (1.0 + 3.0 * GELU_CUBIC * values * values)
    return (result, derivative)


def up_to(value, unit):
    return -(-value // unit) * unit


def chips_fit(chips):
    return 8 <= chips <= DIRECT_LIMIT and chips & (chips - 1) == 0


class Plan:
    def __init__(self, chips, cores, rows, own):
        self.chips, self.cores, self.rows, self.own = chips, cores, rows, own
        self.width = own * chips * cores
        self.half = self.width // cores
        self.tiles = self.half // LANES
        self.chunk = up_to(-(-self.tiles * rows // chips), ROW_TILE)
        self.flat = self.chunk * chips
        self.tail = own - LANES
        if self.tail > 0:
            self.fold_rows = min(
                size
                for size in range(ROW_TILE, rows + ROW_TILE, ROW_TILE)
                if -(-rows // size) * self.tail <= LANES
            )
            self.packed = rows + self.fold_rows
        self.columns = list(range(0, chips, 2))
        self.doubling = [1 << k for k in reversed(range(1, (chips - 1).bit_length()))]
        self.doubled = [0]
        for bit in self.doubling:
            self.doubled = self.doubled + [place ^ bit for place in self.doubled]

    def side_blocks(self, refs):
        me = lax.axis_index("latent")
        stack_ref, *crossed_refs = refs
        for place, column in enumerate(self.columns):
            yield me ^ column, stack_ref[place]
        places = iter(self.columns)
        for ref in crossed_refs:
            for place in range(ref.shape[0]):
                yield me ^ next(places) ^ 1, ref[place]

    def pieces(self):
        for tile in range(self.tiles):
            row = 0
            while row < self.rows:
                chip, place = divmod(tile * self.rows + row, self.chunk)
                count = min(self.rows - row, self.chunk - place)
                yield tile, chip, place, row, count
                row += count

    def fits(self):
        return (
            self.cores == 2
            and chips_fit(self.chips)
            and self.rows % ROW_TILE == 0
            and self.half % LANES == 0
            and 0 < self.tail < LANES
            and self.packed == self.chunk
        )


HBM = pl.BlockSpec(memory_space=pltpu.HBM)
ONCHIP = pl.BlockSpec(memory_space=pltpu.VMEM)


def shaped(*dims, dtype=F32):
    return jax.ShapeDtypeStruct(dims, dtype)


HBM = pl.BlockSpec(memory_space=pltpu.HBM)
ONCHIP = pl.BlockSpec(memory_space=pltpu.VMEM)


def shaped(*dims, dtype=F32):
    return jax.ShapeDtypeStruct(dims, dtype)


def call(body, out_shapes, operands, scratch=(), out_specs=None, flops=0, moved=0):
    return pl.pallas_call(
        body,
        out_shape=out_shapes,
        in_specs=[ONCHIP] * len(operands),
        out_specs=jax.tree.map(lambda _: ONCHIP, out_shapes) if out_specs is None else out_specs,
        scratch_shapes=list(scratch),
        compiler_params=pltpu.CompilerParams(vmem_limit_bytes=VMEM_BYTES),
        cost_estimate=pl.CostEstimate(flops=flops, bytes_accessed=moved, transcendentals=0),
    )(*operands)


def padded_bytes(array):
    *lead, rows, columns = array.shape
    item = jnp.dtype(array.dtype).itemsize
    return math.prod(lead) * up_to(rows, ROW_TILE) * up_to(columns, LANES) * item


def copies(sources, targets, sems):
    started = []
    for index, (source, target) in enumerate(zip(sources, targets)):
        one = pltpu.make_async_copy(source, target, sems.at[index])
        one.start()
        started.append(one)
    return started


def pack_block(plan, block):
    tail = block[:, LANES:]
    folded = []
    for start in range(0, plan.rows, plan.fold_rows):
        piece = tail[start : min(start + plan.fold_rows, plan.rows), :]
        short = plan.fold_rows - piece.shape[0]
        if short:
            piece = jnp.concatenate([piece, jnp.zeros((short, plan.tail), block.dtype)], axis=0)
        folded.append(piece)
    fill = LANES - len(folded) * plan.tail
    if fill:
        folded.append(jnp.zeros((plan.fold_rows, fill), block.dtype))
    return block[:, :LANES], jnp.concatenate(folded, axis=1)


def unpack_block(plan, packed):
    pieces = []
    for fold, start in enumerate(range(0, plan.rows, plan.fold_rows)):
        count = min(plan.fold_rows, plan.rows - start)
        pieces.append(
            packed[plan.rows : plan.rows + count, fold * plan.tail : (fold + 1) * plan.tail]
        )
    return jnp.concatenate([packed[: plan.rows, :], jnp.concatenate(pieces, axis=0)], axis=1)


def pack_values_body(plan, values_ref, *block_refs):
    for index, block_ref in enumerate(block_refs):
        main, tail = pack_block(plan, values_ref[index].astype(F32))
        block_ref[0, : plan.rows, :] = main.astype(BF16)
        block_ref[0, plan.rows :, :] = tail.astype(BF16)


def pack_values(plan, values):
    return call(
        functools.partial(pack_values_body, plan),
        [shaped(1, plan.packed, LANES, dtype=BF16)] * values.shape[0],
        (values,),
        moved=values.size * 6,
    )


def assemble(plan, own_refs, other_refs, both, full_ref):
    core = lax.axis_index("hidden")
    for side, refs in ((core, own_refs), (1 - core, other_refs)):
        for chip, block in plan.side_blocks(refs):
            both[side, chip] = block
    for chip in range(plan.chips):
        for side in range(plan.cores):
            column = (chip * plan.cores + side) * plan.own
            full_ref[:, column : column + plan.own] = unpack_block(plan, both[side, chip])


def both_scratch(plan, dtype=BF16):
    return pltpu.VMEM((plan.cores, plan.chips, plan.packed, LANES), dtype)


def chunk_scratch(plan):
    return pltpu.VMEM((plan.chips, plan.chunk, LANES), F32)


def side_shapes(plan, dtype=F32):
    return [shaped(len(plan.columns), plan.chunk, LANES, dtype=dtype)] * 2


def half_product(plan, pairs, side, kept_ref, sent_ref, target, gain_ref=None, bias_ref=None):
    span = pl.ds(pl.multiple_of(side * plan.half, LANES), plan.half)
    total = None
    for left, right_ref in pairs:
        term = jnp.dot(left, right_ref[:, span], preferred_element_type=F32)
        total = term if total is None else total + term
    if bias_ref is not None:
        total = total + bias_ref[:, span] * jnp.where(lax.axis_index("latent") == 0, 1.0, 0.0)
    if gain_ref is not None:
        total = total * gain_ref[:, span]
    for tile, chip, place, row, count in plan.pieces():
        target[chip, place : place + count, :] = total[
            row : row + count, tile * LANES : (tile + 1) * LANES
        ]
    used = plan.tiles * plan.rows
    while used < plan.flat:
        chip, place = divmod(used, plan.chunk)
        target[chip, place:, :] = jnp.zeros((plan.chunk - place, LANES), F32)
        used += plan.chunk - place
    me = lax.axis_index("latent")
    for place, column in enumerate(plan.columns):
        kept_ref[place] = target[me ^ column]
        sent_ref[place] = target[me ^ column ^ 1]


def bring_encoder_body(dict_hbm, vectors_hbm, dict_ref, bias_ref, decoder_ref, gain_ref, sems):
    sources, targets = [dict_hbm], [dict_ref]
    start = 0
    for target in (bias_ref, decoder_ref, gain_ref):
        sources.append(vectors_hbm.at[:, start : start + target.shape[1]])
        targets.append(target)
        start += target.shape[1]
    for copy in copies(sources, targets, sems):
        copy.wait()


def bring_encoder(plan, dictionary, vectors):
    outputs = [
        shaped(*dictionary.shape, dtype=BF16),
        shaped(1, dictionary.shape[0]),
        shaped(1, plan.width),
        shaped(1, plan.width),
    ]
    return pl.pallas_call(
        bring_encoder_body,
        out_shape=outputs,
        in_specs=[HBM] * 2,
        out_specs=[ONCHIP] * len(outputs),
        scratch_shapes=[pltpu.SemaphoreType.DMA((len(outputs),))],
        compiler_params=pltpu.CompilerParams(
            vmem_limit_bytes=VMEM_BRING - sum(map(padded_bytes, outputs))
        ),
        cost_estimate=pl.CostEstimate(
            flops=0, bytes_accessed=dictionary.size * 4, transcendentals=0
        ),
    )(dictionary, vectors)


def encode_body(plan, *refs):
    own, other, (dict_ref, bias_ref, gain_ref) = refs[:2], refs[2:4], refs[4:7]
    inputs_ref, latents_ref, kept_ref, sent_ref, both, target = refs[7:]
    assemble(plan, own, other, both, inputs_ref)
    preact = (
        lax.dot_general(inputs_ref[...], dict_ref[...], ACROSS, preferred_element_type=F32)
        + bias_ref[...]
    )
    latents = jnp.maximum(preact, 0.0).astype(BF16)
    latents_ref[...] = latents
    theirs = 1 - lax.axis_index("hidden")
    half_product(plan, [(latents, dict_ref)], theirs, kept_ref, sent_ref, target, gain_ref)


def encode(plan, own, other, dictionary, encoder_bias, gain):
    latents = dictionary.shape[0]
    return call(
        functools.partial(encode_body, plan),
        [
            shaped(plan.rows, plan.width, dtype=BF16),
            shaped(plan.rows, latents, dtype=BF16),
            *side_shapes(plan),
        ],
        (*own, *other, dictionary, encoder_bias, gain),
        [both_scratch(plan), chunk_scratch(plan)],
        flops=3 * plan.rows * plan.width * latents,
        moved=dictionary.size * 2,
    )


def decode_own_body(plan, latents_ref, dict_ref, decoder_ref, gain_ref, kept_ref, sent_ref, target):
    pairs = [(latents_ref[...], dict_ref)]
    mine = lax.axis_index("hidden")
    half_product(plan, pairs, mine, kept_ref, sent_ref, target, gain_ref, decoder_ref)


def decode_own(plan, latents, dictionary, decoder_bias, gain):
    return call(
        functools.partial(decode_own_body, plan),
        side_shapes(plan),
        (latents, dictionary, decoder_bias, gain),
        [chunk_scratch(plan)],
        flops=plan.rows * plan.width * dictionary.shape[0],
        moved=dictionary.size,
    )


def back_project_body(plan, *refs):
    own, other, (down_ref, grad_ref, both, full) = refs[:2], refs[2:4], refs[4:]
    assemble(plan, own, other, both, full)
    grad_ref[...] = lax.dot_general(
        full[...], down_ref[...], ACROSS, preferred_element_type=F32
    )


def back_project(plan, own, other, down_weight):
    units = down_weight.shape[0]
    return call(
        functools.partial(back_project_body, plan),
        shaped(plan.rows, units),
        (*own, *other, down_weight),
        [both_scratch(plan), pltpu.VMEM((plan.rows, plan.width), BF16)],
        flops=2 * plan.rows * plan.width * units,
        moved=down_weight.size * 2,
    )


def join_half(plan, source, first, full_ref):
    for tile, chip, place, row, count in plan.pieces():
        column = pl.multiple_of(first + tile * LANES, LANES)
        full_ref[row : row + count, pl.ds(column, LANES)] = source[
            chip, place : place + count, :
        ]


def half_terms(plan, half, side, gate_ref, up_ref, gain_ref):
    span = pl.ds(pl.multiple_of(side * plan.half, LANES), plan.half)
    rebuilt = half.astype(F32) / gain_ref[:, span]
    squares = jnp.sum(rebuilt * rebuilt, axis=1, keepdims=True)
    gate = lax.dot_general(half, gate_ref[:, span], ACROSS, preferred_element_type=F32)
    up = lax.dot_general(half, up_ref[:, span], ACROSS, preferred_element_type=F32)
    return squares, gate, up


def mlp_first_body(plan, own_ref, gate_ref, up_ref, gain_ref, half_ref, squares_ref, gate_part_ref, up_part_ref):
    join_half(plan, own_ref, 0, half_ref)
    squares_ref[...], gate_part_ref[...], up_part_ref[...] = half_terms(
        plan, half_ref[...], lax.axis_index("hidden"), gate_ref, up_ref, gain_ref
    )


def mlp_first(plan, own, gate_weight, up_weight, gain):
    units = gate_weight.shape[0]
    return call(
        functools.partial(mlp_first_body, plan),
        [
            shaped(plan.rows, plan.half, dtype=BF16),
            shaped(plan.rows, 1),
            shaped(plan.rows, units),
            shaped(plan.rows, units),
        ],
        (own, gate_weight, up_weight, gain),
        flops=2 * plan.rows * plan.width * units,
        moved=gate_weight.size * 4,
    )


def mlp_body(plan, other_ref, gate_ref, up_ref, gain_ref, grad_ref, half_ref, squares_ref, gate_part_ref, up_part_ref, scaled_ref, inverse_ref, hidden_ref, gate_grad_ref, up_grad_ref, kept_ref, sent_ref, target):
    core = lax.axis_index("hidden")
    join_half(plan, other_ref, (1 - core) * plan.half, scaled_ref)
    other_span = pl.ds(pl.multiple_of((1 - core) * plan.half, LANES), plan.half)
    own_span = pl.ds(pl.multiple_of(core * plan.half, LANES), plan.half)
    scaled_ref[:, own_span] = half_ref[...]
    squares, gate, up = half_terms(
        plan, scaled_ref[:, other_span], 1 - core, gate_ref, up_ref, gain_ref
    )
    inverse = lax.rsqrt((squares + squares_ref[...]) / plan.width + NORM_EPSILON)
    inverse_ref[...] = inverse
    gate_proj = inverse * (gate + gate_part_ref[...])
    up_proj = inverse * (up + up_part_ref[...])
    gelu_value, gelu_slope = gelu_parts(gate_proj)
    hidden_ref[...] = (gelu_value * up_proj).astype(BF16)
    hidden_grad = grad_ref[...]
    gate_grad = (hidden_grad * up_proj * gelu_slope).astype(BF16)
    up_grad = (hidden_grad * gelu_value).astype(BF16)
    gate_grad_ref[...] = gate_grad
    up_grad_ref[...] = up_grad
    pairs = [(gate_grad, gate_ref), (up_grad, up_ref)]
    half_product(plan, pairs, 1 - core, kept_ref, sent_ref, target)


def mlp(plan, other, gate_weight, up_weight, gain, hidden_grad, first):
    units = gate_weight.shape[0]
    return call(
        functools.partial(mlp_body, plan),
        [
            shaped(plan.rows, plan.width, dtype=BF16),
            shaped(plan.rows, 1),
            shaped(plan.rows, units, dtype=BF16),
            shaped(plan.rows, units, dtype=BF16),
            shaped(plan.rows, units, dtype=BF16),
            *side_shapes(plan),
        ],
        (other, gate_weight, up_weight, gain, hidden_grad, *first),
        [chunk_scratch(plan)],
        flops=6 * plan.rows * plan.width * units,
        moved=gate_weight.size * 4,
    )


def mlp_own_body(plan, gate_grad_ref, up_grad_ref, gate_ref, up_ref, kept_ref, sent_ref, target):
    pairs = [(gate_grad_ref[...], gate_ref), (up_grad_ref[...], up_ref)]
    half_product(plan, pairs, lax.axis_index("hidden"), kept_ref, sent_ref, target)


def mlp_own(plan, gate_grad, up_grad, gate_weight, up_weight):
    return call(
        functools.partial(mlp_own_body, plan),
        side_shapes(plan),
        (gate_grad, up_grad, gate_weight, up_weight),
        [chunk_scratch(plan)],
        flops=2 * plan.rows * plan.width * gate_weight.shape[0],
        moved=gate_weight.size * 2,
    )


def project_body(plan, hidden_ref, down_ref, mine_ref, theirs_ref, both):
    core = lax.axis_index("hidden")
    terms = jnp.dot(hidden_ref[...], down_ref[...], preferred_element_type=F32).astype(BF16)
    for chip in range(plan.chips):
        for side in range(plan.cores):
            start = (chip * plan.cores + side) * plan.own
            main, tail = pack_block(plan, terms[:, start : start + plan.own])
            both[side, chip, : plan.rows, :] = main
            both[side, chip, plan.rows :, :] = tail
    mine_ref[...] = both[core]
    theirs_ref[...] = both[1 - core]


def project(plan, hidden, down_weight):
    units = down_weight.shape[0]
    shape = (plan.chips, plan.packed, LANES)
    return call(
        functools.partial(project_body, plan),
        [shaped(*shape, dtype=BF16)] * 2,
        (hidden, down_weight),
        [both_scratch(plan)],
        flops=2 * plan.rows * plan.width * units,
        moved=down_weight.size * 2,
    )


def add_pair_body(plan, first_ref, mine_ref, theirs_ref, kept_ref, sent_ref):
    me = lax.axis_index("latent")
    sent_ref[0] = first_ref[0]
    for place, column in enumerate(plan.columns):
        kept, sent = me ^ column, me ^ column ^ 1
        kept_ref[place] = mine_ref[kept].astype(F32) + theirs_ref[kept].astype(F32)
        sent_ref[1 + place] = (
            mine_ref[sent].astype(F32) + theirs_ref[sent].astype(F32)
        ).astype(BF16)


def add_pair(plan, first, mine, theirs):
    count, dims = len(plan.columns), mine.shape[1:]
    return call(
        functools.partial(add_pair_body, plan),
        [shaped(count, *dims), shaped(1 + count, *dims, dtype=BF16)],
        (first, mine, theirs),
        moved=mine.size * 10,
    )


def add_sent_body(mine_ref, theirs_ref, first_ref, rest_ref):
    total = (mine_ref[...] + theirs_ref[...]).astype(BF16)
    first_ref[...] = total[:1]
    rest_ref[...] = total[1:]


def add_sent(plan, mine, theirs):
    count, *dims = mine.shape
    return call(
        add_sent_body,
        [shaped(1, *dims, dtype=BF16), shaped(count - 1, *dims, dtype=BF16)],
        (mine, theirs),
        moved=mine.size * 10,
    )


def add_across_body(mine_ref, theirs_ref, got_ref, *sent_refs):
    for place, out_ref in enumerate(sent_refs):
        total = mine_ref[1 + place] + theirs_ref[1 + place] + got_ref[place].astype(F32)
        out_ref[0] = total.astype(BF16)


def add_across(plan, mine, theirs, got):
    return call(
        add_across_body,
        [shaped(1, *mine.shape[1:], dtype=BF16)] * got.shape[0],
        (mine, theirs, got),
        moved=mine.size * 10,
    )


def column_total(mine_ref, theirs_ref, *refs):
    total = mine_ref[0] + theirs_ref[0]
    for ref in refs:
        total = total + ref[0].astype(F32)
    return total.astype(BF16)


def add_column_body(*refs):
    *sources, block_ref, more_ref = refs
    block_ref[0] = column_total(*sources)
    more_ref[...] = sources[-1][1:]


def add_column(plan, mine, theirs, got, first):
    dims = mine.shape[1:]
    return call(
        add_column_body,
        [shaped(1, *dims, dtype=BF16), shaped(first.shape[0] - 1, *dims, dtype=BF16)],
        (mine, theirs, *reversed(got), first),
        moved=mine.size * 8,
    )


def add_with_output_body(plan, count, *refs):
    total = column_total(*refs[:count])
    first_ref, kept_ref, block_ref, own_ref = refs[count - 1 : count + 3]
    block_ref[0] = total
    own_ref[0] = kept_ref[0] + first_ref[1].astype(F32)
    for place, both_ref in enumerate(refs[count + 3 :], 1):
        both_ref[0, : plan.chunk, :] = total
        both_ref[0, plan.chunk :, :] = (
            kept_ref[place] + first_ref[1 + place].astype(F32)
        ).astype(BF16)


def add_with_output(plan, mine, theirs, got, first, kept):
    both = shaped(1, plan.chunk + plan.packed, LANES, dtype=BF16)
    block, out_own, *messages = call(
        functools.partial(add_with_output_body, plan, 3 + len(got)),
        [shaped(1, plan.chunk, LANES, dtype=BF16), shaped(1, plan.packed, LANES)]
        + [both] * (len(plan.columns) - 1),
        (mine, theirs, *reversed(got), first, kept),
        moved=mine.size * 12,
    )
    return block, out_own, messages


def stack_body(places, *refs):
    count = len(places)
    stack_ref, *rest_refs = refs[count:]
    rows = stack_ref.shape[1]
    for place, ref in zip(places, refs):
        stack_ref[place] = ref[0, :rows, :]
        for rest_ref in rest_refs:
            if place:
                rest_ref[place - 1] = ref[0, :rows, :]


def stack_up(plan, block, got, with_rest=False):
    dims = block.shape[1:]
    operands = [block, *got]
    places = list(range(len(operands)))
    if with_rest:
        operands, places = operands[::-1], places[::-1]
    outs = [shaped(1 + len(got), *dims, dtype=BF16), shaped(len(got), *dims, dtype=BF16)]
    return call(
        functools.partial(stack_body, places),
        outs if with_rest else outs[0],
        operands,
        moved=block.size * 16,
    )


def join_body(*refs):
    *sources, joined_ref = refs
    start = 0
    for ref in sources:
        joined_ref[start : start + ref.shape[0]] = ref[...]
        start += ref.shape[0]


def join(plan, *stacks):
    count = sum(one.shape[0] for one in stacks)
    return call(
        join_body,
        shaped(count, *stacks[0].shape[1:], dtype=BF16),
        stacks,
        moved=count * stacks[0].size,
    )


def double(plan, stack, bit):
    return join(plan, stack, partner_swap(stack, bit))


def add_message_body(plan, first_ref, here_ref, there_ref, stack_ref, message_ref):
    message_ref[0] = first_ref[0]
    half = here_ref.shape[0]
    for index, column in enumerate(plan.doubled):
        block = here_ref[index] if index < half else there_ref[index - half]
        place = plan.columns.index(column)
        stack_ref[place] = block
        message_ref[1 + place] = block


def add_message(plan, first, here, there):
    count, dims = len(plan.columns), first.shape[1:]
    return call(
        functools.partial(add_message_body, plan),
        [shaped(count, *dims, dtype=BF16), shaped(1 + count, *dims, dtype=BF16)],
        (first, here, there),
        moved=first.size * 40,
    )


def line_up_body(plan, *refs):
    for chip, block in plan.side_blocks(refs[:-1]):
        refs[-1][chip] = block


def line_up(plan, stack, *crossed):
    return call(
        functools.partial(line_up_body, plan),
        shaped(plan.chips, *stack.shape[1:], dtype=BF16),
        (stack, *crossed),
        moved=stack.size * 8,
    )


def finish_output_body(plan, own_ref, *refs):
    total = own_ref[0]
    for ref in refs[:-1]:
        total = total + ref[0, plan.chunk :, :].astype(F32)
    refs[-1][...] = unpack_block(plan, total).astype(BF16)


def finish_output(plan, own, messages):
    return call(
        functools.partial(finish_output_body, plan),
        shaped(plan.rows, plan.own, dtype=BF16),
        (own, *reversed(messages)),
        moved=own.size * 8,
    )


def prepare_body(plan, scaled_ref, inputs_ref, gain_ref, inverse_ref, factor_ref, slope_ref, base_ref):
    gain = gain_ref[...]
    inverse = inverse_ref[...]
    rebuilt = scaled_ref[...].astype(F32) / gain
    factor_ref[...] = inverse * gain
    slope_ref[...] = rebuilt * (inverse * inverse * inverse / plan.width)
    base_ref[...] = rebuilt - inputs_ref[...].astype(F32)


def prepare(plan, scaled, inputs, gain, inverse):
    return call(
        functools.partial(prepare_body, plan),
        [shaped(plan.rows, plan.width)] * 3,
        (scaled, inputs, gain, inverse),
        moved=scaled.size * 16,
    )


def dictionary_body(plan, pieces, own_ref, other_ref, scaled_ref, factor_ref, slope_ref, base_ref, inputs_ref, latents_ref, dict_ref, out_hbm, full, out_ref, out_sems):
    core = lax.axis_index("hidden")
    join_half(plan, own_ref, core * plan.half, full)
    join_half(plan, other_ref, (1 - core) * plan.half, full)
    grad = full[...].astype(F32)
    inner_row = jnp.sum(grad * scaled_ref[...].astype(F32), axis=1, keepdims=True)
    inputs = inputs_ref[...]
    rebuilt_grad = (
        grad * factor_ref[...] - inner_row * slope_ref[...] + base_ref[...]
    ).astype(BF16)
    latents = latents_ref[...]
    latent_grad = lax.dot_general(
        rebuilt_grad, dict_ref[...], ACROSS, preferred_element_type=F32
    )
    preact_grad = jnp.where(latents.astype(F32) > 0.0, latent_grad, 0.0).astype(BF16)
    left = jnp.concatenate([latents, preact_grad], axis=0)
    right = jnp.concatenate([rebuilt_grad, inputs], axis=0)
    size = plan.width // pieces
    writes = []
    for piece in range(pieces):
        span = slice(piece * size, (piece + 1) * size)
        out_ref[:, span] = lax.dot_general(
            left, right[:, span], DOWNWARD, preferred_element_type=F32
        ).astype(BF16)
        one = pltpu.make_async_copy(
            out_ref.at[:, span], out_hbm.at[:, span], out_sems.at[piece]
        )
        one.start()
        writes.append(one)
    for one in writes:
        one.wait()


def dictionary_step(plan, own, other, scaled, prepared, inputs, latents, dictionary):
    units = dictionary.shape[0]
    pieces = plan.tiles
    return call(
        functools.partial(dictionary_body, plan, pieces),
        shaped(*dictionary.shape, dtype=BF16),
        (own, other, scaled, *prepared, inputs, latents, dictionary),
        [
            pltpu.VMEM((plan.rows, plan.width), BF16),
            pltpu.VMEM(dictionary.shape, BF16),
            pltpu.SemaphoreType.DMA((pieces,)),
        ],
        out_specs=HBM,
        flops=6 * plan.rows * plan.width * units,
        moved=dictionary.size * 4,
    )


def swap(value):
    size = lax.axis_size("hidden")
    return lax.ppermute(value, "hidden", [(i, (i + 1) % size) for i in range(size)])


def partner_swap(value, bits):
    size = lax.axis_size("latent")
    return lax.ppermute(value, "latent", [(i, i ^ bits) for i in range(size)])


def cross(value):
    return partner_swap(value, 1)


def to_column(plan, blocks):
    pairs = list(zip(blocks, plan.columns[1:]))
    got = [partner_swap(one, column) for one, column in reversed(pairs)]
    return got[::-1]


def to_all_columns(plan, block):
    return [partner_swap(block, column) for column in plan.columns[1:]]


def tie(*values):
    return lax.optimization_barrier(values)


def per_device(
    input_codes,
    cotangent_codes,
    dictionary,
    encoder_bias,
    decoder_bias,
    norm_gain,
    gate_weight,
    up_weight,
    down_weight,
):
    plan = Plan(
        lax.axis_size("latent"), lax.axis_size("hidden"), input_codes.shape[0], input_codes.shape[1]
    )
    if not plan.fits():
        return per_device_plain(
            input_codes,
            cotangent_codes,
            dictionary,
            encoder_bias,
            decoder_bias,
            norm_gain,
            gate_weight,
            up_weight,
            down_weight,
        )
    vectors = jnp.concatenate([encoder_bias, decoder_bias, norm_gain]).reshape(1, -1)
    codes = jnp.stack([input_codes, cotangent_codes])
    values = (codes.astype(F32) * CODE_STEP).astype(BF16)
    block, cotangent = pack_values(plan, values)
    stack = stack_up(plan, block, to_all_columns(plan, block))
    stack, vectors, late_dictionary, cotangent = tie(stack, vectors, dictionary, cotangent)
    stack_other, crossed = swap(stack), cross(stack)
    encoder = bring_encoder(plan, late_dictionary, vectors)
    cotangent = double(plan, cotangent, plan.doubling[0])
    stack_other, crossed, encoder, cotangent = tie(stack_other, crossed, encoder, cotangent)
    brought, bias, decoder, gain = encoder
    inputs, latents, kept, sent = encode(
        plan, (stack, crossed), (stack_other, swap(crossed)), brought, bias, gain
    )
    sent, kept = swap(sent), swap(kept)
    own_kept, own_sent = decode_own(plan, latents, brought, decoder, gain)
    sent_first, sent_rest = add_sent(plan, own_sent, sent)
    sent_rest, cotangent = tie(sent_rest, cotangent)
    for bit in plan.doubling[1:-1]:
        cotangent = double(plan, cotangent, bit)
    there = partner_swap(cotangent, plan.doubling[-1])
    sent = add_across(plan, own_kept, kept, cross(sent_rest))
    sent, sent_first, cotangent, there = tie(sent, sent_first, cotangent, there)
    cotangent, sent_first = add_message(plan, sent_first, cotangent, there)
    got, first = to_column(plan, sent), cross(sent_first)
    block, crossed = add_column(plan, own_kept, kept, got, first)
    cotangent_own = (cotangent, crossed)
    hidden_grad = back_project(
        plan, cotangent_own, [swap(one) for one in cotangent_own], down_weight
    )
    stack = stack_up(plan, block, to_all_columns(plan, block))
    stack_other, crossed = swap(stack), cross(stack)
    stack_other, crossed, hidden_grad = tie(stack_other, crossed, hidden_grad)
    terms = mlp_first(plan, line_up(plan, stack, crossed), gate_weight, up_weight, gain)
    scaled_other = line_up(plan, stack_other, swap(crossed))
    scaled, inverse, hidden, gate_grad, up_grad, kept, sent = mlp(
        plan, scaled_other, gate_weight, up_weight, gain, hidden_grad, terms
    )
    sent, kept = swap(sent), swap(kept)
    own_kept, own_sent = mlp_own(plan, gate_grad, up_grad, gate_weight, up_weight)
    out_mine, out_theirs = project(plan, hidden, down_weight)
    sent_first, sent_rest = add_sent(plan, own_sent, sent)
    sent_first, sent_rest, out_mine, out_theirs = tie(sent_first, sent_rest, out_mine, out_theirs)
    crossed = cross(sent_rest)
    out_kept, sent_first = add_pair(plan, sent_first, out_mine, swap(out_theirs))
    sent = add_across(plan, own_kept, kept, crossed)
    sent, sent_first, out_kept = tie(sent, sent_first, out_kept)
    got = to_column(plan, sent)
    first = cross(sent_first)
    block, out_own, messages = add_with_output(plan, own_kept, kept, got, first, out_kept)
    got = list(tie(*to_column(plan, messages)))
    stack = stack_up(plan, block, got)
    stack, scaled_late, inputs_late = tie(stack, scaled, inputs)
    crossed, stack_other = cross(stack), swap(stack)
    prepared = prepare(plan, scaled_late, inputs_late, gain, inverse)
    block_output = finish_output(plan, out_own, got)
    grad_own = line_up(plan, stack, crossed)
    grad_other = line_up(plan, stack_other, swap(crossed))
    dictionary_grad = dictionary_step(
        plan, grad_own, grad_other, scaled, prepared, inputs, latents, brought
    )
    return (block_output, dictionary_grad)


def per_device_plain(
    input_codes,
    cotangent_codes,
    dictionary,
    encoder_bias,
    decoder_bias,
    norm_gain,
    gate_weight,
    up_weight,
    down_weight,
):
    own_width = input_codes.shape[1]
    model_width = own_width * lax.axis_size(("latent", "hidden"))
    cotangent_local = (cotangent_codes.astype(jnp.float32) * CODE_STEP).astype(jnp.bfloat16)
    inputs_local = (input_codes.astype(jnp.float32) * CODE_STEP).astype(jnp.bfloat16)
    inputs = lax.all_gather(inputs_local, ("latent", "hidden"), axis=1, tiled=True)
    preact = (
        lax.dot_general(inputs, dictionary, ACROSS, preferred_element_type=jnp.float32)
        + encoder_bias
    )
    latents = jnp.maximum(preact, 0.0).astype(jnp.bfloat16)
    partial_value = jnp.dot(latents, dictionary, preferred_element_type=jnp.float32)
    rebuilt = lax.psum(partial_value, ("latent", "hidden")) + decoder_bias
    inverse = lax.rsqrt(
        jnp.sum(rebuilt * rebuilt, axis=1, keepdims=True) / model_width + NORM_EPSILON
    )
    normed = (rebuilt * inverse * norm_gain).astype(jnp.bfloat16)
    target = inputs.astype(jnp.float32)
    gate_proj = lax.dot_general(normed, gate_weight, ACROSS, preferred_element_type=jnp.float32)
    up_proj = lax.dot_general(normed, up_weight, ACROSS, preferred_element_type=jnp.float32)
    gelu_value, gelu_slope = gelu_parts(gate_proj)
    hidden = (gelu_value * up_proj).astype(jnp.bfloat16)
    output_terms = jnp.dot(hidden, down_weight, preferred_element_type=jnp.float32)
    block_output = lax.psum_scatter(
        output_terms, ("latent", "hidden"), scatter_dimension=1, tiled=True
    ).astype(jnp.bfloat16)
    hidden_grad = lax.dot_general(
        lax.all_gather(cotangent_local, ("latent", "hidden"), axis=1, tiled=True),
        down_weight,
        ACROSS,
        preferred_element_type=jnp.float32,
    )
    gate_grad = (hidden_grad * up_proj * gelu_slope).astype(jnp.bfloat16)
    up_grad = (hidden_grad * gelu_value).astype(jnp.bfloat16)
    partial_grad = jnp.dot(gate_grad, gate_weight, preferred_element_type=jnp.float32) + jnp.dot(
        up_grad, up_weight, preferred_element_type=jnp.float32
    )
    scaled = lax.psum(partial_grad, ("latent", "hidden")) * norm_gain
    inner_row = jnp.sum(scaled * rebuilt, axis=1, keepdims=True)
    inverse_cube = inverse * inverse * inverse
    rebuilt_grad = (
        inverse * scaled - inverse_cube * rebuilt * (inner_row / model_width) + (rebuilt - target)
    ).astype(jnp.bfloat16)
    latent_grad = lax.dot_general(
        rebuilt_grad, dictionary, ACROSS, preferred_element_type=jnp.float32
    )
    preact_grad = jnp.where(preact > 0.0, latent_grad, 0.0).astype(jnp.bfloat16)
    dictionary_grad = lax.dot_general(
        latents, rebuilt_grad, DOWNWARD, preferred_element_type=jnp.float32
    ) + lax.dot_general(preact_grad, inputs, DOWNWARD, preferred_element_type=jnp.float32)
    return (block_output, dictionary_grad.astype(jnp.bfloat16))


def solution(mesh):
    in_specs = (
        P("groups", ("latent", "hidden")),
        P("groups", ("latent", "hidden")),
        P(("latent", "hidden"), None),
        P(("latent", "hidden")),
        P(),
        P(),
        P(("latent", "hidden"), None),
        P(("latent", "hidden"), None),
        P(("latent", "hidden"), None),
    )
    out_specs = (P("groups", ("latent", "hidden")), P(("latent", "hidden"), "groups"))
    return jax.shard_map(
        per_device, mesh=mesh, in_specs=in_specs, out_specs=out_specs, check_vma=False
    )
```

```python
import functools
import math

import jax
import jax.numpy as jnp
from jax import lax
from jax.experimental import pallas as pl
from jax.experimental.pallas import tpu as pltpu
from jax.sharding import PartitionSpec as P

CODE_STEP = 2.0 ** (-6)
NORM_EPSILON = 1e-06
GELU_ROOT = 0.7978845608028654
GELU_CUBIC = 0.044715
ACROSS = (((1,), (1,)), ((), ()))
DOWNWARD = (((0,), (0,)), ((), ()))
LANES = 128
ROW_TILE = 16
DIRECT_LIMIT = 16
VMEM_BYTES = 24 * 1024 * 1024
VMEM_BRING = 53 * 1024 * 1024
F32 = jnp.float32
BF16 = jnp.bfloat16


def gelu_parts(values):
    argument = GELU_ROOT * (values + GELU_CUBIC * values * values * values)
    tanh_value = jnp.tanh(argument)
    result = 0.5 * values * (1.0 + tanh_value)
    derivative = 0.5 * (1.0 + tanh_value) + 0.5 * values * (
        1.0 - tanh_value * tanh_value
    ) * GELU_ROOT * (1.0 + 3.0 * GELU_CUBIC * values * values)
    return (result, derivative)


def up_to(value, unit):
    return -(-value // unit) * unit


def chips_fit(chips):
    return 8 <= chips <= DIRECT_LIMIT and chips & (chips - 1) == 0


class Plan:
    def __init__(self, chips, cores, rows, own):
        self.chips, self.cores, self.rows, self.own = chips, cores, rows, own
        self.width = own * chips * cores
        self.half = self.width // cores
        self.tiles = self.half // LANES
        self.chunk = up_to(-(-self.tiles * rows // chips), ROW_TILE)
        self.flat = self.chunk * chips
        self.tail = own - LANES
        if self.tail > 0:
            self.fold_rows = min(
                size
                for size in range(ROW_TILE, rows + ROW_TILE, ROW_TILE)
                if -(-rows // size) * self.tail <= LANES
            )
            self.packed = rows + self.fold_rows
        self.columns = list(range(0, chips, 2))
        self.doubling = [1 << k for k in range(1, (chips - 1).bit_length())]
        self.doubled = [0]
        for bit in self.doubling:
            self.doubled = self.doubled + [place ^ bit for place in self.doubled]

    def side_blocks(self, refs):
        me = lax.axis_index("latent")
        stack_ref, *crossed_refs = refs
        for place, column in enumerate(self.columns):
            yield me ^ column, stack_ref[place]
        places = iter(self.columns)
        for ref in crossed_refs:
            for place in range(ref.shape[0]):
                yield me ^ next(places) ^ 1, ref[place]

    def pieces(self):
        for tile in range(self.tiles):
            row = 0
            while row < self.rows:
                chip, place = divmod(tile * self.rows + row, self.chunk)
                count = min(self.rows - row, self.chunk - place)
                yield tile, chip, place, row, count
                row += count

    def fits(self):
        return (
            self.cores == 2
            and chips_fit(self.chips)
            and self.rows % ROW_TILE == 0
            and self.half % LANES == 0
            and 0 < self.tail < LANES
            and self.packed == self.chunk
        )


HBM = pl.BlockSpec(memory_space=pltpu.HBM)
ONCHIP = pl.BlockSpec(memory_space=pltpu.VMEM)


def shaped(*dims, dtype=F32):
    return jax.ShapeDtypeStruct(dims, dtype)


HBM = pl.BlockSpec(memory_space=pltpu.HBM)
ONCHIP = pl.BlockSpec(memory_space=pltpu.VMEM)


def shaped(*dims, dtype=F32):
    return jax.ShapeDtypeStruct(dims, dtype)


def call(body, out_shapes, operands, scratch=(), out_specs=None, flops=0, moved=0):
    return pl.pallas_call(
        body,
        out_shape=out_shapes,
        in_specs=[ONCHIP] * len(operands),
        out_specs=jax.tree.map(lambda _: ONCHIP, out_shapes) if out_specs is None else out_specs,
        scratch_shapes=list(scratch),
        compiler_params=pltpu.CompilerParams(vmem_limit_bytes=VMEM_BYTES),
        cost_estimate=pl.CostEstimate(flops=flops, bytes_accessed=moved, transcendentals=0),
    )(*operands)


def padded_bytes(array):
    *lead, rows, columns = array.shape
    item = jnp.dtype(array.dtype).itemsize
    return math.prod(lead) * up_to(rows, ROW_TILE) * up_to(columns, LANES) * item


def copies(sources, targets, sems):
    started = []
    for index, (source, target) in enumerate(zip(sources, targets)):
        one = pltpu.make_async_copy(source, target, sems.at[index])
        one.start()
        started.append(one)
    return started


def pack_block(plan, block):
    tail = block[:, LANES:]
    folded = []
    for start in range(0, plan.rows, plan.fold_rows):
        piece = tail[start : min(start + plan.fold_rows, plan.rows), :]
        short = plan.fold_rows - piece.shape[0]
        if short:
            piece = jnp.concatenate([piece, jnp.zeros((short, plan.tail), block.dtype)], axis=0)
        folded.append(piece)
    fill = LANES - len(folded) * plan.tail
    if fill:
        folded.append(jnp.zeros((plan.fold_rows, fill), block.dtype))
    return block[:, :LANES], jnp.concatenate(folded, axis=1)


def unpack_block(plan, packed):
    pieces = []
    for fold, start in enumerate(range(0, plan.rows, plan.fold_rows)):
        count = min(plan.fold_rows, plan.rows - start)
        pieces.append(
            packed[plan.rows : plan.rows + count, fold * plan.tail : (fold + 1) * plan.tail]
        )
    return jnp.concatenate([packed[: plan.rows, :], jnp.concatenate(pieces, axis=0)], axis=1)


def pack_values_body(plan, values_ref, *block_refs):
    for index, block_ref in enumerate(block_refs):
        main, tail = pack_block(plan, values_ref[index].astype(F32))
        block_ref[0, : plan.rows, :] = main.astype(BF16)
        block_ref[0, plan.rows :, :] = tail.astype(BF16)


def pack_values(plan, values):
    return call(
        functools.partial(pack_values_body, plan),
        [shaped(1, plan.packed, LANES, dtype=BF16)] * values.shape[0],
        (values,),
        moved=values.size * 6,
    )


def assemble(plan, own_refs, other_refs, both, full_ref):
    core = lax.axis_index("hidden")
    for side, refs in ((core, own_refs), (1 - core, other_refs)):
        for chip, block in plan.side_blocks(refs):
            both[side, chip] = block
    for chip in range(plan.chips):
        for side in range(plan.cores):
            column = (chip * plan.cores + side) * plan.own
            full_ref[:, column : column + plan.own] = unpack_block(plan, both[side, chip])


def both_scratch(plan, dtype=BF16):
    return pltpu.VMEM((plan.cores, plan.chips, plan.packed, LANES), dtype)


def chunk_scratch(plan):
    return pltpu.VMEM((plan.chips, plan.chunk, LANES), F32)


def side_shapes(plan, dtype=F32):
    return [shaped(len(plan.columns), plan.chunk, LANES, dtype=dtype)] * 2


def half_product(plan, pairs, side, kept_ref, sent_ref, target, gain_ref=None, bias_ref=None):
    span = pl.ds(pl.multiple_of(side * plan.half, LANES), plan.half)
    total = None
    for left, right_ref in pairs:
        term = jnp.dot(left, right_ref[:, span], preferred_element_type=F32)
        total = term if total is None else total + term
    if bias_ref is not None:
        total = total + bias_ref[:, span] * jnp.where(lax.axis_index("latent") == 0, 1.0, 0.0)
    if gain_ref is not None:
        total = total * gain_ref[:, span]
    for tile, chip, place, row, count in plan.pieces():
        target[chip, place : place + count, :] = total[
            row : row + count, tile * LANES : (tile + 1) * LANES
        ]
    used = plan.tiles * plan.rows
    while used < plan.flat:
        chip, place = divmod(used, plan.chunk)
        target[chip, place:, :] = jnp.zeros((plan.chunk - place, LANES), F32)
        used += plan.chunk - place
    me = lax.axis_index("latent")
    for place, column in enumerate(plan.columns):
        kept_ref[place] = target[me ^ column]
        sent_ref[place] = target[me ^ column ^ 1]


def bring_encoder_body(dict_hbm, vectors_hbm, dict_ref, bias_ref, decoder_ref, gain_ref, sems):
    sources, targets = [dict_hbm], [dict_ref]
    start = 0
    for target in (bias_ref, decoder_ref, gain_ref):
        sources.append(vectors_hbm.at[:, start : start + target.shape[1]])
        targets.append(target)
        start += target.shape[1]
    for copy in copies(sources, targets, sems):
        copy.wait()


def bring_encoder(plan, dictionary, vectors):
    outputs = [
        shaped(*dictionary.shape, dtype=BF16),
        shaped(1, dictionary.shape[0]),
        shaped(1, plan.width),
        shaped(1, plan.width),
    ]
    return pl.pallas_call(
        bring_encoder_body,
        out_shape=outputs,
        in_specs=[HBM] * 2,
        out_specs=[ONCHIP] * len(outputs),
        scratch_shapes=[pltpu.SemaphoreType.DMA((len(outputs),))],
        compiler_params=pltpu.CompilerParams(
            vmem_limit_bytes=VMEM_BRING - sum(map(padded_bytes, outputs))
        ),
        cost_estimate=pl.CostEstimate(
            flops=0, bytes_accessed=dictionary.size * 4, transcendentals=0
        ),
    )(dictionary, vectors)


def encode_body(plan, *refs):
    own, other, (dict_ref, bias_ref, gain_ref) = refs[:2], refs[2:4], refs[4:7]
    inputs_ref, latents_ref, kept_ref, sent_ref, both, target = refs[7:]
    assemble(plan, own, other, both, inputs_ref)
    preact = (
        lax.dot_general(inputs_ref[...], dict_ref[...], ACROSS, preferred_element_type=F32)
        + bias_ref[...]
    )
    latents = jnp.maximum(preact, 0.0).astype(BF16)
    latents_ref[...] = latents
    theirs = 1 - lax.axis_index("hidden")
    half_product(plan, [(latents, dict_ref)], theirs, kept_ref, sent_ref, target, gain_ref)


def encode(plan, own, other, dictionary, encoder_bias, gain):
    latents = dictionary.shape[0]
    return call(
        functools.partial(encode_body, plan),
        [
            shaped(plan.rows, plan.width, dtype=BF16),
            shaped(plan.rows, latents, dtype=BF16),
            *side_shapes(plan),
        ],
        (*own, *other, dictionary, encoder_bias, gain),
        [both_scratch(plan), chunk_scratch(plan)],
        flops=3 * plan.rows * plan.width * latents,
        moved=dictionary.size * 2,
    )


def decode_own_body(plan, latents_ref, dict_ref, decoder_ref, gain_ref, kept_ref, sent_ref, target):
    pairs = [(latents_ref[...], dict_ref)]
    mine = lax.axis_index("hidden")
    half_product(plan, pairs, mine, kept_ref, sent_ref, target, gain_ref, decoder_ref)


def decode_own(plan, latents, dictionary, decoder_bias, gain):
    return call(
        functools.partial(decode_own_body, plan),
        side_shapes(plan),
        (latents, dictionary, decoder_bias, gain),
        [chunk_scratch(plan)],
        flops=plan.rows * plan.width * dictionary.shape[0],
        moved=dictionary.size,
    )


def back_project_body(plan, *refs):
    own, other, (down_ref, grad_ref, both, full) = refs[:2], refs[2:4], refs[4:]
    assemble(plan, own, other, both, full)
    grad_ref[...] = lax.dot_general(
        full[...], down_ref[...], ACROSS, preferred_element_type=F32
    )


def back_project(plan, own, other, down_weight):
    units = down_weight.shape[0]
    return call(
        functools.partial(back_project_body, plan),
        shaped(plan.rows, units),
        (*own, *other, down_weight),
        [both_scratch(plan), pltpu.VMEM((plan.rows, plan.width), BF16)],
        flops=2 * plan.rows * plan.width * units,
        moved=down_weight.size * 2,
    )


def join_half(plan, source, first, full_ref):
    for tile, chip, place, row, count in plan.pieces():
        column = pl.multiple_of(first + tile * LANES, LANES)
        full_ref[row : row + count, pl.ds(column, LANES)] = source[
            chip, place : place + count, :
        ]


def half_terms(plan, half, side, gate_ref, up_ref, gain_ref):
    span = pl.ds(pl.multiple_of(side * plan.half, LANES), plan.half)
    rebuilt = half.astype(F32) / gain_ref[:, span]
    squares = jnp.sum(rebuilt * rebuilt, axis=1, keepdims=True)
    gate = lax.dot_general(half, gate_ref[:, span], ACROSS, preferred_element_type=F32)
    up = lax.dot_general(half, up_ref[:, span], ACROSS, preferred_element_type=F32)
    return squares, gate, up


def mlp_first_body(plan, own_ref, gate_ref, up_ref, gain_ref, half_ref, squares_ref, gate_part_ref, up_part_ref):
    join_half(plan, own_ref, 0, half_ref)
    squares_ref[...], gate_part_ref[...], up_part_ref[...] = half_terms(
        plan, half_ref[...], lax.axis_index("hidden"), gate_ref, up_ref, gain_ref
    )


def mlp_first(plan, own, gate_weight, up_weight, gain):
    units = gate_weight.shape[0]
    return call(
        functools.partial(mlp_first_body, plan),
        [
            shaped(plan.rows, plan.half, dtype=BF16),
            shaped(plan.rows, 1),
            shaped(plan.rows, units),
            shaped(plan.rows, units),
        ],
        (own, gate_weight, up_weight, gain),
        flops=2 * plan.rows * plan.width * units,
        moved=gate_weight.size * 4,
    )


def mlp_body(plan, other_ref, gate_ref, up_ref, gain_ref, grad_ref, half_ref, squares_ref, gate_part_ref, up_part_ref, scaled_ref, inverse_ref, hidden_ref, gate_grad_ref, up_grad_ref, kept_ref, sent_ref, target):
    core = lax.axis_index("hidden")
    join_half(plan, other_ref, (1 - core) * plan.half, scaled_ref)
    other_span = pl.ds(pl.multiple_of((1 - core) * plan.half, LANES), plan.half)
    own_span = pl.ds(pl.multiple_of(core * plan.half, LANES), plan.half)
    scaled_ref[:, own_span] = half_ref[...]
    squares, gate, up = half_terms(
        plan, scaled_ref[:, other_span], 1 - core, gate_ref, up_ref, gain_ref
    )
    inverse = lax.rsqrt((squares + squares_ref[...]) / plan.width + NORM_EPSILON)
    inverse_ref[...] = inverse
    gate_proj = inverse * (gate + gate_part_ref[...])
    up_proj = inverse * (up + up_part_ref[...])
    gelu_value, gelu_slope = gelu_parts(gate_proj)
    hidden_ref[...] = (gelu_value * up_proj).astype(BF16)
    hidden_grad = grad_ref[...]
    gate_grad = (hidden_grad * up_proj * gelu_slope).astype(BF16)
    up_grad = (hidden_grad * gelu_value).astype(BF16)
    gate_grad_ref[...] = gate_grad
    up_grad_ref[...] = up_grad
    pairs = [(gate_grad, gate_ref), (up_grad, up_ref)]
    half_product(plan, pairs, 1 - core, kept_ref, sent_ref, target)


def mlp(plan, other, gate_weight, up_weight, gain, hidden_grad, first):
    units = gate_weight.shape[0]
    return call(
        functools.partial(mlp_body, plan),
        [
            shaped(plan.rows, plan.width, dtype=BF16),
            shaped(plan.rows, 1),
            shaped(plan.rows, units, dtype=BF16),
            shaped(plan.rows, units, dtype=BF16),
            shaped(plan.rows, units, dtype=BF16),
            *side_shapes(plan),
        ],
        (other, gate_weight, up_weight, gain, hidden_grad, *first),
        [chunk_scratch(plan)],
        flops=6 * plan.rows * plan.width * units,
        moved=gate_weight.size * 4,
    )


def mlp_own_body(plan, gate_grad_ref, up_grad_ref, gate_ref, up_ref, kept_ref, sent_ref, target):
    pairs = [(gate_grad_ref[...], gate_ref), (up_grad_ref[...], up_ref)]
    half_product(plan, pairs, lax.axis_index("hidden"), kept_ref, sent_ref, target)


def mlp_own(plan, gate_grad, up_grad, gate_weight, up_weight):
    return call(
        functools.partial(mlp_own_body, plan),
        side_shapes(plan),
        (gate_grad, up_grad, gate_weight, up_weight),
        [chunk_scratch(plan)],
        flops=2 * plan.rows * plan.width * gate_weight.shape[0],
        moved=gate_weight.size * 2,
    )


def project_body(plan, hidden_ref, down_ref, mine_ref, theirs_ref, both):
    core = lax.axis_index("hidden")
    terms = jnp.dot(hidden_ref[...], down_ref[...], preferred_element_type=F32).astype(BF16)
    for chip in range(plan.chips):
        for side in range(plan.cores):
            start = (chip * plan.cores + side) * plan.own
            main, tail = pack_block(plan, terms[:, start : start + plan.own])
            both[side, chip, : plan.rows, :] = main
            both[side, chip, plan.rows :, :] = tail
    mine_ref[...] = both[core]
    theirs_ref[...] = both[1 - core]


def project(plan, hidden, down_weight):
    units = down_weight.shape[0]
    shape = (plan.chips, plan.packed, LANES)
    return call(
        functools.partial(project_body, plan),
        [shaped(*shape, dtype=BF16)] * 2,
        (hidden, down_weight),
        [both_scratch(plan)],
        flops=2 * plan.rows * plan.width * units,
        moved=down_weight.size * 2,
    )


def add_pair_body(plan, first_ref, mine_ref, theirs_ref, kept_ref, sent_ref):
    me = lax.axis_index("latent")
    sent_ref[0] = first_ref[0]
    for place, column in enumerate(plan.columns):
        kept, sent = me ^ column, me ^ column ^ 1
        kept_ref[place] = mine_ref[kept].astype(F32) + theirs_ref[kept].astype(F32)
        sent_ref[1 + place] = (
            mine_ref[sent].astype(F32) + theirs_ref[sent].astype(F32)
        ).astype(BF16)


def add_pair(plan, first, mine, theirs):
    count, dims = len(plan.columns), mine.shape[1:]
    return call(
        functools.partial(add_pair_body, plan),
        [shaped(count, *dims), shaped(1 + count, *dims, dtype=BF16)],
        (first, mine, theirs),
        moved=mine.size * 10,
    )


def add_sent_body(mine_ref, theirs_ref, first_ref, rest_ref):
    total = (mine_ref[...] + theirs_ref[...]).astype(BF16)
    first_ref[...] = total[:1]
    rest_ref[...] = total[1:]


def add_sent(plan, mine, theirs):
    count, *dims = mine.shape
    return call(
        add_sent_body,
        [shaped(1, *dims, dtype=BF16), shaped(count - 1, *dims, dtype=BF16)],
        (mine, theirs),
        moved=mine.size * 10,
    )


def add_across_body(mine_ref, theirs_ref, got_ref, *sent_refs):
    for place, out_ref in enumerate(sent_refs):
        total = mine_ref[1 + place] + theirs_ref[1 + place] + got_ref[place].astype(F32)
        out_ref[0] = total.astype(BF16)


def add_across(plan, mine, theirs, got):
    return call(
        add_across_body,
        [shaped(1, *mine.shape[1:], dtype=BF16)] * got.shape[0],
        (mine, theirs, got),
        moved=mine.size * 10,
    )


def column_total(mine_ref, theirs_ref, *refs):
    total = mine_ref[0] + theirs_ref[0]
    for ref in refs:
        total = total + ref[0].astype(F32)
    return total.astype(BF16)


def add_column_body(*refs):
    *sources, block_ref, more_ref = refs
    block_ref[0] = column_total(*sources)
    more_ref[...] = sources[-1][1:]


def add_column(plan, mine, theirs, got, first):
    dims = mine.shape[1:]
    return call(
        add_column_body,
        [shaped(1, *dims, dtype=BF16), shaped(first.shape[0] - 1, *dims, dtype=BF16)],
        (mine, theirs, *reversed(got), first),
        moved=mine.size * 8,
    )


def add_with_output_body(plan, count, *refs):
    total = column_total(*refs[:count])
    first_ref, out_ref, block_ref, message_ref, kept_ref = refs[count - 1 : count + 4]
    block_ref[0] = total
    message_ref[0, : plan.chunk, :] = total
    near = plan.doubling[0]
    halves = [[], []]
    for place, column in enumerate(plan.columns):
        halves[column & near != 0].append(out_ref[place] + first_ref[1 + place].astype(F32))
    for index, (kept, sent) in enumerate(zip(*halves)):
        kept_ref[index] = kept
        start = plan.chunk + index * plan.packed
        message_ref[0, start : start + plan.packed, :] = sent.astype(BF16)


def add_with_output(plan, mine, theirs, got, first, kept):
    half = len(plan.columns) // 2
    return call(
        functools.partial(add_with_output_body, plan, 3 + len(got)),
        [
            shaped(1, plan.chunk, LANES, dtype=BF16),
            shaped(1, plan.chunk + half * plan.packed, LANES, dtype=BF16),
            shaped(half, plan.packed, LANES),
        ],
        (mine, theirs, *reversed(got), first, kept),
        moved=mine.size * 12,
    )


def halve_body(rows, skip, kept_ref, got_ref, left_ref, sent_ref):
    half = left_ref.shape[0]
    for index in range(2 * half):
        start = skip + index * rows
        total = kept_ref[index] + got_ref[0, start : start + rows, :].astype(F32)
        if index < half:
            left_ref[index] = total
        else:
            begin = (index - half) * rows
            sent_ref[0, begin : begin + rows, :] = total.astype(BF16)


def halve(plan, kept, got, skip):
    half, rows = kept.shape[0] // 2, plan.packed
    return call(
        functools.partial(halve_body, rows, skip),
        [shaped(half, rows, LANES), shaped(1, half * rows, LANES, dtype=BF16)],
        (kept, got),
        moved=kept.size * 10,
    )


def stack_body(places, *refs):
    count = len(places)
    stack_ref, *rest_refs = refs[count:]
    rows = stack_ref.shape[1]
    for place, ref in zip(places, refs):
        stack_ref[place] = ref[0, :rows, :]
        for rest_ref in rest_refs:
            if place:
                rest_ref[place - 1] = ref[0, :rows, :]


def stack_up(plan, block, got, with_rest=False):
    dims = block.shape[1:]
    operands = [block, *got]
    places = list(range(len(operands)))
    if with_rest:
        operands, places = operands[::-1], places[::-1]
    outs = [shaped(1 + len(got), *dims, dtype=BF16), shaped(len(got), *dims, dtype=BF16)]
    return call(
        functools.partial(stack_body, places),
        outs if with_rest else outs[0],
        operands,
        moved=block.size * 16,
    )


def join_body(*refs):
    *sources, joined_ref = refs
    start = 0
    for ref in sources:
        joined_ref[start : start + ref.shape[0]] = ref[...]
        start += ref.shape[0]


def join(plan, *stacks):
    count = sum(one.shape[0] for one in stacks)
    return call(
        join_body,
        shaped(count, *stacks[0].shape[1:], dtype=BF16),
        stacks,
        moved=count * stacks[0].size,
    )


def double(plan, stack, bit):
    return join(plan, stack, partner_swap(stack, bit))


def add_message_body(plan, first_ref, here_ref, there_ref, stack_ref, message_ref):
    message_ref[0] = first_ref[0]
    half = here_ref.shape[0]
    for index, column in enumerate(plan.doubled):
        block = here_ref[index] if index < half else there_ref[index - half]
        place = plan.columns.index(column)
        stack_ref[place] = block
        message_ref[1 + place] = block


def add_message(plan, first, here, there):
    count, dims = len(plan.columns), first.shape[1:]
    return call(
        functools.partial(add_message_body, plan),
        [shaped(count, *dims, dtype=BF16), shaped(1 + count, *dims, dtype=BF16)],
        (first, here, there),
        moved=first.size * 40,
    )


def line_up_body(plan, *refs):
    for chip, block in plan.side_blocks(refs[:-1]):
        refs[-1][chip] = block


def line_up(plan, stack, *crossed):
    return call(
        functools.partial(line_up_body, plan),
        shaped(plan.chips, *stack.shape[1:], dtype=BF16),
        (stack, *crossed),
        moved=stack.size * 8,
    )


def finish_output_body(plan, kept_ref, got_ref, out_ref):
    total = kept_ref[0] + got_ref[0].astype(F32)
    out_ref[...] = unpack_block(plan, total).astype(BF16)


def finish_output(plan, kept, got):
    return call(
        functools.partial(finish_output_body, plan),
        shaped(plan.rows, plan.own, dtype=BF16),
        (kept, got),
        moved=kept.size * 8,
    )


def prepare_body(plan, scaled_ref, inputs_ref, gain_ref, inverse_ref, factor_ref, slope_ref, base_ref):
    gain = gain_ref[...]
    inverse = inverse_ref[...]
    rebuilt = scaled_ref[...].astype(F32) / gain
    factor_ref[...] = inverse * gain
    slope_ref[...] = rebuilt * (inverse * inverse * inverse / plan.width)
    base_ref[...] = rebuilt - inputs_ref[...].astype(F32)


def prepare(plan, scaled, inputs, gain, inverse):
    return call(
        functools.partial(prepare_body, plan),
        [shaped(plan.rows, plan.width)] * 3,
        (scaled, inputs, gain, inverse),
        moved=scaled.size * 16,
    )


def dictionary_body(plan, pieces, own_ref, other_ref, scaled_ref, factor_ref, slope_ref, base_ref, inputs_ref, latents_ref, dict_ref, out_hbm, full, out_ref, out_sems):
    core = lax.axis_index("hidden")
    join_half(plan, own_ref, core * plan.half, full)
    join_half(plan, other_ref, (1 - core) * plan.half, full)
    grad = full[...].astype(F32)
    inner_row = jnp.sum(grad * scaled_ref[...].astype(F32), axis=1, keepdims=True)
    inputs = inputs_ref[...]
    rebuilt_grad = (
        grad * factor_ref[...] - inner_row * slope_ref[...] + base_ref[...]
    ).astype(BF16)
    latents = latents_ref[...]
    latent_grad = lax.dot_general(
        rebuilt_grad, dict_ref[...], ACROSS, preferred_element_type=F32
    )
    preact_grad = jnp.where(latents.astype(F32) > 0.0, latent_grad, 0.0).astype(BF16)
    left = jnp.concatenate([latents, preact_grad], axis=0)
    right = jnp.concatenate([rebuilt_grad, inputs], axis=0)
    size = plan.width // pieces
    writes = []
    for piece in range(pieces):
        span = slice(piece * size, (piece + 1) * size)
        out_ref[:, span] = lax.dot_general(
            left, right[:, span], DOWNWARD, preferred_element_type=F32
        ).astype(BF16)
        one = pltpu.make_async_copy(
            out_ref.at[:, span], out_hbm.at[:, span], out_sems.at[piece]
        )
        one.start()
        writes.append(one)
    for one in writes:
        one.wait()


def dictionary_step(plan, own, other, scaled, prepared, inputs, latents, dictionary):
    units = dictionary.shape[0]
    pieces = plan.tiles
    return call(
        functools.partial(dictionary_body, plan, pieces),
        shaped(*dictionary.shape, dtype=BF16),
        (own, other, scaled, *prepared, inputs, latents, dictionary),
        [
            pltpu.VMEM((plan.rows, plan.width), BF16),
            pltpu.VMEM(dictionary.shape, BF16),
            pltpu.SemaphoreType.DMA((pieces,)),
        ],
        out_specs=HBM,
        flops=6 * plan.rows * plan.width * units,
        moved=dictionary.size * 4,
    )


def swap(value):
    size = lax.axis_size("hidden")
    return lax.ppermute(value, "hidden", [(i, (i + 1) % size) for i in range(size)])


def partner_swap(value, bits):
    size = lax.axis_size("latent")
    return lax.ppermute(value, "latent", [(i, i ^ bits) for i in range(size)])


def cross(value):
    return partner_swap(value, 1)


def to_column(plan, blocks):
    pairs = list(zip(blocks, plan.columns[1:]))
    got = [partner_swap(one, column) for one, column in reversed(pairs)]
    return got[::-1]


def to_all_columns(plan, block):
    return [partner_swap(block, column) for column in plan.columns[1:]]


def tie(*values):
    return lax.optimization_barrier(values)


def per_device(
    input_codes,
    cotangent_codes,
    dictionary,
    encoder_bias,
    decoder_bias,
    norm_gain,
    gate_weight,
    up_weight,
    down_weight,
):
    plan = Plan(
        lax.axis_size("latent"), lax.axis_size("hidden"), input_codes.shape[0], input_codes.shape[1]
    )
    if not plan.fits():
        return per_device_plain(
            input_codes,
            cotangent_codes,
            dictionary,
            encoder_bias,
            decoder_bias,
            norm_gain,
            gate_weight,
            up_weight,
            down_weight,
        )
    vectors = jnp.concatenate([encoder_bias, decoder_bias, norm_gain]).reshape(1, -1)
    codes = jnp.stack([input_codes, cotangent_codes])
    values = (codes.astype(F32) * CODE_STEP).astype(BF16)
    block, cotangent = pack_values(plan, values)
    stack = stack_up(plan, block, to_all_columns(plan, block))
    stack, vectors, late_dictionary, cotangent = tie(stack, vectors, dictionary, cotangent)
    stack_other, crossed = swap(stack), cross(stack)
    encoder = bring_encoder(plan, late_dictionary, vectors)
    cotangent = double(plan, cotangent, plan.doubling[0])
    stack_other, crossed, encoder, cotangent = tie(stack_other, crossed, encoder, cotangent)
    brought, bias, decoder, gain = encoder
    inputs, latents, kept, sent = encode(
        plan, (stack, crossed), (stack_other, swap(crossed)), brought, bias, gain
    )
    sent, kept = swap(sent), swap(kept)
    own_kept, own_sent = decode_own(plan, latents, brought, decoder, gain)
    sent_first, sent_rest = add_sent(plan, own_sent, sent)
    sent_rest, cotangent = tie(sent_rest, cotangent)
    for bit in plan.doubling[1:-1]:
        cotangent = double(plan, cotangent, bit)
    there = partner_swap(cotangent, plan.doubling[-1])
    sent = add_across(plan, own_kept, kept, cross(sent_rest))
    sent, sent_first, cotangent, there = tie(sent, sent_first, cotangent, there)
    cotangent, sent_first = add_message(plan, sent_first, cotangent, there)
    got, first = to_column(plan, sent), cross(sent_first)
    block, crossed = add_column(plan, own_kept, kept, got, first)
    cotangent_own = (cotangent, crossed)
    hidden_grad = back_project(
        plan, cotangent_own, [swap(one) for one in cotangent_own], down_weight
    )
    stack = stack_up(plan, block, to_all_columns(plan, block))
    stack_other, crossed = swap(stack), cross(stack)
    stack_other, crossed, hidden_grad = tie(stack_other, crossed, hidden_grad)
    terms = mlp_first(plan, line_up(plan, stack, crossed), gate_weight, up_weight, gain)
    scaled_other = line_up(plan, stack_other, swap(crossed))
    scaled, inverse, hidden, gate_grad, up_grad, kept, sent = mlp(
        plan, scaled_other, gate_weight, up_weight, gain, hidden_grad, terms
    )
    sent, kept = swap(sent), swap(kept)
    own_kept, own_sent = mlp_own(plan, gate_grad, up_grad, gate_weight, up_weight)
    out_mine, out_theirs = project(plan, hidden, down_weight)
    sent_first, sent_rest = add_sent(plan, own_sent, sent)
    sent_first, sent_rest, out_mine, out_theirs = tie(sent_first, sent_rest, out_mine, out_theirs)
    crossed = cross(sent_rest)
    out_kept, sent_first = add_pair(plan, sent_first, out_mine, swap(out_theirs))
    sent = add_across(plan, own_kept, kept, crossed)
    sent, sent_first, out_kept = tie(sent, sent_first, out_kept)
    got = to_column(plan, sent)
    first = cross(sent_first)
    block, message, out_kept = add_with_output(plan, own_kept, kept, got, first, out_kept)
    got = to_column(plan, [message] + [block] * (len(plan.columns) - 2))
    stack = stack_up(plan, block, got)
    out_kept, out_sent = halve(plan, out_kept, got[0], plan.chunk)
    stack, scaled_late, inputs_late, out_sent = tie(stack, scaled, inputs, out_sent)
    stack_other, crossed = swap(stack), cross(stack)
    prepared = prepare(plan, scaled_late, inputs_late, gain, inverse)
    for bit in reversed(plan.doubling[2:]):
        out_kept, out_sent = halve(plan, out_kept, partner_swap(out_sent, bit), 0)
    out_got = partner_swap(out_sent, plan.doubling[1])
    stack_other, crossed, out_got = tie(stack_other, crossed, out_got)
    block_output = finish_output(plan, out_kept, out_got)
    grad_own = line_up(plan, stack, crossed)
    grad_other = line_up(plan, stack_other, swap(crossed))
    dictionary_grad = dictionary_step(
        plan, grad_own, grad_other, scaled, prepared, inputs, latents, brought
    )
    return (block_output, dictionary_grad)


def per_device_plain(
    input_codes,
    cotangent_codes,
    dictionary,
    encoder_bias,
    decoder_bias,
    norm_gain,
    gate_weight,
    up_weight,
    down_weight,
):
    own_width = input_codes.shape[1]
    model_width = own_width * lax.axis_size(("latent", "hidden"))
    cotangent_local = (cotangent_codes.astype(jnp.float32) * CODE_STEP).astype(jnp.bfloat16)
    inputs_local = (input_codes.astype(jnp.float32) * CODE_STEP).astype(jnp.bfloat16)
    inputs = lax.all_gather(inputs_local, ("latent", "hidden"), axis=1, tiled=True)
    preact = (
        lax.dot_general(inputs, dictionary, ACROSS, preferred_element_type=jnp.float32)
        + encoder_bias
    )
    latents = jnp.maximum(preact, 0.0).astype(jnp.bfloat16)
    partial_value = jnp.dot(latents, dictionary, preferred_element_type=jnp.float32)
    rebuilt = lax.psum(partial_value, ("latent", "hidden")) + decoder_bias
    inverse = lax.rsqrt(
        jnp.sum(rebuilt * rebuilt, axis=1, keepdims=True) / model_width + NORM_EPSILON
    )
    normed = (rebuilt * inverse * norm_gain).astype(jnp.bfloat16)
    target = inputs.astype(jnp.float32)
    gate_proj = lax.dot_general(normed, gate_weight, ACROSS, preferred_element_type=jnp.float32)
    up_proj = lax.dot_general(normed, up_weight, ACROSS, preferred_element_type=jnp.float32)
    gelu_value, gelu_slope = gelu_parts(gate_proj)
    hidden = (gelu_value * up_proj).astype(jnp.bfloat16)
    output_terms = jnp.dot(hidden, down_weight, preferred_element_type=jnp.float32)
    block_output = lax.psum_scatter(
        output_terms, ("latent", "hidden"), scatter_dimension=1, tiled=True
    ).astype(jnp.bfloat16)
    hidden_grad = lax.dot_general(
        lax.all_gather(cotangent_local, ("latent", "hidden"), axis=1, tiled=True),
        down_weight,
        ACROSS,
        preferred_element_type=jnp.float32,
    )
    gate_grad = (hidden_grad * up_proj * gelu_slope).astype(jnp.bfloat16)
    up_grad = (hidden_grad * gelu_value).astype(jnp.bfloat16)
    partial_grad = jnp.dot(gate_grad, gate_weight, preferred_element_type=jnp.float32) + jnp.dot(
        up_grad, up_weight, preferred_element_type=jnp.float32
    )
    scaled = lax.psum(partial_grad, ("latent", "hidden")) * norm_gain
    inner_row = jnp.sum(scaled * rebuilt, axis=1, keepdims=True)
    inverse_cube = inverse * inverse * inverse
    rebuilt_grad = (
        inverse * scaled - inverse_cube * rebuilt * (inner_row / model_width) + (rebuilt - target)
    ).astype(jnp.bfloat16)
    latent_grad = lax.dot_general(
        rebuilt_grad, dictionary, ACROSS, preferred_element_type=jnp.float32
    )
    preact_grad = jnp.where(preact > 0.0, latent_grad, 0.0).astype(jnp.bfloat16)
    dictionary_grad = lax.dot_general(
        latents, rebuilt_grad, DOWNWARD, preferred_element_type=jnp.float32
    ) + lax.dot_general(preact_grad, inputs, DOWNWARD, preferred_element_type=jnp.float32)
    return (block_output, dictionary_grad.astype(jnp.bfloat16))


def solution(mesh):
    in_specs = (
        P("groups", ("latent", "hidden")),
        P("groups", ("latent", "hidden")),
        P(("latent", "hidden"), None),
        P(("latent", "hidden")),
        P(),
        P(),
        P(("latent", "hidden"), None),
        P(("latent", "hidden"), None),
        P(("latent", "hidden"), None),
    )
    out_specs = (P("groups", ("latent", "hidden")), P(("latent", "hidden"), "groups"))
    return jax.shard_map(
        per_device, mesh=mesh, in_specs=in_specs, out_specs=out_specs, check_vma=False
    )
```

```python
import functools
import math

import jax
import jax.numpy as jnp
from jax import lax
from jax.experimental import pallas as pl
from jax.experimental.pallas import tpu as pltpu
from jax.sharding import PartitionSpec as P

CODE_STEP = 2.0 ** (-6)
NORM_EPSILON = 1e-06
GELU_ROOT = 0.7978845608028654
GELU_CUBIC = 0.044715
ACROSS = (((1,), (1,)), ((), ()))
DOWNWARD = (((0,), (0,)), ((), ()))
LANES = 128
ROW_TILE = 16
DIRECT_LIMIT = 16
VMEM_BYTES = 24 * 1024 * 1024
VMEM_BRING = 53 * 1024 * 1024
F32 = jnp.float32
BF16 = jnp.bfloat16


def gelu_parts(values):
    argument = GELU_ROOT * (values + GELU_CUBIC * values * values * values)
    tanh_value = jnp.tanh(argument)
    result = 0.5 * values * (1.0 + tanh_value)
    derivative = 0.5 * (1.0 + tanh_value) + 0.5 * values * (
        1.0 - tanh_value * tanh_value
    ) * GELU_ROOT * (1.0 + 3.0 * GELU_CUBIC * values * values)
    return (result, derivative)


def up_to(value, unit):
    return -(-value // unit) * unit


def chips_fit(chips):
    return 8 <= chips <= DIRECT_LIMIT and chips & (chips - 1) == 0


class Plan:
    def __init__(self, chips, cores, rows, own):
        self.chips, self.cores, self.rows, self.own = chips, cores, rows, own
        self.width = own * chips * cores
        self.half = self.width // cores
        self.tiles = self.half // LANES
        self.chunk = up_to(-(-self.tiles * rows // chips), ROW_TILE)
        self.flat = self.chunk * chips
        self.tail = own - LANES
        if self.tail > 0:
            self.fold_rows = min(
                size
                for size in range(ROW_TILE, rows + ROW_TILE, ROW_TILE)
                if -(-rows // size) * self.tail <= LANES
            )
            self.packed = rows + self.fold_rows
        self.columns = list(range(0, chips, 2))
        self.doubling = [1 << k for k in range(1, (chips - 1).bit_length())]
        self.doubled = [0]
        for bit in reversed(self.doubling):
            self.doubled = self.doubled + [place ^ bit for place in self.doubled]

    def side_blocks(self, refs):
        me = lax.axis_index("latent")
        stack_ref, *crossed_refs = refs
        for place, column in enumerate(self.columns):
            yield me ^ column, stack_ref[place]
        places = iter(self.columns)
        for ref in crossed_refs:
            for place in range(ref.shape[0]):
                yield me ^ next(places) ^ 1, ref[place]

    def pieces(self):
        for tile in range(self.tiles):
            row = 0
            while row < self.rows:
                chip, place = divmod(tile * self.rows + row, self.chunk)
                count = min(self.rows - row, self.chunk - place)
                yield tile, chip, place, row, count
                row += count

    def fits(self):
        return (
            self.cores == 2
            and chips_fit(self.chips)
            and self.rows % ROW_TILE == 0
            and self.half % LANES == 0
            and 0 < self.tail < LANES
            and self.packed == self.chunk
        )


HBM = pl.BlockSpec(memory_space=pltpu.HBM)
ONCHIP = pl.BlockSpec(memory_space=pltpu.VMEM)


def shaped(*dims, dtype=F32):
    return jax.ShapeDtypeStruct(dims, dtype)


HBM = pl.BlockSpec(memory_space=pltpu.HBM)
ONCHIP = pl.BlockSpec(memory_space=pltpu.VMEM)


def shaped(*dims, dtype=F32):
    return jax.ShapeDtypeStruct(dims, dtype)


def call(body, out_shapes, operands, scratch=(), out_specs=None, flops=0, moved=0):
    return pl.pallas_call(
        body,
        out_shape=out_shapes,
        in_specs=[ONCHIP] * len(operands),
        out_specs=jax.tree.map(lambda _: ONCHIP, out_shapes) if out_specs is None else out_specs,
        scratch_shapes=list(scratch),
        compiler_params=pltpu.CompilerParams(vmem_limit_bytes=VMEM_BYTES),
        cost_estimate=pl.CostEstimate(flops=flops, bytes_accessed=moved, transcendentals=0),
    )(*operands)


def padded_bytes(array):
    *lead, rows, columns = array.shape
    item = jnp.dtype(array.dtype).itemsize
    return math.prod(lead) * up_to(rows, ROW_TILE) * up_to(columns, LANES) * item


def copies(sources, targets, sems):
    started = []
    for index, (source, target) in enumerate(zip(sources, targets)):
        one = pltpu.make_async_copy(source, target, sems.at[index])
        one.start()
        started.append(one)
    return started


def pack_block(plan, block):
    tail = block[:, LANES:]
    folded = []
    for start in range(0, plan.rows, plan.fold_rows):
        piece = tail[start : min(start + plan.fold_rows, plan.rows), :]
        short = plan.fold_rows - piece.shape[0]
        if short:
            piece = jnp.concatenate([piece, jnp.zeros((short, plan.tail), block.dtype)], axis=0)
        folded.append(piece)
    fill = LANES - len(folded) * plan.tail
    if fill:
        folded.append(jnp.zeros((plan.fold_rows, fill), block.dtype))
    return block[:, :LANES], jnp.concatenate(folded, axis=1)


def unpack_block(plan, packed):
    pieces = []
    for fold, start in enumerate(range(0, plan.rows, plan.fold_rows)):
        count = min(plan.fold_rows, plan.rows - start)
        pieces.append(
            packed[plan.rows : plan.rows + count, fold * plan.tail : (fold + 1) * plan.tail]
        )
    return jnp.concatenate([packed[: plan.rows, :], jnp.concatenate(pieces, axis=0)], axis=1)


def pack_values_body(plan, values_ref, *block_refs):
    for index, block_ref in enumerate(block_refs):
        main, tail = pack_block(plan, values_ref[index].astype(F32))
        block_ref[0, : plan.rows, :] = main.astype(BF16)
        block_ref[0, plan.rows :, :] = tail.astype(BF16)


def pack_values(plan, values):
    return call(
        functools.partial(pack_values_body, plan),
        [shaped(1, plan.packed, LANES, dtype=BF16)] * values.shape[0],
        (values,),
        moved=values.size * 6,
    )


def assemble(plan, own_refs, other_refs, both, full_ref):
    core = lax.axis_index("hidden")
    for side, refs in ((core, own_refs), (1 - core, other_refs)):
        for chip, block in plan.side_blocks(refs):
            both[side, chip] = block
    for chip in range(plan.chips):
        for side in range(plan.cores):
            column = (chip * plan.cores + side) * plan.own
            full_ref[:, column : column + plan.own] = unpack_block(plan, both[side, chip])


def both_scratch(plan, dtype=BF16):
    return pltpu.VMEM((plan.cores, plan.chips, plan.packed, LANES), dtype)


def chunk_scratch(plan):
    return pltpu.VMEM((plan.chips, plan.chunk, LANES), F32)


def side_shapes(plan, dtype=F32):
    return [shaped(len(plan.columns), plan.chunk, LANES, dtype=dtype)] * 2


def half_product(plan, pairs, side, kept_ref, sent_ref, target, gain_ref=None, bias_ref=None):
    span = pl.ds(pl.multiple_of(side * plan.half, LANES), plan.half)
    total = None
    for left, right_ref in pairs:
        term = jnp.dot(left, right_ref[:, span], preferred_element_type=F32)
        total = term if total is None else total + term
    if bias_ref is not None:
        total = total + bias_ref[:, span] * jnp.where(lax.axis_index("latent") == 0, 1.0, 0.0)
    if gain_ref is not None:
        total = total * gain_ref[:, span]
    for tile, chip, place, row, count in plan.pieces():
        target[chip, place : place + count, :] = total[
            row : row + count, tile * LANES : (tile + 1) * LANES
        ]
    used = plan.tiles * plan.rows
    while used < plan.flat:
        chip, place = divmod(used, plan.chunk)
        target[chip, place:, :] = jnp.zeros((plan.chunk - place, LANES), F32)
        used += plan.chunk - place
    me = lax.axis_index("latent")
    for place, column in enumerate(plan.columns):
        kept_ref[place] = target[me ^ column]
        sent_ref[place] = target[me ^ column ^ 1]


def bring_encoder_body(dict_hbm, vectors_hbm, dict_ref, bias_ref, decoder_ref, gain_ref, sems):
    sources, targets = [dict_hbm], [dict_ref]
    start = 0
    for target in (bias_ref, decoder_ref, gain_ref):
        sources.append(vectors_hbm.at[:, start : start + target.shape[1]])
        targets.append(target)
        start += target.shape[1]
    for copy in copies(sources, targets, sems):
        copy.wait()


def bring_encoder(plan, dictionary, vectors):
    outputs = [
        shaped(*dictionary.shape, dtype=BF16),
        shaped(1, dictionary.shape[0]),
        shaped(1, plan.width),
        shaped(1, plan.width),
    ]
    return pl.pallas_call(
        bring_encoder_body,
        out_shape=outputs,
        in_specs=[HBM] * 2,
        out_specs=[ONCHIP] * len(outputs),
        scratch_shapes=[pltpu.SemaphoreType.DMA((len(outputs),))],
        compiler_params=pltpu.CompilerParams(
            vmem_limit_bytes=VMEM_BRING - sum(map(padded_bytes, outputs))
        ),
        cost_estimate=pl.CostEstimate(
            flops=0, bytes_accessed=dictionary.size * 4, transcendentals=0
        ),
    )(dictionary, vectors)


def encode_body(plan, *refs):
    own, other, (dict_ref, bias_ref, gain_ref) = refs[:2], refs[2:4], refs[4:7]
    inputs_ref, latents_ref, kept_ref, sent_ref, both, target = refs[7:]
    assemble(plan, own, other, both, inputs_ref)
    preact = (
        lax.dot_general(inputs_ref[...], dict_ref[...], ACROSS, preferred_element_type=F32)
        + bias_ref[...]
    )
    latents = jnp.maximum(preact, 0.0).astype(BF16)
    latents_ref[...] = latents
    theirs = 1 - lax.axis_index("hidden")
    half_product(plan, [(latents, dict_ref)], theirs, kept_ref, sent_ref, target, gain_ref)


def encode(plan, own, other, dictionary, encoder_bias, gain):
    latents = dictionary.shape[0]
    return call(
        functools.partial(encode_body, plan),
        [
            shaped(plan.rows, plan.width, dtype=BF16),
            shaped(plan.rows, latents, dtype=BF16),
            *side_shapes(plan),
        ],
        (*own, *other, dictionary, encoder_bias, gain),
        [both_scratch(plan), chunk_scratch(plan)],
        flops=3 * plan.rows * plan.width * latents,
        moved=dictionary.size * 2,
    )


def decode_own_body(plan, latents_ref, dict_ref, decoder_ref, gain_ref, kept_ref, sent_ref, target):
    pairs = [(latents_ref[...], dict_ref)]
    mine = lax.axis_index("hidden")
    half_product(plan, pairs, mine, kept_ref, sent_ref, target, gain_ref, decoder_ref)


def decode_own(plan, latents, dictionary, decoder_bias, gain):
    return call(
        functools.partial(decode_own_body, plan),
        side_shapes(plan),
        (latents, dictionary, decoder_bias, gain),
        [chunk_scratch(plan)],
        flops=plan.rows * plan.width * dictionary.shape[0],
        moved=dictionary.size,
    )


def back_project_body(plan, *refs):
    own, other, (down_ref, grad_ref, both, full) = refs[:2], refs[2:4], refs[4:]
    assemble(plan, own, other, both, full)
    grad_ref[...] = lax.dot_general(
        full[...], down_ref[...], ACROSS, preferred_element_type=F32
    )


def back_project(plan, own, other, down_weight):
    units = down_weight.shape[0]
    return call(
        functools.partial(back_project_body, plan),
        shaped(plan.rows, units),
        (*own, *other, down_weight),
        [both_scratch(plan), pltpu.VMEM((plan.rows, plan.width), BF16)],
        flops=2 * plan.rows * plan.width * units,
        moved=down_weight.size * 2,
    )


def join_half(plan, source, first, full_ref):
    for tile, chip, place, row, count in plan.pieces():
        column = pl.multiple_of(first + tile * LANES, LANES)
        full_ref[row : row + count, pl.ds(column, LANES)] = source[
            chip, place : place + count, :
        ]


def half_terms(plan, half, side, gate_ref, up_ref, gain_ref):
    span = pl.ds(pl.multiple_of(side * plan.half, LANES), plan.half)
    rebuilt = half.astype(F32) / gain_ref[:, span]
    squares = jnp.sum(rebuilt * rebuilt, axis=1, keepdims=True)
    gate = lax.dot_general(half, gate_ref[:, span], ACROSS, preferred_element_type=F32)
    up = lax.dot_general(half, up_ref[:, span], ACROSS, preferred_element_type=F32)
    return squares, gate, up


def mlp_first_body(plan, own_ref, gate_ref, up_ref, gain_ref, half_ref, squares_ref, gate_part_ref, up_part_ref):
    join_half(plan, own_ref, 0, half_ref)
    squares_ref[...], gate_part_ref[...], up_part_ref[...] = half_terms(
        plan, half_ref[...], lax.axis_index("hidden"), gate_ref, up_ref, gain_ref
    )


def mlp_first(plan, own, gate_weight, up_weight, gain):
    units = gate_weight.shape[0]
    return call(
        functools.partial(mlp_first_body, plan),
        [
            shaped(plan.rows, plan.half, dtype=BF16),
            shaped(plan.rows, 1),
            shaped(plan.rows, units),
            shaped(plan.rows, units),
        ],
        (own, gate_weight, up_weight, gain),
        flops=2 * plan.rows * plan.width * units,
        moved=gate_weight.size * 4,
    )


def mlp_body(plan, other_ref, gate_ref, up_ref, gain_ref, grad_ref, half_ref, squares_ref, gate_part_ref, up_part_ref, scaled_ref, inverse_ref, hidden_ref, gate_grad_ref, up_grad_ref, kept_ref, sent_ref, target):
    core = lax.axis_index("hidden")
    join_half(plan, other_ref, (1 - core) * plan.half, scaled_ref)
    other_span = pl.ds(pl.multiple_of((1 - core) * plan.half, LANES), plan.half)
    own_span = pl.ds(pl.multiple_of(core * plan.half, LANES), plan.half)
    scaled_ref[:, own_span] = half_ref[...]
    squares, gate, up = half_terms(
        plan, scaled_ref[:, other_span], 1 - core, gate_ref, up_ref, gain_ref
    )
    inverse = lax.rsqrt((squares + squares_ref[...]) / plan.width + NORM_EPSILON)
    inverse_ref[...] = inverse
    gate_proj = inverse * (gate + gate_part_ref[...])
    up_proj = inverse * (up + up_part_ref[...])
    gelu_value, gelu_slope = gelu_parts(gate_proj)
    hidden_ref[...] = (gelu_value * up_proj).astype(BF16)
    hidden_grad = grad_ref[...]
    gate_grad = (hidden_grad * up_proj * gelu_slope).astype(BF16)
    up_grad = (hidden_grad * gelu_value).astype(BF16)
    gate_grad_ref[...] = gate_grad
    up_grad_ref[...] = up_grad
    pairs = [(gate_grad, gate_ref), (up_grad, up_ref)]
    half_product(plan, pairs, 1 - core, kept_ref, sent_ref, target)


def mlp(plan, other, gate_weight, up_weight, gain, hidden_grad, first):
    units = gate_weight.shape[0]
    return call(
        functools.partial(mlp_body, plan),
        [
            shaped(plan.rows, plan.width, dtype=BF16),
            shaped(plan.rows, 1),
            shaped(plan.rows, units, dtype=BF16),
            shaped(plan.rows, units, dtype=BF16),
            shaped(plan.rows, units, dtype=BF16),
            *side_shapes(plan),
        ],
        (other, gate_weight, up_weight, gain, hidden_grad, *first),
        [chunk_scratch(plan)],
        flops=6 * plan.rows * plan.width * units,
        moved=gate_weight.size * 4,
    )


def mlp_own_body(plan, gate_grad_ref, up_grad_ref, gate_ref, up_ref, kept_ref, sent_ref, target):
    pairs = [(gate_grad_ref[...], gate_ref), (up_grad_ref[...], up_ref)]
    half_product(plan, pairs, lax.axis_index("hidden"), kept_ref, sent_ref, target)


def mlp_own(plan, gate_grad, up_grad, gate_weight, up_weight):
    return call(
        functools.partial(mlp_own_body, plan),
        side_shapes(plan),
        (gate_grad, up_grad, gate_weight, up_weight),
        [chunk_scratch(plan)],
        flops=2 * plan.rows * plan.width * gate_weight.shape[0],
        moved=gate_weight.size * 2,
    )


def pack_side(plan, terms_ref, side, out_ref):
    for core in range(plan.cores):

        @pl.when(side == core)
        def _():
            for chip in range(plan.chips):
                start = (chip * plan.cores + core) * plan.own
                main, tail = pack_block(plan, terms_ref[:, start : start + plan.own])
                out_ref[chip, : plan.rows, :] = main
                out_ref[chip, plan.rows :, :] = tail


def project_body(plan, hidden_ref, down_ref, terms_ref, theirs_ref):
    terms_ref[...] = jnp.dot(
        hidden_ref[...], down_ref[...], preferred_element_type=F32
    ).astype(BF16)
    pack_side(plan, terms_ref, 1 - lax.axis_index("hidden"), theirs_ref)


def project(plan, hidden, down_weight):
    units = down_weight.shape[0]
    return call(
        functools.partial(project_body, plan),
        [
            shaped(plan.rows, plan.width, dtype=BF16),
            shaped(plan.chips, plan.packed, LANES, dtype=BF16),
        ],
        (hidden, down_weight),
        flops=2 * plan.rows * plan.width * units,
        moved=down_weight.size * 2,
    )


def pack_own_body(plan, terms_ref, mine_ref):
    pack_side(plan, terms_ref, lax.axis_index("hidden"), mine_ref)


def pack_own(plan, terms):
    return call(
        functools.partial(pack_own_body, plan),
        shaped(plan.chips, plan.packed, LANES, dtype=BF16),
        (terms,),
        moved=terms.size * 4,
    )


def add_pair_body(plan, first_ref, mine_ref, theirs_ref, kept_ref, sent_ref):
    me = lax.axis_index("latent")
    sent_ref[0] = first_ref[0]
    for place, column in enumerate(plan.columns):
        kept, sent = me ^ column, me ^ column ^ 1
        kept_ref[place] = mine_ref[kept].astype(F32) + theirs_ref[kept].astype(F32)
        sent_ref[1 + place] = (
            mine_ref[sent].astype(F32) + theirs_ref[sent].astype(F32)
        ).astype(BF16)


def add_pair(plan, first, mine, theirs):
    count, dims = len(plan.columns), mine.shape[1:]
    return call(
        functools.partial(add_pair_body, plan),
        [shaped(count, *dims), shaped(1 + count, *dims, dtype=BF16)],
        (first, mine, theirs),
        moved=mine.size * 10,
    )


def add_sent_body(mine_ref, theirs_ref, first_ref, rest_ref):
    total = (mine_ref[...] + theirs_ref[...]).astype(BF16)
    first_ref[...] = total[:1]
    rest_ref[...] = total[1:]


def add_sent(plan, mine, theirs):
    count, *dims = mine.shape
    return call(
        add_sent_body,
        [shaped(1, *dims, dtype=BF16), shaped(count - 1, *dims, dtype=BF16)],
        (mine, theirs),
        moved=mine.size * 10,
    )


def add_across_body(mine_ref, theirs_ref, got_ref, *sent_refs):
    for place, out_ref in enumerate(sent_refs):
        total = mine_ref[1 + place] + theirs_ref[1 + place] + got_ref[place].astype(F32)
        out_ref[0] = total.astype(BF16)


def add_across(plan, mine, theirs, got):
    return call(
        add_across_body,
        [shaped(1, *mine.shape[1:], dtype=BF16)] * got.shape[0],
        (mine, theirs, got),
        moved=mine.size * 10,
    )


def column_total(mine_ref, theirs_ref, *refs):
    total = mine_ref[0] + theirs_ref[0]
    for ref in refs:
        total = total + ref[0].astype(F32)
    return total.astype(BF16)


def add_column_body(*refs):
    *sources, block_ref, more_ref = refs
    block_ref[0] = column_total(*sources)
    more_ref[...] = sources[-1][1:]


def add_column(plan, mine, theirs, got, first):
    dims = mine.shape[1:]
    return call(
        add_column_body,
        [shaped(1, *dims, dtype=BF16), shaped(first.shape[0] - 1, *dims, dtype=BF16)],
        (mine, theirs, *reversed(got), first),
        moved=mine.size * 8,
    )


def add_with_output_body(plan, count, *refs):
    total = column_total(*refs[:count])
    first_ref, out_ref, block_ref, message_ref, kept_ref = refs[count - 1 : count + 4]
    block_ref[0] = total
    message_ref[0, : plan.chunk, :] = total
    near = plan.doubling[0]
    halves = [[], []]
    for place, column in enumerate(plan.columns):
        halves[column & near != 0].append(out_ref[place] + first_ref[1 + place].astype(F32))
    for index, (kept, sent) in enumerate(zip(*halves)):
        kept_ref[index] = kept
        start = plan.chunk + index * plan.packed
        message_ref[0, start : start + plan.packed, :] = sent.astype(BF16)


def add_with_output(plan, mine, theirs, got, first, kept):
    half = len(plan.columns) // 2
    return call(
        functools.partial(add_with_output_body, plan, 3 + len(got)),
        [
            shaped(1, plan.chunk, LANES, dtype=BF16),
            shaped(1, plan.chunk + half * plan.packed, LANES, dtype=BF16),
            shaped(half, plan.packed, LANES),
        ],
        (mine, theirs, *reversed(got), first, kept),
        moved=mine.size * 12,
    )


def halve_body(rows, skip, kept_ref, got_ref, left_ref, sent_ref):
    half = left_ref.shape[0]
    for index in range(2 * half):
        start = skip + index * rows
        total = kept_ref[index] + got_ref[0, start : start + rows, :].astype(F32)
        if index < half:
            left_ref[index] = total
        else:
            begin = (index - half) * rows
            sent_ref[0, begin : begin + rows, :] = total.astype(BF16)


def halve(plan, kept, got, skip):
    half, rows = kept.shape[0] // 2, plan.packed
    return call(
        functools.partial(halve_body, rows, skip),
        [shaped(half, rows, LANES), shaped(1, half * rows, LANES, dtype=BF16)],
        (kept, got),
        moved=kept.size * 10,
    )


def stack_body(places, *refs):
    count = len(places)
    stack_ref, *rest_refs = refs[count:]
    rows = stack_ref.shape[1]
    for place, ref in zip(places, refs):
        stack_ref[place] = ref[0, :rows, :]
        for rest_ref in rest_refs:
            if place:
                rest_ref[place - 1] = ref[0, :rows, :]


def stack_up(plan, block, got, with_rest=False):
    dims = block.shape[1:]
    operands = [block, *got]
    places = list(range(len(operands)))
    if with_rest:
        operands, places = operands[::-1], places[::-1]
    outs = [shaped(1 + len(got), *dims, dtype=BF16), shaped(len(got), *dims, dtype=BF16)]
    return call(
        functools.partial(stack_body, places),
        outs if with_rest else outs[0],
        operands,
        moved=block.size * 16,
    )


def join_body(*refs):
    *sources, joined_ref = refs
    start = 0
    for ref in sources:
        joined_ref[start : start + ref.shape[0]] = ref[...]
        start += ref.shape[0]


def join(plan, *stacks):
    count = sum(one.shape[0] for one in stacks)
    return call(
        join_body,
        shaped(count, *stacks[0].shape[1:], dtype=BF16),
        stacks,
        moved=count * stacks[0].size,
    )


def double(plan, stack, bit):
    return join(plan, stack, partner_swap(stack, bit))


def add_message_body(plan, first_ref, here_ref, there_ref, stack_ref, message_ref):
    message_ref[0] = first_ref[0]
    half = here_ref.shape[0]
    for index, column in enumerate(plan.doubled):
        block = here_ref[index] if index < half else there_ref[index - half]
        place = plan.columns.index(column)
        stack_ref[place] = block
        message_ref[1 + place] = block


def add_message(plan, first, here, there):
    count, dims = len(plan.columns), first.shape[1:]
    return call(
        functools.partial(add_message_body, plan),
        [shaped(count, *dims, dtype=BF16), shaped(1 + count, *dims, dtype=BF16)],
        (first, here, there),
        moved=first.size * 40,
    )


def line_up_body(plan, *refs):
    for chip, block in plan.side_blocks(refs[:-1]):
        refs[-1][chip] = block


def line_up(plan, stack, *crossed):
    return call(
        functools.partial(line_up_body, plan),
        shaped(plan.chips, *stack.shape[1:], dtype=BF16),
        (stack, *crossed),
        moved=stack.size * 8,
    )


def finish_output_body(plan, kept_ref, got_ref, out_ref):
    total = kept_ref[0] + got_ref[0].astype(F32)
    out_ref[...] = unpack_block(plan, total).astype(BF16)


def finish_output(plan, kept, got):
    return call(
        functools.partial(finish_output_body, plan),
        shaped(plan.rows, plan.own, dtype=BF16),
        (kept, got),
        moved=kept.size * 8,
    )


def prepare_body(plan, scaled_ref, inputs_ref, gain_ref, inverse_ref, factor_ref, slope_ref, base_ref):
    gain = gain_ref[...]
    inverse = inverse_ref[...]
    rebuilt = scaled_ref[...].astype(F32) / gain
    factor_ref[...] = inverse * gain
    slope_ref[...] = rebuilt * (inverse * inverse * inverse / plan.width)
    base_ref[...] = rebuilt - inputs_ref[...].astype(F32)


def prepare(plan, scaled, inputs, gain, inverse):
    return call(
        functools.partial(prepare_body, plan),
        [shaped(plan.rows, plan.width)] * 3,
        (scaled, inputs, gain, inverse),
        moved=scaled.size * 16,
    )


def dictionary_body(plan, pieces, own_ref, other_ref, scaled_ref, factor_ref, slope_ref, base_ref, inputs_ref, latents_ref, dict_ref, out_hbm, full, out_ref, out_sems):
    core = lax.axis_index("hidden")
    join_half(plan, own_ref, core * plan.half, full)
    join_half(plan, other_ref, (1 - core) * plan.half, full)
    grad = full[...].astype(F32)
    inner_row = jnp.sum(grad * scaled_ref[...].astype(F32), axis=1, keepdims=True)
    inputs = inputs_ref[...]
    rebuilt_grad = (
        grad * factor_ref[...] - inner_row * slope_ref[...] + base_ref[...]
    ).astype(BF16)
    latents = latents_ref[...]
    latent_grad = lax.dot_general(
        rebuilt_grad, dict_ref[...], ACROSS, preferred_element_type=F32
    )
    preact_grad = jnp.where(latents.astype(F32) > 0.0, latent_grad, 0.0).astype(BF16)
    left = jnp.concatenate([latents, preact_grad], axis=0)
    right = jnp.concatenate([rebuilt_grad, inputs], axis=0)
    size = plan.width // pieces
    writes = []
    for piece in range(pieces):
        span = slice(piece * size, (piece + 1) * size)
        out_ref[:, span] = lax.dot_general(
            left, right[:, span], DOWNWARD, preferred_element_type=F32
        ).astype(BF16)
        one = pltpu.make_async_copy(
            out_ref.at[:, span], out_hbm.at[:, span], out_sems.at[piece]
        )
        one.start()
        writes.append(one)
    for one in writes:
        one.wait()


def dictionary_step(plan, own, other, scaled, prepared, inputs, latents, dictionary):
    units = dictionary.shape[0]
    pieces = plan.tiles
    return call(
        functools.partial(dictionary_body, plan, pieces),
        shaped(*dictionary.shape, dtype=BF16),
        (own, other, scaled, *prepared, inputs, latents, dictionary),
        [
            pltpu.VMEM((plan.rows, plan.width), BF16),
            pltpu.VMEM(dictionary.shape, BF16),
            pltpu.SemaphoreType.DMA((pieces,)),
        ],
        out_specs=HBM,
        flops=6 * plan.rows * plan.width * units,
        moved=dictionary.size * 4,
    )


def swap(value):
    size = lax.axis_size("hidden")
    return lax.ppermute(value, "hidden", [(i, (i + 1) % size) for i in range(size)])


def partner_swap(value, bits):
    size = lax.axis_size("latent")
    return lax.ppermute(value, "latent", [(i, i ^ bits) for i in range(size)])


def cross(value):
    return partner_swap(value, 1)


def to_column(plan, blocks):
    pairs = list(zip(blocks, plan.columns[1:]))
    got = [partner_swap(one, column) for one, column in reversed(pairs)]
    return got[::-1]


def to_all_columns(plan, block):
    return [partner_swap(block, column) for column in plan.columns[1:]]


def tie(*values):
    return lax.optimization_barrier(values)


def per_device(
    input_codes,
    cotangent_codes,
    dictionary,
    encoder_bias,
    decoder_bias,
    norm_gain,
    gate_weight,
    up_weight,
    down_weight,
):
    plan = Plan(
        lax.axis_size("latent"), lax.axis_size("hidden"), input_codes.shape[0], input_codes.shape[1]
    )
    if not plan.fits():
        return per_device_plain(
            input_codes,
            cotangent_codes,
            dictionary,
            encoder_bias,
            decoder_bias,
            norm_gain,
            gate_weight,
            up_weight,
            down_weight,
        )
    vectors = jnp.concatenate([encoder_bias, decoder_bias, norm_gain]).reshape(1, -1)
    codes = jnp.stack([input_codes, cotangent_codes])
    values = (codes.astype(F32) * CODE_STEP).astype(BF16)
    block, cotangent = pack_values(plan, values)
    stack = stack_up(plan, block, to_all_columns(plan, block))
    stack, vectors, late_dictionary, cotangent = tie(stack, vectors, dictionary, cotangent)
    stack_other, crossed = swap(stack), cross(stack)
    encoder = bring_encoder(plan, late_dictionary, vectors)
    cotangent = double(plan, cotangent, plan.doubling[-1])
    stack_other, crossed, encoder, cotangent = tie(stack_other, crossed, encoder, cotangent)
    brought, bias, decoder, gain = encoder
    inputs, latents, kept, sent = encode(
        plan, (stack, crossed), (stack_other, swap(crossed)), brought, bias, gain
    )
    sent, kept = swap(sent), swap(kept)
    own_kept, own_sent = decode_own(plan, latents, brought, decoder, gain)
    sent_first, sent_rest = add_sent(plan, own_sent, sent)
    sent_rest, cotangent = tie(sent_rest, cotangent)
    for bit in reversed(plan.doubling[1:-1]):
        cotangent = double(plan, cotangent, bit)
    there = partner_swap(cotangent, plan.doubling[0])
    sent = add_across(plan, own_kept, kept, cross(sent_rest))
    sent, sent_first, cotangent, there = tie(sent, sent_first, cotangent, there)
    cotangent, sent_first = add_message(plan, sent_first, cotangent, there)
    got, first = to_column(plan, sent), cross(sent_first)
    block, crossed = add_column(plan, own_kept, kept, got, first)
    cotangent_own = (cotangent, crossed)
    hidden_grad = back_project(
        plan, cotangent_own, [swap(one) for one in cotangent_own], down_weight
    )
    stack = stack_up(plan, block, to_all_columns(plan, block))
    stack_other, crossed = swap(stack), cross(stack)
    stack_other, crossed, hidden_grad = tie(stack_other, crossed, hidden_grad)
    terms = mlp_first(plan, line_up(plan, stack, crossed), gate_weight, up_weight, gain)
    scaled_other = line_up(plan, stack_other, swap(crossed))
    scaled, inverse, hidden, gate_grad, up_grad, kept, sent = mlp(
        plan, scaled_other, gate_weight, up_weight, gain, hidden_grad, terms
    )
    sent, kept = swap(sent), swap(kept)
    own_kept, own_sent = mlp_own(plan, gate_grad, up_grad, gate_weight, up_weight)
    out_terms, out_theirs = project(plan, hidden, down_weight)
    sent_first, sent_rest = add_sent(plan, own_sent, sent)
    sent_first, sent_rest, out_terms, out_theirs = tie(
        sent_first, sent_rest, out_terms, out_theirs
    )
    crossed = cross(sent_rest)
    out_theirs = swap(out_theirs)
    out_kept, sent_first = add_pair(plan, sent_first, pack_own(plan, out_terms), out_theirs)
    sent = add_across(plan, own_kept, kept, crossed)
    sent, sent_first, out_kept = tie(sent, sent_first, out_kept)
    got = to_column(plan, sent)
    first = cross(sent_first)
    block, message, out_kept = add_with_output(plan, own_kept, kept, got, first, out_kept)
    got = to_column(plan, [message] + [block] * (len(plan.columns) - 2))
    stack = stack_up(plan, block, got)
    out_kept, out_sent = halve(plan, out_kept, got[0], plan.chunk)
    stack, scaled_late, inputs_late, out_sent = tie(stack, scaled, inputs, out_sent)
    stack_other, crossed = swap(stack), cross(stack)
    prepared = prepare(plan, scaled_late, inputs_late, gain, inverse)
    for bit in reversed(plan.doubling[2:]):
        out_kept, out_sent = halve(plan, out_kept, partner_swap(out_sent, bit), 0)
    out_got = partner_swap(out_sent, plan.doubling[1])
    stack_other, crossed, out_got = tie(stack_other, crossed, out_got)
    block_output = finish_output(plan, out_kept, out_got)
    grad_own = line_up(plan, stack, crossed)
    grad_other = line_up(plan, stack_other, swap(crossed))
    dictionary_grad = dictionary_step(
        plan, grad_own, grad_other, scaled, prepared, inputs, latents, brought
    )
    return (block_output, dictionary_grad)


def per_device_plain(
    input_codes,
    cotangent_codes,
    dictionary,
    encoder_bias,
    decoder_bias,
    norm_gain,
    gate_weight,
    up_weight,
    down_weight,
):
    own_width = input_codes.shape[1]
    model_width = own_width * lax.axis_size(("latent", "hidden"))
    cotangent_local = (cotangent_codes.astype(jnp.float32) * CODE_STEP).astype(jnp.bfloat16)
    inputs_local = (input_codes.astype(jnp.float32) * CODE_STEP).astype(jnp.bfloat16)
    inputs = lax.all_gather(inputs_local, ("latent", "hidden"), axis=1, tiled=True)
    preact = (
        lax.dot_general(inputs, dictionary, ACROSS, preferred_element_type=jnp.float32)
        + encoder_bias
    )
    latents = jnp.maximum(preact, 0.0).astype(jnp.bfloat16)
    partial_value = jnp.dot(latents, dictionary, preferred_element_type=jnp.float32)
    rebuilt = lax.psum(partial_value, ("latent", "hidden")) + decoder_bias
    inverse = lax.rsqrt(
        jnp.sum(rebuilt * rebuilt, axis=1, keepdims=True) / model_width + NORM_EPSILON
    )
    normed = (rebuilt * inverse * norm_gain).astype(jnp.bfloat16)
    target = inputs.astype(jnp.float32)
    gate_proj = lax.dot_general(normed, gate_weight, ACROSS, preferred_element_type=jnp.float32)
    up_proj = lax.dot_general(normed, up_weight, ACROSS, preferred_element_type=jnp.float32)
    gelu_value, gelu_slope = gelu_parts(gate_proj)
    hidden = (gelu_value * up_proj).astype(jnp.bfloat16)
    output_terms = jnp.dot(hidden, down_weight, preferred_element_type=jnp.float32)
    block_output = lax.psum_scatter(
        output_terms, ("latent", "hidden"), scatter_dimension=1, tiled=True
    ).astype(jnp.bfloat16)
    hidden_grad = lax.dot_general(
        lax.all_gather(cotangent_local, ("latent", "hidden"), axis=1, tiled=True),
        down_weight,
        ACROSS,
        preferred_element_type=jnp.float32,
    )
    gate_grad = (hidden_grad * up_proj * gelu_slope).astype(jnp.bfloat16)
    up_grad = (hidden_grad * gelu_value).astype(jnp.bfloat16)
    partial_grad = jnp.dot(gate_grad, gate_weight, preferred_element_type=jnp.float32) + jnp.dot(
        up_grad, up_weight, preferred_element_type=jnp.float32
    )
    scaled = lax.psum(partial_grad, ("latent", "hidden")) * norm_gain
    inner_row = jnp.sum(scaled * rebuilt, axis=1, keepdims=True)
    inverse_cube = inverse * inverse * inverse
    rebuilt_grad = (
        inverse * scaled - inverse_cube * rebuilt * (inner_row / model_width) + (rebuilt - target)
    ).astype(jnp.bfloat16)
    latent_grad = lax.dot_general(
        rebuilt_grad, dictionary, ACROSS, preferred_element_type=jnp.float32
    )
    preact_grad = jnp.where(preact > 0.0, latent_grad, 0.0).astype(jnp.bfloat16)
    dictionary_grad = lax.dot_general(
        latents, rebuilt_grad, DOWNWARD, preferred_element_type=jnp.float32
    ) + lax.dot_general(preact_grad, inputs, DOWNWARD, preferred_element_type=jnp.float32)
    return (block_output, dictionary_grad.astype(jnp.bfloat16))


def solution(mesh):
    in_specs = (
        P("groups", ("latent", "hidden")),
        P("groups", ("latent", "hidden")),
        P(("latent", "hidden"), None),
        P(("latent", "hidden")),
        P(),
        P(),
        P(("latent", "hidden"), None),
        P(("latent", "hidden"), None),
        P(("latent", "hidden"), None),
    )
    out_specs = (P("groups", ("latent", "hidden")), P(("latent", "hidden"), "groups"))
    return jax.shard_map(
        per_device, mesh=mesh, in_specs=in_specs, out_specs=out_specs, check_vma=False
    )
```

```python
import functools
import math

import jax
import jax.numpy as jnp
from jax import lax
from jax.experimental import pallas as pl
from jax.experimental.pallas import tpu as pltpu
from jax.sharding import PartitionSpec as P

CODE_STEP = 2.0 ** (-6)
NORM_EPSILON = 1e-06
GELU_ROOT = 0.7978845608028654
GELU_CUBIC = 0.044715
ACROSS = (((1,), (1,)), ((), ()))
DOWNWARD = (((0,), (0,)), ((), ()))
LANES = 128
ROW_TILE = 16
DIRECT_LIMIT = 16
VMEM_BYTES = 24 * 1024 * 1024
VMEM_BRING = 53 * 1024 * 1024
F32 = jnp.float32
BF16 = jnp.bfloat16


def gelu_parts(values):
    argument = GELU_ROOT * (values + GELU_CUBIC * values * values * values)
    tanh_value = jnp.tanh(argument)
    result = 0.5 * values * (1.0 + tanh_value)
    derivative = 0.5 * (1.0 + tanh_value) + 0.5 * values * (
        1.0 - tanh_value * tanh_value
    ) * GELU_ROOT * (1.0 + 3.0 * GELU_CUBIC * values * values)
    return (result, derivative)


def up_to(value, unit):
    return -(-value // unit) * unit


def chips_fit(chips):
    return 8 <= chips <= DIRECT_LIMIT and chips & (chips - 1) == 0


class Plan:
    def __init__(self, chips, cores, rows, own):
        self.chips, self.cores, self.rows, self.own = chips, cores, rows, own
        self.width = own * chips * cores
        self.half = self.width // cores
        self.tiles = self.half // LANES
        self.chunk = up_to(-(-self.tiles * rows // chips), ROW_TILE)
        self.flat = self.chunk * chips
        self.tail = own - LANES
        if self.tail > 0:
            self.fold_rows = min(
                size
                for size in range(ROW_TILE, rows + ROW_TILE, ROW_TILE)
                if -(-rows // size) * self.tail <= LANES
            )
            self.packed = rows + self.fold_rows
        self.columns = list(range(0, chips, 2))
        self.doubling = [1 << k for k in range(1, (chips - 1).bit_length())]
        self.doubled = [0]
        for bit in reversed(self.doubling):
            self.doubled = self.doubled + [place ^ bit for place in self.doubled]

    def side_blocks(self, refs):
        me = lax.axis_index("latent")
        stack_ref, *crossed_refs = refs
        for place, column in enumerate(self.columns):
            yield me ^ column, stack_ref[place]
        places = iter(self.columns)
        for ref in crossed_refs:
            for place in range(ref.shape[0]):
                yield me ^ next(places) ^ 1, ref[place]

    def pieces(self):
        for tile in range(self.tiles):
            row = 0
            while row < self.rows:
                chip, place = divmod(tile * self.rows + row, self.chunk)
                count = min(self.rows - row, self.chunk - place)
                yield tile, chip, place, row, count
                row += count

    def fits(self):
        return (
            self.cores == 2
            and chips_fit(self.chips)
            and self.rows % ROW_TILE == 0
            and self.half % LANES == 0
            and 0 < self.tail < LANES
            and self.packed == self.chunk
        )


HBM = pl.BlockSpec(memory_space=pltpu.HBM)
ONCHIP = pl.BlockSpec(memory_space=pltpu.VMEM)


def shaped(*dims, dtype=F32):
    return jax.ShapeDtypeStruct(dims, dtype)


HBM = pl.BlockSpec(memory_space=pltpu.HBM)
ONCHIP = pl.BlockSpec(memory_space=pltpu.VMEM)


def shaped(*dims, dtype=F32):
    return jax.ShapeDtypeStruct(dims, dtype)


def call(body, out_shapes, operands, scratch=(), out_specs=None, flops=0, moved=0):
    return pl.pallas_call(
        body,
        out_shape=out_shapes,
        in_specs=[ONCHIP] * len(operands),
        out_specs=jax.tree.map(lambda _: ONCHIP, out_shapes) if out_specs is None else out_specs,
        scratch_shapes=list(scratch),
        compiler_params=pltpu.CompilerParams(vmem_limit_bytes=VMEM_BYTES),
        cost_estimate=pl.CostEstimate(flops=flops, bytes_accessed=moved, transcendentals=0),
    )(*operands)


def padded_bytes(array):
    *lead, rows, columns = array.shape
    item = jnp.dtype(array.dtype).itemsize
    return math.prod(lead) * up_to(rows, ROW_TILE) * up_to(columns, LANES) * item


def copies(sources, targets, sems):
    started = []
    for index, (source, target) in enumerate(zip(sources, targets)):
        one = pltpu.make_async_copy(source, target, sems.at[index])
        one.start()
        started.append(one)
    return started


def pack_block(plan, block):
    tail = block[:, LANES:]
    folded = []
    for start in range(0, plan.rows, plan.fold_rows):
        piece = tail[start : min(start + plan.fold_rows, plan.rows), :]
        short = plan.fold_rows - piece.shape[0]
        if short:
            piece = jnp.concatenate([piece, jnp.zeros((short, plan.tail), block.dtype)], axis=0)
        folded.append(piece)
    fill = LANES - len(folded) * plan.tail
    if fill:
        folded.append(jnp.zeros((plan.fold_rows, fill), block.dtype))
    return block[:, :LANES], jnp.concatenate(folded, axis=1)


def unpack_block(plan, packed):
    pieces = []
    for fold, start in enumerate(range(0, plan.rows, plan.fold_rows)):
        count = min(plan.fold_rows, plan.rows - start)
        pieces.append(
            packed[plan.rows : plan.rows + count, fold * plan.tail : (fold + 1) * plan.tail]
        )
    return jnp.concatenate([packed[: plan.rows, :], jnp.concatenate(pieces, axis=0)], axis=1)


def pack_values_body(plan, values_ref, *block_refs):
    for index, block_ref in enumerate(block_refs):
        main, tail = pack_block(plan, values_ref[index].astype(F32))
        block_ref[0, : plan.rows, :] = main.astype(BF16)
        block_ref[0, plan.rows :, :] = tail.astype(BF16)


def pack_values(plan, values):
    return call(
        functools.partial(pack_values_body, plan),
        [shaped(1, plan.packed, LANES, dtype=BF16)] * values.shape[0],
        (values,),
        moved=values.size * 6,
    )


def assemble(plan, own_refs, other_refs, both, full_ref):
    core = lax.axis_index("hidden")
    for side, refs in ((core, own_refs), (1 - core, other_refs)):
        for chip, block in plan.side_blocks(refs):
            both[side, chip] = block
    for chip in range(plan.chips):
        for side in range(plan.cores):
            column = (chip * plan.cores + side) * plan.own
            full_ref[:, column : column + plan.own] = unpack_block(plan, both[side, chip])


def both_scratch(plan, dtype=BF16):
    return pltpu.VMEM((plan.cores, plan.chips, plan.packed, LANES), dtype)


def chunk_scratch(plan):
    return pltpu.VMEM((plan.chips, plan.chunk, LANES), F32)


def side_shapes(plan, dtype=F32):
    return [shaped(len(plan.columns), plan.chunk, LANES, dtype=dtype)] * 2


def half_product(plan, pairs, side, kept_ref, sent_ref, target, gain_ref=None, bias_ref=None):
    span = pl.ds(pl.multiple_of(side * plan.half, LANES), plan.half)
    total = None
    for left, right_ref in pairs:
        term = jnp.dot(left, right_ref[:, span], preferred_element_type=F32)
        total = term if total is None else total + term
    if bias_ref is not None:
        total = total + bias_ref[:, span] * jnp.where(lax.axis_index("latent") == 0, 1.0, 0.0)
    if gain_ref is not None:
        total = total * gain_ref[:, span]
    for tile, chip, place, row, count in plan.pieces():
        target[chip, place : place + count, :] = total[
            row : row + count, tile * LANES : (tile + 1) * LANES
        ]
    used = plan.tiles * plan.rows
    while used < plan.flat:
        chip, place = divmod(used, plan.chunk)
        target[chip, place:, :] = jnp.zeros((plan.chunk - place, LANES), F32)
        used += plan.chunk - place
    me = lax.axis_index("latent")
    for place, column in enumerate(plan.columns):
        kept_ref[place] = target[me ^ column]
        sent_ref[place] = target[me ^ column ^ 1]


def bring_encoder_body(dict_hbm, vectors_hbm, dict_ref, bias_ref, decoder_ref, gain_ref, sems):
    sources, targets = [dict_hbm], [dict_ref]
    start = 0
    for target in (bias_ref, decoder_ref, gain_ref):
        sources.append(vectors_hbm.at[:, start : start + target.shape[1]])
        targets.append(target)
        start += target.shape[1]
    for copy in copies(sources, targets, sems):
        copy.wait()


def bring_encoder(plan, dictionary, vectors):
    outputs = [
        shaped(*dictionary.shape, dtype=BF16),
        shaped(1, dictionary.shape[0]),
        shaped(1, plan.width),
        shaped(1, plan.width),
    ]
    return pl.pallas_call(
        bring_encoder_body,
        out_shape=outputs,
        in_specs=[HBM] * 2,
        out_specs=[ONCHIP] * len(outputs),
        scratch_shapes=[pltpu.SemaphoreType.DMA((len(outputs),))],
        compiler_params=pltpu.CompilerParams(
            vmem_limit_bytes=VMEM_BRING - sum(map(padded_bytes, outputs))
        ),
        cost_estimate=pl.CostEstimate(
            flops=0, bytes_accessed=dictionary.size * 4, transcendentals=0
        ),
    )(dictionary, vectors)


def encode_body(plan, *refs):
    own, other, (dict_ref, bias_ref, gain_ref) = refs[:2], refs[2:4], refs[4:7]
    inputs_ref, latents_ref, kept_ref, sent_ref, both, target = refs[7:]
    assemble(plan, own, other, both, inputs_ref)
    preact = (
        lax.dot_general(inputs_ref[...], dict_ref[...], ACROSS, preferred_element_type=F32)
        + bias_ref[...]
    )
    latents = jnp.maximum(preact, 0.0).astype(BF16)
    latents_ref[...] = latents
    theirs = 1 - lax.axis_index("hidden")
    half_product(plan, [(latents, dict_ref)], theirs, kept_ref, sent_ref, target, gain_ref)


def encode(plan, own, other, dictionary, encoder_bias, gain):
    latents = dictionary.shape[0]
    return call(
        functools.partial(encode_body, plan),
        [
            shaped(plan.rows, plan.width, dtype=BF16),
            shaped(plan.rows, latents, dtype=BF16),
            *side_shapes(plan),
        ],
        (*own, *other, dictionary, encoder_bias, gain),
        [both_scratch(plan), chunk_scratch(plan)],
        flops=3 * plan.rows * plan.width * latents,
        moved=dictionary.size * 2,
    )


def decode_own_body(plan, latents_ref, dict_ref, decoder_ref, gain_ref, kept_ref, sent_ref, target):
    pairs = [(latents_ref[...], dict_ref)]
    mine = lax.axis_index("hidden")
    half_product(plan, pairs, mine, kept_ref, sent_ref, target, gain_ref, decoder_ref)


def decode_own(plan, latents, dictionary, decoder_bias, gain):
    return call(
        functools.partial(decode_own_body, plan),
        side_shapes(plan),
        (latents, dictionary, decoder_bias, gain),
        [chunk_scratch(plan)],
        flops=plan.rows * plan.width * dictionary.shape[0],
        moved=dictionary.size,
    )


def back_project_body(plan, *refs):
    own, other, (down_ref, grad_ref, both, full) = refs[:2], refs[2:4], refs[4:]
    assemble(plan, own, other, both, full)
    grad_ref[...] = lax.dot_general(
        full[...], down_ref[...], ACROSS, preferred_element_type=F32
    )


def back_project(plan, own, other, down_weight):
    units = down_weight.shape[0]
    return call(
        functools.partial(back_project_body, plan),
        shaped(plan.rows, units),
        (*own, *other, down_weight),
        [both_scratch(plan), pltpu.VMEM((plan.rows, plan.width), BF16)],
        flops=2 * plan.rows * plan.width * units,
        moved=down_weight.size * 2,
    )


def join_half(plan, source, first, full_ref):
    for tile, chip, place, row, count in plan.pieces():
        column = pl.multiple_of(first + tile * LANES, LANES)
        full_ref[row : row + count, pl.ds(column, LANES)] = source[
            chip, place : place + count, :
        ]


def half_terms(plan, half, side, gate_ref, up_ref, gain_ref):
    span = pl.ds(pl.multiple_of(side * plan.half, LANES), plan.half)
    rebuilt = half.astype(F32) / gain_ref[:, span]
    squares = jnp.sum(rebuilt * rebuilt, axis=1, keepdims=True)
    gate = lax.dot_general(half, gate_ref[:, span], ACROSS, preferred_element_type=F32)
    up = lax.dot_general(half, up_ref[:, span], ACROSS, preferred_element_type=F32)
    return squares, gate, up


def mlp_first_body(plan, own_ref, gate_ref, up_ref, gain_ref, half_ref, squares_ref, gate_part_ref, up_part_ref):
    join_half(plan, own_ref, 0, half_ref)
    squares_ref[...], gate_part_ref[...], up_part_ref[...] = half_terms(
        plan, half_ref[...], lax.axis_index("hidden"), gate_ref, up_ref, gain_ref
    )


def mlp_first(plan, own, gate_weight, up_weight, gain):
    units = gate_weight.shape[0]
    return call(
        functools.partial(mlp_first_body, plan),
        [
            shaped(plan.rows, plan.half, dtype=BF16),
            shaped(plan.rows, 1),
            shaped(plan.rows, units),
            shaped(plan.rows, units),
        ],
        (own, gate_weight, up_weight, gain),
        flops=2 * plan.rows * plan.width * units,
        moved=gate_weight.size * 4,
    )


def mlp_body(plan, other_ref, gate_ref, up_ref, gain_ref, grad_ref, half_ref, squares_ref, gate_part_ref, up_part_ref, scaled_ref, inverse_ref, hidden_ref, gate_grad_ref, up_grad_ref, kept_ref, sent_ref, target):
    core = lax.axis_index("hidden")
    join_half(plan, other_ref, (1 - core) * plan.half, scaled_ref)
    other_span = pl.ds(pl.multiple_of((1 - core) * plan.half, LANES), plan.half)
    own_span = pl.ds(pl.multiple_of(core * plan.half, LANES), plan.half)
    scaled_ref[:, own_span] = half_ref[...]
    squares, gate, up = half_terms(
        plan, scaled_ref[:, other_span], 1 - core, gate_ref, up_ref, gain_ref
    )
    inverse = lax.rsqrt((squares + squares_ref[...]) / plan.width + NORM_EPSILON)
    inverse_ref[...] = inverse
    gate_proj = inverse * (gate + gate_part_ref[...])
    up_proj = inverse * (up + up_part_ref[...])
    gelu_value, gelu_slope = gelu_parts(gate_proj)
    hidden_ref[...] = (gelu_value * up_proj).astype(BF16)
    hidden_grad = grad_ref[...]
    gate_grad = (hidden_grad * up_proj * gelu_slope).astype(BF16)
    up_grad = (hidden_grad * gelu_value).astype(BF16)
    gate_grad_ref[...] = gate_grad
    up_grad_ref[...] = up_grad
    pairs = [(gate_grad, gate_ref), (up_grad, up_ref)]
    half_product(plan, pairs, 1 - core, kept_ref, sent_ref, target)


def mlp(plan, other, gate_weight, up_weight, gain, hidden_grad, first):
    units = gate_weight.shape[0]
    return call(
        functools.partial(mlp_body, plan),
        [
            shaped(plan.rows, plan.width, dtype=BF16),
            shaped(plan.rows, 1),
            shaped(plan.rows, units, dtype=BF16),
            shaped(plan.rows, units, dtype=BF16),
            shaped(plan.rows, units, dtype=BF16),
            *side_shapes(plan),
        ],
        (other, gate_weight, up_weight, gain, hidden_grad, *first),
        [chunk_scratch(plan)],
        flops=6 * plan.rows * plan.width * units,
        moved=gate_weight.size * 4,
    )


def mlp_own_body(plan, gate_grad_ref, up_grad_ref, gate_ref, up_ref, kept_ref, sent_ref, target):
    pairs = [(gate_grad_ref[...], gate_ref), (up_grad_ref[...], up_ref)]
    half_product(plan, pairs, lax.axis_index("hidden"), kept_ref, sent_ref, target)


def mlp_own(plan, gate_grad, up_grad, gate_weight, up_weight):
    return call(
        functools.partial(mlp_own_body, plan),
        side_shapes(plan),
        (gate_grad, up_grad, gate_weight, up_weight),
        [chunk_scratch(plan)],
        flops=2 * plan.rows * plan.width * gate_weight.shape[0],
        moved=gate_weight.size * 2,
    )


def pack_side(plan, terms_ref, side, out_ref):
    for core in range(plan.cores):

        @pl.when(side == core)
        def _():
            for chip in range(plan.chips):
                start = (chip * plan.cores + core) * plan.own
                main, tail = pack_block(plan, terms_ref[:, start : start + plan.own])
                out_ref[chip, : plan.rows, :] = main
                out_ref[chip, plan.rows :, :] = tail


def project_body(plan, hidden_ref, down_ref, terms_ref, theirs_ref):
    terms_ref[...] = jnp.dot(
        hidden_ref[...], down_ref[...], preferred_element_type=F32
    ).astype(BF16)
    pack_side(plan, terms_ref, 1 - lax.axis_index("hidden"), theirs_ref)


def project(plan, hidden, down_weight):
    units = down_weight.shape[0]
    return call(
        functools.partial(project_body, plan),
        [
            shaped(plan.rows, plan.width, dtype=BF16),
            shaped(plan.chips, plan.packed, LANES, dtype=BF16),
        ],
        (hidden, down_weight),
        flops=2 * plan.rows * plan.width * units,
        moved=down_weight.size * 2,
    )


def pack_own_body(plan, terms_ref, mine_ref):
    pack_side(plan, terms_ref, lax.axis_index("hidden"), mine_ref)


def pack_own(plan, terms):
    return call(
        functools.partial(pack_own_body, plan),
        shaped(plan.chips, plan.packed, LANES, dtype=BF16),
        (terms,),
        moved=terms.size * 4,
    )


def add_pair_body(plan, first_ref, mine_ref, theirs_ref, kept_ref, sent_ref):
    me = lax.axis_index("latent")
    sent_ref[0] = first_ref[0]
    for place, column in enumerate(plan.columns):
        kept, sent = me ^ column, me ^ column ^ 1
        kept_ref[place] = mine_ref[kept].astype(F32) + theirs_ref[kept].astype(F32)
        sent_ref[1 + place] = (
            mine_ref[sent].astype(F32) + theirs_ref[sent].astype(F32)
        ).astype(BF16)


def add_pair(plan, first, mine, theirs):
    count, dims = len(plan.columns), mine.shape[1:]
    return call(
        functools.partial(add_pair_body, plan),
        [shaped(count, *dims), shaped(1 + count, *dims, dtype=BF16)],
        (first, mine, theirs),
        moved=mine.size * 10,
    )


def add_sent_body(mine_ref, theirs_ref, first_ref, rest_ref):
    total = (mine_ref[...] + theirs_ref[...]).astype(BF16)
    first_ref[...] = total[:1]
    rest_ref[...] = total[1:]


def add_sent(plan, mine, theirs):
    count, *dims = mine.shape
    return call(
        add_sent_body,
        [shaped(1, *dims, dtype=BF16), shaped(count - 1, *dims, dtype=BF16)],
        (mine, theirs),
        moved=mine.size * 10,
    )


def add_across_body(mine_ref, theirs_ref, got_ref, *sent_refs):
    for place, out_ref in enumerate(sent_refs):
        total = mine_ref[1 + place] + theirs_ref[1 + place] + got_ref[place].astype(F32)
        out_ref[0] = total.astype(BF16)


def add_across(plan, mine, theirs, got):
    return call(
        add_across_body,
        [shaped(1, *mine.shape[1:], dtype=BF16)] * got.shape[0],
        (mine, theirs, got),
        moved=mine.size * 10,
    )


def column_total(mine_ref, theirs_ref, *refs):
    total = mine_ref[0] + theirs_ref[0]
    for ref in refs:
        total = total + ref[0].astype(F32)
    return total.astype(BF16)


def add_column_body(*refs):
    *sources, block_ref, more_ref = refs
    block_ref[0] = column_total(*sources)
    more_ref[...] = sources[-1][1:]


def add_column(plan, mine, theirs, got, first):
    dims = mine.shape[1:]
    return call(
        add_column_body,
        [shaped(1, *dims, dtype=BF16), shaped(first.shape[0] - 1, *dims, dtype=BF16)],
        (mine, theirs, *reversed(got), first),
        moved=mine.size * 8,
    )


def add_with_output_body(plan, count, *refs):
    total = column_total(*refs[:count])
    first_ref, out_ref, block_ref, message_ref, kept_ref = refs[count - 1 : count + 4]
    block_ref[0] = total
    message_ref[0, : plan.chunk, :] = total
    near = plan.doubling[0]
    halves = [[], []]
    for place, column in enumerate(plan.columns):
        halves[column & near != 0].append(out_ref[place] + first_ref[1 + place].astype(F32))
    for index, (kept, sent) in enumerate(zip(*halves)):
        kept_ref[index] = kept
        start = plan.chunk + index * plan.packed
        message_ref[0, start : start + plan.packed, :] = sent.astype(BF16)


def add_with_output(plan, mine, theirs, got, first, kept):
    half = len(plan.columns) // 2
    return call(
        functools.partial(add_with_output_body, plan, 3 + len(got)),
        [
            shaped(1, plan.chunk, LANES, dtype=BF16),
            shaped(1, plan.chunk + half * plan.packed, LANES, dtype=BF16),
            shaped(half, plan.packed, LANES),
        ],
        (mine, theirs, *reversed(got), first, kept),
        moved=mine.size * 12,
    )


def halve_body(rows, skip, kept_ref, got_ref, left_ref, sent_ref):
    half = left_ref.shape[0]
    for index in range(2 * half):
        start = skip + index * rows
        total = kept_ref[index] + got_ref[0, start : start + rows, :].astype(F32)
        if index < half:
            left_ref[index] = total
        else:
            begin = (index - half) * rows
            sent_ref[0, begin : begin + rows, :] = total.astype(BF16)


def halve(plan, kept, got, skip):
    half, rows = kept.shape[0] // 2, plan.packed
    return call(
        functools.partial(halve_body, rows, skip),
        [shaped(half, rows, LANES), shaped(1, half * rows, LANES, dtype=BF16)],
        (kept, got),
        moved=kept.size * 10,
    )


def stack_body(places, *refs):
    count = len(places)
    stack_ref, *rest_refs = refs[count:]
    rows = stack_ref.shape[1]
    for place, ref in zip(places, refs):
        stack_ref[place] = ref[0, :rows, :]
        for rest_ref in rest_refs:
            if place:
                rest_ref[place - 1] = ref[0, :rows, :]


def stack_up(plan, block, got, with_rest=False):
    dims = block.shape[1:]
    operands = [block, *got]
    places = list(range(len(operands)))
    if with_rest:
        operands, places = operands[::-1], places[::-1]
    outs = [shaped(1 + len(got), *dims, dtype=BF16), shaped(len(got), *dims, dtype=BF16)]
    return call(
        functools.partial(stack_body, places),
        outs if with_rest else outs[0],
        operands,
        moved=block.size * 16,
    )


def join_body(*refs):
    *sources, joined_ref = refs
    start = 0
    for ref in sources:
        joined_ref[start : start + ref.shape[0]] = ref[...]
        start += ref.shape[0]


def join(plan, *stacks):
    count = sum(one.shape[0] for one in stacks)
    return call(
        join_body,
        shaped(count, *stacks[0].shape[1:], dtype=BF16),
        stacks,
        moved=count * stacks[0].size,
    )


def double(plan, stack, bit):
    return join(plan, stack, partner_swap(stack, bit))


def add_message_body(plan, first_ref, here_ref, there_ref, stack_ref, message_ref):
    message_ref[0] = first_ref[0]
    half = here_ref.shape[0]
    for index, column in enumerate(plan.doubled):
        block = here_ref[index] if index < half else there_ref[index - half]
        place = plan.columns.index(column)
        stack_ref[place] = block
        message_ref[1 + place] = block


def add_message(plan, first, here, there):
    count, dims = len(plan.columns), first.shape[1:]
    return call(
        functools.partial(add_message_body, plan),
        [shaped(count, *dims, dtype=BF16), shaped(1 + count, *dims, dtype=BF16)],
        (first, here, there),
        moved=first.size * 40,
    )


def line_up_body(plan, *refs):
    for chip, block in plan.side_blocks(refs[:-1]):
        refs[-1][chip] = block


def line_up(plan, stack, *crossed):
    return call(
        functools.partial(line_up_body, plan),
        shaped(plan.chips, *stack.shape[1:], dtype=BF16),
        (stack, *crossed),
        moved=stack.size * 8,
    )


def finish_output_body(plan, kept_ref, got_ref, out_ref):
    total = kept_ref[0] + got_ref[0].astype(F32)
    out_ref[...] = unpack_block(plan, total).astype(BF16)


def finish_output(plan, kept, got):
    return call(
        functools.partial(finish_output_body, plan),
        shaped(plan.rows, plan.own, dtype=BF16),
        (kept, got),
        moved=kept.size * 8,
    )


def prepare_body(plan, scaled_ref, inputs_ref, gain_ref, inverse_ref, factor_ref, slope_ref, base_ref):
    gain = gain_ref[...]
    inverse = inverse_ref[...]
    rebuilt = scaled_ref[...].astype(F32) / gain
    factor_ref[...] = inverse * gain
    slope_ref[...] = rebuilt * (inverse * inverse * inverse / plan.width)
    base_ref[...] = rebuilt - inputs_ref[...].astype(F32)


def prepare(plan, scaled, inputs, gain, inverse):
    return call(
        functools.partial(prepare_body, plan),
        [shaped(plan.rows, plan.width)] * 3,
        (scaled, inputs, gain, inverse),
        moved=scaled.size * 16,
    )


def dictionary_body(plan, pieces, own_ref, other_ref, scaled_ref, factor_ref, slope_ref, base_ref, inputs_ref, latents_ref, dict_ref, out_hbm, full, out_ref, out_sems):
    core = lax.axis_index("hidden")
    join_half(plan, own_ref, core * plan.half, full)
    join_half(plan, other_ref, (1 - core) * plan.half, full)
    grad = full[...].astype(F32)
    inner_row = jnp.sum(grad * scaled_ref[...].astype(F32), axis=1, keepdims=True)
    inputs = inputs_ref[...]
    rebuilt_grad = (
        grad * factor_ref[...] - inner_row * slope_ref[...] + base_ref[...]
    ).astype(BF16)
    latents = latents_ref[...]
    latent_grad = lax.dot_general(
        rebuilt_grad, dict_ref[...], ACROSS, preferred_element_type=F32
    )
    preact_grad = jnp.where(latents.astype(F32) > 0.0, latent_grad, 0.0).astype(BF16)
    left = jnp.concatenate([latents, preact_grad], axis=0)
    right = jnp.concatenate([rebuilt_grad, inputs], axis=0)
    size = plan.width // pieces
    writes = []
    for piece in range(pieces):
        span = slice(piece * size, (piece + 1) * size)
        out_ref[:, span] = lax.dot_general(
            left, right[:, span], DOWNWARD, preferred_element_type=F32
        ).astype(BF16)
        one = pltpu.make_async_copy(
            out_ref.at[:, span], out_hbm.at[:, span], out_sems.at[piece]
        )
        one.start()
        writes.append(one)
    for one in writes:
        one.wait()


def dictionary_step(plan, own, other, scaled, prepared, inputs, latents, dictionary):
    units = dictionary.shape[0]
    pieces = plan.tiles
    return call(
        functools.partial(dictionary_body, plan, pieces),
        shaped(*dictionary.shape, dtype=BF16),
        (own, other, scaled, *prepared, inputs, latents, dictionary),
        [
            pltpu.VMEM((plan.rows, plan.width), BF16),
            pltpu.VMEM(dictionary.shape, BF16),
            pltpu.SemaphoreType.DMA((pieces,)),
        ],
        out_specs=HBM,
        flops=6 * plan.rows * plan.width * units,
        moved=dictionary.size * 4,
    )


def swap(value):
    size = lax.axis_size("hidden")
    return lax.ppermute(value, "hidden", [(i, (i + 1) % size) for i in range(size)])


def partner_swap(value, bits):
    size = lax.axis_size("latent")
    return lax.ppermute(value, "latent", [(i, i ^ bits) for i in range(size)])


def cross(value):
    return partner_swap(value, 1)


def to_column(plan, blocks):
    pairs = list(zip(blocks, plan.columns[1:]))
    got = [partner_swap(one, column) for one, column in reversed(pairs)]
    return got[::-1]


def to_all_columns(plan, block):
    return [partner_swap(block, column) for column in plan.columns[1:]]


def tie(*values):
    return lax.optimization_barrier(values)


def per_device(
    input_codes,
    cotangent_codes,
    dictionary,
    encoder_bias,
    decoder_bias,
    norm_gain,
    gate_weight,
    up_weight,
    down_weight,
):
    plan = Plan(
        lax.axis_size("latent"), lax.axis_size("hidden"), input_codes.shape[0], input_codes.shape[1]
    )
    if not plan.fits():
        return per_device_plain(
            input_codes,
            cotangent_codes,
            dictionary,
            encoder_bias,
            decoder_bias,
            norm_gain,
            gate_weight,
            up_weight,
            down_weight,
        )
    vectors = jnp.concatenate([encoder_bias, decoder_bias, norm_gain]).reshape(1, -1)
    codes = jnp.stack([input_codes, cotangent_codes])
    values = (codes.astype(F32) * CODE_STEP).astype(BF16)
    block, cotangent = pack_values(plan, values)
    stack = stack_up(plan, block, to_all_columns(plan, block))
    stack, vectors, late_dictionary, cotangent = tie(stack, vectors, dictionary, cotangent)
    stack_other, crossed = swap(stack), cross(stack)
    encoder = bring_encoder(plan, late_dictionary, vectors)
    cotangent = double(plan, cotangent, plan.doubling[-1])
    stack_other, crossed, encoder, cotangent = tie(stack_other, crossed, encoder, cotangent)
    brought, bias, decoder, gain = encoder
    inputs, latents, kept, sent = encode(
        plan, (stack, crossed), (stack_other, swap(crossed)), brought, bias, gain
    )
    sent, kept = swap(sent), swap(kept)
    own_kept, own_sent = decode_own(plan, latents, brought, decoder, gain)
    sent_first, sent_rest = add_sent(plan, own_sent, sent)
    sent_rest, cotangent = tie(sent_rest, cotangent)
    for bit in reversed(plan.doubling[1:-1]):
        cotangent = double(plan, cotangent, bit)
    there = partner_swap(cotangent, plan.doubling[0])
    sent = add_across(plan, own_kept, kept, cross(sent_rest))
    sent, sent_first, cotangent, there = tie(sent, sent_first, cotangent, there)
    cotangent, sent_first = add_message(plan, sent_first, cotangent, there)
    got, first = to_column(plan, sent), cross(sent_first)
    block, crossed = add_column(plan, own_kept, kept, got, first)
    cotangent_own = (cotangent, crossed)
    hidden_grad = back_project(
        plan, cotangent_own, [swap(one) for one in cotangent_own], down_weight
    )
    stack = stack_up(plan, block, to_all_columns(plan, block))
    stack_other, crossed = swap(stack), cross(stack)
    stack_other, crossed, hidden_grad = tie(stack_other, crossed, hidden_grad)
    terms = mlp_first(plan, line_up(plan, stack, crossed), gate_weight, up_weight, gain)
    scaled_other = line_up(plan, stack_other, swap(crossed))
    scaled, inverse, hidden, gate_grad, up_grad, kept, sent = mlp(
        plan, scaled_other, gate_weight, up_weight, gain, hidden_grad, terms
    )
    sent, kept = swap(sent), swap(kept)
    own_kept, own_sent = mlp_own(plan, gate_grad, up_grad, gate_weight, up_weight)
    out_terms, out_theirs = project(plan, hidden, down_weight)
    sent_first, sent_rest = add_sent(plan, own_sent, sent)
    sent_first, sent_rest, out_terms, out_theirs = tie(
        sent_first, sent_rest, out_terms, out_theirs
    )
    crossed = cross(sent_rest)
    out_theirs = swap(out_theirs)
    out_kept, sent_first = add_pair(plan, sent_first, pack_own(plan, out_terms), out_theirs)
    sent = add_across(plan, own_kept, kept, crossed)
    sent, sent_first, out_kept = tie(sent, sent_first, out_kept)
    got = to_column(plan, sent)
    first = cross(sent_first)
    block, message, out_kept = add_with_output(plan, own_kept, kept, got, first, out_kept)
    got = to_column(plan, [message] + [block] * (len(plan.columns) - 2))
    got = list(tie(got[-1], *got[:-1]))
    got = got[1:] + got[:1]
    stack = stack_up(plan, block, got)
    out_kept, out_sent = halve(plan, out_kept, got[0], plan.chunk)
    stack, scaled_late, inputs_late, out_sent = tie(stack, scaled, inputs, out_sent)
    stack_other, crossed = swap(stack), cross(stack)
    prepared = prepare(plan, scaled_late, inputs_late, gain, inverse)
    for bit in reversed(plan.doubling[2:]):
        out_kept, out_sent = halve(plan, out_kept, partner_swap(out_sent, bit), 0)
    out_got = partner_swap(out_sent, plan.doubling[1])
    stack_other, crossed, out_got = tie(stack_other, crossed, out_got)
    block_output = finish_output(plan, out_kept, out_got)
    grad_own = line_up(plan, stack, crossed)
    grad_other = line_up(plan, stack_other, swap(crossed))
    dictionary_grad = dictionary_step(
        plan, grad_own, grad_other, scaled, prepared, inputs, latents, brought
    )
    return (block_output, dictionary_grad)


def per_device_plain(
    input_codes,
    cotangent_codes,
    dictionary,
    encoder_bias,
    decoder_bias,
    norm_gain,
    gate_weight,
    up_weight,
    down_weight,
):
    own_width = input_codes.shape[1]
    model_width = own_width * lax.axis_size(("latent", "hidden"))
    cotangent_local = (cotangent_codes.astype(jnp.float32) * CODE_STEP).astype(jnp.bfloat16)
    inputs_local = (input_codes.astype(jnp.float32) * CODE_STEP).astype(jnp.bfloat16)
    inputs = lax.all_gather(inputs_local, ("latent", "hidden"), axis=1, tiled=True)
    preact = (
        lax.dot_general(inputs, dictionary, ACROSS, preferred_element_type=jnp.float32)
        + encoder_bias
    )
    latents = jnp.maximum(preact, 0.0).astype(jnp.bfloat16)
    partial_value = jnp.dot(latents, dictionary, preferred_element_type=jnp.float32)
    rebuilt = lax.psum(partial_value, ("latent", "hidden")) + decoder_bias
    inverse = lax.rsqrt(
        jnp.sum(rebuilt * rebuilt, axis=1, keepdims=True) / model_width + NORM_EPSILON
    )
    normed = (rebuilt * inverse * norm_gain).astype(jnp.bfloat16)
    target = inputs.astype(jnp.float32)
    gate_proj = lax.dot_general(normed, gate_weight, ACROSS, preferred_element_type=jnp.float32)
    up_proj = lax.dot_general(normed, up_weight, ACROSS, preferred_element_type=jnp.float32)
    gelu_value, gelu_slope = gelu_parts(gate_proj)
    hidden = (gelu_value * up_proj).astype(jnp.bfloat16)
    output_terms = jnp.dot(hidden, down_weight, preferred_element_type=jnp.float32)
    block_output = lax.psum_scatter(
        output_terms, ("latent", "hidden"), scatter_dimension=1, tiled=True
    ).astype(jnp.bfloat16)
    hidden_grad = lax.dot_general(
        lax.all_gather(cotangent_local, ("latent", "hidden"), axis=1, tiled=True),
        down_weight,
        ACROSS,
        preferred_element_type=jnp.float32,
    )
    gate_grad = (hidden_grad * up_proj * gelu_slope).astype(jnp.bfloat16)
    up_grad = (hidden_grad * gelu_value).astype(jnp.bfloat16)
    partial_grad = jnp.dot(gate_grad, gate_weight, preferred_element_type=jnp.float32) + jnp.dot(
        up_grad, up_weight, preferred_element_type=jnp.float32
    )
    scaled = lax.psum(partial_grad, ("latent", "hidden")) * norm_gain
    inner_row = jnp.sum(scaled * rebuilt, axis=1, keepdims=True)
    inverse_cube = inverse * inverse * inverse
    rebuilt_grad = (
        inverse * scaled - inverse_cube * rebuilt * (inner_row / model_width) + (rebuilt - target)
    ).astype(jnp.bfloat16)
    latent_grad = lax.dot_general(
        rebuilt_grad, dictionary, ACROSS, preferred_element_type=jnp.float32
    )
    preact_grad = jnp.where(preact > 0.0, latent_grad, 0.0).astype(jnp.bfloat16)
    dictionary_grad = lax.dot_general(
        latents, rebuilt_grad, DOWNWARD, preferred_element_type=jnp.float32
    ) + lax.dot_general(preact_grad, inputs, DOWNWARD, preferred_element_type=jnp.float32)
    return (block_output, dictionary_grad.astype(jnp.bfloat16))


def solution(mesh):
    in_specs = (
        P("groups", ("latent", "hidden")),
        P("groups", ("latent", "hidden")),
        P(("latent", "hidden"), None),
        P(("latent", "hidden")),
        P(),
        P(),
        P(("latent", "hidden"), None),
        P(("latent", "hidden"), None),
        P(("latent", "hidden"), None),
    )
    out_specs = (P("groups", ("latent", "hidden")), P(("latent", "hidden"), "groups"))
    return jax.shard_map(
        per_device, mesh=mesh, in_specs=in_specs, out_specs=out_specs, check_vma=False
    )
```

```python
import functools
import math

import jax
import jax.numpy as jnp
from jax import lax
from jax.experimental import pallas as pl
from jax.experimental.pallas import tpu as pltpu
from jax.sharding import PartitionSpec as P

CODE_STEP = 2.0 ** (-6)
NORM_EPSILON = 1e-06
GELU_ROOT = 0.7978845608028654
GELU_CUBIC = 0.044715
ACROSS = (((1,), (1,)), ((), ()))
DOWNWARD = (((0,), (0,)), ((), ()))
LANES = 128
ROW_TILE = 16
DIRECT_LIMIT = 16
VMEM_BYTES = 24 * 1024 * 1024
VMEM_BRING = 53 * 1024 * 1024
F32 = jnp.float32
BF16 = jnp.bfloat16


def gelu_parts(values):
    argument = GELU_ROOT * (values + GELU_CUBIC * values * values * values)
    tanh_value = jnp.tanh(argument)
    result = 0.5 * values * (1.0 + tanh_value)
    derivative = 0.5 * (1.0 + tanh_value) + 0.5 * values * (
        1.0 - tanh_value * tanh_value
    ) * GELU_ROOT * (1.0 + 3.0 * GELU_CUBIC * values * values)
    return (result, derivative)


def up_to(value, unit):
    return -(-value // unit) * unit


def chips_fit(chips):
    return 8 <= chips <= DIRECT_LIMIT and chips & (chips - 1) == 0


class Plan:
    def __init__(self, chips, cores, rows, own):
        self.chips, self.cores, self.rows, self.own = chips, cores, rows, own
        self.width = own * chips * cores
        self.half = self.width // cores
        self.tiles = self.half // LANES
        self.chunk = up_to(-(-self.tiles * rows // chips), ROW_TILE)
        self.flat = self.chunk * chips
        self.tail = own - LANES
        if self.tail > 0:
            self.fold_rows = min(
                size
                for size in range(ROW_TILE, rows + ROW_TILE, ROW_TILE)
                if -(-rows // size) * self.tail <= LANES
            )
            self.packed = rows + self.fold_rows
        self.columns = list(range(0, chips, 2))
        self.doubling = [1 << k for k in range(1, (chips - 1).bit_length())]
        self.doubled = [0]
        for bit in reversed(self.doubling):
            self.doubled = self.doubled + [place ^ bit for place in self.doubled]

    def side_blocks(self, refs):
        me = lax.axis_index("latent")
        stack_ref, *crossed_refs = refs
        for place, column in enumerate(self.columns):
            yield me ^ column, stack_ref[place]
        places = iter(self.columns)
        for ref in crossed_refs:
            for place in range(ref.shape[0]):
                yield me ^ next(places) ^ 1, ref[place]

    def pieces(self):
        for tile in range(self.tiles):
            row = 0
            while row < self.rows:
                chip, place = divmod(tile * self.rows + row, self.chunk)
                count = min(self.rows - row, self.chunk - place)
                yield tile, chip, place, row, count
                row += count

    def fits(self):
        return (
            self.cores == 2
            and chips_fit(self.chips)
            and self.rows % ROW_TILE == 0
            and self.half % LANES == 0
            and 0 < self.tail < LANES
            and self.packed == self.chunk
        )


HBM = pl.BlockSpec(memory_space=pltpu.HBM)
ONCHIP = pl.BlockSpec(memory_space=pltpu.VMEM)


def shaped(*dims, dtype=F32):
    return jax.ShapeDtypeStruct(dims, dtype)


HBM = pl.BlockSpec(memory_space=pltpu.HBM)
ONCHIP = pl.BlockSpec(memory_space=pltpu.VMEM)


def shaped(*dims, dtype=F32):
    return jax.ShapeDtypeStruct(dims, dtype)


def call(body, out_shapes, operands, scratch=(), out_specs=None, flops=0, moved=0):
    return pl.pallas_call(
        body,
        out_shape=out_shapes,
        in_specs=[ONCHIP] * len(operands),
        out_specs=jax.tree.map(lambda _: ONCHIP, out_shapes) if out_specs is None else out_specs,
        scratch_shapes=list(scratch),
        compiler_params=pltpu.CompilerParams(vmem_limit_bytes=VMEM_BYTES),
        cost_estimate=pl.CostEstimate(flops=flops, bytes_accessed=moved, transcendentals=0),
    )(*operands)


def padded_bytes(array):
    *lead, rows, columns = array.shape
    item = jnp.dtype(array.dtype).itemsize
    return math.prod(lead) * up_to(rows, ROW_TILE) * up_to(columns, LANES) * item


def copies(sources, targets, sems):
    started = []
    for index, (source, target) in enumerate(zip(sources, targets)):
        one = pltpu.make_async_copy(source, target, sems.at[index])
        one.start()
        started.append(one)
    return started


def pack_block(plan, block):
    tail = block[:, LANES:]
    folded = []
    for start in range(0, plan.rows, plan.fold_rows):
        piece = tail[start : min(start + plan.fold_rows, plan.rows), :]
        short = plan.fold_rows - piece.shape[0]
        if short:
            piece = jnp.concatenate([piece, jnp.zeros((short, plan.tail), block.dtype)], axis=0)
        folded.append(piece)
    fill = LANES - len(folded) * plan.tail
    if fill:
        folded.append(jnp.zeros((plan.fold_rows, fill), block.dtype))
    return block[:, :LANES], jnp.concatenate(folded, axis=1)


def unpack_block(plan, packed):
    pieces = []
    for fold, start in enumerate(range(0, plan.rows, plan.fold_rows)):
        count = min(plan.fold_rows, plan.rows - start)
        pieces.append(
            packed[plan.rows : plan.rows + count, fold * plan.tail : (fold + 1) * plan.tail]
        )
    return jnp.concatenate([packed[: plan.rows, :], jnp.concatenate(pieces, axis=0)], axis=1)


def pack_values_body(plan, values_ref, *block_refs):
    for index, block_ref in enumerate(block_refs):
        main, tail = pack_block(plan, values_ref[index].astype(F32))
        block_ref[0, : plan.rows, :] = main.astype(BF16)
        block_ref[0, plan.rows :, :] = tail.astype(BF16)


def pack_values(plan, values):
    return call(
        functools.partial(pack_values_body, plan),
        [shaped(1, plan.packed, LANES, dtype=BF16)] * values.shape[0],
        (values,),
        moved=values.size * 6,
    )


def assemble(plan, own_refs, other_refs, both, full_ref):
    core = lax.axis_index("hidden")
    for side, refs in ((core, own_refs), (1 - core, other_refs)):
        for chip, block in plan.side_blocks(refs):
            both[side, chip] = block
    for chip in range(plan.chips):
        for side in range(plan.cores):
            column = (chip * plan.cores + side) * plan.own
            full_ref[:, column : column + plan.own] = unpack_block(plan, both[side, chip])


def both_scratch(plan, dtype=BF16):
    return pltpu.VMEM((plan.cores, plan.chips, plan.packed, LANES), dtype)


def chunk_scratch(plan):
    return pltpu.VMEM((plan.chips, plan.chunk, LANES), F32)


def side_shapes(plan, sent_as=F32):
    dims = (len(plan.columns), plan.chunk, LANES)
    return [shaped(*dims), shaped(*dims, dtype=sent_as)]


def half_product(plan, pairs, side, kept_ref, sent_ref, target, gain_ref=None, bias_ref=None):
    span = pl.ds(pl.multiple_of(side * plan.half, LANES), plan.half)
    total = None
    for left, right_ref in pairs:
        term = jnp.dot(left, right_ref[:, span], preferred_element_type=F32)
        total = term if total is None else total + term
    if bias_ref is not None:
        total = total + bias_ref[:, span] * jnp.where(lax.axis_index("latent") == 0, 1.0, 0.0)
    if gain_ref is not None:
        total = total * gain_ref[:, span]
    for tile, chip, place, row, count in plan.pieces():
        target[chip, place : place + count, :] = total[
            row : row + count, tile * LANES : (tile + 1) * LANES
        ]
    used = plan.tiles * plan.rows
    while used < plan.flat:
        chip, place = divmod(used, plan.chunk)
        target[chip, place:, :] = jnp.zeros((plan.chunk - place, LANES), F32)
        used += plan.chunk - place
    me = lax.axis_index("latent")
    for place, column in enumerate(plan.columns):
        kept_ref[place] = target[me ^ column]
        sent_ref[place] = target[me ^ column ^ 1].astype(sent_ref.dtype)


def bring_encoder_body(dict_hbm, vectors_hbm, dict_ref, bias_ref, decoder_ref, gain_ref, sems):
    sources, targets = [dict_hbm], [dict_ref]
    start = 0
    for target in (bias_ref, decoder_ref, gain_ref):
        sources.append(vectors_hbm.at[:, start : start + target.shape[1]])
        targets.append(target)
        start += target.shape[1]
    for copy in copies(sources, targets, sems):
        copy.wait()


def bring_encoder(plan, dictionary, vectors):
    outputs = [
        shaped(*dictionary.shape, dtype=BF16),
        shaped(1, dictionary.shape[0]),
        shaped(1, plan.width),
        shaped(1, plan.width),
    ]
    return pl.pallas_call(
        bring_encoder_body,
        out_shape=outputs,
        in_specs=[HBM] * 2,
        out_specs=[ONCHIP] * len(outputs),
        scratch_shapes=[pltpu.SemaphoreType.DMA((len(outputs),))],
        compiler_params=pltpu.CompilerParams(
            vmem_limit_bytes=VMEM_BRING - sum(map(padded_bytes, outputs))
        ),
        cost_estimate=pl.CostEstimate(
            flops=0, bytes_accessed=dictionary.size * 4, transcendentals=0
        ),
    )(dictionary, vectors)


def encode_body(plan, *refs):
    own, other, (dict_ref, bias_ref, gain_ref) = refs[:2], refs[2:4], refs[4:7]
    inputs_ref, latents_ref, kept_ref, sent_ref, both, target = refs[7:]
    assemble(plan, own, other, both, inputs_ref)
    preact = (
        lax.dot_general(inputs_ref[...], dict_ref[...], ACROSS, preferred_element_type=F32)
        + bias_ref[...]
    )
    latents = jnp.maximum(preact, 0.0).astype(BF16)
    latents_ref[...] = latents
    theirs = 1 - lax.axis_index("hidden")
    half_product(plan, [(latents, dict_ref)], theirs, kept_ref, sent_ref, target, gain_ref)


def encode(plan, own, other, dictionary, encoder_bias, gain):
    latents = dictionary.shape[0]
    return call(
        functools.partial(encode_body, plan),
        [
            shaped(plan.rows, plan.width, dtype=BF16),
            shaped(plan.rows, latents, dtype=BF16),
            *side_shapes(plan, BF16),
        ],
        (*own, *other, dictionary, encoder_bias, gain),
        [both_scratch(plan), chunk_scratch(plan)],
        flops=3 * plan.rows * plan.width * latents,
        moved=dictionary.size * 2,
    )


def decode_own_body(plan, latents_ref, dict_ref, decoder_ref, gain_ref, kept_ref, sent_ref, target):
    pairs = [(latents_ref[...], dict_ref)]
    mine = lax.axis_index("hidden")
    half_product(plan, pairs, mine, kept_ref, sent_ref, target, gain_ref, decoder_ref)


def decode_own(plan, latents, dictionary, decoder_bias, gain):
    return call(
        functools.partial(decode_own_body, plan),
        side_shapes(plan),
        (latents, dictionary, decoder_bias, gain),
        [chunk_scratch(plan)],
        flops=plan.rows * plan.width * dictionary.shape[0],
        moved=dictionary.size,
    )


def back_project_body(plan, *refs):
    own, other, (down_ref, grad_ref, both, full) = refs[:2], refs[2:4], refs[4:]
    assemble(plan, own, other, both, full)
    grad_ref[...] = lax.dot_general(
        full[...], down_ref[...], ACROSS, preferred_element_type=F32
    )


def back_project(plan, own, other, down_weight):
    units = down_weight.shape[0]
    return call(
        functools.partial(back_project_body, plan),
        shaped(plan.rows, units),
        (*own, *other, down_weight),
        [both_scratch(plan), pltpu.VMEM((plan.rows, plan.width), BF16)],
        flops=2 * plan.rows * plan.width * units,
        moved=down_weight.size * 2,
    )


def join_half(plan, source, first, full_ref):
    for tile, chip, place, row, count in plan.pieces():
        column = pl.multiple_of(first + tile * LANES, LANES)
        full_ref[row : row + count, pl.ds(column, LANES)] = source[
            chip, place : place + count, :
        ]


def half_terms(plan, half, side, gate_ref, up_ref, gain_ref):
    span = pl.ds(pl.multiple_of(side * plan.half, LANES), plan.half)
    rebuilt = half.astype(F32) / gain_ref[:, span]
    squares = jnp.sum(rebuilt * rebuilt, axis=1, keepdims=True)
    gate = lax.dot_general(half, gate_ref[:, span], ACROSS, preferred_element_type=F32)
    up = lax.dot_general(half, up_ref[:, span], ACROSS, preferred_element_type=F32)
    return squares, gate, up


def mlp_first_body(plan, own_ref, gate_ref, up_ref, gain_ref, half_ref, squares_ref, gate_part_ref, up_part_ref):
    join_half(plan, own_ref, 0, half_ref)
    squares_ref[...], gate_part_ref[...], up_part_ref[...] = half_terms(
        plan, half_ref[...], lax.axis_index("hidden"), gate_ref, up_ref, gain_ref
    )


def mlp_first(plan, own, gate_weight, up_weight, gain):
    units = gate_weight.shape[0]
    return call(
        functools.partial(mlp_first_body, plan),
        [
            shaped(plan.rows, plan.half, dtype=BF16),
            shaped(plan.rows, 1),
            shaped(plan.rows, units),
            shaped(plan.rows, units),
        ],
        (own, gate_weight, up_weight, gain),
        flops=2 * plan.rows * plan.width * units,
        moved=gate_weight.size * 4,
    )


def mlp_body(plan, other_ref, gate_ref, up_ref, gain_ref, grad_ref, half_ref, squares_ref, gate_part_ref, up_part_ref, scaled_ref, inverse_ref, hidden_ref, gate_grad_ref, up_grad_ref, kept_ref, sent_ref, target):
    core = lax.axis_index("hidden")
    join_half(plan, other_ref, (1 - core) * plan.half, scaled_ref)
    other_span = pl.ds(pl.multiple_of((1 - core) * plan.half, LANES), plan.half)
    own_span = pl.ds(pl.multiple_of(core * plan.half, LANES), plan.half)
    scaled_ref[:, own_span] = half_ref[...]
    squares, gate, up = half_terms(
        plan, scaled_ref[:, other_span], 1 - core, gate_ref, up_ref, gain_ref
    )
    inverse = lax.rsqrt((squares + squares_ref[...]) / plan.width + NORM_EPSILON)
    inverse_ref[...] = inverse
    gate_proj = inverse * (gate + gate_part_ref[...])
    up_proj = inverse * (up + up_part_ref[...])
    gelu_value, gelu_slope = gelu_parts(gate_proj)
    hidden_ref[...] = (gelu_value * up_proj).astype(BF16)
    hidden_grad = grad_ref[...]
    gate_grad = (hidden_grad * up_proj * gelu_slope).astype(BF16)
    up_grad = (hidden_grad * gelu_value).astype(BF16)
    gate_grad_ref[...] = gate_grad
    up_grad_ref[...] = up_grad
    pairs = [(gate_grad, gate_ref), (up_grad, up_ref)]
    half_product(plan, pairs, 1 - core, kept_ref, sent_ref, target)


def mlp(plan, other, gate_weight, up_weight, gain, hidden_grad, first):
    units = gate_weight.shape[0]
    return call(
        functools.partial(mlp_body, plan),
        [
            shaped(plan.rows, plan.width, dtype=BF16),
            shaped(plan.rows, 1),
            shaped(plan.rows, units, dtype=BF16),
            shaped(plan.rows, units, dtype=BF16),
            shaped(plan.rows, units, dtype=BF16),
            *side_shapes(plan),
        ],
        (other, gate_weight, up_weight, gain, hidden_grad, *first),
        [chunk_scratch(plan)],
        flops=6 * plan.rows * plan.width * units,
        moved=gate_weight.size * 4,
    )


def mlp_own_body(plan, gate_grad_ref, up_grad_ref, gate_ref, up_ref, kept_ref, sent_ref, target):
    pairs = [(gate_grad_ref[...], gate_ref), (up_grad_ref[...], up_ref)]
    half_product(plan, pairs, lax.axis_index("hidden"), kept_ref, sent_ref, target)


def mlp_own(plan, gate_grad, up_grad, gate_weight, up_weight):
    return call(
        functools.partial(mlp_own_body, plan),
        side_shapes(plan),
        (gate_grad, up_grad, gate_weight, up_weight),
        [chunk_scratch(plan)],
        flops=2 * plan.rows * plan.width * gate_weight.shape[0],
        moved=gate_weight.size * 2,
    )


def pack_side(plan, terms_ref, side, out_ref):
    for core in range(plan.cores):

        @pl.when(side == core)
        def _():
            for chip in range(plan.chips):
                start = (chip * plan.cores + core) * plan.own
                main, tail = pack_block(plan, terms_ref[:, start : start + plan.own])
                out_ref[chip, : plan.rows, :] = main
                out_ref[chip, plan.rows :, :] = tail


def project_body(plan, hidden_ref, down_ref, terms_ref, theirs_ref):
    terms_ref[...] = jnp.dot(
        hidden_ref[...], down_ref[...], preferred_element_type=F32
    ).astype(BF16)
    pack_side(plan, terms_ref, 1 - lax.axis_index("hidden"), theirs_ref)


def project(plan, hidden, down_weight):
    units = down_weight.shape[0]
    return call(
        functools.partial(project_body, plan),
        [
            shaped(plan.rows, plan.width, dtype=BF16),
            shaped(plan.chips, plan.packed, LANES, dtype=BF16),
        ],
        (hidden, down_weight),
        flops=2 * plan.rows * plan.width * units,
        moved=down_weight.size * 2,
    )


def pack_own_body(plan, terms_ref, mine_ref):
    pack_side(plan, terms_ref, lax.axis_index("hidden"), mine_ref)


def pack_own(plan, terms):
    return call(
        functools.partial(pack_own_body, plan),
        shaped(plan.chips, plan.packed, LANES, dtype=BF16),
        (terms,),
        moved=terms.size * 4,
    )


def add_pair_body(plan, first_ref, mine_ref, theirs_ref, kept_ref, sent_ref):
    me = lax.axis_index("latent")
    sent_ref[0] = first_ref[0]
    for place, column in enumerate(plan.columns):
        kept, sent = me ^ column, me ^ column ^ 1
        kept_ref[place] = mine_ref[kept].astype(F32) + theirs_ref[kept].astype(F32)
        sent_ref[1 + place] = (
            mine_ref[sent].astype(F32) + theirs_ref[sent].astype(F32)
        ).astype(BF16)


def add_pair(plan, first, mine, theirs):
    count, dims = len(plan.columns), mine.shape[1:]
    return call(
        functools.partial(add_pair_body, plan),
        [shaped(count, *dims), shaped(1 + count, *dims, dtype=BF16)],
        (first, mine, theirs),
        moved=mine.size * 10,
    )


def add_sent_body(mine_ref, theirs_ref, first_ref, rest_ref):
    total = (mine_ref[...] + theirs_ref[...].astype(F32)).astype(BF16)
    first_ref[...] = total[:1]
    rest_ref[...] = total[1:]


def add_sent(plan, mine, theirs):
    count, *dims = mine.shape
    return call(
        add_sent_body,
        [shaped(1, *dims, dtype=BF16), shaped(count - 1, *dims, dtype=BF16)],
        (mine, theirs),
        moved=mine.size * 10,
    )


def add_across_body(mine_ref, theirs_ref, got_ref, *sent_refs):
    for place, out_ref in enumerate(sent_refs):
        total = mine_ref[1 + place] + theirs_ref[1 + place] + got_ref[place].astype(F32)
        out_ref[0] = total.astype(BF16)


def add_across(plan, mine, theirs, got):
    return call(
        add_across_body,
        [shaped(1, *mine.shape[1:], dtype=BF16)] * got.shape[0],
        (mine, theirs, got),
        moved=mine.size * 10,
    )


def column_total(mine_ref, theirs_ref, *refs):
    total = mine_ref[0] + theirs_ref[0]
    for ref in refs:
        total = total + ref[0].astype(F32)
    return total.astype(BF16)


def add_column_body(*refs):
    *sources, block_ref, more_ref = refs
    block_ref[0] = column_total(*sources)
    more_ref[...] = sources[-1][1:]


def add_column(plan, mine, theirs, got, first):
    dims = mine.shape[1:]
    return call(
        add_column_body,
        [shaped(1, *dims, dtype=BF16), shaped(first.shape[0] - 1, *dims, dtype=BF16)],
        (mine, theirs, *reversed(got), first),
        moved=mine.size * 8,
    )


def add_with_output_body(plan, count, *refs):
    total = column_total(*refs[:count])
    first_ref, out_ref, block_ref, message_ref, kept_ref = refs[count - 1 : count + 4]
    block_ref[0] = total
    message_ref[0, : plan.chunk, :] = total
    near = plan.doubling[0]
    halves = [[], []]
    for place, column in enumerate(plan.columns):
        halves[column & near != 0].append(out_ref[place] + first_ref[1 + place].astype(F32))
    for index, (kept, sent) in enumerate(zip(*halves)):
        kept_ref[index] = kept
        start = plan.chunk + index * plan.packed
        message_ref[0, start : start + plan.packed, :] = sent.astype(BF16)


def add_with_output(plan, mine, theirs, got, first, kept):
    half = len(plan.columns) // 2
    return call(
        functools.partial(add_with_output_body, plan, 3 + len(got)),
        [
            shaped(1, plan.chunk, LANES, dtype=BF16),
            shaped(1, plan.chunk + half * plan.packed, LANES, dtype=BF16),
            shaped(half, plan.packed, LANES),
        ],
        (mine, theirs, *reversed(got), first, kept),
        moved=mine.size * 12,
    )


def halve_body(rows, skip, kept_ref, got_ref, left_ref, sent_ref):
    half = left_ref.shape[0]
    for index in range(2 * half):
        start = skip + index * rows
        total = kept_ref[index] + got_ref[0, start : start + rows, :].astype(F32)
        if index < half:
            left_ref[index] = total
        else:
            begin = (index - half) * rows
            sent_ref[0, begin : begin + rows, :] = total.astype(BF16)


def halve(plan, kept, got, skip):
    half, rows = kept.shape[0] // 2, plan.packed
    return call(
        functools.partial(halve_body, rows, skip),
        [shaped(half, rows, LANES), shaped(1, half * rows, LANES, dtype=BF16)],
        (kept, got),
        moved=kept.size * 10,
    )


def stack_body(places, *refs):
    count = len(places)
    stack_ref, *rest_refs = refs[count:]
    rows = stack_ref.shape[1]
    for place, ref in zip(places, refs):
        stack_ref[place] = ref[0, :rows, :]
        for rest_ref in rest_refs:
            if place:
                rest_ref[place - 1] = ref[0, :rows, :]


def stack_up(plan, block, got, with_rest=False):
    dims = block.shape[1:]
    operands = [block, *got]
    places = list(range(len(operands)))
    if with_rest:
        operands, places = operands[::-1], places[::-1]
    outs = [shaped(1 + len(got), *dims, dtype=BF16), shaped(len(got), *dims, dtype=BF16)]
    return call(
        functools.partial(stack_body, places),
        outs if with_rest else outs[0],
        operands,
        moved=block.size * 16,
    )


def join_body(*refs):
    *sources, joined_ref = refs
    start = 0
    for ref in sources:
        joined_ref[start : start + ref.shape[0]] = ref[...]
        start += ref.shape[0]


def join(plan, *stacks):
    count = sum(one.shape[0] for one in stacks)
    return call(
        join_body,
        shaped(count, *stacks[0].shape[1:], dtype=BF16),
        stacks,
        moved=count * stacks[0].size,
    )


def double(plan, stack, bit):
    return join(plan, stack, partner_swap(stack, bit))


def add_message_body(plan, first_ref, here_ref, there_ref, stack_ref, message_ref):
    message_ref[0] = first_ref[0]
    half = here_ref.shape[0]
    for index, column in enumerate(plan.doubled):
        block = here_ref[index] if index < half else there_ref[index - half]
        place = plan.columns.index(column)
        stack_ref[place] = block
        message_ref[1 + place] = block


def add_message(plan, first, here, there):
    count, dims = len(plan.columns), first.shape[1:]
    return call(
        functools.partial(add_message_body, plan),
        [shaped(count, *dims, dtype=BF16), shaped(1 + count, *dims, dtype=BF16)],
        (first, here, there),
        moved=first.size * 40,
    )


def line_up_body(plan, *refs):
    for chip, block in plan.side_blocks(refs[:-1]):
        refs[-1][chip] = block


def line_up(plan, stack, *crossed):
    return call(
        functools.partial(line_up_body, plan),
        shaped(plan.chips, *stack.shape[1:], dtype=BF16),
        (stack, *crossed),
        moved=stack.size * 8,
    )


def finish_output_body(plan, kept_ref, got_ref, out_ref):
    total = kept_ref[0] + got_ref[0].astype(F32)
    out_ref[...] = unpack_block(plan, total).astype(BF16)


def finish_output(plan, kept, got):
    return call(
        functools.partial(finish_output_body, plan),
        shaped(plan.rows, plan.own, dtype=BF16),
        (kept, got),
        moved=kept.size * 8,
    )


def prepare_body(plan, scaled_ref, inputs_ref, gain_ref, inverse_ref, factor_ref, slope_ref, base_ref):
    gain = gain_ref[...]
    inverse = inverse_ref[...]
    rebuilt = scaled_ref[...].astype(F32) / gain
    factor_ref[...] = inverse * gain
    slope_ref[...] = rebuilt * (inverse * inverse * inverse / plan.width)
    base_ref[...] = rebuilt - inputs_ref[...].astype(F32)


def prepare(plan, scaled, inputs, gain, inverse):
    return call(
        functools.partial(prepare_body, plan),
        [shaped(plan.rows, plan.width)] * 3,
        (scaled, inputs, gain, inverse),
        moved=scaled.size * 16,
    )


def dictionary_body(plan, pieces, own_ref, other_ref, scaled_ref, factor_ref, slope_ref, base_ref, inputs_ref, latents_ref, dict_ref, out_hbm, full, out_ref, out_sems):
    core = lax.axis_index("hidden")
    join_half(plan, own_ref, core * plan.half, full)
    join_half(plan, other_ref, (1 - core) * plan.half, full)
    grad = full[...].astype(F32)
    inner_row = jnp.sum(grad * scaled_ref[...].astype(F32), axis=1, keepdims=True)
    inputs = inputs_ref[...]
    rebuilt_grad = (
        grad * factor_ref[...] - inner_row * slope_ref[...] + base_ref[...]
    ).astype(BF16)
    latents = latents_ref[...]
    latent_grad = lax.dot_general(
        rebuilt_grad, dict_ref[...], ACROSS, preferred_element_type=F32
    )
    preact_grad = jnp.where(latents.astype(F32) > 0.0, latent_grad, 0.0).astype(BF16)
    left = jnp.concatenate([latents, preact_grad], axis=0)
    right = jnp.concatenate([rebuilt_grad, inputs], axis=0)
    size = plan.width // pieces
    writes = []
    for piece in range(pieces):
        span = slice(piece * size, (piece + 1) * size)
        out_ref[:, span] = lax.dot_general(
            left, right[:, span], DOWNWARD, preferred_element_type=F32
        ).astype(BF16)
        one = pltpu.make_async_copy(
            out_ref.at[:, span], out_hbm.at[:, span], out_sems.at[piece]
        )
        one.start()
        writes.append(one)
    for one in writes:
        one.wait()


def dictionary_step(plan, own, other, scaled, prepared, inputs, latents, dictionary):
    units = dictionary.shape[0]
    pieces = plan.tiles
    return call(
        functools.partial(dictionary_body, plan, pieces),
        shaped(*dictionary.shape, dtype=BF16),
        (own, other, scaled, *prepared, inputs, latents, dictionary),
        [
            pltpu.VMEM((plan.rows, plan.width), BF16),
            pltpu.VMEM(dictionary.shape, BF16),
            pltpu.SemaphoreType.DMA((pieces,)),
        ],
        out_specs=HBM,
        flops=6 * plan.rows * plan.width * units,
        moved=dictionary.size * 4,
    )


def swap(value):
    size = lax.axis_size("hidden")
    return lax.ppermute(value, "hidden", [(i, (i + 1) % size) for i in range(size)])


def partner_swap(value, bits):
    size = lax.axis_size("latent")
    return lax.ppermute(value, "latent", [(i, i ^ bits) for i in range(size)])


def cross(value):
    return partner_swap(value, 1)


def to_column(plan, blocks):
    pairs = list(zip(blocks, plan.columns[1:]))
    got = [partner_swap(one, column) for one, column in reversed(pairs)]
    return got[::-1]


def to_all_columns(plan, block):
    return [partner_swap(block, column) for column in plan.columns[1:]]


def tie(*values):
    return lax.optimization_barrier(values)


def per_device(
    input_codes,
    cotangent_codes,
    dictionary,
    encoder_bias,
    decoder_bias,
    norm_gain,
    gate_weight,
    up_weight,
    down_weight,
):
    plan = Plan(
        lax.axis_size("latent"), lax.axis_size("hidden"), input_codes.shape[0], input_codes.shape[1]
    )
    if not plan.fits():
        return per_device_plain(
            input_codes,
            cotangent_codes,
            dictionary,
            encoder_bias,
            decoder_bias,
            norm_gain,
            gate_weight,
            up_weight,
            down_weight,
        )
    vectors = jnp.concatenate([encoder_bias, decoder_bias, norm_gain]).reshape(1, -1)
    codes = jnp.stack([input_codes, cotangent_codes])
    values = (codes.astype(F32) * CODE_STEP).astype(BF16)
    block, cotangent = pack_values(plan, values)
    stack = stack_up(plan, block, to_all_columns(plan, block))
    stack, vectors, late_dictionary, cotangent = tie(stack, vectors, dictionary, cotangent)
    stack_other, crossed = swap(stack), cross(stack)
    encoder = bring_encoder(plan, late_dictionary, vectors)
    cotangent = double(plan, cotangent, plan.doubling[-1])
    stack_other, crossed, encoder, cotangent = tie(stack_other, crossed, encoder, cotangent)
    brought, bias, decoder, gain = encoder
    inputs, latents, kept, sent = encode(
        plan, (stack, crossed), (stack_other, swap(crossed)), brought, bias, gain
    )
    sent, kept = swap(sent), swap(kept)
    own_kept, own_sent = decode_own(plan, latents, brought, decoder, gain)
    sent_first, sent_rest = add_sent(plan, own_sent, sent)
    sent_rest, cotangent = tie(sent_rest, cotangent)
    for bit in reversed(plan.doubling[1:-1]):
        cotangent = double(plan, cotangent, bit)
    there = partner_swap(cotangent, plan.doubling[0])
    sent = add_across(plan, own_kept, kept, cross(sent_rest))
    sent, sent_first, cotangent, there = tie(sent, sent_first, cotangent, there)
    cotangent, sent_first = add_message(plan, sent_first, cotangent, there)
    got, first = to_column(plan, sent), cross(sent_first)
    block, crossed = add_column(plan, own_kept, kept, got, first)
    cotangent_own = (cotangent, crossed)
    hidden_grad = back_project(
        plan, cotangent_own, [swap(one) for one in cotangent_own], down_weight
    )
    stack = stack_up(plan, block, to_all_columns(plan, block))
    stack_other, crossed = swap(stack), cross(stack)
    stack_other, crossed, hidden_grad = tie(stack_other, crossed, hidden_grad)
    terms = mlp_first(plan, line_up(plan, stack, crossed), gate_weight, up_weight, gain)
    scaled_other = line_up(plan, stack_other, swap(crossed))
    scaled, inverse, hidden, gate_grad, up_grad, kept, sent = mlp(
        plan, scaled_other, gate_weight, up_weight, gain, hidden_grad, terms
    )
    sent, kept = swap(sent), swap(kept)
    own_kept, own_sent = mlp_own(plan, gate_grad, up_grad, gate_weight, up_weight)
    out_terms, out_theirs = project(plan, hidden, down_weight)
    sent_first, sent_rest = add_sent(plan, own_sent, sent)
    sent_first, sent_rest, out_terms, out_theirs = tie(
        sent_first, sent_rest, out_terms, out_theirs
    )
    crossed = cross(sent_rest)
    out_theirs = swap(out_theirs)
    out_kept, sent_first = add_pair(plan, sent_first, pack_own(plan, out_terms), out_theirs)
    sent = add_across(plan, own_kept, kept, crossed)
    sent, sent_first, out_kept = tie(sent, sent_first, out_kept)
    got = to_column(plan, sent)
    first = cross(sent_first)
    block, message, out_kept = add_with_output(plan, own_kept, kept, got, first, out_kept)
    got = to_column(plan, [message] + [block] * (len(plan.columns) - 2))
    got = list(tie(got[-1], *got[:-1]))
    got = got[1:] + got[:1]
    stack = stack_up(plan, block, got)
    out_kept, out_sent = halve(plan, out_kept, got[0], plan.chunk)
    stack, scaled_late, inputs_late, out_sent = tie(stack, scaled, inputs, out_sent)
    stack_other, crossed = swap(stack), cross(stack)
    prepared = prepare(plan, scaled_late, inputs_late, gain, inverse)
    for bit in reversed(plan.doubling[2:]):
        out_kept, out_sent = halve(plan, out_kept, partner_swap(out_sent, bit), 0)
    out_got = partner_swap(out_sent, plan.doubling[1])
    stack_other, crossed, out_got = tie(stack_other, crossed, out_got)
    block_output = finish_output(plan, out_kept, out_got)
    grad_own = line_up(plan, stack, crossed)
    grad_other = line_up(plan, stack_other, swap(crossed))
    dictionary_grad = dictionary_step(
        plan, grad_own, grad_other, scaled, prepared, inputs, latents, brought
    )
    return (block_output, dictionary_grad)


def per_device_plain(
    input_codes,
    cotangent_codes,
    dictionary,
    encoder_bias,
    decoder_bias,
    norm_gain,
    gate_weight,
    up_weight,
    down_weight,
):
    own_width = input_codes.shape[1]
    model_width = own_width * lax.axis_size(("latent", "hidden"))
    cotangent_local = (cotangent_codes.astype(jnp.float32) * CODE_STEP).astype(jnp.bfloat16)
    inputs_local = (input_codes.astype(jnp.float32) * CODE_STEP).astype(jnp.bfloat16)
    inputs = lax.all_gather(inputs_local, ("latent", "hidden"), axis=1, tiled=True)
    preact = (
        lax.dot_general(inputs, dictionary, ACROSS, preferred_element_type=jnp.float32)
        + encoder_bias
    )
    latents = jnp.maximum(preact, 0.0).astype(jnp.bfloat16)
    partial_value = jnp.dot(latents, dictionary, preferred_element_type=jnp.float32)
    rebuilt = lax.psum(partial_value, ("latent", "hidden")) + decoder_bias
    inverse = lax.rsqrt(
        jnp.sum(rebuilt * rebuilt, axis=1, keepdims=True) / model_width + NORM_EPSILON
    )
    normed = (rebuilt * inverse * norm_gain).astype(jnp.bfloat16)
    target = inputs.astype(jnp.float32)
    gate_proj = lax.dot_general(normed, gate_weight, ACROSS, preferred_element_type=jnp.float32)
    up_proj = lax.dot_general(normed, up_weight, ACROSS, preferred_element_type=jnp.float32)
    gelu_value, gelu_slope = gelu_parts(gate_proj)
    hidden = (gelu_value * up_proj).astype(jnp.bfloat16)
    output_terms = jnp.dot(hidden, down_weight, preferred_element_type=jnp.float32)
    block_output = lax.psum_scatter(
        output_terms, ("latent", "hidden"), scatter_dimension=1, tiled=True
    ).astype(jnp.bfloat16)
    hidden_grad = lax.dot_general(
        lax.all_gather(cotangent_local, ("latent", "hidden"), axis=1, tiled=True),
        down_weight,
        ACROSS,
        preferred_element_type=jnp.float32,
    )
    gate_grad = (hidden_grad * up_proj * gelu_slope).astype(jnp.bfloat16)
    up_grad = (hidden_grad * gelu_value).astype(jnp.bfloat16)
    partial_grad = jnp.dot(gate_grad, gate_weight, preferred_element_type=jnp.float32) + jnp.dot(
        up_grad, up_weight, preferred_element_type=jnp.float32
    )
    scaled = lax.psum(partial_grad, ("latent", "hidden")) * norm_gain
    inner_row = jnp.sum(scaled * rebuilt, axis=1, keepdims=True)
    inverse_cube = inverse * inverse * inverse
    rebuilt_grad = (
        inverse * scaled - inverse_cube * rebuilt * (inner_row / model_width) + (rebuilt - target)
    ).astype(jnp.bfloat16)
    latent_grad = lax.dot_general(
        rebuilt_grad, dictionary, ACROSS, preferred_element_type=jnp.float32
    )
    preact_grad = jnp.where(preact > 0.0, latent_grad, 0.0).astype(jnp.bfloat16)
    dictionary_grad = lax.dot_general(
        latents, rebuilt_grad, DOWNWARD, preferred_element_type=jnp.float32
    ) + lax.dot_general(preact_grad, inputs, DOWNWARD, preferred_element_type=jnp.float32)
    return (block_output, dictionary_grad.astype(jnp.bfloat16))


def solution(mesh):
    in_specs = (
        P("groups", ("latent", "hidden")),
        P("groups", ("latent", "hidden")),
        P(("latent", "hidden"), None),
        P(("latent", "hidden")),
        P(),
        P(),
        P(("latent", "hidden"), None),
        P(("latent", "hidden"), None),
        P(("latent", "hidden"), None),
    )
    out_specs = (P("groups", ("latent", "hidden")), P(("latent", "hidden"), "groups"))
    return jax.shard_map(
        per_device, mesh=mesh, in_specs=in_specs, out_specs=out_specs, check_vma=False
    )
```
